32 devices in a mesh: dp: 8 (over z, x), grp: 4 (over y, core).
Axes of the slice: x: 2, y: 2, z: 4, core: 2. Of those that a mesh axis runs over, the one named last changes fastest.
Arguments:
- tokens: bfloat16 [8192, 1024], P(('dp', 'grp')), may hold values from -6 to 6
- memory: bfloat16 [2048, 1024], P(('dp', 'grp')), may hold values from -6 to 6
- cotangent: bfloat16 [8192, 1024], P(('dp', 'grp')), may hold values from -6 to 6
- bucket: int32 [8], P('dp'), may hold values from 0 to 2
- gain_self: bfloat16 [1024], replicated, may hold values from 0.099609375 to 1.8984375
- self_query: bfloat16 [1024, 1024], replicated, may hold values from -0.046875 to 0.046875
- self_key: bfloat16 [1024, 512], replicated, may hold values from -0.1875 to 0.1875
- self_value: bfloat16 [1024, 512], replicated, may hold values from -0.1875 to 0.1875
- self_out: bfloat16 [1024, 1024], replicated, may hold values from -0.75 to 0.75
- rel_bias: bfloat16 [32, 16], replicated, may hold values from -5 to 5
- gain_cross: bfloat16 [1024], replicated, may hold values from 0.099609375 to 1.8984375
- cross_query: bfloat16 [1024, 1024], replicated, may hold values from -0.046875 to 0.046875
- cross_key: bfloat16 [1024, 512], replicated, may hold values from -0.1875 to 0.1875
- cross_value: bfloat16 [1024, 512], replicated, may hold values from -0.1875 to 0.1875
- cross_out: bfloat16 [1024, 1024], replicated, may hold values from -0.75 to 0.75
- gain_ffn: bfloat16 [1024], replicated, may hold values from 0.099609375 to 1.8984375
- ffn_gate: bfloat16 [1024, 2816], replicated, may hold values from -0.1875 to 0.1875
- ffn_up: bfloat16 [1024, 2816], replicated, may hold values from -0.1875 to 0.1875
- ffn_down: bfloat16 [2816, 1024], replicated, may hold values from -0.109375 to 0.109375
Outputs:
- layer_out: bfloat16 [8192, 1024], P(('dp', 'grp'))
- grad_tokens: bfloat16 [8192, 1024], P(('dp', 'grp'))
- grad_memory: bfloat16 [2048, 1024], P(('dp', 'grp'))
- grad_gain_self: float32 [1024], P(('dp', 'grp'))
- grad_self_query: float32 [1024, 1024], P(('dp', 'grp'))
- grad_self_key: float32 [1024, 512], P(('dp', 'grp'))
- grad_self_value: float32 [1024, 512], P(('dp', 'grp'))
- grad_self_out: float32 [1024, 1024], P(('dp', 'grp'))
- grad_rel_bias: float32 [512], P(('dp', 'grp'))
- grad_gain_cross: float32 [1024], P(('dp', 'grp'))
- grad_cross_query: float32 [1024, 1024], P(('dp', 'grp'))
- grad_cross_key: float32 [1024, 512], P(('dp', 'grp'))
- grad_cross_value: float32 [1024, 512], P(('dp', 'grp'))
- grad_cross_out: float32 [1024, 1024], P(('dp', 'grp'))
- grad_gain_ffn: float32 [1024], P(('dp', 'grp'))
- grad_ffn_gate: float32 [1024, 2816], P(('dp', 'grp'))
- grad_ffn_up: float32 [1024, 2816], P(('dp', 'grp'))
- grad_ffn_down: float32 [2816, 1024], P(('dp', 'grp'))
The draws below stay inside these ranges and needn't reach their ends.
All inputs are finite; a program needn't handle non-finite values.
Results may differ from the reference program's by a relative error of at most 0.04.
Values may be sent and summed in bfloat16 or wider, within the bound.
No kernel may reach another device: no remote copies, remote signals or barrier semaphores. Data moves between devices by JAX's collectives and lax.ppermute only.
A program may use at most 256 MiB of HBM per device.

```python
import jax
import jax.numpy as jnp
from jax import lax

D = 1024
HEADS = 16
HEAD = 64
KV = 8
FF = 2816
BUCKETS = 32
SHORT = 1024
RATIO = 4
BLOCK = 512
TOKENS = 8192
MEMORY = 2048
N_DP = 8


def with_ends(array, stream_key, low, high):
    shape = array.shape
    spot = [jax.random.randint(jax.random.fold_in(stream_key, axis), (), 0, shape[axis]) for axis in range(len(shape))]
    array = array.at[tuple(spot)].set(low)
    longest = shape.index(max(shape))
    spot[longest] = (spot[longest] + 1) % shape[longest]
    return array.at[tuple(spot)].set(high)


def levels(key, extent, split, least, high):
    loudness, own = 1.0, jax.random.fold_in(key, 6)
    for axis_at, parts in split:
        steps = jnp.exp(jax.random.uniform(jax.random.fold_in(own, axis_at), (parts,), jnp.float32, least / len(split), high / len(split)))
        loudness = loudness * jnp.repeat(steps, extent[axis_at] // parts).reshape([-1 if axis == axis_at else 1 for axis in range(len(extent))])
    return loudness


def normal_values(key, shape, scale, most, split=(), held_as=jnp.bfloat16):
    result = scale * jax.random.normal(key, shape, jnp.float32)
    if split:
        result = result * levels(key, shape, split, -0.22, 0.18)
    return jnp.clip(result, -most, most).astype(held_as)


def setup_inputs(seed: int = 0) -> dict:
    key_of = jax.random.split(jax.random.key(seed), 20)
    tokens = normal_values(key_of[0], (TOKENS, D), 1.0, 6.0, ((0, 32),))
    memory = normal_values(key_of[1], (MEMORY, D), 1.0, 6.0, ((0, 32),))
    cotangent = normal_values(key_of[2], (TOKENS, D), 1.0, 6.0, ((0, 32),))
    bucket = with_ends(jax.random.randint(key_of[3], (N_DP,), 0, 3), jax.random.fold_in(key_of[3], 1), 0, 2).astype(jnp.int32)
    gain_self = jnp.clip(1.0 + 0.18 * jax.random.normal(key_of[4], (D,), jnp.float32), 0.099609375, 1.8984375).astype(jnp.bfloat16)
    self_query = normal_values(key_of[5], (D, HEADS * HEAD), (16 * D) ** -0.5, 0.046875)
    self_key = normal_values(key_of[6], (D, KV * HEAD), D ** -0.5, 0.1875)
    self_value = normal_values(key_of[7], (D, KV * HEAD), D ** -0.5, 0.1875)
    self_out = normal_values(key_of[8], (HEADS * HEAD, D), (HEADS * HEAD // 16) ** -0.5, 0.75)
    rel_bias = normal_values(key_of[9], (BUCKETS, HEADS), 1.0, 5.0)
    gain_cross = jnp.clip(1.0 + 0.18 * jax.random.normal(key_of[10], (D,), jnp.float32), 0.099609375, 1.8984375).astype(jnp.bfloat16)
    cross_query = normal_values(key_of[11], (D, HEADS * HEAD), (16 * D) ** -0.5, 0.046875)
    cross_key = normal_values(key_of[12], (D, KV * HEAD), D ** -0.5, 0.1875)
    cross_value = normal_values(key_of[13], (D, KV * HEAD), D ** -0.5, 0.1875)
    cross_out = normal_values(key_of[14], (HEADS * HEAD, D), (HEADS * HEAD // 16) ** -0.5, 0.75)
    gain_ffn = jnp.clip(1.0 + 0.18 * jax.random.normal(key_of[15], (D,), jnp.float32), 0.099609375, 1.8984375).astype(jnp.bfloat16)
    ffn_gate = normal_values(key_of[16], (D, FF), D ** -0.5, 0.1875)
    ffn_up = normal_values(key_of[17], (D, FF), D ** -0.5, 0.1875)
    ffn_down = normal_values(key_of[18], (FF, D), FF ** -0.5, 0.109375)
    return {"tokens": tokens, "memory": memory, "cotangent": cotangent, "bucket": bucket, "gain_self": gain_self, "self_query": self_query, "self_key": self_key, "self_value": self_value, "self_out": self_out, "rel_bias": rel_bias, "gain_cross": gain_cross, "cross_query": cross_query, "cross_key": cross_key, "cross_value": cross_value, "cross_out": cross_out, "gain_ffn": gain_ffn, "ffn_gate": ffn_gate, "ffn_up": ffn_up, "ffn_down": ffn_down}


@jax.custom_vjp
def low(v):
    return lax.optimization_barrier(v.astype(jnp.bfloat16)).astype(jnp.float32)

@jax.custom_vjp
def low_back(v):
    return v

def low_keep(v):
    return (low(v), None)

def low_pass(kept, grad):
    return (grad,)

def back_keep(v):
    return (v, None)

def back_low(kept, grad):
    return (low(grad),)
low.defvjp(low_keep, low_pass)
low_back.defvjp(back_keep, back_low)
EPSILON = 1e-06
NEGATIVE = -1e+30
THRESHOLDS = (19, 21, 24, 27, 31, 35, 40, 46, 52, 59, 67, 77, 87, 99, 113)
HIGHEST = lax.Precision.HIGHEST

def rel_bucket(distance):
    distance = jnp.maximum(distance, 0)
    beyond = 16 + sum(((distance >= border).astype(jnp.int32) for border in THRESHOLDS))
    return jnp.where(distance < 16, distance, beyond).astype(jnp.int32)

def doc_length(bucket_id, group_rows):
    halved = jnp.right_shift(jnp.int32(group_rows), bucket_id.astype(jnp.int32))
    return jnp.minimum(group_rows, jnp.maximum(SHORT, halved)).astype(jnp.int32)

def product(left_op, right_op):
    return jnp.dot(left_op, right_op, precision=HIGHEST, preferred_element_type=jnp.float32)

def rms_norm(hidden, gain_vec):
    return hidden * lax.rsqrt(lax.optimization_barrier(jnp.mean(hidden * hidden, axis=-1, keepdims=True)) + EPSILON) * gain_vec

def group_layer(token_rows, memory_rows, bucket_id, weights):
    gain_self, self_query, self_key, self_value, self_out, rel_bias, gain_cross, cross_query, cross_key, cross_value, cross_out, gain_ffn, ffn_gate, ffn_up, ffn_down = weights
    group_rows = token_rows.shape[0]
    mem_rows = memory_rows.shape[0]
    length = doc_length(bucket_id, group_rows)
    mem_length = length // RATIO
    group_ratio = HEADS // KV
    blocks = group_rows // BLOCK
    positions = jnp.arange(group_rows, dtype=jnp.int32)
    documents = positions // length
    mem_docs = jnp.arange(mem_rows, dtype=jnp.int32) // mem_length
    starts = jnp.arange(blocks, dtype=jnp.int32) * BLOCK
    normed_one = low(rms_norm(token_rows, gain_self))
    queries = low_back(low(product(normed_one, self_query))).reshape(blocks, BLOCK, HEADS, HEAD)
    key_heads = jnp.repeat(low_back(low(product(normed_one, self_key))).reshape(group_rows, KV, HEAD), group_ratio, axis=1)
    value_heads = jnp.repeat(low_back(low(product(normed_one, self_value))).reshape(group_rows, KV, HEAD), group_ratio, axis=1)

    def self_block(block_args):
        q_block, first_row = block_args
        q_rows = first_row + jnp.arange(BLOCK, dtype=jnp.int32)
        distance = q_rows[:, None] - positions[None, :]
        scores = jnp.einsum('ahd,chd->hac', q_block, key_heads, precision=HIGHEST)
        scores = scores + jnp.transpose(jnp.take(rel_bias, rel_bucket(distance), axis=0), (2, 0, 1))
        scores = low_back(scores)
        allowed = (distance >= 0) & ((q_rows // length)[:, None] == documents[None, :])
        soft_low = low(jax.nn.softmax(jnp.where(allowed[None], scores, NEGATIVE), axis=-1))
        return jnp.einsum('hac,chd->ahd', soft_low, value_heads, precision=HIGHEST)
    attended = lax.map(jax.checkpoint(self_block), (queries, starts)).reshape(group_rows, HEADS * HEAD)
    attended = low_back(low(attended))
    hidden_mid = token_rows + low_back(product(attended, self_out))
    normed_two = low(rms_norm(hidden_mid, gain_cross))
    cross_q = low_back(low(product(normed_two, cross_query))).reshape(blocks, BLOCK, HEADS, HEAD)
    mem_keys = jnp.repeat(low_back(low(product(memory_rows, cross_key))).reshape(mem_rows, KV, HEAD), group_ratio, axis=1)
    mem_values = jnp.repeat(low_back(low(product(memory_rows, cross_value))).reshape(mem_rows, KV, HEAD), group_ratio, axis=1)

    def cross_block(block_args):
        q_block, first_row = block_args
        q_docs = (first_row + jnp.arange(BLOCK, dtype=jnp.int32)) // length
        scores = low_back(jnp.einsum('ahd,chd->hac', q_block, mem_keys, precision=HIGHEST))
        allowed = q_docs[:, None] == mem_docs[None, :]
        soft_low = low(jax.nn.softmax(jnp.where(allowed[None], scores, NEGATIVE), axis=-1))
        return jnp.einsum('hac,chd->ahd', soft_low, mem_values, precision=HIGHEST)
    crossed = lax.map(jax.checkpoint(cross_block), (cross_q, starts)).reshape(group_rows, HEADS * HEAD)
    crossed = low_back(low(crossed))
    hidden_late = hidden_mid + low_back(product(crossed, cross_out))
    normed_three = low(rms_norm(hidden_late, gain_ffn))
    gate_pre = low_back(product(normed_three, ffn_gate))
    up_pre = low_back(product(normed_three, ffn_up))
    inner_act = low_back(low(jax.nn.gelu(gate_pre, approximate=True) * up_pre))
    return hidden_late + low_back(product(inner_act, ffn_down))

def reference(tokens, memory, cotangent, bucket, gain_self, self_query, self_key, self_value, self_out, rel_bias, gain_cross, cross_query, cross_key, cross_value, cross_out, gain_ffn, ffn_gate, ffn_up, ffn_down):
    weights = tuple((weight_in.astype(jnp.float32) for weight_in in (gain_self, self_query, self_key, self_value, self_out, rel_bias, gain_cross, cross_query, cross_key, cross_value, cross_out, gain_ffn, ffn_gate, ffn_up, ffn_down)))
    group_rows = tokens.shape[0] // N_DP
    mem_rows = memory.shape[0] // N_DP
    token_groups = tokens.astype(jnp.float32).reshape(N_DP, group_rows, D)
    mem_groups = memory.astype(jnp.float32).reshape(N_DP, mem_rows, D)

    def forward(token_in, memory_in, weight_set):

        def one_group(group_args):
            return group_layer(group_args[0], group_args[1], group_args[2], weight_set)
        return lax.map(jax.checkpoint(one_group), (token_in, memory_in, bucket))
    layer_out, pullback = jax.vjp(forward, token_groups, mem_groups, weights)
    grad_tokens, grad_memory, grad_weights = pullback(cotangent.astype(jnp.float32).reshape(N_DP, group_rows, D))
    return (layer_out.reshape(tokens.shape).astype(jnp.bfloat16), grad_tokens.reshape(tokens.shape).astype(jnp.bfloat16), grad_memory.reshape(memory.shape).astype(jnp.bfloat16), grad_weights[0], grad_weights[1], grad_weights[2], grad_weights[3], grad_weights[4], grad_weights[5].reshape(BUCKETS * HEADS), grad_weights[6], grad_weights[7], grad_weights[8], grad_weights[9], grad_weights[10], grad_weights[11], grad_weights[12], grad_weights[13], grad_weights[14])
```

```python
import functools

import jax
import jax.numpy as jnp
from jax import lax
from jax.experimental import pallas as pl
from jax.experimental.pallas import tpu as pltpu
from jax.sharding import PartitionSpec as P

SHORT = 1024
RATIO = 4
BUCKETS = 32
HEADS = 16
EPSILON = 1e-06
THRESHOLDS = (19, 21, 24, 27, 31, 35, 40, 46, 52, 59, 67, 77, 87, 99, 113)
CORES = 2
BF16 = jnp.bfloat16
F32 = jnp.float32
NEGATIVE = -1e30
HEAD = 64
TILE = 256
NEAR = 128
VMEM_LIMIT = 56 * 1024 * 1024


def dot(a, b):
    return jnp.dot(a, b, preferred_element_type=jnp.float32)


def place_rows(half, at):
    zero = jnp.zeros_like(half)
    return jnp.concatenate([half, zero] if at == 0 else [zero, half], axis=0)


def place_lanes(pair, source, at):
    lane = lax.broadcasted_iota(jnp.int32, pair.shape, 1)
    if source != at:
        pair = jnp.concatenate([pair[:, HEAD:], pair[:, :HEAD]], axis=1)
    return jnp.where((lane < HEAD) == (at == 0), pair, jnp.zeros_like(pair))


def near_tiles(table_row):
    skewed = pltpu.roll(jnp.broadcast_to(table_row, (NEAR, 2 * NEAR)), 0, 1, stride=1, stride_axis=0)
    key_at = lax.broadcasted_iota(jnp.int32, (NEAR, NEAR), 0)
    row_at = lax.broadcasted_iota(jnp.int32, (NEAR, NEAR), 1)
    return (jnp.where(key_at <= row_at, skewed[:, :NEAR], NEGATIVE), skewed[:, NEAR:])


def add_corner(scores, tile):
    rows = scores.shape[0]
    low_rows = scores[rows - NEAR :]
    low_rows = jnp.concatenate([low_rows[:, :NEAR] + tile, low_rows[:, NEAR:]], axis=1)
    return jnp.concatenate([scores[: rows - NEAR], low_rows], axis=0)


def add_diagonal(scores, at_zero, at_one):
    rows = scores.shape[0]
    first = scores[rows - TILE : rows - NEAR]
    second = scores[rows - NEAR :]
    last = [
        jnp.concatenate([first[:, :NEAR] + at_zero, first[:, NEAR:] + at_one], axis=1),
        jnp.concatenate([jnp.full((NEAR, NEAR), NEGATIVE, jnp.float32), second[:, NEAR:] + at_zero], axis=1),
    ]
    if rows > TILE:
        last = [add_corner(scores[: rows - TILE], at_one)] + last
    return jnp.concatenate(last, axis=0)


def by_distance(near):
    level = near[:8]
    for first in range(8, NEAR, 8):
        level = level + pltpu.roll(near[first : first + 8], 2 * NEAR - first, 1)
    row = lax.broadcasted_iota(jnp.int32, level.shape, 0)
    for bit in (1, 2, 4):
        level = jnp.where(row & bit > 0, pltpu.roll(level, 2 * NEAR - bit, 1), level)
    return jnp.sum(level, axis=0, keepdims=True)


def self_forward_kernel(valid_ref, table_ref, q_ref, k_ref, v_ref, kp_ref, vp_ref, o_ref, lse_ref, *, earlier):
    rows = q_ref.shape[0]
    v_turned = v_ref[...].T
    vp_turned = [vp_ref[s].T for s in range(earlier)]
    for e in range(2):
        lanes = pl.ds(e * 2 * HEAD, 2 * HEAD)
        q_turned = q_ref[:, lanes].T
        tiles = [near_tiles(table_ref[0, 2 * e + r : 2 * e + r + 1, :]) for r in range(2)]
        for t in range(rows // TILE):
            cols = slice(t * TILE, (t + 1) * TILE)
            outs = []
            for r in range(2):
                at_zero, at_one = tiles[r]
                q_tile = place_rows(q_turned[r * HEAD : (r + 1) * HEAD, cols], e)
                seen = (t + 1) * TILE
                scores = add_diagonal(dot(k_ref[:seen], q_tile), at_zero, at_one)
                peak = jnp.max(scores, axis=0, keepdims=True)
                weights = jnp.exp(scores - peak)
                summed = jnp.sum(weights, axis=0, keepdims=True)
                acc = dot(v_turned[:, :seen], weights.astype(jnp.bfloat16))[e * HEAD : (e + 1) * HEAD]

                for s in range(earlier):

                    def visit(state, s=s, q_tile=q_tile, at_one=at_one, t=t):
                        peak, summed, acc = state
                        scores = dot(kp_ref[s], q_tile)
                        if s == 0 and t == 0:
                            scores = add_corner(scores, at_one)
                        new_peak = jnp.maximum(peak, jnp.max(scores, axis=0, keepdims=True))
                        rescale = jnp.exp(peak - new_peak)
                        weights = jnp.exp(scores - new_peak)
                        summed = summed * rescale + jnp.sum(weights, axis=0, keepdims=True)
                        add = dot(vp_turned[s], weights.astype(jnp.bfloat16))[e * HEAD : (e + 1) * HEAD]
                        return (new_peak, summed, acc * rescale + add)

                    peak, summed, acc = lax.cond(
                        valid_ref[s] > 0, visit, lambda state: state, (peak, summed, acc)
                    )
                outs.append(acc / summed)
                lse_ref[0, 2 * e + r : 2 * e + r + 1, cols] = peak + jnp.log(summed)
            o_ref[cols, lanes] = jnp.concatenate(outs, axis=0).T.astype(jnp.bfloat16)


def self_forward(valid, table, q, k, v, kp, vp):
    rows = q.shape[0]
    blocks = k.shape[1] // (2 * HEAD)
    earlier = kp.shape[0]
    return pl.pallas_call(
        functools.partial(self_forward_kernel, earlier=earlier),
        grid=(blocks,),
        in_specs=[
            pl.BlockSpec(memory_space=pltpu.SMEM),
            pl.BlockSpec((1, 8, 2 * NEAR), lambda p: (p, 0, 0)),
            pl.BlockSpec((rows, 4 * HEAD), lambda p: (0, p)),
            pl.BlockSpec((rows, 2 * HEAD), lambda p: (0, p)),
            pl.BlockSpec((rows, 2 * HEAD), lambda p: (0, p)),
            pl.BlockSpec((earlier, rows, 2 * HEAD), lambda p: (0, 0, p)),
            pl.BlockSpec((earlier, rows, 2 * HEAD), lambda p: (0, 0, p)),
        ],
        out_specs=[
            pl.BlockSpec((rows, 4 * HEAD), lambda p: (0, p)),
            pl.BlockSpec((1, 8, rows), lambda p: (p, 0, 0)),
        ],
        out_shape=[
            jax.ShapeDtypeStruct(q.shape, jnp.bfloat16),
            jax.ShapeDtypeStruct((blocks, 8, rows), jnp.float32),
        ],
        compiler_params=pltpu.CompilerParams(vmem_limit_bytes=VMEM_LIMIT),
        name="self_forward",
    )(valid, table, q, k, v, kp, vp)


def self_backward_kernel(
    valid_ref, table_ref, q_ref, k_ref, v_ref, kp_ref, vp_ref, do_ref, o_ref, lse_ref,
    dq_ref, dk_ref, dv_ref, dkp_ref, dvp_ref, db_ref, total_ref,
    dk_sum, dv_sum, dkp_sum, dvp_sum, near_sum, *, earlier,
):
    rows = q_ref.shape[0]
    dk_sum[...] = jnp.zeros_like(dk_sum)
    dv_sum[...] = jnp.zeros_like(dv_sum)
    dkp_sum[...] = jnp.zeros_like(dkp_sum)
    dvp_sum[...] = jnp.zeros_like(dvp_sum)
    k_turned = k_ref[...].T
    kp_turned = [kp_ref[s].T for s in range(earlier)]
    for e in range(2):
        lanes = pl.ds(e * 2 * HEAD, 2 * HEAD)
        q_pair = q_ref[:, lanes]
        do_pair = do_ref[:, lanes]
        q_turned = q_pair.T
        do_turned = do_pair.T
        product = (do_pair.astype(jnp.float32) * o_ref[:, lanes].astype(jnp.float32)).T
        half = slice(e * HEAD, (e + 1) * HEAD)
        tiles = [near_tiles(table_ref[0, 2 * e + r : 2 * e + r + 1, :]) for r in range(2)]
        q_placed = [place_lanes(q_pair, r, e) for r in range(2)]
        do_placed = [place_lanes(do_pair, r, e) for r in range(2)]
        totals = [jnp.zeros((1, TILE), jnp.float32) for _ in range(2)]
        for t in range(rows // TILE):
            cols = slice(t * TILE, (t + 1) * TILE)
            d_queries = []
            for r in range(2):
                at_zero, at_one = tiles[r]
                head = slice(r * HEAD, (r + 1) * HEAD)
                q_tile_t = place_rows(q_turned[head, cols], e)
                do_tile_t = place_rows(do_turned[head, cols], e)
                q_tile = q_placed[r][cols]
                do_tile = do_placed[r][cols]
                delta = jnp.sum(product[head, cols], axis=0, keepdims=True)
                lse = lse_ref[0, 2 * e + r : 2 * e + r + 1, cols]

                def one(scores, v_rows, lse=lse, delta=delta, do_tile_t=do_tile_t):
                    prob = jnp.exp(scores - lse)
                    d_prob = dot(v_rows, do_tile_t)
                    d_score = prob * (d_prob - delta)
                    return prob.astype(jnp.bfloat16), d_score.astype(jnp.bfloat16)

                seen = (t + 1) * TILE
                scores = add_diagonal(dot(k_ref[:seen], q_tile_t), at_zero, at_one)
                prob, d_score = one(scores, v_ref[:seen])
                dv_sum[:seen] += dot(prob, do_tile)
                dk_sum[:seen] += dot(d_score, q_tile)
                d_query = dot(k_turned[:, :seen], d_score)[half]
                d_wide = d_score.astype(jnp.float32)
                totals[r] = totals[r] + jnp.sum(d_wide, axis=0, keepdims=True)
                base = seen - TILE
                zero_part = d_wide[base : base + NEAR, :NEAR] + d_wide[base + NEAR :, NEAR:]
                one_part = d_wide[base : base + NEAR, NEAR:]
                if t > 0:
                    one_part = one_part + d_wide[base - NEAR : base, :NEAR]
                both = jnp.concatenate([zero_part, one_part], axis=1)
                if t == 0:
                    near_sum[r] = both
                else:
                    near_sum[r] += both
                for s in range(earlier):

                    def visit(state, s=s, t=t, r=r, q_tile_t=q_tile_t, q_tile=q_tile, do_tile=do_tile, at_one=at_one, one=one):
                        d_query, total = state
                        scores = dot(kp_ref[s], q_tile_t)
                        if s == 0 and t == 0:
                            scores = add_corner(scores, at_one)
                        prob, d_score = one(scores, vp_ref[s])
                        dvp_sum[s] += dot(prob, do_tile)
                        dkp_sum[s] += dot(d_score, q_tile)
                        d_query = d_query + dot(kp_turned[s], d_score)[half]
                        d_wide = d_score.astype(jnp.float32)
                        if s == 0 and t == 0:
                            near_sum[r, :, NEAR:] += d_wide[rows - NEAR :, :NEAR]
                        return (d_query, total + jnp.sum(d_wide, axis=0, keepdims=True))

                    d_query, totals[r] = lax.cond(
                        valid_ref[s] > 0, visit, lambda state: state, (d_query, totals[r])
                    )
                d_queries.append(d_query)
            dq_ref[cols, lanes] = jnp.concatenate(d_queries, axis=0).T.astype(jnp.bfloat16)
        for r in range(2):
            db_ref[0, 2 * e + r : 2 * e + r + 1, :] = by_distance(near_sum[r])
            total_ref[0, 2 * e + r : 2 * e + r + 1, :] = totals[r]
    dk_ref[...] = dk_sum[...].astype(jnp.bfloat16)
    dv_ref[...] = dv_sum[...].astype(jnp.bfloat16)
    dkp_ref[...] = dkp_sum[...].astype(jnp.bfloat16)
    dvp_ref[...] = dvp_sum[...].astype(jnp.bfloat16)


def self_backward(valid, table, q, k, v, kp, vp, do, o, lse):
    rows = q.shape[0]
    blocks = k.shape[1] // (2 * HEAD)
    earlier = kp.shape[0]
    wide = pl.BlockSpec((rows, 4 * HEAD), lambda p: (0, p))
    slim = pl.BlockSpec((rows, 2 * HEAD), lambda p: (0, p))
    past = pl.BlockSpec((earlier, rows, 2 * HEAD), lambda p: (0, 0, p))
    tab = pl.BlockSpec((1, 8, 2 * NEAR), lambda p: (p, 0, 0))
    return pl.pallas_call(
        functools.partial(self_backward_kernel, earlier=earlier),
        grid=(blocks,),
        in_specs=[
            pl.BlockSpec(memory_space=pltpu.SMEM), tab, wide, slim, slim, past, past, wide, wide,
            pl.BlockSpec((1, 8, rows), lambda p: (p, 0, 0)),
        ],
        out_specs=[wide, slim, slim, past, past, tab, tab],
        out_shape=[
            jax.ShapeDtypeStruct(q.shape, jnp.bfloat16),
            jax.ShapeDtypeStruct(k.shape, jnp.bfloat16),
            jax.ShapeDtypeStruct(k.shape, jnp.bfloat16),
            jax.ShapeDtypeStruct(kp.shape, jnp.bfloat16),
            jax.ShapeDtypeStruct(kp.shape, jnp.bfloat16),
            jax.ShapeDtypeStruct(table.shape, jnp.float32),
            jax.ShapeDtypeStruct(table.shape, jnp.float32),
        ],
        scratch_shapes=[
            pltpu.VMEM((rows, 2 * HEAD), jnp.float32),
            pltpu.VMEM((rows, 2 * HEAD), jnp.float32),
            pltpu.VMEM((earlier, rows, 2 * HEAD), jnp.float32),
            pltpu.VMEM((earlier, rows, 2 * HEAD), jnp.float32),
            pltpu.VMEM((2, NEAR, 2 * NEAR), jnp.float32),
        ],
        compiler_params=pltpu.CompilerParams(vmem_limit_bytes=VMEM_LIMIT),
        name="self_backward",
    )(valid, table, q, k, v, kp, vp, do, o, lse)


def cross_forward_kernel(q_ref, k_ref, v_ref, own_ref, o_ref, lse_ref, *, masked):
    rows = q_ref.shape[0]
    v_turned = v_ref[...].T
    if masked:
        blocked = jnp.where(own_ref[...] > 0, 0.0, NEGATIVE)
    for e in range(2):
        lanes = pl.ds(e * 2 * HEAD, 2 * HEAD)
        q_turned = q_ref[:, lanes].T
        for t in range(rows // TILE):
            cols = slice(t * TILE, (t + 1) * TILE)
            outs = []
            for r in range(2):
                q_tile = place_rows(q_turned[r * HEAD : (r + 1) * HEAD, cols], e)
                scores = dot(k_ref[...], q_tile)
                if masked:
                    scores = scores + blocked
                peak = jnp.max(scores, axis=0, keepdims=True)
                weights = jnp.exp(scores - peak)
                summed = jnp.sum(weights, axis=0, keepdims=True)
                acc = dot(v_turned, weights.astype(jnp.bfloat16))[e * HEAD : (e + 1) * HEAD]
                outs.append(acc / summed)
                lse_ref[0, 2 * e + r : 2 * e + r + 1, cols] = peak + jnp.log(summed)
            o_ref[cols, lanes] = jnp.concatenate(outs, axis=0).T.astype(jnp.bfloat16)


def cross_forward(q, k, v, own, masked):
    rows, keys = q.shape[0], k.shape[0]
    blocks = k.shape[1] // (2 * HEAD)
    wide = pl.BlockSpec((rows, 4 * HEAD), lambda p: (0, p))
    slim = pl.BlockSpec((keys, 2 * HEAD), lambda p: (0, p))
    return pl.pallas_call(
        functools.partial(cross_forward_kernel, masked=masked),
        grid=(blocks,),
        in_specs=[wide, slim, slim, pl.BlockSpec(own.shape, lambda p: (0, 0))],
        out_specs=[wide, pl.BlockSpec((1, 8, rows), lambda p: (p, 0, 0))],
        out_shape=[
            jax.ShapeDtypeStruct(q.shape, jnp.bfloat16),
            jax.ShapeDtypeStruct((blocks, 8, rows), jnp.float32),
        ],
        compiler_params=pltpu.CompilerParams(vmem_limit_bytes=VMEM_LIMIT),
        name="cross_forward",
    )(q, k, v, own)


def cross_backward_kernel(q_ref, k_ref, v_ref, own_ref, do_ref, o_ref, lse_ref, dq_ref, dk_ref, dv_ref, dk_sum, dv_sum, *, masked):
    rows = q_ref.shape[0]
    dk_sum[...] = jnp.zeros_like(dk_sum)
    dv_sum[...] = jnp.zeros_like(dv_sum)
    k_turned = k_ref[...].T
    if masked:
        blocked = jnp.where(own_ref[...] > 0, 0.0, NEGATIVE)
    for e in range(2):
        lanes = pl.ds(e * 2 * HEAD, 2 * HEAD)
        q_pair = q_ref[:, lanes]
        do_pair = do_ref[:, lanes]
        q_turned = q_pair.T
        do_turned = do_pair.T
        product = (do_pair.astype(jnp.float32) * o_ref[:, lanes].astype(jnp.float32)).T
        half = slice(e * HEAD, (e + 1) * HEAD)
        for t in range(rows // TILE):
            cols = slice(t * TILE, (t + 1) * TILE)
            d_queries = []
            for r in range(2):
                head = slice(r * HEAD, (r + 1) * HEAD)
                scores = dot(k_ref[...], place_rows(q_turned[head, cols], e))
                if masked:
                    scores = scores + blocked
                delta = jnp.sum(product[head, cols], axis=0, keepdims=True)
                prob = jnp.exp(scores - lse_ref[0, 2 * e + r : 2 * e + r + 1, cols])
                d_prob = dot(v_ref[...], place_rows(do_turned[head, cols], e))
                d_score = (prob * (d_prob - delta)).astype(jnp.bfloat16)
                dv_sum[...] += dot(prob.astype(jnp.bfloat16), place_lanes(do_pair[cols], r, e))
                dk_sum[...] += dot(d_score, place_lanes(q_pair[cols], r, e))
                d_queries.append(dot(k_turned, d_score)[half])
            dq_ref[cols, lanes] = jnp.concatenate(d_queries, axis=0).T.astype(jnp.bfloat16)
    dk_ref[...] = dk_sum[...].astype(jnp.bfloat16)
    dv_ref[...] = dv_sum[...].astype(jnp.bfloat16)


def cross_backward(q, k, v, own, do, o, lse, masked):
    rows, keys = q.shape[0], k.shape[0]
    blocks = k.shape[1] // (2 * HEAD)
    wide = pl.BlockSpec((rows, 4 * HEAD), lambda p: (0, p))
    slim = pl.BlockSpec((keys, 2 * HEAD), lambda p: (0, p))
    return pl.pallas_call(
        functools.partial(cross_backward_kernel, masked=masked),
        grid=(blocks,),
        in_specs=[wide, slim, slim, pl.BlockSpec(own.shape, lambda p: (0, 0)), wide, wide, pl.BlockSpec((1, 8, rows), lambda p: (p, 0, 0))],
        out_specs=[wide, slim, slim],
        out_shape=[
            jax.ShapeDtypeStruct(q.shape, jnp.bfloat16),
            jax.ShapeDtypeStruct(k.shape, jnp.bfloat16),
            jax.ShapeDtypeStruct(k.shape, jnp.bfloat16),
        ],
        scratch_shapes=[pltpu.VMEM((keys, 2 * HEAD), jnp.float32), pltpu.VMEM((keys, 2 * HEAD), jnp.float32)],
        compiler_params=pltpu.CompilerParams(vmem_limit_bytes=VMEM_LIMIT),
        name="cross_backward",
    )(q, k, v, own, do, o, lse)


def place_of(position, order):
    spot = jnp.int32(0)
    for bit in order:
        spot = spot * 2 + jnp.bitwise_and(lax.shift_right_logical(position, jnp.int32(bit)), 1)
    return spot


def weight_kernel(place_ref, *refs, n_x, n_y, columns, chunk, order):
    x_refs, y_refs = refs[:n_x], refs[n_x : n_x + n_y]
    send_ref, keep_ref = refs[n_x + n_y :]
    half = 1 << (len(order) - 1)
    chip, core = place_ref[0], place_ref[1]
    turned = [x_ref[...].T for x_ref in x_refs]
    start = 0
    for terms in columns:
        width = y_refs[terms[0][1]].shape[1]
        cols = slice(start, start + width)
        start += width
        parts = len(terms[0][0])
        for part in range(parts):
            part_rows = turned[terms[0][0][part]].shape[0]
            step = part_rows
            while step > 512 and step % (2 * chunk) == 0:
                step //= 2
            per_part = part_rows // chunk
            for first in range(0, part_rows, step):
                tile = None
                for x_ids, y_id in terms:
                    term = dot(turned[x_ids[part]][first : first + step], y_refs[y_id][...])
                    tile = term if tile is None else tile + term
                tile = tile.astype(BF16)
                for inner in range(step // chunk):
                    number = jnp.int32(first // chunk + inner)
                    if parts == 2:
                        number = number + (core if part == 0 else 1 - core) * per_part
                    spot = place_of(jnp.bitwise_xor(number, chip), order)
                    piece = tile[inner * chunk : (inner + 1) * chunk]

                    @pl.when(spot >= half)
                    def _(spot=spot, piece=piece, cols=cols):
                        send_ref[spot - half, :, cols] = piece

                    @pl.when(spot < half)
                    def _(spot=spot, piece=piece, cols=cols):
                        keep_ref[spot, :, cols] = piece


def weight_sums(place, xs, ys, columns, rows_out, order, name):
    chips = 1 << len(order)
    chunk = rows_out // chips
    width = sum(ys[terms[0][1]].shape[1] for terms in columns)
    half = chips // 2
    if chunk % 16:
        pieces = []
        for terms in columns:
            total = 0.0
            for x_ids, y_id in terms:
                parts = [matmul_left(xs[x], ys[y_id]) for x in x_ids]
                if len(parts) == 2:
                    parts = [jnp.where(place[1] == 0, parts[0], parts[1]), jnp.where(place[1] == 0, parts[1], parts[0])]
                total = total + jnp.concatenate(parts, axis=0)
            pieces.append(total.astype(BF16))
        whole = jnp.concatenate(pieces, axis=1).reshape(chips, chunk, width)
        where = jnp.arange(chips, dtype=jnp.int32)
        position = sum((((where >> (len(order) - 1 - at)) & 1) << bit) for at, bit in enumerate(order))
        whole = jnp.take(whole, jnp.bitwise_xor(position, place[0]), axis=0)
        return whole[half:], whole[:half]
    full = lambda a: pl.BlockSpec(a.shape, lambda i, p: (0, 0))
    flops = 2 * sum(xs[0].shape[0] * rows_out * ys[y].shape[1] for terms in columns for _, y in terms)
    out = jax.ShapeDtypeStruct((half, chunk, width), BF16)
    spec = pl.BlockSpec((half, chunk, width), lambda i, p: (0, 0, 0))
    return pl.pallas_call(
        functools.partial(weight_kernel, n_x=len(xs), n_y=len(ys), columns=columns, chunk=chunk, order=order),
        grid_spec=pltpu.PrefetchScalarGridSpec(
            num_scalar_prefetch=1,
            grid=(1,),
            in_specs=[full(a) for a in xs + ys],
            out_specs=[spec, spec],
        ),
        out_shape=[out, out],
        compiler_params=pltpu.CompilerParams(vmem_limit_bytes=VMEM_LIMIT),
        cost_estimate=pl.CostEstimate(
            flops=flops, bytes_accessed=2 * (sum(a.size for a in xs + ys) + rows_out * width), transcendentals=0
        ),
        name=name,
    )(place, *xs, *ys)


def matmul_left(a, b):
    return lax.dot_general(a, b, (((0,), (0,)), ((), ())), preferred_element_type=F32)


def matmul_right(a, b):
    return lax.dot_general(a, b, (((1,), (1,)), ((), ())), preferred_element_type=F32)


def rel_bucket(distance):
    beyond = 16 + sum((distance >= border).astype(jnp.int32) for border in THRESHOLDS)
    return jnp.where(distance < 16, distance, beyond)


def inverse_norm(hidden):
    return lax.rsqrt(jnp.mean(hidden * hidden, axis=-1, keepdims=True) + EPSILON)


def norm_low(hidden, inverse, gain):
    return (hidden * inverse * gain).astype(BF16)


def norm_back(hidden, inverse, gain, dz):
    scaled = gain * dz
    inner = jnp.mean(scaled * hidden, axis=-1, keepdims=True)
    return inverse * scaled - hidden * (inverse * inverse * inverse) * inner


def gain_sum(hidden, inverse, dz):
    return jnp.sum(dz * hidden * inverse, axis=0)


def shards(
    tokens, memory, cotangent, bucket, gain_self, self_query, self_key, self_value, self_out, rel_bias,
    gain_cross, cross_query, cross_key, cross_value, cross_out, gain_ffn, ffn_gate, ffn_up, ffn_down,
):
    groups = lax.axis_size("grp")
    dp_size = lax.axis_size("dp")
    n_chips = groups // CORES
    chips = dp_size * n_chips
    grp_at = lax.axis_index("grp")
    core = grp_at % CORES
    y_at = grp_at // CORES
    chip = lax.axis_index("dp") * n_chips + y_at
    place = jnp.stack([chip, core]).astype(jnp.int32)
    rows = tokens.shape[0]
    chip_rows = rows * CORES
    group_rows = chip_rows * n_chips
    mem_rows = memory.shape[0]
    length = jnp.minimum(group_rows, jnp.maximum(SHORT, jnp.right_shift(jnp.int32(group_rows), bucket[0])))
    masked = group_rows > SHORT
    y_bits = n_chips.bit_length() - 1
    bits = chips.bit_length() - 1

    def swap_core(v):
        return lax.ppermute(v, "grp", [(g, g ^ 1) for g in range(groups)])

    def swap_chip(v, bit):
        return lax.ppermute(v, ("dp", "grp"), [(i, i ^ (CORES << bit)) for i in range(chips * CORES)])

    def in_order(own, peer, axis=0):
        return jnp.where(core == 0, jnp.concatenate([own, peer], axis), jnp.concatenate([peer, own], axis))

    def part_of(v, at, axis):
        size = v.shape[axis] // CORES
        return lax.dynamic_slice_in_dim(v, at * size, size, axis)

    gain_one, gain_two, gain_three = (g.astype(F32) for g in (gain_self, gain_cross, gain_ffn))

    tokens_peer = swap_core(tokens)
    past_own = [
        lax.ppermute(tokens, "grp", [(g, g + CORES * s) for g in range(groups - CORES * s)]) for s in range(1, n_chips)
    ]
    cot_peer = swap_core(cotangent)
    mem_all = in_order(memory, swap_core(memory))
    for bit in range(y_bits):
        other = lax.ppermute(mem_all, "grp", [(g, g ^ (CORES << bit)) for g in range(groups)])
        low_first = jnp.concatenate([mem_all, other], 0)
        mem_all = jnp.where((y_at >> bit) & 1 == 0, low_first, jnp.concatenate([other, mem_all], 0))
    past_tokens = [in_order(own, swap_core(own)) for own in past_own]

    distances = jnp.arange(2 * NEAR, dtype=jnp.int32)
    onehot = (rel_bucket(distances)[:, None] == jnp.arange(BUCKETS, dtype=jnp.int32)).astype(F32)
    rel_local = part_of(rel_bias.astype(F32), core, 1)
    heads = rel_local.shape[1]
    by_dist = jnp.dot(onehot, rel_local - rel_local[BUCKETS - 1 :], precision=lax.Precision.HIGHEST)
    table = jnp.pad(by_dist.T.reshape(heads // 4, 4, 2 * NEAR), ((0, 0), (0, 4), (0, 0)))

    hidden_in = in_order(tokens, tokens_peer).astype(F32)
    inv_one = inverse_norm(hidden_in)
    low_one = norm_low(hidden_in, inv_one, gain_one)
    w_key, w_value = part_of(self_key, core, 1), part_of(self_value, core, 1)
    q = dot(low_one, part_of(self_query, core, 1)).astype(BF16)
    k = dot(low_one, w_key).astype(BF16)
    v = dot(low_one, w_value).astype(BF16)
    low_past = []
    for past in past_tokens:
        wide = past.astype(F32)
        low_past.append(norm_low(wide, inverse_norm(wide), gain_one))
    k_past = jnp.stack([dot(low, w_key).astype(BF16) for low in low_past])
    v_past = jnp.stack([dot(low, w_value).astype(BF16) for low in low_past])
    first_chip = y_at * chip_rows // length * length // chip_rows
    valid = jnp.stack([(y_at - s >= first_chip).astype(jnp.int32) for s in range(1, n_chips)])
    att, lse_self = self_forward(valid, table, q, k, v, k_past, v_past)
    att_peer = swap_core(att)
    hidden_mid = hidden_in + dot(att, part_of(self_out, core, 0)) + dot(att_peer, part_of(self_out, 1 - core, 0))

    inv_two = inverse_norm(hidden_mid)
    low_two = norm_low(hidden_mid, inv_two, gain_two)
    cq = dot(low_two, part_of(cross_query, core, 1)).astype(BF16)
    w_ckey, w_cvalue = part_of(cross_key, core, 1), part_of(cross_value, core, 1)
    km = dot(mem_all, w_ckey).astype(BF16)
    vm = dot(mem_all, w_cvalue).astype(BF16)
    mem_doc = jnp.arange(mem_all.shape[0], dtype=jnp.int32) // (length // RATIO)
    own_doc = jnp.broadcast_to((mem_doc == y_at * chip_rows // length).astype(F32)[:, None], (mem_all.shape[0], TILE))
    crs, lse_cross = cross_forward(cq, km, vm, own_doc, masked)
    crs_peer = swap_core(crs)
    hidden_late = hidden_mid + dot(crs, part_of(cross_out, core, 0)) + dot(crs_peer, part_of(cross_out, 1 - core, 0))

    inv_three = inverse_norm(hidden_late)
    low_three = norm_low(hidden_late, inv_three, gain_three)
    w_gate, w_up = part_of(ffn_gate, core, 1), part_of(ffn_up, core, 1)
    gate = dot(low_three, w_gate)
    up = dot(low_three, w_up)
    cot = in_order(cotangent, cot_peer)
    d_inner = matmul_right(cot, part_of(ffn_down, core, 0)).astype(BF16).astype(F32)
    inner, gated_back = jax.vjp(lambda g, u: jax.nn.gelu(g, approximate=True) * u, gate, up)
    inner = inner.astype(BF16)
    d_gate, d_up = (d.astype(BF16) for d in gated_back(d_inner))
    inner_peer = swap_core(inner)
    dz_part = (matmul_right(d_gate, w_gate) + matmul_right(d_up, w_up)).astype(BF16)
    dz_peer = swap_core(dz_part)
    layer_out = (
        part_of(hidden_late, core, 0)
        + dot(part_of(inner, core, 0), part_of(ffn_down, core, 0))
        + dot(part_of(inner_peer, core, 0), part_of(ffn_down, 1 - core, 0))
    ).astype(BF16)

    x_bit, z_bit, far_bits = y_bits, y_bits + 1, tuple(range(y_bits + 2, bits))
    y_order = tuple(range(y_bits))
    orders = (
        (x_bit,) + y_order + (z_bit,) + far_bits,
        y_order + (z_bit, x_bit) + far_bits,
        (z_bit, x_bit) + y_order + far_bits,
    )

    def column_half(v):
        return part_of(v, core, 1)

    sums = {}
    model = low_one.shape[1]
    hidden_units = ffn_down.shape[0]
    sums["down"] = (
        weight_sums(place, [inner, inner_peer], [column_half(cot)], [[((0, 1), 0)]], hidden_units, orders[2], "down_sums"),
        orders[2],
    )
    sums["gate"] = (weight_sums(place, [low_three], [d_gate], [[((0,), 0)]], model, orders[0], "gate_sums"), orders[0])
    sums["up"] = (weight_sums(place, [low_three], [d_up], [[((0,), 0)]], model, orders[1], "up_sums"), orders[1])
    dz = dz_part.astype(F32) + dz_peer.astype(F32)
    d_gain_three = gain_sum(hidden_late, inv_three, dz)
    g_late = cot.astype(F32) + norm_back(hidden_late, inv_three, gain_three, dz)
    late_low = g_late.astype(BF16)

    d_crs = matmul_right(late_low, part_of(cross_out, core, 0)).astype(BF16)
    dcq, dkm, dvm = cross_backward(cq, km, vm, own_doc, d_crs, crs, lse_cross, masked)
    dcq_peer = swap_core(dcq)
    dz = matmul_right(dcq, part_of(cross_query, core, 1)) + matmul_right(dcq_peer, part_of(cross_query, 1 - core, 1))
    d_gain_two = gain_sum(hidden_mid, inv_two, dz)
    g_mid = g_late + norm_back(hidden_mid, inv_two, gain_two, dz)
    mid_low = g_mid.astype(BF16)
    sums["cross"] = (
        weight_sums(
            place,
            [crs, crs_peer, low_two, mem_all, att, att_peer],
            [column_half(late_low), dcq, dkm, dvm, column_half(mid_low)],
            [[((0, 1), 0)], [((2,), 1)], [((3,), 2)], [((3,), 3)], [((4, 5), 4)]],
            model,
            orders[0],
            "cross_sums",
        ),
        orders[0],
    )
    grad_mem = (matmul_right(dkm, w_ckey) + matmul_right(dvm, w_cvalue)).astype(BF16)
    grad_mem = grad_mem.reshape(groups, mem_rows, model)
    grad_mem = jnp.take(grad_mem, jnp.bitwise_xor(jnp.arange(groups, dtype=jnp.int32), grp_at), axis=0)
    for bit in reversed(range(y_bits + 1)):
        half = grad_mem.shape[0] // 2
        got = lax.ppermute(grad_mem[half:], "grp", [(g, g ^ (1 << bit)) for g in range(groups)])
        grad_mem = (grad_mem[:half].astype(F32) + got.astype(F32)).astype(BF16)
    grad_memory = grad_mem[0]

    d_att = matmul_right(mid_low, part_of(self_out, core, 0)).astype(BF16)
    dq, dk, dv, dk_past, dv_past, d_near, d_total = self_backward(
        valid, table, q, k, v, k_past, v_past, d_att, att, lse_self
    )
    self_terms_x = [low_one] + low_past
    sums["self"] = (
        weight_sums(
            place,
            self_terms_x,
            [dq, dk, dv] + [dk_past[s] for s in range(n_chips - 1)] + [dv_past[s] for s in range(n_chips - 1)],
            [
                [((0,), 0)],
                [((0,), 1)] + [((1 + s,), 3 + s) for s in range(n_chips - 1)],
                [((0,), 2)] + [((1 + s,), 2 + n_chips + s) for s in range(n_chips - 1)],
            ],
            model,
            orders[1],
            "self_sums",
        ),
        orders[1],
    )
    dkv_total = jnp.concatenate([dk, dv], axis=1).astype(F32)
    for s in range(1, n_chips):
        both = jnp.concatenate([dk_past[s - 1], dv_past[s - 1]], axis=1)
        dkv_total = dkv_total + lax.ppermute(
            both, "grp", [(g, g - CORES * s) for g in range(CORES * s, groups)]
        ).astype(F32)
    dkv_total = dkv_total.astype(BF16)
    kv_cols = dk.shape[1]
    dz_part = (
        matmul_right(dq, part_of(self_query, core, 1))
        + matmul_right(dkv_total[:, :kv_cols], w_key)
        + matmul_right(dkv_total[:, kv_cols:], w_value)
    )
    dz_got = swap_core(part_of(dz_part, 1 - core, 0).astype(BF16))
    dz = part_of(dz_part, core, 0) + dz_got.astype(F32)
    own_in = tokens.astype(F32)
    own_inv = inverse_norm(own_in)
    d_gain_one = gain_sum(own_in, own_inv, dz)
    grad_tokens = (part_of(g_mid, core, 0) + norm_back(own_in, own_inv, gain_one, dz)).astype(BF16)

    near = d_near[:, :4].reshape(heads, 2 * NEAR)
    total = jnp.sum(d_total[:, :4], axis=-1).reshape(heads)
    by_bucket = jnp.dot(near, onehot, precision=lax.Precision.HIGHEST)
    far = total - jnp.sum(near, axis=1)
    by_bucket = by_bucket + far[:, None] * onehot[2 * NEAR - 1]
    rel_grad = lax.dynamic_update_slice(jnp.zeros((BUCKETS, HEADS), F32), by_bucket.T, (jnp.int32(0), core * heads))
    small = jnp.concatenate(
        [
            d_gain_one.reshape(chips, -1),
            jnp.where(core == 0, d_gain_two, 0.0).reshape(chips, -1),
            jnp.where(core == 0, d_gain_three, 0.0).reshape(chips, -1),
            rel_grad.reshape(chips, -1),
        ],
        axis=1,
    )
    small = jnp.take(small, jnp.bitwise_xor(jnp.arange(chips, dtype=jnp.int32), chip), axis=0)
    for bit in reversed(range(bits)):
        half = small.shape[0] // 2
        small = small[:half] + swap_chip(small[half:], bit)
    small = small[0]
    gain_cols = model // chips

    def core_share(vec, at):
        return part_of(vec, at, 0)

    pieces = [small[i * gain_cols : (i + 1) * gain_cols] for i in range(3)] + [small[3 * gain_cols :]]
    mine = jnp.concatenate([core_share(piece, core) for piece in pieces])
    other = jnp.concatenate([core_share(piece, 1 - core) for piece in pieces])
    mine = mine + swap_core(other)
    gain_share = gain_cols // CORES
    small_out = [mine[i * gain_share : (i + 1) * gain_share] for i in range(3)] + [mine[3 * gain_share :]]

    done = {}
    for name, ((send, keep), order) in sums.items():
        for at, bit in enumerate(order):
            got = swap_chip(send, bit)
            if at + 1 < len(order):
                half = keep.shape[0] // 2
                send = (keep[half:].astype(F32) + got[half:].astype(F32)).astype(BF16)
                keep = (keep[:half].astype(F32) + got[:half].astype(F32)).astype(BF16)
            else:
                keep = keep.astype(F32) + got.astype(F32)
        result = keep[0]
        peer = swap_core(part_of(result, 1 - core, 0).astype(BF16)).astype(F32)
        done[name] = (part_of(result, core, 0), peer)

    def columns_of(name, start, width):
        own, peer = (v[:, start : start + width] for v in done[name])
        return in_order(own, peer, 1)

    wide = model // 2
    slim = self_key.shape[1] // 2
    ff = hidden_units // 2
    return (
        layer_out,
        grad_tokens,
        grad_memory,
        small_out[0],
        columns_of("self", 0, wide),
        columns_of("self", wide, slim),
        columns_of("self", wide + slim, slim),
        columns_of("cross", 2 * wide + 2 * slim, wide),
        small_out[3],
        small_out[1],
        columns_of("cross", wide, wide),
        columns_of("cross", 2 * wide, slim),
        columns_of("cross", 2 * wide + slim, slim),
        columns_of("cross", 0, wide),
        small_out[2],
        columns_of("gate", 0, ff),
        columns_of("up", 0, ff),
        columns_of("down", 0, wide),
    )


def solution(mesh):
    rows = P(("dp", "grp"), None)
    flat = P(("dp", "grp"))
    in_specs = (rows, rows, rows, P("dp")) + (P(),) * 15
    out_specs = (rows,) * 3 + (flat,) + (rows,) * 4 + (flat,) * 2 + (rows,) * 4 + (flat,) + (rows,) * 3
    return jax.shard_map(shards, mesh=mesh, in_specs=in_specs, out_specs=out_specs, check_vma=False)
```

```python
import functools

import jax
import jax.numpy as jnp
from jax import lax
from jax.experimental import pallas as pl
from jax.experimental.pallas import tpu as pltpu
from jax.sharding import PartitionSpec as P

SHORT = 1024
RATIO = 4
BUCKETS = 32
HEADS = 16
EPSILON = 1e-06
THRESHOLDS = (19, 21, 24, 27, 31, 35, 40, 46, 52, 59, 67, 77, 87, 99, 113)
CORES = 2
BF16 = jnp.bfloat16
F32 = jnp.float32
NEGATIVE = -1e30
HEAD = 64
TILE = 256
NEAR = 128
VMEM_LIMIT = 24 * 1024 * 1024


def dot(a, b):
    return jnp.dot(a, b, preferred_element_type=jnp.float32)


def cost(microseconds):
    return pl.CostEstimate(
        flops=int(1.15e9 * microseconds), bytes_accessed=int(3.69e6 * microseconds), transcendentals=0
    )


def place_rows(half, at):
    zero = jnp.zeros_like(half)
    return jnp.concatenate([half, zero] if at == 0 else [zero, half], axis=0)


def place_lanes(pair, source, at):
    lane = lax.broadcasted_iota(jnp.int32, pair.shape, 1)
    if source != at:
        pair = jnp.concatenate([pair[:, HEAD:], pair[:, :HEAD]], axis=1)
    return jnp.where((lane < HEAD) == (at == 0), pair, jnp.zeros_like(pair))


def near_tiles(table_row):
    skewed = pltpu.roll(jnp.broadcast_to(table_row, (NEAR, 2 * NEAR)), 0, 1, stride=1, stride_axis=0)
    key_at = lax.broadcasted_iota(jnp.int32, (NEAR, NEAR), 0)
    row_at = lax.broadcasted_iota(jnp.int32, (NEAR, NEAR), 1)
    return (jnp.where(key_at <= row_at, skewed[:, :NEAR], NEGATIVE), skewed[:, NEAR:])


def heads_of(pair_turned, cols):
    return jnp.concatenate(
        [place_rows(pair_turned[h * HEAD : (h + 1) * HEAD, cols], h // 2) for h in range(4)], axis=1
    )


def add_corner(scores, tiles):
    rows = scores.shape[0]
    last = scores[rows - NEAR :]
    pieces = []
    for h in range(4):
        pieces += [last[:, h * TILE : h * TILE + NEAR] + tiles[h][1], last[:, h * TILE + NEAR : (h + 1) * TILE]]
    return jnp.concatenate([scores[: rows - NEAR], jnp.concatenate(pieces, axis=1)], axis=0)


def add_diagonal(scores, tiles):
    rows = scores.shape[0]
    first = scores[rows - TILE : rows - NEAR]
    second = scores[rows - NEAR :]
    upper, lower = [], []
    for h in range(4):
        left, right = slice(h * TILE, h * TILE + NEAR), slice(h * TILE + NEAR, (h + 1) * TILE)
        upper += [first[:, left] + tiles[h][0], first[:, right] + tiles[h][1]]
        lower += [jnp.full((NEAR, NEAR), NEGATIVE, jnp.float32), second[:, right] + tiles[h][0]]
    last = [jnp.concatenate(upper, axis=1), jnp.concatenate(lower, axis=1)]
    if rows > TILE:
        last = [add_corner(scores[: rows - TILE], tiles)] + last
    return jnp.concatenate(last, axis=0)


def by_distance(near):
    level = near[:8]
    for first in range(8, NEAR, 8):
        level = level + pltpu.roll(near[first : first + 8], 2 * NEAR - first, 1)
    row = lax.broadcasted_iota(jnp.int32, level.shape, 0)
    for bit in (1, 2, 4):
        level = jnp.where(row & bit > 0, pltpu.roll(level, 2 * NEAR - bit, 1), level)
    return jnp.sum(level, axis=0, keepdims=True)


def soft(scores):
    peak = jnp.max(scores, axis=0, keepdims=True)
    weights = jnp.exp(scores - peak)
    return peak, weights.astype(jnp.bfloat16), jnp.sum(weights, axis=0, keepdims=True)


def finish(o_ref, lse_ref, cols, peak, summed, acc):
    out = acc / summed
    lse = peak + jnp.log(summed)
    pieces = []
    for h in range(4):
        e = h // 2
        lanes = slice(h * TILE, (h + 1) * TILE)
        pieces.append(out[e * HEAD : (e + 1) * HEAD, lanes])
        lse_ref[0, h : h + 1, cols] = lse[:, lanes]
    o_ref[cols, :] = jnp.concatenate(pieces, axis=0).T.astype(jnp.bfloat16)


def self_forward_kernel(
    valid_ref, table_ref, q_ref, k_ref, v_ref, kp_ref, vp_ref, o_ref, lse_ref, peak_ref, sum_ref, acc_ref, *, earlier
):
    rows = q_ref.shape[0]
    steps = rows // TILE
    v_turned = v_ref[...].T
    q_turned = q_ref[...].T
    tiles = [near_tiles(table_ref[0, h : h + 1, :]) for h in range(4)]
    spans = [slice(t * TILE, (t + 1) * TILE) for t in range(steps)]
    queries = [heads_of(q_turned, cols) for cols in spans]
    scores = [add_diagonal(dot(k_ref[: cols.stop], queries[t]), tiles) for t, cols in enumerate(spans)]
    parts = [soft(score) for score in scores]
    for t, cols in enumerate(spans):
        peak_ref[t], sum_ref[t] = parts[t][0], parts[t][2]
        acc_ref[t] = dot(v_turned[:, : cols.stop], parts[t][1])
    for s in range(earlier):

        @pl.when(valid_ref[s] > 0)
        def _(s=s):
            vp_turned = vp_ref[s].T
            scores = [dot(kp_ref[s], query) for query in queries]
            if s == 0:
                scores[0] = add_corner(scores[0], tiles)
            for t in range(steps):
                peak = peak_ref[t]
                new_peak = jnp.maximum(peak, jnp.max(scores[t], axis=0, keepdims=True))
                rescale = jnp.exp(peak - new_peak)
                weights = jnp.exp(scores[t] - new_peak)
                peak_ref[t] = new_peak
                sum_ref[t] = sum_ref[t] * rescale + jnp.sum(weights, axis=0, keepdims=True)
                acc_ref[t] = acc_ref[t] * rescale + dot(vp_turned, weights.astype(jnp.bfloat16))

    for t, cols in enumerate(spans):
        finish(o_ref, lse_ref, cols, peak_ref[t], sum_ref[t], acc_ref[t])


def self_forward(valid, table, q, k, v, kp, vp):
    rows = q.shape[0]
    blocks = k.shape[1] // (2 * HEAD)
    earlier = kp.shape[0]
    return pl.pallas_call(
        functools.partial(self_forward_kernel, earlier=earlier),
        grid=(blocks,),
        in_specs=[
            pl.BlockSpec(memory_space=pltpu.SMEM),
            pl.BlockSpec((1, 8, 2 * NEAR), lambda p: (p, 0, 0)),
            pl.BlockSpec((rows, 4 * HEAD), lambda p: (0, p)),
            pl.BlockSpec((rows, 2 * HEAD), lambda p: (0, p)),
            pl.BlockSpec((rows, 2 * HEAD), lambda p: (0, p)),
            pl.BlockSpec((earlier, rows, 2 * HEAD), lambda p: (0, 0, p)),
            pl.BlockSpec((earlier, rows, 2 * HEAD), lambda p: (0, 0, p)),
        ],
        out_specs=[
            pl.BlockSpec((rows, 4 * HEAD), lambda p: (0, p)),
            pl.BlockSpec((1, 8, rows), lambda p: (p, 0, 0)),
        ],
        out_shape=[
            jax.ShapeDtypeStruct(q.shape, jnp.bfloat16),
            jax.ShapeDtypeStruct((blocks, 8, rows), jnp.float32),
        ],
        scratch_shapes=[
            pltpu.VMEM((rows // TILE, 1, 4 * TILE), jnp.float32),
            pltpu.VMEM((rows // TILE, 1, 4 * TILE), jnp.float32),
            pltpu.VMEM((rows // TILE, 2 * HEAD, 4 * TILE), jnp.float32),
        ],
        compiler_params=pltpu.CompilerParams(vmem_limit_bytes=VMEM_LIMIT),
        cost_estimate=cost(0.01),
        name="self_forward",
    )(valid, table, q, k, v, kp, vp)


def placed_heads(block, cols):
    rows = []
    for h in range(4):
        pair = block[cols, (h // 2) * 2 * HEAD : (h // 2 + 1) * 2 * HEAD]
        rows.append(place_lanes(pair, h % 2, h // 2))
    return jnp.concatenate(rows, axis=0)


def row_of_heads(ref, cols):
    return jnp.concatenate([ref[0, h : h + 1, cols] for h in range(4)], axis=1)


def deltas(product, cols):
    return jnp.concatenate(
        [jnp.sum(product[h * HEAD : (h + 1) * HEAD, cols], axis=0, keepdims=True) for h in range(4)], axis=1
    )


def back_scores(scores, lse, d_prob, delta):
    prob = jnp.exp(scores - lse)
    d_score = prob * (d_prob - delta)
    return prob.astype(jnp.bfloat16), d_score.astype(jnp.bfloat16)


def query_rows(d_query):
    pieces = [
        d_query[(h // 2) * HEAD : (h // 2 + 1) * HEAD, h * TILE : (h + 1) * TILE] for h in range(4)
    ]
    return jnp.concatenate(pieces, axis=0).T.astype(jnp.bfloat16)


def self_backward_kernel(
    valid_ref, table_ref, q_ref, k_ref, v_ref, kp_ref, vp_ref, do_ref, o_ref, lse_ref,
    dq_ref, dk_ref, dv_ref, past_ref, db_ref, total_ref,
    near_sum, dq_sum, *, earlier,
):
    rows = q_ref.shape[0]
    steps = rows // TILE
    spans = [slice(t * TILE, (t + 1) * TILE) for t in range(steps)]
    k_turned = k_ref[...].T
    q_turned = q_ref[...].T
    do_turned = do_ref[...].T
    product = (do_ref[...].astype(jnp.float32) * o_ref[...].astype(jnp.float32)).T
    tiles = [near_tiles(table_ref[0, h : h + 1, :]) for h in range(4)]
    queries = [heads_of(q_turned, cols) for cols in spans]
    outs = [heads_of(do_turned, cols) for cols in spans]
    q_placed = [placed_heads(q_ref, cols) for cols in spans]
    do_placed = [placed_heads(do_ref, cols) for cols in spans]
    lses = [row_of_heads(lse_ref, cols) for cols in spans]
    delta = [deltas(product, cols) for cols in spans]

    for t, cols in enumerate(spans):
        seen = cols.stop
        scores = add_diagonal(dot(k_ref[:seen], queries[t]), tiles)
        prob, d_score = back_scores(scores, lses[t], dot(v_ref[:seen], outs[t]), delta[t])
        d_value = dot(prob, do_placed[t])
        d_key = dot(d_score, q_placed[t])
        if t == 0:
            dv_whole, dk_whole = d_value, d_key
        else:
            more = seen - dv_whole.shape[0]
            dv_whole = jnp.concatenate([dv_whole + d_value[: seen - more], d_value[seen - more :]], axis=0)
            dk_whole = jnp.concatenate([dk_whole + d_key[: seen - more], d_key[seen - more :]], axis=0)
        dq_sum[t] = dot(k_turned[:, :seen], d_score)
        d_wide = d_score.astype(jnp.float32)
        total = jnp.sum(d_wide, axis=0, keepdims=True)
        base = seen - TILE
        for h in range(4):
            left, right = slice(h * TILE, h * TILE + NEAR), slice(h * TILE + NEAR, (h + 1) * TILE)
            zero_part = d_wide[base : base + NEAR, left] + d_wide[base + NEAR :, right]
            one_part = d_wide[base : base + NEAR, right]
            if t > 0:
                one_part = one_part + d_wide[base - NEAR : base, left]
            both = jnp.concatenate([zero_part, one_part], axis=1)
            part = total[:, h * TILE : (h + 1) * TILE]
            if t == 0:
                near_sum[h] = both
                total_ref[0, h : h + 1, :] = part
            else:
                near_sum[h] += both
                total_ref[0, h : h + 1, :] += part
    dk_ref[...] = dk_whole.astype(jnp.bfloat16)
    dv_ref[...] = dv_whole.astype(jnp.bfloat16)

    for s in range(earlier):

        @pl.when(valid_ref[s] > 0)
        def _(s=s):
            kp_turned = kp_ref[s].T
            for t in range(steps):
                scores = dot(kp_ref[s], queries[t])
                if s == 0 and t == 0:
                    scores = add_corner(scores, tiles)
                prob, d_score = back_scores(scores, lses[t], dot(vp_ref[s], outs[t]), delta[t])
                d_value = dot(prob, do_placed[t])
                d_key = dot(d_score, q_placed[t])
                dv_whole = d_value if t == 0 else dv_whole + d_value
                dk_whole = d_key if t == 0 else dk_whole + d_key
                dq_sum[t] += dot(kp_turned, d_score)
                d_wide = d_score.astype(jnp.float32)
                total = jnp.sum(d_wide, axis=0, keepdims=True)
                for h in range(4):
                    total_ref[0, h : h + 1, :] += total[:, h * TILE : (h + 1) * TILE]
                    if s == 0 and t == 0:
                        near_sum[h, :, NEAR:] += d_wide[rows - NEAR :, h * TILE : h * TILE + NEAR]
            past_ref[s, 0] = dk_whole.astype(jnp.bfloat16)
            past_ref[s, 1] = dv_whole.astype(jnp.bfloat16)

        @pl.when(valid_ref[s] == 0)
        def _(s=s):
            past_ref[s] = jnp.zeros_like(past_ref[s])

    for t, cols in enumerate(spans):
        dq_ref[cols, :] = query_rows(dq_sum[t])
    for h in range(4):
        db_ref[0, h : h + 1, :] = by_distance(near_sum[h])
    db_ref[0, 4:, :] = jnp.zeros((4, 2 * NEAR), jnp.float32)
    total_ref[0, 4:, :] = jnp.zeros((4, 2 * NEAR), jnp.float32)


def self_backward(valid, table, q, k, v, kp, vp, do, o, lse):
    rows = q.shape[0]
    blocks = k.shape[1] // (2 * HEAD)
    earlier = kp.shape[0]
    wide = pl.BlockSpec((rows, 4 * HEAD), lambda p: (0, p))
    slim = pl.BlockSpec((rows, 2 * HEAD), lambda p: (0, p))
    past = pl.BlockSpec((earlier, rows, 2 * HEAD), lambda p: (0, 0, p))
    tab = pl.BlockSpec((1, 8, 2 * NEAR), lambda p: (p, 0, 0))
    return pl.pallas_call(
        functools.partial(self_backward_kernel, earlier=earlier),
        grid=(blocks,),
        in_specs=[
            pl.BlockSpec(memory_space=pltpu.SMEM), tab, wide, slim, slim, past, past, wide, wide,
            pl.BlockSpec((1, 8, rows), lambda p: (p, 0, 0)),
        ],
        out_specs=[wide, slim, slim, pl.BlockSpec((earlier, 2, rows, 2 * HEAD), lambda p: (0, 0, 0, p)), tab, tab],
        out_shape=[
            jax.ShapeDtypeStruct(q.shape, jnp.bfloat16),
            jax.ShapeDtypeStruct(k.shape, jnp.bfloat16),
            jax.ShapeDtypeStruct(k.shape, jnp.bfloat16),
            jax.ShapeDtypeStruct((earlier, 2) + k.shape, jnp.bfloat16),
            jax.ShapeDtypeStruct(table.shape, jnp.float32),
            jax.ShapeDtypeStruct(table.shape, jnp.float32),
        ],
        scratch_shapes=[
            pltpu.VMEM((4, NEAR, 2 * NEAR), jnp.float32),
            pltpu.VMEM((rows // TILE, 2 * HEAD, 4 * TILE), jnp.float32),
        ],
        compiler_params=pltpu.CompilerParams(vmem_limit_bytes=VMEM_LIMIT),
        cost_estimate=cost(0.01),
        name="self_backward",
    )(valid, table, q, k, v, kp, vp, do, o, lse)


def cross_forward_kernel(q_ref, k_ref, v_ref, own_ref, o_ref, lse_ref, *, masked):
    rows = q_ref.shape[0]
    v_turned = v_ref[...].T
    q_turned = q_ref[...].T
    spans = [slice(t * TILE, (t + 1) * TILE) for t in range(rows // TILE)]
    scores = [dot(k_ref[...], heads_of(q_turned, cols)) for cols in spans]
    if masked:
        blocked = jnp.where(own_ref[...] > 0, 0.0, NEGATIVE)
        blocked = jnp.concatenate([blocked] * 4, axis=1)
        scores = [score + blocked for score in scores]
    for t, cols in enumerate(spans):
        peak, weights, summed = soft(scores[t])
        finish(o_ref, lse_ref, cols, peak, summed, dot(v_turned, weights))


def cross_forward(q, k, v, own, masked):
    rows, keys = q.shape[0], k.shape[0]
    blocks = k.shape[1] // (2 * HEAD)
    wide = pl.BlockSpec((rows, 4 * HEAD), lambda p: (0, p))
    slim = pl.BlockSpec((keys, 2 * HEAD), lambda p: (0, p))
    return pl.pallas_call(
        functools.partial(cross_forward_kernel, masked=masked),
        grid=(blocks,),
        in_specs=[wide, slim, slim, pl.BlockSpec(own.shape, lambda p: (0, 0))],
        out_specs=[wide, pl.BlockSpec((1, 8, rows), lambda p: (p, 0, 0))],
        out_shape=[
            jax.ShapeDtypeStruct(q.shape, jnp.bfloat16),
            jax.ShapeDtypeStruct((blocks, 8, rows), jnp.float32),
        ],
        compiler_params=pltpu.CompilerParams(vmem_limit_bytes=VMEM_LIMIT),
        cost_estimate=cost(0.01),
        name="cross_forward",
    )(q, k, v, own)


def cross_backward_kernel(
    q_ref, k_ref, v_ref, own_ref, do_ref, o_ref, lse_ref, dq_ref, dk_ref, dv_ref, *, masked
):
    rows = q_ref.shape[0]
    k_turned = k_ref[...].T
    q_turned = q_ref[...].T
    do_turned = do_ref[...].T
    product = (do_ref[...].astype(jnp.float32) * o_ref[...].astype(jnp.float32)).T
    spans = [slice(t * TILE, (t + 1) * TILE) for t in range(rows // TILE)]
    dk_whole, dv_whole = 0.0, 0.0
    for t, cols in enumerate(spans):
        scores = dot(k_ref[...], heads_of(q_turned, cols))
        if masked:
            blocked = jnp.where(own_ref[...] > 0, 0.0, NEGATIVE)
            scores = scores + jnp.concatenate([blocked] * 4, axis=1)
        d_prob = dot(v_ref[...], heads_of(do_turned, cols))
        prob, d_score = back_scores(scores, row_of_heads(lse_ref, cols), d_prob, deltas(product, cols))
        dv_whole = dv_whole + dot(prob, placed_heads(do_ref, cols))
        dk_whole = dk_whole + dot(d_score, placed_heads(q_ref, cols))
        dq_ref[cols, :] = query_rows(dot(k_turned, d_score))
    dk_ref[...] = dk_whole.astype(jnp.bfloat16)
    dv_ref[...] = dv_whole.astype(jnp.bfloat16)


def cross_backward(q, k, v, own, do, o, lse, masked):
    rows, keys = q.shape[0], k.shape[0]
    blocks = k.shape[1] // (2 * HEAD)
    wide = pl.BlockSpec((rows, 4 * HEAD), lambda p: (0, p))
    slim = pl.BlockSpec((keys, 2 * HEAD), lambda p: (0, p))
    return pl.pallas_call(
        functools.partial(cross_backward_kernel, masked=masked),
        grid=(blocks,),
        in_specs=[wide, slim, slim, pl.BlockSpec(own.shape, lambda p: (0, 0)), wide, wide, pl.BlockSpec((1, 8, rows), lambda p: (p, 0, 0))],
        out_specs=[wide, slim, slim],
        out_shape=[
            jax.ShapeDtypeStruct(q.shape, jnp.bfloat16),
            jax.ShapeDtypeStruct(k.shape, jnp.bfloat16),
            jax.ShapeDtypeStruct(k.shape, jnp.bfloat16),
        ],
        compiler_params=pltpu.CompilerParams(vmem_limit_bytes=VMEM_LIMIT),
        cost_estimate=cost(0.01),
        name="cross_backward",
    )(q, k, v, own, do, o, lse)


def fixed(shape):
    return pl.BlockSpec(shape, lambda i, p: (0,) * len(shape))


def of_core(shape, axis):
    return pl.BlockSpec(shape, lambda i, p: tuple(p[1] if a == axis else 0 for a in range(len(shape))))


def of_peer(shape, axis):
    return pl.BlockSpec(shape, lambda i, p: tuple(1 - p[1] if a == axis else 0 for a in range(len(shape))))


def one_step(body, place, inputs, specs, outs, name, scratch=(), room=VMEM_LIMIT):
    return pl.pallas_call(
        body,
        grid_spec=pltpu.PrefetchScalarGridSpec(
            num_scalar_prefetch=1,
            grid=(1,),
            in_specs=specs,
            out_specs=[fixed(out.shape) for out in outs],
            scratch_shapes=list(scratch),
        ),
        out_shape=list(outs),
        compiler_params=pltpu.CompilerParams(vmem_limit_bytes=room),
        cost_estimate=cost(0.01),
        name=name,
    )(place, *inputs)


def shaped(shape, dtype=BF16):
    return jax.ShapeDtypeStruct(tuple(shape), dtype)


def in_place_order(core, own_ref, peer_ref):
    own, peer = own_ref[...].astype(F32), peer_ref[...].astype(F32)
    return jnp.concatenate([jnp.where(core == 0, own, peer), jnp.where(core == 0, peer, own)], axis=0)


def column_half(core, value):
    half = value.shape[1] // CORES
    return jnp.where(core == 0, value[:, :half], value[:, half:])


def dot_right(a, b):
    return lax.dot_general(a, b, (((1,), (1,)), ((), ())), preferred_element_type=F32)


def project_kernel(place_ref, own_ref, peer_ref, gain_ref, wq_ref, wk_ref, wv_ref, low_ref, q_ref, k_ref, v_ref):
    hidden = in_place_order(place_ref[1], own_ref, peer_ref)
    low = norm_low(hidden, inverse_norm(hidden), gain_ref[...].astype(F32))
    low_ref[...] = low
    q_ref[...] = dot(low, wq_ref[...]).astype(BF16)
    k_ref[...] = dot(low, wk_ref[...]).astype(BF16)
    v_ref[...] = dot(low, wv_ref[...]).astype(BF16)


def project(place, own, peer, gain, wq, wk, wv):
    rows, model = own.shape
    wide, slim = wq.shape[1] // CORES, wk.shape[1] // CORES
    return one_step(
        project_kernel,
        place,
        [own, peer, gain, wq, wk, wv],
        [
            fixed(own.shape),
            fixed(own.shape),
            fixed(gain.shape),
            of_core((model, wide), 1),
            of_core((model, slim), 1),
            of_core((model, slim), 1),
        ],
        [shaped((CORES * rows, n)) for n in (model, wide, slim, slim)],
        "project",
    )


def past_kernel(place_ref, *refs, earlier, groups):
    own_refs, peer_refs = refs[:earlier], refs[earlier : 2 * earlier]
    refs = refs[2 * earlier :]
    mem_refs, refs = refs[:groups], refs[groups:]
    gain_ref, wk_ref, wv_ref, wck_ref, wcv_ref = refs[:5]
    low_refs = refs[5 : 5 + earlier]
    k_ref, v_ref, mem_ref, km_ref, vm_ref = refs[5 + earlier :]
    rows = mem_refs[0].shape[0]
    for at, piece_ref in enumerate(mem_refs):
        block = jnp.bitwise_xor(place_ref[2], jnp.int32(at))
        mem_ref[pl.ds(pl.multiple_of(block * rows, rows), rows)] = piece_ref[...]
    mem = mem_ref[...]
    km_ref[...] = dot(mem, wck_ref[...]).astype(BF16)
    vm_ref[...] = dot(mem, wcv_ref[...]).astype(BF16)
    for s in range(earlier):
        hidden = in_place_order(place_ref[1], own_refs[s], peer_refs[s])
        low = norm_low(hidden, inverse_norm(hidden), gain_ref[...].astype(F32))
        low_refs[s][...] = low
        k_ref[s] = dot(low, wk_ref[...]).astype(BF16)
        v_ref[s] = dot(low, wv_ref[...]).astype(BF16)


def project_past(place, owns, peers, mems, gain, wk, wv, wck, wcv):
    rows, model = owns[0].shape
    earlier, groups = len(owns), len(mems)
    slim = wk.shape[1] // CORES
    weight = of_core((model, slim), 1)
    mem_rows = groups * mems[0].shape[0]
    outs = one_step(
        functools.partial(past_kernel, earlier=earlier, groups=groups),
        place,
        owns + peers + mems + [gain, wk, wv, wck, wcv],
        [fixed((rows, model))] * (2 * earlier)
        + [fixed(mems[0].shape)] * groups
        + [fixed(gain.shape), weight, weight, weight, weight],
        [shaped((CORES * rows, model))] * earlier
        + [shaped((earlier, CORES * rows, slim))] * 2
        + [shaped((mem_rows, model)), shaped((mem_rows, slim)), shaped((mem_rows, slim))],
        "project_past",
    )
    return outs[:earlier], *outs[earlier:]


def mid_kernel(
    place_ref, own_ref, peer_ref, att_ref, att_peer_ref, wo_ref, wo_peer_ref, gain_ref, wq_ref, mid_ref, low_ref, q_ref
):
    hidden = in_place_order(place_ref[1], own_ref, peer_ref)
    hidden = hidden + dot(att_ref[...], wo_ref[...]) + dot(att_peer_ref[...], wo_peer_ref[...])
    mid_ref[...] = hidden.astype(BF16)
    low = norm_low(hidden, inverse_norm(hidden), gain_ref[...].astype(F32))
    low_ref[...] = low
    q_ref[...] = dot(low, wq_ref[...]).astype(BF16)


def mid_forward(place, own, peer, att, att_peer, wo, gain, wq):
    rows, model = own.shape
    half = wo.shape[0] // CORES
    wide = wq.shape[1] // CORES
    return one_step(
        mid_kernel,
        place,
        [own, peer, att, att_peer, wo, wo, gain, wq],
        [fixed(own.shape)] * 2
        + [fixed(att.shape)] * 2
        + [of_core((half, model), 0), of_peer((half, model), 0), fixed(gain.shape), of_core((model, wide), 1)],
        [shaped((CORES * rows, model)), shaped((CORES * rows, model)), shaped((CORES * rows, wide))],
        "mid_forward",
    )


def ffn_kernel(
    place_ref, mid_ref, crs_ref, crs_peer_ref, gain_ref, cot_ref, cot_peer_ref, wc_hbm, wg_hbm, wu_hbm, wd_hbm,
    late_ref, low_ref, inner_ref, dg_ref, du_ref, dz_ref, cot_half_ref,
    wc, wg, wu, wd, sems, *, steps,
):
    core = place_ref[1]
    half, hidden_half = wc.shape[1], wd.shape[0]
    copies = [
        pltpu.make_async_copy(wc_hbm.at[pl.ds(pl.multiple_of(core * half, half), half)], wc.at[0], sems.at[0]),
        pltpu.make_async_copy(wc_hbm.at[pl.ds(pl.multiple_of((1 - core) * half, half), half)], wc.at[1], sems.at[1]),
        pltpu.make_async_copy(wg_hbm.at[:, pl.ds(pl.multiple_of(core * hidden_half, 128), hidden_half)], wg, sems.at[2]),
        pltpu.make_async_copy(wu_hbm.at[:, pl.ds(pl.multiple_of(core * hidden_half, 128), hidden_half)], wu, sems.at[3]),
        pltpu.make_async_copy(wd_hbm.at[pl.ds(pl.multiple_of(core * hidden_half, 16), hidden_half)], wd, sems.at[4]),
    ]
    for copy in copies:
        copy.start()
    cot = in_place_order(core, cot_ref, cot_peer_ref).astype(BF16)
    cot_half_ref[...] = column_half(core, cot)
    copies[0].wait()
    copies[1].wait()
    hidden = mid_ref[...].astype(F32) + dot(crs_ref[...], wc[0]) + dot(crs_peer_ref[...], wc[1])
    late_ref[...] = hidden.astype(BF16)
    low = norm_low(hidden, inverse_norm(hidden), gain_ref[...].astype(F32))
    low_ref[...] = low
    for copy in copies[2:]:
        copy.wait()
    scale = 0.7978845608028654
    start = 0
    for width in steps:
        cols = slice(start, start + width)
        start += width
        gate = dot(low, wg[:, cols])
        up = dot(low, wu[:, cols])
        d_inner = dot_right(cot, wd[cols]).astype(BF16).astype(F32)
        square = gate * gate
        bent = jnp.tanh(scale * gate * (1.0 + 0.044715 * square))
        whole = 0.5 * (1.0 + bent)
        slope = whole + 0.5 * gate * (1.0 - bent * bent) * (scale * (1.0 + 3 * 0.044715 * square))
        curve = gate * whole
        inner_ref[:, cols] = (curve * up).astype(BF16)
        dg_ref[:, cols] = (d_inner * up * slope).astype(BF16)
        du_ref[:, cols] = (d_inner * curve).astype(BF16)
    dz_ref[...] = (dot_right(dg_ref[...], wg[...]) + dot_right(du_ref[...], wu[...])).astype(BF16)


def ffn(place, mid, crs, crs_peer, gain, cot, cot_peer, wc, wg, wu, wd):
    rows, model = mid.shape
    half = wc.shape[0] // CORES
    hidden_half = wd.shape[0] // CORES
    steps = [256] * (hidden_half // 256) + [hidden_half % 256] * (hidden_half % 256 > 0)
    anywhere = pl.BlockSpec(memory_space=pl.ANY)
    return one_step(
        functools.partial(ffn_kernel, steps=steps),
        place,
        [mid, crs, crs_peer, gain, cot, cot_peer, wc, wg, wu, wd],
        [fixed(mid.shape), fixed(crs.shape), fixed(crs.shape), fixed(gain.shape), fixed(cot.shape), fixed(cot.shape)]
        + [anywhere] * 4,
        [shaped((rows, model))] * 2
        + [shaped((rows, hidden_half))] * 3
        + [shaped((rows, model)), shaped((rows, model // CORES))],
        "ffn",
        [
            pltpu.VMEM((2, half, model), BF16),
            pltpu.VMEM((model, hidden_half), BF16),
            pltpu.VMEM((model, hidden_half), BF16),
            pltpu.VMEM((hidden_half, model), BF16),
            pltpu.SemaphoreType.DMA((5,)),
        ],
        56 * 1024 * 1024,
    )


def late_kernel(
    place_ref, dz_ref, dz_peer_ref, late_ref, cot_ref, cot_peer_ref, gain_ref, wc_ref, g_ref, half_ref, d_ref, gain_out
):
    dz = dz_ref[...].astype(F32) + dz_peer_ref[...].astype(F32)
    hidden = late_ref[...].astype(F32)
    inverse = inverse_norm(hidden)
    gain_out[...] = jnp.sum(dz * hidden * inverse, axis=0, keepdims=True)
    grad = in_place_order(place_ref[1], cot_ref, cot_peer_ref) + norm_back(
        hidden, inverse, gain_ref[...].astype(F32), dz
    )
    low = grad.astype(BF16)
    g_ref[...] = low
    half_ref[...] = column_half(place_ref[1], low)
    d_ref[...] = dot_right(low, wc_ref[...]).astype(BF16)


def late_backward(place, dz, dz_peer, late, cot, cot_peer, gain, wc):
    rows, model = late.shape
    half = wc.shape[0] // CORES
    return one_step(
        late_kernel,
        place,
        [dz, dz_peer, late, cot, cot_peer, gain, wc],
        [fixed(a.shape) for a in (dz, dz_peer, late, cot, cot_peer, gain)] + [of_core((half, model), 0)],
        [shaped((rows, model)), shaped((rows, model // CORES)), shaped((rows, half)), shaped((1, model), F32)],
        "late_backward",
    )


def mid_back_kernel(
    place_ref, dq_ref, dq_peer_ref, wq_ref, wq_peer_ref, mid_ref, g_ref, gain_ref, wo_ref, out_ref, half_ref, d_ref, gain_out
):
    dz = dot_right(dq_ref[...], wq_ref[...]) + dot_right(dq_peer_ref[...], wq_peer_ref[...])
    hidden = mid_ref[...].astype(F32)
    inverse = inverse_norm(hidden)
    gain_out[...] = jnp.sum(dz * hidden * inverse, axis=0, keepdims=True)
    grad = g_ref[...].astype(F32) + norm_back(hidden, inverse, gain_ref[...].astype(F32), dz)
    core, rows = place_ref[1], g_ref.shape[0] // CORES
    out_ref[...] = jnp.where(core == 0, grad[:rows], grad[rows:]).astype(BF16)
    low = grad.astype(BF16)
    half_ref[...] = column_half(core, low)
    d_ref[...] = dot_right(low, wo_ref[...]).astype(BF16)


def mid_backward(place, dq, dq_peer, wq, mid, g_late, gain, wo):
    rows, model = mid.shape
    half = wo.shape[0] // CORES
    wide = wq.shape[1] // CORES
    return one_step(
        mid_back_kernel,
        place,
        [dq, dq_peer, wq, wq, mid, g_late, gain, wo],
        [fixed(dq.shape)] * 2
        + [of_core((model, wide), 1), of_peer((model, wide), 1)]
        + [fixed(mid.shape)] * 2
        + [fixed(gain.shape), of_core((half, model), 0)],
        [shaped((rows // CORES, model)), shaped((rows, model // CORES)), shaped((rows, half)), shaped((1, model), F32)],
        "mid_backward",
    )


def first_kernel(place_ref, dq_ref, dk_ref, dv_ref, *refs, extra):
    past = refs[:extra]
    wq_ref, wk_ref, wv_ref, own_ref, peer_ref = refs[extra:]
    dk, dv = dk_ref[...].astype(F32), dv_ref[...].astype(F32)
    for ref in past:
        dk = dk + ref[0].astype(F32)
        dv = dv + ref[1].astype(F32)
    dz = dot_right(dq_ref[...], wq_ref[...])
    dz = dz + dot_right(dk.astype(BF16), wk_ref[...]) + dot_right(dv.astype(BF16), wv_ref[...])
    core, rows = place_ref[1], own_ref.shape[0]
    own_ref[...] = jnp.where(core == 0, dz[:rows], dz[rows:])
    peer_ref[...] = jnp.where(core == 0, dz[rows:], dz[:rows]).astype(BF16)


def first_backward(place, dq, dk, dv, past, wq, wk, wv):
    rows = dq.shape[0]
    model = wq.shape[0]
    wide, slim = wq.shape[1] // CORES, wk.shape[1] // CORES
    return one_step(
        functools.partial(first_kernel, extra=len(past)),
        place,
        [dq, dk, dv] + past + [wq, wk, wv],
        [fixed(dq.shape), fixed(dk.shape), fixed(dv.shape)]
        + [fixed(a.shape) for a in past]
        + [of_core((model, wide), 1), of_core((model, slim), 1), of_core((model, slim), 1)],
        [shaped((rows // CORES, model), F32), shaped((rows // CORES, model))],
        "first_backward",
    )


def tokens_kernel(place_ref, dz_ref, dz_got_ref, tokens_ref, g_ref, gain_ref, out_ref, gain_out):
    dz = dz_ref[...] + dz_got_ref[...].astype(F32)
    hidden = tokens_ref[...].astype(F32)
    inverse = inverse_norm(hidden)
    gain_out[...] = jnp.sum(dz * hidden * inverse, axis=0, keepdims=True)
    out_ref[...] = (g_ref[...].astype(F32) + norm_back(hidden, inverse, gain_ref[...].astype(F32), dz)).astype(BF16)


def tokens_backward(place, dz, dz_got, tokens, g_mid, gain):
    return one_step(
        tokens_kernel,
        place,
        [dz, dz_got, tokens, g_mid, gain],
        [fixed(a.shape) for a in (dz, dz_got, tokens, g_mid, gain)],
        [shaped(tokens.shape), shaped((1, tokens.shape[1]), F32)],
        "tokens_backward",
    )


def out_kernel(place_ref, late_ref, inner_ref, inner_peer_ref, wd_ref, wd_peer_ref, out_ref):
    rows = out_ref.shape[0]
    core = place_ref[1]
    own = jnp.where(core == 0, late_ref[:rows], late_ref[rows:]).astype(F32)
    inner = jnp.where(core == 0, inner_ref[:rows], inner_ref[rows:])
    inner_peer = jnp.where(core == 0, inner_peer_ref[:rows], inner_peer_ref[rows:])
    out_ref[...] = (own + dot(inner, wd_ref[...]) + dot(inner_peer, wd_peer_ref[...])).astype(BF16)


def layer_output(place, late, inner, inner_peer, wd):
    rows, model = late.shape
    half = wd.shape[0] // CORES
    return one_step(
        out_kernel,
        place,
        [late, inner, inner_peer, wd, wd],
        [fixed(late.shape), fixed(inner.shape), fixed(inner.shape), of_core((half, model), 0), of_peer((half, model), 0)],
        [shaped((rows // CORES, model))],
        "layer_output",
    )[0]


def place_of(position, order):
    spot = jnp.int32(0)
    for bit in order:
        spot = spot * 2 + jnp.bitwise_and(lax.shift_right_logical(position, jnp.int32(bit)), 1)
    return spot


def sums_kernel(place_ref, *refs, n_x, n_y, flows):
    n = len(flows)
    x_refs, y_refs = refs[:n_x], refs[n_x : n_x + n_y]
    outs = refs[n_x + n_y : n_x + n_y + 2 * n]
    buffers, sems = refs[n_x + n_y + 2 * n : n_x + n_y + 3 * n], refs[n_x + n_y + 3 * n :]
    chip, core = place_ref[0], place_ref[1]
    turned = {}
    pending = []
    for f, (columns, rows_out, order, _) in enumerate(flows):
        send_ref, keep_ref = outs[2 * f], outs[2 * f + 1]
        buffer, sem = buffers[f], sems[f]
        chips = 1 << len(order)
        half, chunk = chips // 2, rows_out // chips

        def leave(number, at):
            spot = place_of(jnp.bitwise_xor(number, chip), order)
            send = pltpu.make_async_copy(buffer.at[number], send_ref.at[jnp.maximum(spot - half, 0)], sem.at[at])
            keep = pltpu.make_async_copy(buffer.at[number], keep_ref.at[jnp.minimum(spot, half - 1)], sem.at[at])
            pl.when(spot >= half)(send.start)
            pl.when(spot < half)(keep.start)
            pending.append((spot >= half, send, keep))

        start = 0
        for c, terms in enumerate(columns):
            width = y_refs[terms[0][1]].shape[1]
            parts = len(terms[0][0])
            part_rows = rows_out // parts
            step = max(s for s in range(chunk, 513, chunk) if part_rows % s == 0)
            for part in range(parts):
                for first in range(0, part_rows, step):
                    tile = None
                    for x_ids, y_id in terms:
                        x = x_ids[part]
                        if x not in turned:
                            turned[x] = x_refs[x][...].T
                        term = dot(turned[x][first : first + step], y_refs[y_id][...])
                        tile = term if tile is None else tile + term
                    number = first // chunk
                    if parts == 2:
                        number = number + (core if part == 0 else 1 - core) * (part_rows // chunk)
                    count = step // chunk
                    buffer[pl.ds(number, count), :, start : start + width] = tile.astype(BF16).reshape(
                        count, chunk, width
                    )
                    if len(columns) == 1:
                        for inner in range(count):
                            leave(number + inner, (part * part_rows + first) // chunk + inner)
            start += width
        if len(columns) > 1:
            for number in range(chips):
                leave(number, number)
    for leaves, send, keep in pending:
        pl.when(leaves)(send.wait)
        pl.when(jnp.logical_not(leaves))(keep.wait)


def array_of(y):
    return y[0] if isinstance(y, tuple) else y


def page_of(y):
    if not isinstance(y, tuple):
        return fixed(y.shape)
    array, at = y
    return pl.BlockSpec((None,) * len(at) + array.shape[len(at) :], lambda i, p: at + (0, 0))


def plain_sums(place, xs, ys, columns, rows_out, order):
    ys = [y[0][y[1]] if isinstance(y, tuple) else y for y in ys]
    chips = 1 << len(order)
    half, chunk = chips // 2, rows_out // chips
    pieces = []
    for terms in columns:
        total = 0.0
        for x_ids, y_id in terms:
            parts = [matmul_left(xs[x], ys[y_id]) for x in x_ids]
            if len(parts) == 2:
                swapped = place[1] == 1
                parts = [jnp.where(swapped, parts[1], parts[0]), jnp.where(swapped, parts[0], parts[1])]
            total = total + jnp.concatenate(parts, axis=0)
        pieces.append(total.astype(BF16))
    whole = jnp.concatenate(pieces, axis=1).reshape(chips, chunk, -1)
    where = jnp.arange(chips, dtype=jnp.int32)
    position = sum((((where >> (len(order) - 1 - at)) & 1) << bit) for at, bit in enumerate(order))
    whole = jnp.take(whole, jnp.bitwise_xor(position, place[0]), axis=0)
    return [whole[half:], whole[:half]]


def weight_sums(place, xs, ys, flows, name):
    if any((rows_out >> len(order)) % 16 for _, rows_out, order, _ in flows):
        return sum((plain_sums(place, xs, ys, *flow[:3]) for flow in flows), [])
    outs, buffers, sems = [], [], []
    for columns, rows_out, order, _ in flows:
        chips = 1 << len(order)
        width = sum(array_of(ys[terms[0][1]]).shape[-1] for terms in columns)
        outs += [shaped((chips // 2, rows_out // chips, width))] * 2
        buffers.append(pltpu.VMEM((chips, rows_out // chips, width), BF16))
        sems.append(pltpu.SemaphoreType.DMA((chips,)))
    return pl.pallas_call(
        functools.partial(sums_kernel, n_x=len(xs), n_y=len(ys), flows=flows),
        grid_spec=pltpu.PrefetchScalarGridSpec(
            num_scalar_prefetch=1,
            grid=(1,),
            in_specs=[fixed(a.shape) for a in xs] + [page_of(y) for y in ys],
            out_specs=[pl.BlockSpec(memory_space=pl.ANY)] * len(outs),
            scratch_shapes=buffers + sems,
        ),
        out_shape=outs,
        compiler_params=pltpu.CompilerParams(vmem_limit_bytes=VMEM_LIMIT),
        cost_estimate=cost(0.01),
        name=name,
    )(place, *xs, *[array_of(y) for y in ys])


def add_kernel(*refs, n):
    for f in range(n):
        keep_low, keep_high, got_low, got_high = refs[4 * f : 4 * f + 4]
        send_ref, keep_ref = refs[4 * n + 2 * f : 4 * n + 2 * f + 2]
        keep_ref[...] = (keep_low[...].astype(F32) + got_low[...].astype(F32)).astype(keep_ref.dtype)
        send_ref[...] = (keep_high[...].astype(F32) + got_high[...].astype(F32)).astype(send_ref.dtype)


def add_halves(pairs, name):
    half = pairs[0][0].shape[0] // 2
    inputs, specs, outs, out_specs = [], [], [], []
    for keep, got in pairs:
        block = (1,) + keep.shape[1:]
        low = pl.BlockSpec(block, lambda i: (i, 0, 0))
        high = pl.BlockSpec(block, lambda i: (i + half, 0, 0))
        inputs += [keep, keep, got, got]
        specs += [low, high, low, high]
        outs += [shaped((half,) + keep.shape[1:], keep.dtype)] * 2
        out_specs += [low, low]
    return pl.pallas_call(
        functools.partial(add_kernel, n=len(pairs)),
        grid=(half,),
        in_specs=specs,
        out_specs=out_specs,
        out_shape=outs,
        compiler_params=pltpu.CompilerParams(vmem_limit_bytes=VMEM_LIMIT),
        cost_estimate=cost(0.01),
        name=name,
    )(*inputs)


def halves_of(core, value):
    rows = value.shape[0] // CORES
    return jnp.where(core == 0, value[:rows], value[rows:]), jnp.where(core == 0, value[rows:], value[:rows])


def last_add_kernel(place_ref, *refs, groups, n):
    owns, leaves = refs[2 * n : 3 * n], refs[3 * n :]
    for leave_ref, members in zip(leaves, groups):
        start = 0
        for f in members:
            value = refs[2 * f][0].astype(F32) + refs[2 * f + 1][0].astype(F32)
            own, leave = halves_of(place_ref[1], value)
            owns[f][...] = own
            leave_ref[:, start : start + value.shape[1]] = leave.astype(BF16)
            start += value.shape[1]


def last_add(place, pairs, groups, name):
    inputs, outs = [], []
    for keep, got in pairs:
        inputs += [keep, got]
        outs.append(shaped((keep.shape[1] // CORES, keep.shape[2]), F32))
    for members in groups:
        rows = pairs[members[0]][0].shape[1] // CORES
        outs.append(shaped((rows, sum(pairs[f][0].shape[2] for f in members))))
    made = one_step(
        functools.partial(last_add_kernel, groups=groups, n=len(pairs)),
        place,
        inputs,
        [fixed(a.shape) for a in inputs],
        outs,
        name,
    )
    return made[: len(pairs)], made[len(pairs) :]


def join_kernel(place_ref, *refs, n_own, n_got, columns):
    owns, gots, outs = refs[:n_own], refs[n_own : n_own + n_got], refs[n_own + n_got :]
    core = place_ref[1]
    for (f, g, start, got_start, width), out_ref in zip(columns, outs):
        own = owns[f][:, start : start + width]
        got = gots[g][:, got_start : got_start + width].astype(F32)
        out_ref[:, :width] = jnp.where(core == 0, own, got)
        out_ref[:, width:] = jnp.where(core == 0, got, own)


def join(place, owns, gots, columns, name):
    outs = [shaped((owns[f].shape[0], CORES * width), F32) for f, _, _, _, width in columns]
    return one_step(
        functools.partial(join_kernel, n_own=len(owns), n_got=len(gots), columns=columns),
        place,
        list(owns) + list(gots),
        [fixed(a.shape) for a in list(owns) + list(gots)],
        outs,
        name,
    )


def memory_kernel(place_ref, dk_ref, dv_ref, wk_ref, wv_ref, send_ref, keep_ref):
    grad = (dot_right(dk_ref[...], wk_ref[...]) + dot_right(dv_ref[...], wv_ref[...])).astype(BF16)
    half, rows = send_ref.shape[0], send_ref.shape[1]
    for block in range(2 * half):
        spot = jnp.bitwise_xor(jnp.int32(block), place_ref[2])
        piece = grad[block * rows : (block + 1) * rows]

        @pl.when(spot >= half)
        def _(spot=spot, piece=piece):
            send_ref[spot - half] = piece

        @pl.when(spot < half)
        def _(spot=spot, piece=piece):
            keep_ref[spot] = piece


def memory_backward(place, dk, dv, wk, wv, groups):
    model = wk.shape[0]
    slim = wk.shape[1] // CORES
    out = shaped((groups // 2, dk.shape[0] // groups, model))
    return one_step(
        memory_kernel,
        place,
        [dk, dv, wk, wv],
        [fixed(dk.shape), fixed(dv.shape), of_core((model, slim), 1), of_core((model, slim), 1)],
        [out, out],
        "memory_backward",
    )


def small_kernel(place_ref, one_ref, two_ref, three_ref, near_ref, total_ref, bucket_ref, send_ref, keep_ref, *, heads):
    chip, core = place_ref[0], place_ref[1]
    half = send_ref.shape[0]
    chips = 2 * half
    model = one_ref.shape[1]
    first = core == 0
    gains = [one_ref[...], jnp.where(first, two_ref[...], 0.0), jnp.where(first, three_ref[...], 0.0)]
    near = jnp.concatenate([near_ref[p, :4] for p in range(heads // 4)], axis=0)
    total = jnp.concatenate([total_ref[p, :4] for p in range(heads // 4)], axis=0)
    far = jnp.sum(total, axis=1, keepdims=True) - jnp.sum(near, axis=1, keepdims=True)
    last = lax.broadcasted_iota(jnp.int32, near.shape, 1) == near.shape[1] - 1
    near = near + jnp.where(last, far, 0.0)
    entries = BUCKETS * HEADS
    entry = lax.broadcasted_iota(jnp.int32, (near.shape[1], entries), 1)
    same = (lax.shift_right_logical(entry, jnp.int32(HEADS.bit_length() - 1)) == bucket_ref[...]).astype(F32)
    sums = jnp.dot(near, same, precision=lax.Precision.HIGHEST, preferred_element_type=F32)
    head = lax.broadcasted_iota(jnp.int32, sums.shape, 0) + core * heads
    of_entry = jnp.bitwise_and(lax.broadcasted_iota(jnp.int32, sums.shape, 1), jnp.int32(HEADS - 1))
    relative = jnp.sum(jnp.where(head == of_entry, sums, 0.0), axis=0, keepdims=True)
    vectors = gains + [relative]
    lanes = send_ref.shape[2]
    for block in range(chips):
        rows = []
        for vector in vectors:
            size = vector.shape[1] // chips
            row = vector[:, block * size : (block + 1) * size]
            rows.append(jnp.concatenate([row, jnp.zeros((1, lanes - size), F32)], axis=1))
        tile = jnp.concatenate(rows + [jnp.zeros((4, lanes), F32)], axis=0)
        spot = jnp.bitwise_xor(jnp.int32(block), chip)

        @pl.when(spot >= half)
        def _(spot=spot, tile=tile):
            send_ref[spot - half] = tile

        @pl.when(spot < half)
        def _(spot=spot, tile=tile):
            keep_ref[spot] = tile


def small_sums(place, one, two, three, near, total, buckets, heads, chips):
    inputs = [one, two, three, near, total, buckets]
    out = shaped((chips // 2, 8, 128), F32)
    return one_step(
        functools.partial(small_kernel, heads=heads),
        place,
        inputs,
        [fixed(a.shape) for a in inputs],
        [out, out],
        "small_sums",
    )


def pair_kernel(place_ref, *refs):
    n = len(refs) // 3
    for f in range(n):
        out_ref = refs[2 * n + f]
        out_ref[...] = (refs[2 * f][0].astype(F32) + refs[2 * f + 1][0].astype(F32)).astype(out_ref.dtype)


def pair_sums(place, pairs, name):
    inputs = [a for pair in pairs for a in pair]
    return one_step(
        pair_kernel, place, inputs, [fixed(a.shape) for a in inputs], [shaped(a.shape[1:], a.dtype) for a, _ in pairs], name
    )


def matmul_left(a, b):
    return lax.dot_general(a, b, (((0,), (0,)), ((), ())), preferred_element_type=F32)


def rel_bucket(distance):
    beyond = 16 + sum((distance >= border).astype(jnp.int32) for border in THRESHOLDS)
    return jnp.where(distance < 16, distance, beyond)


def inverse_norm(hidden):
    return lax.rsqrt(jnp.mean(hidden * hidden, axis=-1, keepdims=True) + EPSILON)


def norm_low(hidden, inverse, gain):
    return (hidden * inverse * gain).astype(BF16)


def norm_back(hidden, inverse, gain, dz):
    scaled = gain * dz
    inner = jnp.mean(scaled * hidden, axis=-1, keepdims=True)
    return inverse * scaled - hidden * (inverse * inverse * inverse) * inner


def follow(value, after):
    return lax.optimization_barrier((value, after))[0]


def shards(
    tokens, memory, cotangent, bucket, gain_self, self_query, self_key, self_value, self_out, rel_bias,
    gain_cross, cross_query, cross_key, cross_value, cross_out, gain_ffn, ffn_gate, ffn_up, ffn_down,
):
    groups = lax.axis_size("grp")
    dp_size = lax.axis_size("dp")
    n_chips = groups // CORES
    chips = dp_size * n_chips
    grp_at = lax.axis_index("grp")
    core = grp_at % CORES
    y_at = grp_at // CORES
    chip = lax.axis_index("dp") * n_chips + y_at
    place = jnp.stack([chip, core, grp_at]).astype(jnp.int32)
    rows, model = tokens.shape
    chip_rows = rows * CORES
    group_rows = chip_rows * n_chips
    hidden_units = ffn_down.shape[0]
    length = jnp.minimum(group_rows, jnp.maximum(SHORT, jnp.right_shift(jnp.int32(group_rows), bucket[0])))
    masked = group_rows > SHORT
    y_bits = n_chips.bit_length() - 1
    bits = chips.bit_length() - 1

    def swap(v, bit):
        return lax.ppermute(v, ("dp", "grp"), [(i, i ^ (1 << bit)) for i in range(chips * CORES)])

    def swap_core(v):
        return swap(v, 0)

    def in_order(own, peer, axis=0):
        return jnp.where(core == 0, jnp.concatenate([own, peer], axis), jnp.concatenate([peer, own], axis))

    def part_of(v, at, axis):
        size = v.shape[axis] // CORES
        return lax.dynamic_slice_in_dim(v, at * size, size, axis)

    gain_one, gain_two, gain_three = (g.reshape(1, model) for g in (gain_self, gain_cross, gain_ffn))

    past_own = [
        lax.ppermute(tokens, "grp", [(g, g + CORES * s) for g in range(groups - CORES * s)]) for s in range(1, n_chips)
    ]
    tokens_peer = swap_core(tokens)
    mems = [memory] + [
        lax.ppermute(memory, "grp", [(g, g ^ other) for g in range(groups)]) for other in range(1, groups)
    ]
    cot_peer = swap_core(cotangent)

    distances = jnp.arange(2 * NEAR, dtype=jnp.int32)
    onehot = (rel_bucket(distances)[:, None] == jnp.arange(BUCKETS, dtype=jnp.int32)).astype(F32)
    rel_local = part_of(rel_bias.astype(F32), core, 1)
    heads = rel_local.shape[1]
    by_dist = jnp.dot(onehot, rel_local - rel_local[BUCKETS - 1 :], precision=lax.Precision.HIGHEST)
    table = jnp.pad(by_dist.T.reshape(heads // 4, 4, 2 * NEAR), ((0, 0), (0, 4), (0, 0)))

    low_one, q, k, v = project(place, tokens, tokens_peer, gain_one, self_query, self_key, self_value)
    past_own = [follow(own, q) for own in past_own]
    past_peer = [swap_core(own) for own in past_own]
    low_past, k_past, v_past, mem_all, km, vm = project_past(
        place, past_own, past_peer, mems, gain_one, self_key, self_value, cross_key, cross_value
    )
    first_chip = y_at * chip_rows // length * length // chip_rows
    valid = jnp.stack([(y_at - s >= first_chip).astype(jnp.int32) for s in range(1, n_chips)])
    att, lse_self = self_forward(valid, table, q, k, v, k_past, v_past)
    att_peer = swap_core(att)
    mid, low_two, cq = mid_forward(place, tokens, tokens_peer, att, att_peer, self_out, gain_two, cross_query)
    mem_doc = jnp.arange(mem_all.shape[0], dtype=jnp.int32) // (length // RATIO)
    own_doc = jnp.broadcast_to((mem_doc == y_at * chip_rows // length).astype(F32)[:, None], (mem_all.shape[0], TILE))
    crs, lse_cross = cross_forward(cq, km, vm, own_doc, masked)
    crs_peer = swap_core(crs)
    late, low_three, inner, d_gate, d_up, dz, cot_half = ffn(
        place, mid, crs, crs_peer, gain_three, cotangent, cot_peer, cross_out, ffn_gate, ffn_up, ffn_down
    )

    x_bit, z_bit, far_bits = y_bits, y_bits + 1, tuple(range(y_bits + 2, bits))
    y_order = tuple(range(y_bits))
    orders = (
        (x_bit,) + y_order + (z_bit,) + far_bits,
        y_order + (z_bit, x_bit) + far_bits,
        (z_bit, x_bit) + y_order + far_bits,
    )
    state = {}

    def begin(call, xs, ys, flows):
        made = weight_sums(place, xs, ys, flows, call)
        for f, (_, _, order, name) in enumerate(flows):
            hops = [bit + 1 for bit in order]
            state[name] = {"keep": made[2 * f + 1], "got": swap(made[2 * f], hops[0]), "hops": hops[1:]}
        return made

    def advance(names, after):
        pairs = [(state[name]["keep"], state[name]["got"]) for name in names]
        pairs = follow(pairs, after)
        made = add_halves(pairs, "add_" + "_".join(names))
        for f, name in enumerate(names):
            flow = state[name]
            flow["keep"], flow["got"] = made[2 * f + 1], swap(made[2 * f], flow["hops"][0])
            flow["hops"] = flow["hops"][1:]
        return made

    def conclude(names, wanted, after):
        pairs = [(state[name]["keep"], state[name]["got"]) for name in names]
        pairs = follow(pairs, after)
        by_rows = {}
        for f, (keep, _) in enumerate(pairs):
            by_rows.setdefault(keep.shape[1], []).append(f)
        members = list(by_rows.values())
        owns, leaves = last_add(place, pairs, members, "last_" + "_".join(names))
        gots = [swap_core(leave) for leave in leaves]
        columns = []
        for name, start, width in wanted:
            f = names.index(name)
            g = [f in group for group in members].index(True)
            before = sum(pairs[m][0].shape[2] for m in members[g][: members[g].index(f)])
            columns.append((f, g, start, before + start, width))
        return join(place, owns, gots, columns, "join_" + "_".join(names))

    inner_peer = swap_core(inner)
    dz_peer = swap_core(dz)
    last = begin(
        "gate_up_sums",
        [low_three],
        [d_gate, d_up],
        [([[((0,), 0)]], model, orders[0], "gate"), ([[((0,), 1)]], model, orders[1], "up")],
    )
    last = begin(
        "down_sums",
        [follow(inner, last), inner_peer],
        [cot_half],
        [([[((0, 1), 0)]], hidden_units, orders[2], "down")],
    )
    dz = follow(dz, last)

    g_late, late_half, d_crs, d_gain_three = late_backward(
        place, dz, dz_peer, late, cotangent, cot_peer, gain_three, cross_out
    )
    dcq, dkm, dvm = cross_backward(cq, km, vm, own_doc, d_crs, crs, lse_cross, masked)
    dcq_peer = swap_core(dcq)
    g_mid, mid_half, d_att, d_gain_two = mid_backward(
        place, dcq, dcq_peer, cross_query, mid, g_late, gain_two, self_out
    )
    dq, dk, dv, d_past, d_near, d_total = self_backward(
        valid, table, q, k, v, k_past, v_past, d_att, att, lse_self
    )
    more = n_chips - 1
    past_moved = [
        lax.ppermute(d_past[s - 1], "grp", [(g, g - CORES * s) for g in range(CORES * s, groups)])
        for s in range(1, n_chips)
    ]
    last = advance(["gate", "up", "down"], dq)
    last = begin(
        "attention_sums",
        [follow(low_one, last)] + list(low_past) + [att, att_peer, crs, crs_peer, mem_all, low_two],
        [dq, dk, dv, mid_half, late_half, dkm, dvm, dcq]
        + [(d_past, (s, 0)) for s in range(more)]
        + [(d_past, (s, 1)) for s in range(more)],
        [
            ([[((0,), 0)], [((n_chips, n_chips + 1), 3)]], model, orders[0], "query_att"),
            (
                [
                    [((0,), 1)] + [((1 + s,), 8 + s) for s in range(more)],
                    [((0,), 2)] + [((1 + s,), 8 + more + s) for s in range(more)],
                    [((n_chips + 2, n_chips + 3), 4)],
                ],
                model,
                orders[1],
                "kv_crs",
            ),
            (
                [[((n_chips + 4,), 5)], [((n_chips + 4,), 6)], [((n_chips + 5,), 7)]],
                model,
                orders[2],
                "mem_cq",
            ),
        ],
    )
    mem_send, mem_keep = memory_backward(place, follow(dkm, last), dvm, cross_key, cross_value, groups)
    mem_state = {"keep": mem_keep, "got": swap(mem_send, y_bits), "hops": list(reversed(range(y_bits)))}
    state["memory"] = mem_state
    dz_own, dz_leave = first_backward(
        place, follow(dq, last), dk, dv, past_moved, self_query, self_key, self_value
    )
    layer_out = layer_output(place, late, inner, inner_peer, ffn_down)
    grad_tokens, d_gain_one = tokens_backward(place, dz_own, swap_core(dz_leave), tokens, g_mid, gain_one)

    buckets = rel_bucket(jnp.arange(2 * NEAR, dtype=jnp.int32))[:, None]
    small_send, small_keep = small_sums(
        place, d_gain_one, d_gain_two, d_gain_three, d_near, d_total, buckets, heads, chips
    )
    state["small"] = {"keep": small_keep, "got": swap(small_send, bits), "hops": list(reversed(range(1, bits)))}

    wide = model // 2
    slim = self_key.shape[1] // 2
    first, second = ["gate", "up", "down"], ["query_att", "kv_crs", "mem_cq"]
    last = grad_tokens
    left = {0: bits - 2, 1: bits - 1, 2: y_bits, 3: bits - 1}
    names = (first, second, ["memory"], ["small"])
    for turn in [3, 2, 0, 3, 1, 3] + [0, 1, 2, 3] * bits:
        if left[turn] > 0:
            last = advance(names[turn], last)
            left[turn] -= 1
    grad_memory, small = pair_sums(
        place, [(follow(state[n]["keep"], last), state[n]["got"]) for n in ("memory", "small")], "pair_sums"
    )
    small_got = swap_core(small)
    grads_ffn = conclude(first, [("gate", 0, hidden_units // 2), ("up", 0, hidden_units // 2), ("down", 0, wide)], last)
    grads_all = conclude(
        second,
        [
            ("query_att", 0, wide),
            ("kv_crs", 0, slim),
            ("kv_crs", slim, slim),
            ("query_att", wide, wide),
            ("mem_cq", 2 * slim, wide),
            ("mem_cq", 0, slim),
            ("mem_cq", slim, slim),
            ("kv_crs", 2 * slim, wide),
        ],
        last,
    )
    small = small + small_got
    share = model // chips // CORES
    gain_rows = lax.dynamic_slice(small, (jnp.int32(0), core * share), (3, share))
    rel_share = BUCKETS * HEADS // chips // CORES
    rel_row = lax.dynamic_slice(small, (jnp.int32(3), core * rel_share), (1, rel_share))[0]
    return (
        layer_out,
        grad_tokens,
        grad_memory,
        gain_rows[0],
        *grads_all[:4],
        rel_row,
        gain_rows[1],
        *grads_all[4:],
        gain_rows[2],
        *grads_ffn,
    )


def solution(mesh):
    rows = P(("dp", "grp"), None)
    flat = P(("dp", "grp"))
    in_specs = (rows, rows, rows, P("dp")) + (P(),) * 15
    out_specs = (rows,) * 3 + (flat,) + (rows,) * 4 + (flat,) * 2 + (rows,) * 4 + (flat,) + (rows,) * 3
    return jax.shard_map(shards, mesh=mesh, in_specs=in_specs, out_specs=out_specs, check_vma=False)
```

```python
import functools

import jax
import jax.numpy as jnp
from jax import lax
from jax.experimental import pallas as pl
from jax.experimental.pallas import tpu as pltpu
from jax.sharding import PartitionSpec as P

SHORT = 1024
RATIO = 4
BUCKETS = 32
HEADS = 16
EPSILON = 1e-06
THRESHOLDS = (19, 21, 24, 27, 31, 35, 40, 46, 52, 59, 67, 77, 87, 99, 113)
CORES = 2
BF16 = jnp.bfloat16
F32 = jnp.float32
NEGATIVE = -1e30
HEAD = 64
TILE = 256
NEAR = 128
LANES = 128
ROOM = 24 * 1024 * 1024


def dot(a, b):
    return jnp.dot(a, b, preferred_element_type=F32)


def dot_right(a, b):
    return lax.dot_general(a, b, (((1,), (1,)), ((), ())), preferred_element_type=F32)


def shaped(shape, dtype=BF16):
    return jax.ShapeDtypeStruct(tuple(shape), dtype)


def whole_kernel(body, place, arrays, weights, outs, name, scratch=(), room=ROOM, cost=0):
    n_a, n_w, n_o = len(arrays), len(weights), len(outs)
    buffers = []
    for array, axis, _ in weights:
        shape = list(array.shape)
        shape[axis] //= CORES
        buffers.append(pltpu.VMEM(tuple(shape), array.dtype))

    def kernel(place_ref, *refs):
        array_refs, refs = refs[:n_a], refs[n_a:]
        weight_refs, refs = refs[:n_w], refs[n_w:]
        out_refs, refs = refs[:n_o], refs[n_o:]
        buffer_refs, refs = refs[:n_w], refs[n_w:]
        copies = []
        for at, (ref, buffer, (_, axis, other)) in enumerate(zip(weight_refs, buffer_refs, weights)):
            size = buffer.shape[axis]
            start = pl.multiple_of((1 - place_ref[1] if other else place_ref[1]) * size, size)
            source = ref.at[pl.ds(start, size)] if axis == 0 else ref.at[:, pl.ds(start, size)]
            copies.append(pltpu.make_async_copy(source, buffer, refs[0].at[at]))
        for copy in copies:
            copy.start()
        arrived = set()

        def weight(at):
            if at not in arrived:
                copies[at].wait()
                arrived.add(at)
            return buffer_refs[at]

        body(place_ref, array_refs, weight, out_refs, refs[1:] if n_w else refs)

    inside = pl.BlockSpec(memory_space=pltpu.VMEM)
    scratch = buffers + ([pltpu.SemaphoreType.DMA((n_w,))] if n_w else []) + list(scratch)
    return pl.pallas_call(
        kernel,
        in_specs=[pl.BlockSpec(memory_space=pltpu.SMEM)]
        + [inside] * n_a
        + [pl.BlockSpec(memory_space=pltpu.HBM)] * n_w,
        out_specs=[inside] * n_o,
        out_shape=list(outs),
        scratch_shapes=scratch,
        compiler_params=pltpu.CompilerParams(vmem_limit_bytes=room),
        cost_estimate=pl.CostEstimate(
            flops=int(1.15e9 * cost), bytes_accessed=int(3.69e6 * cost), transcendentals=0
        ),
        name=name,
    )(place, *arrays, *[pltpu.with_memory_space_constraint(array, pltpu.HBM) for array, _, _ in weights])


def inverse_norm(hidden):
    return lax.rsqrt(jnp.mean(hidden * hidden, axis=-1, keepdims=True) + EPSILON)


def norm_low(hidden, inverse, gain):
    return (hidden * inverse * gain).astype(BF16)


def norm_back(hidden, inverse, gain, dz):
    scaled = gain * dz
    inner = jnp.mean(scaled * hidden, axis=-1, keepdims=True)
    return inverse * scaled - hidden * (inverse * inverse * inverse) * inner


def pick(core, value, axis, other=False):
    half = value.shape[axis] // CORES
    low, high = lax.slice_in_dim(value, 0, half, axis=axis), lax.slice_in_dim(value, half, 2 * half, axis=axis)
    return jnp.where(core == (1 if other else 0), low, high)


def in_place_order(core, own_ref, peer_ref):
    own, peer = own_ref[...].astype(F32), peer_ref[...].astype(F32)
    return jnp.concatenate([jnp.where(core == 0, own, peer), jnp.where(core == 0, peer, own)], axis=0)


def place_rows(half, at):
    zero = jnp.zeros_like(half)
    return jnp.concatenate([half, zero] if at == 0 else [zero, half], axis=0)


def place_lanes(pair, source, at):
    lane = lax.broadcasted_iota(jnp.int32, pair.shape, 1)
    if source != at:
        pair = jnp.concatenate([pair[:, HEAD:], pair[:, :HEAD]], axis=1)
    return jnp.where((lane < HEAD) == (at == 0), pair, jnp.zeros_like(pair))


def near_tiles(table_row):
    skewed = pltpu.roll(jnp.broadcast_to(table_row, (NEAR, 2 * NEAR)), 0, 1, stride=1, stride_axis=0)
    key_at = lax.broadcasted_iota(jnp.int32, (NEAR, NEAR), 0)
    row_at = lax.broadcasted_iota(jnp.int32, (NEAR, NEAR), 1)
    return (jnp.where(key_at <= row_at, skewed[:, :NEAR], NEGATIVE), skewed[:, NEAR:])


def heads_of(pair_turned, cols):
    return jnp.concatenate(
        [place_rows(pair_turned[h * HEAD : (h + 1) * HEAD, cols], h // 2) for h in range(4)], axis=1
    )


def add_corner(scores, tiles):
    rows = scores.shape[0]
    last = scores[rows - NEAR :]
    pieces = []
    for h in range(4):
        pieces += [last[:, h * TILE : h * TILE + NEAR] + tiles[h][1], last[:, h * TILE + NEAR : (h + 1) * TILE]]
    return jnp.concatenate([scores[: rows - NEAR], jnp.concatenate(pieces, axis=1)], axis=0)


def add_diagonal(scores, tiles):
    rows = scores.shape[0]
    first = scores[rows - TILE : rows - NEAR]
    second = scores[rows - NEAR :]
    upper, lower = [], []
    for h in range(4):
        left, right = slice(h * TILE, h * TILE + NEAR), slice(h * TILE + NEAR, (h + 1) * TILE)
        upper += [first[:, left] + tiles[h][0], first[:, right] + tiles[h][1]]
        lower += [jnp.full((NEAR, NEAR), NEGATIVE, F32), second[:, right] + tiles[h][0]]
    last = [jnp.concatenate(upper, axis=1), jnp.concatenate(lower, axis=1)]
    if rows > TILE:
        last = [add_corner(scores[: rows - TILE], tiles)] + last
    return jnp.concatenate(last, axis=0)


def by_distance(near):
    level = near[:8]
    for first in range(8, NEAR, 8):
        level = level + pltpu.roll(near[first : first + 8], 2 * NEAR - first, 1)
    row = lax.broadcasted_iota(jnp.int32, level.shape, 0)
    for bit in (1, 2, 4):
        level = jnp.where(row & bit > 0, pltpu.roll(level, 2 * NEAR - bit, 1), level)
    return jnp.sum(level, axis=0, keepdims=True)


def soft(scores):
    peak = jnp.max(scores, axis=0, keepdims=True)
    weights = jnp.exp(scores - peak)
    return peak, weights.astype(BF16), jnp.sum(weights, axis=0, keepdims=True)


def finish(o_ref, lse_ref, cols, peak, summed, acc):
    out = acc / summed
    lse = peak + jnp.log(summed)
    pieces = []
    for h in range(4):
        e = h // 2
        lanes = slice(h * TILE, (h + 1) * TILE)
        pieces.append(out[e * HEAD : (e + 1) * HEAD, lanes])
        lse_ref[0, h : h + 1, cols] = lse[:, lanes]
    o_ref[cols, :] = jnp.concatenate(pieces, axis=0).T.astype(BF16)


def self_forward_block(
    valid_ref, table_ref, q_ref, k_ref, v_ref, kp_ref, vp_ref, o_ref, lse_ref, peak_ref, sum_ref, acc_ref, *, earlier
):
    rows = q_ref.shape[0]
    steps = rows // TILE
    v_turned = v_ref[...].T
    q_turned = q_ref[...].T
    tiles = [near_tiles(table_ref[0, h : h + 1, :]) for h in range(4)]
    spans = [slice(t * TILE, (t + 1) * TILE) for t in range(steps)]
    queries = [heads_of(q_turned, cols) for cols in spans]
    scores = [add_diagonal(dot(k_ref[: cols.stop], queries[t]), tiles) for t, cols in enumerate(spans)]
    parts = [soft(score) for score in scores]
    for t, cols in enumerate(spans):
        peak_ref[t], sum_ref[t] = parts[t][0], parts[t][2]
        acc_ref[t] = dot(v_turned[:, : cols.stop], parts[t][1])
    for s in range(earlier):

        @pl.when(valid_ref[3 + s] > 0)
        def _(s=s):
            vp_turned = vp_ref[s].T
            scores = [dot(kp_ref[s], query) for query in queries]
            if s == 0:
                scores[0] = add_corner(scores[0], tiles)
            for t in range(steps):
                peak = peak_ref[t]
                new_peak = jnp.maximum(peak, jnp.max(scores[t], axis=0, keepdims=True))
                rescale = jnp.exp(peak - new_peak)
                weights = jnp.exp(scores[t] - new_peak)
                peak_ref[t] = new_peak
                sum_ref[t] = sum_ref[t] * rescale + jnp.sum(weights, axis=0, keepdims=True)
                acc_ref[t] = acc_ref[t] * rescale + dot(vp_turned, weights.astype(BF16))

    for t, cols in enumerate(spans):
        finish(o_ref, lse_ref, cols, peak_ref[t], sum_ref[t], acc_ref[t])


def placed_heads(block, cols):
    rows = []
    for h in range(4):
        pair = block[cols, (h // 2) * 2 * HEAD : (h // 2 + 1) * 2 * HEAD]
        rows.append(place_lanes(pair, h % 2, h // 2))
    return jnp.concatenate(rows, axis=0)


def row_of_heads(ref, cols):
    return jnp.concatenate([ref[0, h : h + 1, cols] for h in range(4)], axis=1)


def deltas(product, cols):
    return jnp.concatenate(
        [jnp.sum(product[h * HEAD : (h + 1) * HEAD, cols], axis=0, keepdims=True) for h in range(4)], axis=1
    )


def back_scores(scores, lse, d_prob, delta):
    prob = jnp.exp(scores - lse)
    d_score = prob * (d_prob - delta)
    return prob.astype(BF16), d_score.astype(BF16)


def query_rows(d_query):
    pieces = [
        d_query[(h // 2) * HEAD : (h // 2 + 1) * HEAD, h * TILE : (h + 1) * TILE] for h in range(4)
    ]
    return jnp.concatenate(pieces, axis=0).T.astype(BF16)


def self_backward_block(
    valid_ref, table_ref, q_ref, k_ref, v_ref, kp_ref, vp_ref, do_ref, o_ref, lse_ref,
    dq_ref, dk_ref, dv_ref, past_ref, db_ref, total_ref,
    near_sum, dq_sum, *, earlier,
):
    rows = q_ref.shape[0]
    steps = rows // TILE
    spans = [slice(t * TILE, (t + 1) * TILE) for t in range(steps)]
    k_turned = k_ref[...].T
    q_turned = q_ref[...].T
    do_turned = do_ref[...].T
    product = (do_ref[...].astype(F32) * o_ref[...].astype(F32)).T
    tiles = [near_tiles(table_ref[0, h : h + 1, :]) for h in range(4)]
    queries = [heads_of(q_turned, cols) for cols in spans]
    outs = [heads_of(do_turned, cols) for cols in spans]
    q_placed = [placed_heads(q_ref, cols) for cols in spans]
    do_placed = [placed_heads(do_ref, cols) for cols in spans]
    lses = [row_of_heads(lse_ref, cols) for cols in spans]
    delta = [deltas(product, cols) for cols in spans]

    for t, cols in enumerate(spans):
        seen = cols.stop
        scores = add_diagonal(dot(k_ref[:seen], queries[t]), tiles)
        prob, d_score = back_scores(scores, lses[t], dot(v_ref[:seen], outs[t]), delta[t])
        d_value = dot(prob, do_placed[t])
        d_key = dot(d_score, q_placed[t])
        if t == 0:
            dv_whole, dk_whole = d_value, d_key
        else:
            more = seen - dv_whole.shape[0]
            dv_whole = jnp.concatenate([dv_whole + d_value[: seen - more], d_value[seen - more :]], axis=0)
            dk_whole = jnp.concatenate([dk_whole + d_key[: seen - more], d_key[seen - more :]], axis=0)
        dq_sum[t] = dot(k_turned[:, :seen], d_score)
        d_wide = d_score.astype(F32)
        total = jnp.sum(d_wide, axis=0, keepdims=True)
        base = seen - TILE
        for h in range(4):
            left, right = slice(h * TILE, h * TILE + NEAR), slice(h * TILE + NEAR, (h + 1) * TILE)
            zero_part = d_wide[base : base + NEAR, left] + d_wide[base + NEAR :, right]
            one_part = d_wide[base : base + NEAR, right]
            if t > 0:
                one_part = one_part + d_wide[base - NEAR : base, left]
            both = jnp.concatenate([zero_part, one_part], axis=1)
            part = total[:, h * TILE : (h + 1) * TILE]
            if t == 0:
                near_sum[h] = both
                total_ref[0, h : h + 1, :] = part
            else:
                near_sum[h] += both
                total_ref[0, h : h + 1, :] += part
    dk_ref[...] = dk_whole.astype(BF16)
    dv_ref[...] = dv_whole.astype(BF16)

    for s in range(earlier):

        @pl.when(valid_ref[3 + s] > 0)
        def _(s=s):
            kp_turned = kp_ref[s].T
            for t in range(steps):
                scores = dot(kp_ref[s], queries[t])
                if s == 0 and t == 0:
                    scores = add_corner(scores, tiles)
                prob, d_score = back_scores(scores, lses[t], dot(vp_ref[s], outs[t]), delta[t])
                d_value = dot(prob, do_placed[t])
                d_key = dot(d_score, q_placed[t])
                dv_whole = d_value if t == 0 else dv_whole + d_value
                dk_whole = d_key if t == 0 else dk_whole + d_key
                dq_sum[t] += dot(kp_turned, d_score)
                d_wide = d_score.astype(F32)
                total = jnp.sum(d_wide, axis=0, keepdims=True)
                for h in range(4):
                    total_ref[0, h : h + 1, :] += total[:, h * TILE : (h + 1) * TILE]
                    if s == 0 and t == 0:
                        near_sum[h, :, NEAR:] += d_wide[rows - NEAR :, h * TILE : h * TILE + NEAR]
            past_ref[s, 0] = dk_whole.astype(BF16)
            past_ref[s, 1] = dv_whole.astype(BF16)

        @pl.when(valid_ref[3 + s] == 0)
        def _(s=s):
            past_ref[s] = jnp.zeros_like(past_ref[s])

    for t, cols in enumerate(spans):
        dq_ref[cols, :] = query_rows(dq_sum[t])
    for h in range(4):
        db_ref[0, h : h + 1, :] = by_distance(near_sum[h])
    db_ref[0, 4:, :] = jnp.zeros((4, 2 * NEAR), F32)
    total_ref[0, 4:, :] = jnp.zeros((4, 2 * NEAR), F32)


def cross_forward_block(q_ref, k_ref, v_ref, own_ref, o_ref, lse_ref, *, masked):
    rows = q_ref.shape[0]
    v_turned = v_ref[...].T
    q_turned = q_ref[...].T
    spans = [slice(t * TILE, (t + 1) * TILE) for t in range(rows // TILE)]
    scores = [dot(k_ref[...], heads_of(q_turned, cols)) for cols in spans]
    if masked:
        blocked = jnp.where(own_ref[...] > 0, 0.0, NEGATIVE)
        blocked = jnp.concatenate([blocked] * 4, axis=1)
        scores = [score + blocked for score in scores]
    for t, cols in enumerate(spans):
        peak, weights, summed = soft(scores[t])
        finish(o_ref, lse_ref, cols, peak, summed, dot(v_turned, weights))


def cross_backward_block(
    q_ref, k_ref, v_ref, own_ref, do_ref, o_ref, lse_ref, dq_ref, dk_ref, dv_ref, *, masked
):
    rows = q_ref.shape[0]
    k_turned = k_ref[...].T
    q_turned = q_ref[...].T
    do_turned = do_ref[...].T
    product = (do_ref[...].astype(F32) * o_ref[...].astype(F32)).T
    spans = [slice(t * TILE, (t + 1) * TILE) for t in range(rows // TILE)]
    dk_whole, dv_whole = 0.0, 0.0
    for t, cols in enumerate(spans):
        scores = dot(k_ref[...], heads_of(q_turned, cols))
        if masked:
            blocked = jnp.where(own_ref[...] > 0, 0.0, NEGATIVE)
            scores = scores + jnp.concatenate([blocked] * 4, axis=1)
        d_prob = dot(v_ref[...], heads_of(do_turned, cols))
        prob, d_score = back_scores(scores, row_of_heads(lse_ref, cols), d_prob, deltas(product, cols))
        dv_whole = dv_whole + dot(prob, placed_heads(do_ref, cols))
        dk_whole = dk_whole + dot(d_score, placed_heads(q_ref, cols))
        dq_ref[cols, :] = query_rows(dot(k_turned, d_score))
    dk_ref[...] = dk_whole.astype(BF16)
    dv_ref[...] = dv_whole.astype(BF16)


def wide_view(ref, p):
    return ref.at[:, pl.ds(p * 4 * HEAD, 4 * HEAD)]


def slim_view(ref, p):
    return ref.at[:, pl.ds(p * 2 * HEAD, 2 * HEAD)]


def past_view(ref, p):
    return ref.at[:, :, pl.ds(p * 2 * HEAD, 2 * HEAD)]


def page_view(ref, p):
    return ref.at[pl.ds(p, 1)]


def self_forward(place, table, q, k, v, kp, vp):
    rows, blocks, earlier = q.shape[0], k.shape[1] // (2 * HEAD), kp.shape[0]
    steps = rows // TILE

    def body(place_ref, arrays, weight, outs, scratch):
        table_ref, q_ref, k_ref, v_ref, kp_ref, vp_ref = arrays
        for p in range(blocks):
            self_forward_block(
                place_ref, page_view(table_ref, p), wide_view(q_ref, p), slim_view(k_ref, p), slim_view(v_ref, p),
                past_view(kp_ref, p), past_view(vp_ref, p), wide_view(outs[0], p), page_view(outs[1], p),
                *[ref.at[p] for ref in scratch], earlier=earlier,
            )

    return whole_kernel(
        body,
        place,
        [table, q, k, v, kp, vp],
        [],
        [shaped(q.shape), shaped((blocks, 8, rows), F32)],
        "self_forward",
        [
            pltpu.VMEM((blocks, steps, 1, 4 * TILE), F32),
            pltpu.VMEM((blocks, steps, 1, 4 * TILE), F32),
            pltpu.VMEM((blocks, steps, 2 * HEAD, 4 * TILE), F32),
        ],
    )


def self_backward(place, table, q, k, v, kp, vp, do, o, lse):
    rows, blocks, earlier = q.shape[0], k.shape[1] // (2 * HEAD), kp.shape[0]
    steps = rows // TILE

    def body(place_ref, arrays, weight, outs, scratch):
        table_ref, q_ref, k_ref, v_ref, kp_ref, vp_ref, do_ref, o_ref, lse_ref = arrays
        dq_ref, dk_ref, dv_ref, past_ref, db_ref, total_ref = outs
        for p in range(blocks):
            self_backward_block(
                place_ref, page_view(table_ref, p), wide_view(q_ref, p), slim_view(k_ref, p), slim_view(v_ref, p),
                past_view(kp_ref, p), past_view(vp_ref, p), wide_view(do_ref, p), wide_view(o_ref, p),
                page_view(lse_ref, p), wide_view(dq_ref, p), slim_view(dk_ref, p), slim_view(dv_ref, p),
                past_ref.at[:, :, :, pl.ds(p * 2 * HEAD, 2 * HEAD)], page_view(db_ref, p), page_view(total_ref, p),
                *[ref.at[p] for ref in scratch], earlier=earlier,
            )

    return whole_kernel(
        body,
        place,
        [table, q, k, v, kp, vp, do, o, lse],
        [],
        [
            shaped(q.shape),
            shaped(k.shape),
            shaped(k.shape),
            shaped((earlier, 2) + k.shape),
            shaped(table.shape, F32),
            shaped(table.shape, F32),
        ],
        "self_backward",
        [pltpu.VMEM((blocks, 4, NEAR, 2 * NEAR), F32), pltpu.VMEM((blocks, steps, 2 * HEAD, 4 * TILE), F32)],
    )


def cross_forward(place, q, k, v, own):
    rows, blocks = q.shape[0], k.shape[1] // (2 * HEAD)

    def body(place_ref, arrays, weight, outs, scratch):
        q_ref, k_ref, v_ref = arrays[:3]
        for p in range(blocks):
            cross_forward_block(
                wide_view(q_ref, p), slim_view(k_ref, p), slim_view(v_ref, p), arrays[-1], wide_view(outs[0], p),
                page_view(outs[1], p), masked=len(own) > 0,
            )

    outs = [shaped(q.shape), shaped((blocks, 8, rows), F32)]
    return whole_kernel(body, place, [q, k, v] + own, [], outs, "cross_forward")


def cross_backward(place, q, k, v, own, do, o, lse):
    blocks = k.shape[1] // (2 * HEAD)

    def body(place_ref, arrays, weight, outs, scratch):
        q_ref, k_ref, v_ref, do_ref, o_ref, lse_ref = arrays[:6]
        for p in range(blocks):
            cross_backward_block(
                wide_view(q_ref, p), slim_view(k_ref, p), slim_view(v_ref, p), arrays[-1], wide_view(do_ref, p),
                wide_view(o_ref, p), page_view(lse_ref, p), wide_view(outs[0], p), slim_view(outs[1], p),
                slim_view(outs[2], p), masked=len(own) > 0,
            )

    outs = [shaped(q.shape), shaped(k.shape), shaped(k.shape)]
    return whole_kernel(body, place, [q, k, v, do, o, lse] + own, [], outs, "cross_backward")


def project(place, own, peer, gain, wq, wk, wv):
    rows, model = own.shape
    wide, slim = wq.shape[1] // CORES, wk.shape[1] // CORES

    def body(place_ref, arrays, weight, outs, scratch):
        hidden = in_place_order(place_ref[1], arrays[0], arrays[1])
        low = norm_low(hidden, inverse_norm(hidden), arrays[2][...].astype(F32))
        outs[0][...] = low
        for at in range(3):
            outs[1 + at][...] = dot(low, weight(at)[...]).astype(BF16)

    return whole_kernel(
        body,
        place,
        [own, peer, gain],
        [(wq, 1, False), (wk, 1, False), (wv, 1, False)],
        [shaped((CORES * rows, n)) for n in (model, wide, slim, slim)],
        "project",
    )


def project_past(place, owns, peers, mems, gain, wk, wv, wck, wcv):
    rows, model = owns[0].shape
    earlier, groups = len(owns), len(mems)
    slim = wk.shape[1] // CORES
    mem_rows = mems[0].shape[0]

    def body(place_ref, arrays, weight, outs, scratch):
        own_refs, peer_refs, mem_refs = arrays[:earlier], arrays[earlier : 2 * earlier], arrays[2 * earlier : -1]
        low_refs, (k_ref, v_ref, mem_ref, km_ref, vm_ref) = outs[:earlier], outs[earlier:]
        gain_value = arrays[-1][...].astype(F32)
        for s in range(earlier):
            hidden = in_place_order(place_ref[1], own_refs[s], peer_refs[s])
            low = norm_low(hidden, inverse_norm(hidden), gain_value)
            low_refs[s][...] = low
            k_ref[s] = dot(low, weight(0)[...]).astype(BF16)
            v_ref[s] = dot(low, weight(1)[...]).astype(BF16)
        for at, piece_ref in enumerate(mem_refs):
            block = jnp.bitwise_xor(place_ref[2], jnp.int32(at))
            mem_ref[pl.ds(pl.multiple_of(block * mem_rows, mem_rows), mem_rows)] = piece_ref[...]
        mem = mem_ref[...]
        km_ref[...] = dot(mem, weight(2)[...]).astype(BF16)
        vm_ref[...] = dot(mem, weight(3)[...]).astype(BF16)

    made = whole_kernel(
        body,
        place,
        owns + peers + mems + [gain],
        [(wk, 1, False), (wv, 1, False), (wck, 1, False), (wcv, 1, False)],
        [shaped((CORES * rows, model))] * earlier
        + [shaped((earlier, CORES * rows, slim))] * 2
        + [shaped((groups * mem_rows, n)) for n in (model, slim, slim)],
        "project_past",
    )
    return made[:earlier], *made[earlier:]


def mid_forward(place, own, peer, att, att_peer, gain, wo, wq):
    rows, model = own.shape

    def body(place_ref, arrays, weight, outs, scratch):
        own_ref, peer_ref, att_ref, att_peer_ref, gain_ref = arrays
        hidden = in_place_order(place_ref[1], own_ref, peer_ref)
        hidden = hidden + dot(att_ref[...], weight(0)[...]) + dot(att_peer_ref[...], weight(1)[...])
        outs[0][...] = hidden.astype(BF16)
        low = norm_low(hidden, inverse_norm(hidden), gain_ref[...].astype(F32))
        outs[1][...] = low
        outs[2][...] = dot(low, weight(2)[...]).astype(BF16)

    return whole_kernel(
        body,
        place,
        [own, peer, att, att_peer, gain],
        [(wo, 0, False), (wo, 0, True), (wq, 1, False)],
        [shaped((CORES * rows, model))] * 2 + [shaped((CORES * rows, wq.shape[1] // CORES))],
        "mid_forward",
    )


def ffn(place, mid, crs, crs_peer, gain, cot, cot_peer, wc, wg, wu, wd):
    rows, model = mid.shape
    hidden_half = wd.shape[0] // CORES
    steps = [256] * (hidden_half // 256) + [hidden_half % 256] * (hidden_half % 256 > 0)
    scale = 0.7978845608028654

    def body(place_ref, arrays, weight, outs, scratch):
        mid_ref, crs_ref, crs_peer_ref, gain_ref, cot_ref, cot_peer_ref = arrays
        late_ref, low_ref, inner_ref, dg_ref, du_ref, dz_ref, cot_half_ref = outs
        cot_value = in_place_order(place_ref[1], cot_ref, cot_peer_ref).astype(BF16)
        cot_half_ref[...] = pick(place_ref[1], cot_value, 1)
        hidden = mid_ref[...].astype(F32) + dot(crs_ref[...], weight(0)[...]) + dot(crs_peer_ref[...], weight(1)[...])
        late_ref[...] = hidden.astype(BF16)
        low = norm_low(hidden, inverse_norm(hidden), gain_ref[...].astype(F32))
        low_ref[...] = low
        start = 0
        for width in steps:
            cols = slice(start, start + width)
            start += width
            gate = dot(low, weight(2)[:, cols])
            up = dot(low, weight(3)[:, cols])
            d_inner = dot_right(cot_value, weight(4)[cols]).astype(BF16).astype(F32)
            square = gate * gate
            bent = jnp.tanh(scale * gate * (1.0 + 0.044715 * square))
            whole = 0.5 * (1.0 + bent)
            slope = whole + 0.5 * gate * (1.0 - bent * bent) * (scale * (1.0 + 3 * 0.044715 * square))
            curve = gate * whole
            inner_ref[:, cols] = (curve * up).astype(BF16)
            dg_ref[:, cols] = (d_inner * up * slope).astype(BF16)
            du_ref[:, cols] = (d_inner * curve).astype(BF16)
        dz_ref[...] = (dot_right(dg_ref[...], weight(2)[...]) + dot_right(du_ref[...], weight(3)[...])).astype(BF16)

    return whole_kernel(
        body,
        place,
        [mid, crs, crs_peer, gain, cot, cot_peer],
        [(wc, 0, False), (wc, 0, True), (wg, 1, False), (wu, 1, False), (wd, 0, False)],
        [shaped((rows, model))] * 2
        + [shaped((rows, hidden_half))] * 3
        + [shaped((rows, model)), shaped((rows, model // CORES))],
        "ffn",
        room=24 * 1024 * 1024,
    )


def late_backward(place, dz, dz_peer, late, cot, cot_peer, gain, wc):
    rows, model = late.shape

    def body(place_ref, arrays, weight, outs, scratch):
        dz_ref, dz_peer_ref, late_ref, cot_ref, cot_peer_ref, gain_ref = arrays
        dz_value = dz_ref[...].astype(F32) + dz_peer_ref[...].astype(F32)
        hidden = late_ref[...].astype(F32)
        inverse = inverse_norm(hidden)
        outs[3][...] = jnp.sum(dz_value * hidden * inverse, axis=0, keepdims=True)
        grad = in_place_order(place_ref[1], cot_ref, cot_peer_ref)
        grad = grad + norm_back(hidden, inverse, gain_ref[...].astype(F32), dz_value)
        low = grad.astype(BF16)
        outs[0][...] = low
        outs[1][...] = pick(place_ref[1], low, 1)
        outs[2][...] = dot_right(low, weight(0)[...]).astype(BF16)

    return whole_kernel(
        body,
        place,
        [dz, dz_peer, late, cot, cot_peer, gain],
        [(wc, 0, False)],
        [
            shaped((rows, model)),
            shaped((rows, model // CORES)),
            shaped((rows, wc.shape[0] // CORES)),
            shaped((1, model), F32),
        ],
        "late_backward",
    )


def mid_backward(place, dq, dq_peer, mid, g_late, gain, wq, wo):
    rows, model = mid.shape

    def body(place_ref, arrays, weight, outs, scratch):
        dq_ref, dq_peer_ref, mid_ref, g_ref, gain_ref = arrays
        dz = dot_right(dq_ref[...], weight(0)[...]) + dot_right(dq_peer_ref[...], weight(1)[...])
        hidden = mid_ref[...].astype(F32)
        inverse = inverse_norm(hidden)
        outs[3][...] = jnp.sum(dz * hidden * inverse, axis=0, keepdims=True)
        grad = g_ref[...].astype(F32) + norm_back(hidden, inverse, gain_ref[...].astype(F32), dz)
        low = grad.astype(BF16)
        outs[0][...] = pick(place_ref[1], low, 0)
        outs[1][...] = pick(place_ref[1], low, 1)
        outs[2][...] = dot_right(low, weight(2)[...]).astype(BF16)

    return whole_kernel(
        body,
        place,
        [dq, dq_peer, mid, g_late, gain],
        [(wq, 1, False), (wq, 1, True), (wo, 0, False)],
        [
            shaped((rows // CORES, model)),
            shaped((rows, model // CORES)),
            shaped((rows, wo.shape[0] // CORES)),
            shaped((1, model), F32),
        ],
        "mid_backward",
    )


def first_backward(place, dq, dk, dv, past, rider, wq, wk, wv):
    rows, model = dq.shape[0], wq.shape[0]
    slim = dk.shape[1]

    def body(place_ref, arrays, weight, outs, scratch):
        dq_ref, dk_ref, dv_ref = arrays[:3]
        dk_value, dv_value = dk_ref[...].astype(F32), dv_ref[...].astype(F32)
        if rider is not None:
            blocks = [
                arrays[3][rider[1] + at * rows : rider[1] + (at + 1) * rows].astype(F32)
                for at in range(2 * slim // LANES)
            ]
            dk_value = dk_value + jnp.concatenate(blocks[: slim // LANES], axis=1)
            dv_value = dv_value + jnp.concatenate(blocks[slim // LANES :], axis=1)
        else:
            for ref in arrays[3:]:
                dk_value = dk_value + ref[0].astype(F32)
                dv_value = dv_value + ref[1].astype(F32)
        dz = dot_right(dq_ref[...], weight(0)[...])
        dz = dz + dot_right(dk_value.astype(BF16), weight(1)[...]) + dot_right(dv_value.astype(BF16), weight(2)[...])
        outs[0][...] = pick(place_ref[1], dz, 0)
        outs[1][...] = pick(place_ref[1], dz, 0, True).astype(BF16)

    return whole_kernel(
        body,
        place,
        [dq, dk, dv] + (past if rider is None else [rider[0]]),
        [(wq, 1, False), (wk, 1, False), (wv, 1, False)],
        [shaped((rows // CORES, model), F32), shaped((rows // CORES, model))],
        "first_backward",
    )


def tokens_backward(place, dz, dz_got, tokens, g_mid, gain):
    def body(place_ref, arrays, weight, outs, scratch):
        dz_ref, dz_got_ref, tokens_ref, g_ref, gain_ref = arrays
        dz_value = dz_ref[...] + dz_got_ref[...].astype(F32)
        hidden = tokens_ref[...].astype(F32)
        inverse = inverse_norm(hidden)
        outs[1][...] = jnp.sum(dz_value * hidden * inverse, axis=0, keepdims=True)
        grad = g_ref[...].astype(F32) + norm_back(hidden, inverse, gain_ref[...].astype(F32), dz_value)
        outs[0][...] = grad.astype(BF16)

    outs = [shaped(tokens.shape), shaped((1, tokens.shape[1]), F32)]
    return whole_kernel(body, place, [dz, dz_got, tokens, g_mid, gain], [], outs, "tokens_backward")


def layer_output(place, late, inner, inner_peer, wd):
    rows, model = late.shape

    def body(place_ref, arrays, weight, outs, scratch):
        own, inner_own, inner_other = (pick(place_ref[1], ref[...], 0) for ref in arrays)
        total = own.astype(F32) + dot(inner_own, weight(0)[...]) + dot(inner_other, weight(1)[...])
        outs[0][...] = total.astype(BF16)

    return whole_kernel(
        body,
        place,
        [late, inner, inner_peer],
        [(wd, 0, False), (wd, 0, True)],
        [shaped((rows // CORES, model))],
        "layer_output",
    )[0]


def memory_backward(place, dk, dv, wk, wv):
    def body(place_ref, arrays, weight, outs, scratch):
        grad = dot_right(arrays[0][...], weight(0)[...]) + dot_right(arrays[1][...], weight(1)[...])
        outs[0][...] = grad.astype(BF16)

    weights = [(wk, 1, False), (wv, 1, False)]
    return whole_kernel(body, place, [dk, dv], weights, [shaped((dk.shape[0], wk.shape[0]))], "memory_backward")[0]


def small_sums(place, one, two, three, near, total, buckets, heads, devices):
    def body(place_ref, arrays, weight, outs, scratch):
        one_ref, two_ref, three_ref, near_ref, total_ref, bucket_ref = arrays
        core = place_ref[1]
        first = core == 0
        gains = [one_ref[...], jnp.where(first, two_ref[...], 0.0), jnp.where(first, three_ref[...], 0.0)]
        near = jnp.concatenate([near_ref[p, :4] for p in range(heads // 4)], axis=0)
        total = jnp.concatenate([total_ref[p, :4] for p in range(heads // 4)], axis=0)
        far = jnp.sum(total, axis=1, keepdims=True) - jnp.sum(near, axis=1, keepdims=True)
        last = lax.broadcasted_iota(jnp.int32, near.shape, 1) == near.shape[1] - 1
        near = near + jnp.where(last, far, 0.0)
        entries = BUCKETS * HEADS
        entry = lax.broadcasted_iota(jnp.int32, (near.shape[1], entries), 1)
        same = (lax.shift_right_logical(entry, jnp.int32(HEADS.bit_length() - 1)) == bucket_ref[...]).astype(F32)
        sums = jnp.dot(near, same, precision=lax.Precision.HIGHEST, preferred_element_type=F32)
        head = lax.broadcasted_iota(jnp.int32, sums.shape, 0) + core * heads
        of_entry = jnp.bitwise_and(lax.broadcasted_iota(jnp.int32, sums.shape, 1), jnp.int32(HEADS - 1))
        vectors = gains + [jnp.sum(jnp.where(head == of_entry, sums, 0.0), axis=0, keepdims=True)]
        for block in range(devices):
            rows = []
            for vector in vectors:
                size = vector.shape[1] // devices
                row = vector[:, block * size : (block + 1) * size]
                rows.append(jnp.concatenate([row, jnp.zeros((1, LANES - size), F32)], axis=1))
            outs[0][block] = jnp.concatenate(rows + [jnp.zeros((4, LANES), F32)], axis=0)

    return whole_kernel(
        body, place, [one, two, three, near, total, buckets], [], [shaped((devices, 8, LANES), F32)], "small_sums"
    )[0]


def gather_sums(place, parts, name):
    def body(place_ref, arrays, weight, outs, scratch):
        for array, out in zip(arrays, outs):
            total = array[0].astype(F32)
            for at in range(1, array.shape[0]):
                total = total + array[at].astype(F32)
            out[...] = total.astype(out.dtype)

    return whole_kernel(body, place, parts, [], [shaped(a.shape[1:], a.dtype) for a in parts], name)


def place_of(position, order):
    spot = jnp.int32(0)
    for bit in order:
        spot = spot * 2 + jnp.bitwise_and(lax.shift_right_logical(position, jnp.int32(bit)), 1)
    return spot


def up_to(value, multiple):
    return (value + multiple - 1) // multiple * multiple


def array_of(y):
    return y[0] if isinstance(y, tuple) else y


class Flow:
    def __init__(self, name, pieces, order):
        self.name, self.pieces, self.order = name, pieces, order
        self.hops = [bit + 1 for bit in order]
        self.chips = 1 << len(order)
        self.layout = []
        start = 0
        for terms, rows in pieces:
            half = rows // self.chips // CORES
            padded = up_to(half, 8)
            width = array_of(terms[0][1]).shape[-1]
            self.layout.append((start, half, padded, width))
            start += CORES * padded * (width // LANES)
        self.rows = start
        self.keep = self.got = None

    def spread(self, x):
        half, padded = self.layout[0][1:3]
        if half == padded:
            return x
        chunks = x.reshape(x.shape[0], -1, half)
        return jnp.pad(chunks, ((0, 0), (0, 0), (0, padded - half))).reshape(x.shape[0], -1)


def sum_flow(flow, refs_of, place_ref, turned, send_ref, base, keep_ref):
    chip, core = place_ref[0], place_ref[1]
    half = flow.chips // 2
    for (terms, _), (start, _, padded, width) in zip(flow.pieces, flow.layout):
        chunk = CORES * padded
        parts = len(terms[0][0])
        part_rows = flow.chips * chunk // parts
        step = max(s for s in range(chunk, 513, chunk) if part_rows % s == 0)
        for part in range(parts):
            for first in range(0, part_rows, step):
                tile = None
                for xs, y in terms:
                    key = id(xs[part])
                    if key not in turned:
                        turned[key] = refs_of[key][...].T
                    y_ref = refs_of[id(array_of(y))]
                    y_value = y_ref[y[1]] if isinstance(y, tuple) else y_ref[...]
                    term = dot(turned[key][first : first + step], y_value)
                    tile = term if tile is None else tile + term
                tile = tile.astype(BF16)
                for inner in range(step // chunk):
                    number = jnp.int32(first // chunk + inner)
                    if parts == CORES:
                        number = number + (core if part == 0 else 1 - core) * (part_rows // chunk)
                    spot = place_of(jnp.bitwise_xor(number, chip), flow.order)
                    rows = tile[inner * chunk : (inner + 1) * chunk]

                    @pl.when(spot >= half)
                    def _(spot=spot, rows=rows):
                        for block in range(width // LANES):
                            at = base + (spot - half) * flow.rows + start + block * chunk
                            send_ref[pl.ds(pl.multiple_of(at, 16), chunk)] = rows[:, block * LANES : (block + 1) * LANES]

                    @pl.when(spot < half)
                    def _(spot=spot, rows=rows):
                        for block in range(width // LANES):
                            at = slice(start + block * chunk, start + (block + 1) * chunk)
                            keep_ref[spot, at] = rows[:, block * LANES : (block + 1) * LANES]


def add_flow(flow, old_ref, got_ref, got_at, send_ref, base, keep_ref):
    half = old_ref.shape[0] // 2
    for spot in range(2 * half):
        at = got_at + spot * flow.rows
        total = (old_ref[spot].astype(F32) + got_ref[at : at + flow.rows].astype(F32)).astype(BF16)
        if spot < half:
            keep_ref[spot] = total
        else:
            send_ref[base + (spot - half) * flow.rows : base + (spot - half + 1) * flow.rows] = total


def hop(place, swap, sums, adds, after, name, cost=0, rider=None):
    arrays, seen = [], {}

    def take(array):
        if id(array) not in seen:
            seen[id(array)] = len(arrays)
            arrays.append(array)

    for flow in sums:
        for terms, _ in flow.pieces:
            for xs, y in terms:
                for array in (*xs, array_of(y)):
                    take(array)
    for flow in adds:
        take(flow.keep)
        take(flow.got[0])
    bits, sends, keeps = {}, {}, {}
    for flow in sums + adds:
        half = (flow.chips if flow in sums else flow.keep.shape[0]) // 2
        bit = flow.hops[0]
        base = bits.setdefault(bit, 0)
        sends[flow.name] = (bit, base)
        bits[bit] = base + half * flow.rows
        keeps[flow.name] = shaped((half, flow.rows, LANES))
    if rider is not None:
        rider_array, rider_bit = rider
        take(rider_array)
        rider_at = bits.setdefault(rider_bit, 0)
        bits[rider_bit] = rider_at + rider_array.size // LANES
    order = list(bits)
    outs = [shaped((bits[bit], LANES)) for bit in order] + list(keeps.values())

    def body(place_ref, refs, weight, out_refs, scratch):
        refs_of = {key: refs[at] for key, at in seen.items()}
        turned = {}
        for at, flow in enumerate(sums + adds):
            bit, base = sends[flow.name]
            send_ref, keep_ref = out_refs[order.index(bit)], out_refs[len(order) + at]
            if flow in sums:
                sum_flow(flow, refs_of, place_ref, turned, send_ref, base, keep_ref)
            else:
                add_flow(
                    flow, refs_of[id(flow.keep)], refs_of[id(flow.got[0])], flow.got[1], send_ref, base, keep_ref
                )
        if rider is not None:
            send_ref, at = out_refs[order.index(rider_bit)], rider_at
            _, pages, rows, width = rider_array.shape
            for page in range(pages):
                for block in range(width // LANES):
                    send_ref[at : at + rows] = refs_of[id(rider_array)][0, page, :, block * LANES : (block + 1) * LANES]
                    at += rows

    made = whole_kernel(body, place, follow(arrays, after), [], outs, name, cost=cost)
    moved = [swap(array, bit) for array, bit in zip(made, order)]
    for at, flow in enumerate(sums + adds):
        bit, base = sends[flow.name]
        flow.keep, flow.got, flow.hops = made[len(order) + at], (moved[order.index(bit)], base), flow.hops[1:]
    if rider is not None:
        return list(made), (moved[order.index(rider_bit)], rider_at)
    return list(made)


def last_hop(place, swap, flows, after, name):
    arrays, seen = [], {}
    for flow in flows:
        for array in (flow.keep, flow.got[0]):
            if id(array) not in seen:
                seen[id(array)] = len(arrays)
                arrays.append(array)
    blocks = []
    size = 0
    for f, flow in enumerate(flows):
        for piece, (start, half, padded, width) in enumerate(flow.layout):
            for block in range(width // LANES):
                blocks.append((f, piece, start + block * CORES * padded, padded, block, size))
                size += up_to(padded, 16)
    own_outs = [
        shaped((padded, width), F32) for flow in flows for _, _, padded, width in flow.layout
    ]
    first = [sum(len(flow.layout) for flow in flows[:f]) for f in range(len(flows))]

    def add_body(place_ref, refs, weight, outs, scratch):
        core = place_ref[1]
        for f, piece, at, padded, block, leave_at in blocks:
            flow = flows[f]
            got_at = flow.got[1] + at
            total = refs[seen[id(flow.keep)]][0, at : at + CORES * padded].astype(F32)
            total = total + refs[seen[id(flow.got[0])]][got_at : got_at + CORES * padded].astype(F32)
            own, leave = pick(core, total, 0), pick(core, total, 0, True)
            outs[1 + first[f] + piece][:, block * LANES : (block + 1) * LANES] = own
            full = up_to(padded, 16)
            if full > padded:
                leave = jnp.concatenate([leave, jnp.zeros((full - padded, LANES), F32)], axis=0)
            outs[0][leave_at : leave_at + full] = leave.astype(BF16)

    made = whole_kernel(add_body, place, follow(arrays, after), [], [shaped((size, LANES))] + own_outs, "last_" + name)
    got = swap(made[0], 0)

    def join_body(place_ref, refs, weight, outs, scratch):
        core = place_ref[1]
        for f, piece, _, padded, block, leave_at in blocks:
            at = first[f] + piece
            width = refs[1 + at].shape[1]
            own = refs[1 + at][:, block * LANES : (block + 1) * LANES]
            other = refs[0][leave_at : leave_at + up_to(padded, 16)].astype(F32)[:padded]
            low, high = slice(block * LANES, (block + 1) * LANES), slice(width + block * LANES, width + (block + 1) * LANES)
            outs[at][:, low] = jnp.where(core == 0, own, other)
            outs[at][:, high] = jnp.where(core == 0, other, own)

    joined = whole_kernel(
        join_body, place, [got] + list(made[1:]), [], [shaped((a.shape[0], CORES * a.shape[1]), F32) for a in own_outs],
        "join_" + name,
    )
    results = {}
    for f, flow in enumerate(flows):
        results[flow.name] = [
            joined[first[f] + piece][:half] for piece, (_, half, _, _) in enumerate(flow.layout)
        ]
    return results


def follow(value, after):
    return lax.optimization_barrier((value, after))[0]


def rel_bucket(distance):
    beyond = 16 + sum((distance >= border).astype(jnp.int32) for border in THRESHOLDS)
    return jnp.where(distance < 16, distance, beyond)


def shards(
    tokens, memory, cotangent, bucket, gain_self, self_query, self_key, self_value, self_out, rel_bias,
    gain_cross, cross_query, cross_key, cross_value, cross_out, gain_ffn, ffn_gate, ffn_up, ffn_down,
):
    groups = lax.axis_size("grp")
    dp_size = lax.axis_size("dp")
    n_chips = groups // CORES
    more = n_chips - 1
    chips = dp_size * n_chips
    devices = chips * CORES
    grp_at = lax.axis_index("grp")
    core = grp_at % CORES
    y_at = grp_at // CORES
    chip = lax.axis_index("dp") * n_chips + y_at
    rows, model = tokens.shape
    chip_rows = rows * CORES
    group_rows = chip_rows * n_chips
    hidden_units = ffn_down.shape[0]
    length = jnp.minimum(group_rows, jnp.maximum(SHORT, jnp.right_shift(jnp.int32(group_rows), bucket[0])))
    y_bits = n_chips.bit_length() - 1
    bits = chips.bit_length() - 1
    first_chip = y_at * chip_rows // length * length // chip_rows
    valid = [(y_at - s >= first_chip).astype(jnp.int32) for s in range(1, n_chips)]
    place = jnp.stack([chip, core, grp_at] + valid).astype(jnp.int32)

    def swap(v, bit):
        return lax.ppermute(v, ("dp", "grp"), [(i, i ^ (1 << bit)) for i in range(devices)])

    gain_one, gain_two, gain_three = (g.reshape(1, model) for g in (gain_self, gain_cross, gain_ffn))

    past_own = [
        lax.ppermute(tokens, "grp", [(g, g + CORES * s) for g in range(groups - CORES * s)]) for s in range(1, n_chips)
    ]
    tokens_peer = swap(tokens, 0)
    mems = [memory] + [
        lax.ppermute(memory, "grp", [(g, g ^ other) for g in range(groups)]) for other in range(1, groups)
    ]

    distances = jnp.arange(2 * NEAR, dtype=jnp.int32)
    buckets = rel_bucket(distances)[:, None]
    onehot = (buckets == jnp.arange(BUCKETS, dtype=jnp.int32)).astype(F32)
    heads = HEADS // CORES
    rel_local = lax.dynamic_slice_in_dim(rel_bias.astype(F32), core * heads, heads, 1)
    by_dist = jnp.dot(onehot, rel_local - rel_local[BUCKETS - 1 :], precision=lax.Precision.HIGHEST)
    table = jnp.pad(by_dist.T.reshape(heads // 4, 4, 2 * NEAR), ((0, 0), (0, 4), (0, 0)))

    low_one, q, k, v = project(place, tokens, tokens_peer, gain_one, self_query, self_key, self_value)
    past_own = follow(past_own, q)
    past_peer = [swap(own, 0) for own in past_own]
    cot_peer = swap(follow(cotangent, q), 0)
    low_past, k_past, v_past, mem_all, km, vm = project_past(
        place, past_own, past_peer, mems, gain_one, self_key, self_value, cross_key, cross_value
    )
    att, lse_self = self_forward(place, table, q, k, v, k_past, v_past)
    att_peer = swap(att, 0)
    mid, low_two, cq = mid_forward(place, tokens, tokens_peer, att, att_peer, gain_two, self_out, cross_query)
    own_doc = []
    if group_rows > SHORT:
        mem_doc = jnp.arange(mem_all.shape[0], dtype=jnp.int32) // (length // RATIO)
        own = (mem_doc == y_at * chip_rows // length).astype(F32)
        own_doc = [jnp.broadcast_to(own[:, None], (mem_all.shape[0], TILE))]
    crs, lse_cross = cross_forward(place, cq, km, vm, own_doc)
    crs_peer = swap(crs, 0)
    late, low_three, inner, d_gate, d_up, dz, cot_half = ffn(
        place, mid, crs, crs_peer, gain_three, cotangent, cot_peer, cross_out, ffn_gate, ffn_up, ffn_down
    )

    axes = {
        "y": tuple(range(y_bits)),
        "x": (y_bits,),
        "z": (y_bits + 1,),
        "f": tuple(range(y_bits + 2, bits)),
    }

    def order_of(letters):
        return sum((axes[letter] for letter in letters), ())

    dz_peer = swap(dz, 0)
    inner_peer = swap(inner, 0)
    gate = Flow("gate", [([((low_three,), d_gate)], model)], order_of("xyzf"))
    up = Flow("up", [([((low_three,), d_up)], model)], order_of("yzfx"))
    last = hop(place, swap, [gate, up], [], place, "gate_up")
    down = Flow("down", [([((inner, inner_peer), cot_half)], hidden_units)], order_of("zxyf"))
    spread = (down.spread(inner), down.spread(inner_peer))
    down = Flow("down", [([(spread, cot_half)], hidden_units)], order_of("zxyf"))
    last = hop(place, swap, [down], [], last, "down")
    ffn_flows = [gate, up, down]

    g_late, late_half, d_crs, d_gain_three = late_backward(
        place, follow(dz, last), dz_peer, late, cotangent, cot_peer, gain_three, cross_out
    )
    dcq, dkm, dvm = cross_backward(place, cq, km, vm, own_doc, d_crs, crs, lse_cross)
    dcq_peer = swap(dcq, 0)
    crs_mem = Flow(
        "crs_mem",
        [([((crs, crs_peer), late_half)], model), ([((mem_all,), dkm)], model), ([((mem_all,), dvm)], model)],
        order_of("zxyf"),
    )
    last = hop(place, swap, [crs_mem], [], dcq, "crs_mem", cost=5)
    g_mid, mid_half, d_att, d_gain_two = mid_backward(
        place, dcq, follow(dcq_peer, last), mid, g_late, gain_two, cross_query, self_out
    )
    att_cq = Flow("att_cq", [([((att, att_peer), mid_half)], model), ([((low_two,), dcq)], model)], order_of("xyzf"))
    last = hop(place, swap, [att_cq], [], d_att, "att_cq")
    dq, dk, dv, d_past, d_near, d_total = self_backward(
        place, table, q, k, v, k_past, v_past, follow(d_att, last), att, lse_self
    )
    past_moved, rider = [], None
    if n_chips == 2:
        last, rider = hop(place, swap, [], ffn_flows, dq, "ffn_1", rider=(d_past, 1))
    else:
        past_moved = [
            lax.ppermute(d_past[s - 1], "grp", [(g, g - CORES * s) for g in range(CORES * s, groups)])
            for s in range(1, n_chips)
        ]
        last = hop(place, swap, [], ffn_flows, dq, "ffn_1")
    mem_parts = memory_backward(place, follow(dkm, last), dvm, cross_key, cross_value)
    layer_out = layer_output(place, follow(late, mem_parts), inner, inner_peer, ffn_down)
    mem_parts = lax.all_to_all(mem_parts, "grp", split_axis=0, concat_axis=0, tiled=True)
    query = Flow("query", [([((low_one,), dq)], model)], order_of("xyzf"))
    kv = Flow(
        "kv",
        [
            ([((low_one,), d)] + [((low_past[s],), (d_past, (s, which))) for s in range(more)], model)
            for which, d in ((0, dk), (1, dv))
        ],
        order_of("yzxf"),
    )
    attention = [att_cq, crs_mem, query, kv]
    last = hop(place, swap, [query, kv], [att_cq, crs_mem], layer_out, "attention_1", cost=4)

    results = {}
    names = {"ffn": ffn_flows, "attention": attention}

    def step(label, after):
        flows = names[label]
        if label in results:
            return after
        moving = [flow for flow in flows if flow.hops]
        if moving:
            return hop(place, swap, [], moving, after, f"{label}_{len(moving[0].hops)}", cost=4)
        results[label] = last_hop(place, swap, flows, after, label)
        return after

    for label in ("ffn", "attention", "ffn"):
        last = step(label, last)
    dz_own, dz_leave = first_backward(
        place, follow(dq, last), dk, dv, past_moved, rider, self_query, self_key, self_value
    )
    dz_got = swap(dz_leave, 0)
    last = step("attention", dz_leave)
    grad_tokens, d_gain_one = tokens_backward(place, follow(dz_own, last), dz_got, tokens, g_mid, gain_one)
    small = small_sums(place, d_gain_one, d_gain_two, d_gain_three, d_near, d_total, buckets, heads, devices)
    last = small
    small = lax.all_to_all(small, ("dp", "grp"), split_axis=0, concat_axis=0, tiled=True)
    while len(results) < 2:
        for label in ("attention", "ffn"):
            last = step(label, last)
    grad_memory, small = gather_sums(
        place, [follow(mem_parts, last).reshape(groups, -1, model), small], "gather_sums"
    )
    share = model // devices
    rel_share = BUCKETS * HEADS // devices
    got = {**results["ffn"], **results["attention"]}
    return (
        layer_out,
        grad_tokens,
        grad_memory,
        small[0, :share],
        got["query"][0],
        got["kv"][0],
        got["kv"][1],
        got["att_cq"][0],
        small[3, :rel_share],
        small[1, :share],
        got["att_cq"][1],
        got["crs_mem"][1],
        got["crs_mem"][2],
        got["crs_mem"][0],
        small[2, :share],
        got["gate"][0],
        got["up"][0],
        got["down"][0],
    )


def solution(mesh):
    rows = P(("dp", "grp"), None)
    flat = P(("dp", "grp"))
    in_specs = (rows, rows, rows, P("dp")) + (P(),) * 15
    out_specs = (rows,) * 3 + (flat,) + (rows,) * 4 + (flat,) * 2 + (rows,) * 4 + (flat,) + (rows,) * 3
    return jax.shard_map(shards, mesh=mesh, in_specs=in_specs, out_specs=out_specs, check_vma=False)
```

```python
import functools

import jax
import jax.numpy as jnp
from jax import lax
from jax.experimental import pallas as pl
from jax.experimental.pallas import tpu as pltpu
from jax.sharding import PartitionSpec as P

SHORT = 1024
RATIO = 4
BUCKETS = 32
HEADS = 16
EPSILON = 1e-06
THRESHOLDS = (19, 21, 24, 27, 31, 35, 40, 46, 52, 59, 67, 77, 87, 99, 113)
CORES = 2
BF16 = jnp.bfloat16
F32 = jnp.float32
NEGATIVE = -1e30
HEAD = 64
TILE = 256
NEAR = 128
LANES = 128
ROOM = 24 * 1024 * 1024


def dot(a, b):
    return jnp.dot(a, b, preferred_element_type=F32)


def dot_right(a, b):
    return lax.dot_general(a, b, (((1,), (1,)), ((), ())), preferred_element_type=F32)


def shaped(shape, dtype=BF16):
    return jax.ShapeDtypeStruct(tuple(shape), dtype)


def half_shape(array, axis):
    shape = list(array.shape)
    shape[axis] //= CORES
    return tuple(shape)


def whole_kernel(body, place, arrays, weights, outs, name, scratch=(), room=ROOM, cost=0, fetch=()):
    ready = [w for w in weights if not isinstance(w, tuple)]
    far = [w for w in weights if isinstance(w, tuple)]
    n_a, n_r, n_w, n_o, n_f = len(arrays), len(ready), len(far), len(outs), len(fetch)
    buffers = [pltpu.VMEM(half_shape(array, axis), array.dtype) for array, axis, _ in far]
    fetched = [shaped(half_shape(array, axis), array.dtype) for array, axis, _ in fetch]

    def kernel(place_ref, *refs):
        array_refs, refs = refs[:n_a], refs[n_a:]
        ready_refs, refs = refs[:n_r], refs[n_r:]
        far_refs, refs = refs[: n_w + n_f], refs[n_w + n_f :]
        out_refs, refs = refs[:n_o], refs[n_o:]
        fetch_refs, refs = refs[:n_f], refs[n_f:]
        buffer_refs, refs = refs[:n_w], refs[n_w:]
        copies = []
        for at, (ref, buffer, (_, axis, other)) in enumerate(
            zip(far_refs, (*buffer_refs, *fetch_refs), (*far, *fetch))
        ):
            size = buffer.shape[axis]
            start = pl.multiple_of((1 - place_ref[1] if other else place_ref[1]) * size, size)
            source = ref.at[pl.ds(start, size)] if axis == 0 else ref.at[:, pl.ds(start, size)]
            copies.append(pltpu.make_async_copy(source, buffer, refs[0].at[at]))
        for copy in copies:
            copy.start()
        arrived = set()
        places = []
        for w in weights:
            places.append((isinstance(w, tuple), sum(isinstance(x, tuple) == isinstance(w, tuple) for x in weights[: len(places)])))

        def weight(at):
            distant, spot = places[at]
            if not distant:
                return ready_refs[spot]
            if spot not in arrived:
                copies[spot].wait()
                arrived.add(spot)
            return buffer_refs[spot]

        body(place_ref, array_refs, weight, out_refs, refs[1:] if n_w + n_f else refs)
        for copy in copies[n_w:]:
            copy.wait()

    inside = pl.BlockSpec(memory_space=pltpu.VMEM)
    scratch = buffers + ([pltpu.SemaphoreType.DMA((n_w + n_f,))] if n_w + n_f else []) + list(scratch)
    return pl.pallas_call(
        kernel,
        in_specs=[pl.BlockSpec(memory_space=pltpu.SMEM)]
        + [inside] * (n_a + n_r)
        + [pl.BlockSpec(memory_space=pltpu.HBM)] * (n_w + n_f),
        out_specs=[inside] * (n_o + n_f),
        out_shape=list(outs) + fetched,
        scratch_shapes=scratch,
        compiler_params=pltpu.CompilerParams(vmem_limit_bytes=room),
        cost_estimate=pl.CostEstimate(
            flops=int(1.15e9 * cost), bytes_accessed=int(3.69e6 * cost), transcendentals=0
        ),
        name=name,
    )(
        place,
        *arrays,
        *ready,
        *[pltpu.with_memory_space_constraint(array, pltpu.HBM) for array, _, _ in (*far, *fetch)],
    )


def inverse_norm(hidden):
    return lax.rsqrt(jnp.mean(hidden * hidden, axis=-1, keepdims=True) + EPSILON)


def norm_low(hidden, inverse, gain):
    return (hidden * inverse * gain).astype(BF16)


def norm_back(hidden, inverse, gain, dz):
    scaled = gain * dz
    inner = jnp.mean(scaled * hidden, axis=-1, keepdims=True)
    return inverse * scaled - hidden * (inverse * inverse * inverse) * inner


def pick(core, value, axis, other=False):
    half = value.shape[axis] // CORES
    low, high = lax.slice_in_dim(value, 0, half, axis=axis), lax.slice_in_dim(value, half, 2 * half, axis=axis)
    return jnp.where(core == (1 if other else 0), low, high)


def in_place_order(core, own_ref, peer_ref):
    own, peer = own_ref[...].astype(F32), peer_ref[...].astype(F32)
    return jnp.concatenate([jnp.where(core == 0, own, peer), jnp.where(core == 0, peer, own)], axis=0)


def place_rows(half, at):
    zero = jnp.zeros_like(half)
    return jnp.concatenate([half, zero] if at == 0 else [zero, half], axis=0)


def place_lanes(pair, source, at):
    lane = lax.broadcasted_iota(jnp.int32, pair.shape, 1)
    if source != at:
        pair = jnp.concatenate([pair[:, HEAD:], pair[:, :HEAD]], axis=1)
    return jnp.where((lane < HEAD) == (at == 0), pair, jnp.zeros_like(pair))


def near_tiles(table_row):
    skewed = pltpu.roll(jnp.broadcast_to(table_row, (NEAR, 2 * NEAR)), 0, 1, stride=1, stride_axis=0)
    key_at = lax.broadcasted_iota(jnp.int32, (NEAR, NEAR), 0)
    row_at = lax.broadcasted_iota(jnp.int32, (NEAR, NEAR), 1)
    return (jnp.where(key_at <= row_at, skewed[:, :NEAR], NEGATIVE), skewed[:, NEAR:])


def heads_of(pair_turned, cols):
    return jnp.concatenate(
        [place_rows(pair_turned[h * HEAD : (h + 1) * HEAD, cols], h // 2) for h in range(4)], axis=1
    )


def add_corner(scores, tiles):
    rows = scores.shape[0]
    last = scores[rows - NEAR :]
    pieces = []
    for h in range(4):
        pieces += [last[:, h * TILE : h * TILE + NEAR] + tiles[h][1], last[:, h * TILE + NEAR : (h + 1) * TILE]]
    return jnp.concatenate([scores[: rows - NEAR], jnp.concatenate(pieces, axis=1)], axis=0)


def add_diagonal(scores, tiles):
    rows = scores.shape[0]
    first = scores[rows - TILE : rows - NEAR]
    second = scores[rows - NEAR :]
    upper, lower = [], []
    for h in range(4):
        left, right = slice(h * TILE, h * TILE + NEAR), slice(h * TILE + NEAR, (h + 1) * TILE)
        upper += [first[:, left] + tiles[h][0], first[:, right] + tiles[h][1]]
        lower += [jnp.full((NEAR, NEAR), NEGATIVE, F32), second[:, right] + tiles[h][0]]
    last = [jnp.concatenate(upper, axis=1), jnp.concatenate(lower, axis=1)]
    if rows > TILE:
        last = [add_corner(scores[: rows - TILE], tiles)] + last
    return jnp.concatenate(last, axis=0)


def by_distance(near):
    level = near[:8]
    for first in range(8, NEAR, 8):
        level = level + pltpu.roll(near[first : first + 8], 2 * NEAR - first, 1)
    row = lax.broadcasted_iota(jnp.int32, level.shape, 0)
    for bit in (1, 2, 4):
        level = jnp.where(row & bit > 0, pltpu.roll(level, 2 * NEAR - bit, 1), level)
    return jnp.sum(level, axis=0, keepdims=True)


def soft(scores):
    peak = jnp.max(scores, axis=0, keepdims=True)
    weights = jnp.exp(scores - peak)
    return peak, weights.astype(BF16), jnp.sum(weights, axis=0, keepdims=True)


def finish(o_ref, lse_ref, cols, peak, summed, acc):
    out = acc / summed
    lse = peak + jnp.log(summed)
    pieces = []
    for h in range(4):
        e = h // 2
        lanes = slice(h * TILE, (h + 1) * TILE)
        pieces.append(out[e * HEAD : (e + 1) * HEAD, lanes])
        lse_ref[0, h : h + 1, cols] = lse[:, lanes]
    o_ref[cols, :] = jnp.concatenate(pieces, axis=0).T.astype(BF16)


def self_diagonal_block(table_ref, q_ref, k_ref, v_ref, peak_ref, sum_ref, acc_ref):
    rows = q_ref.shape[0]
    v_turned = v_ref[...].T
    q_turned = q_ref[...].T
    tiles = [near_tiles(table_ref[0, h : h + 1, :]) for h in range(4)]
    spans = [slice(t * TILE, (t + 1) * TILE) for t in range(rows // TILE)]
    scores = [add_diagonal(dot(k_ref[: cols.stop], heads_of(q_turned, cols)), tiles) for cols in spans]
    parts = [soft(score) for score in scores]
    for t, cols in enumerate(spans):
        peak_ref[t], sum_ref[t] = parts[t][0], parts[t][2]
        acc_ref[t] = dot(v_turned[:, : cols.stop], parts[t][1])


def self_past_block(
    valid_ref, table_ref, q_ref, kp_ref, vp_ref, peak_in, sum_in, acc_in, o_ref, lse_ref, peak_ref, sum_ref, acc_ref,
    *, earlier
):
    rows = q_ref.shape[0]
    steps = rows // TILE
    q_turned = q_ref[...].T
    spans = [slice(t * TILE, (t + 1) * TILE) for t in range(steps)]
    for s in range(earlier):
        old = (peak_in, sum_in, acc_in) if s == 0 else (peak_ref, sum_ref, acc_ref)

        @pl.when(valid_ref[3 + s] > 0)
        def _(s=s, old=old):
            vp_turned = vp_ref[s].T
            scores = [dot(kp_ref[s], heads_of(q_turned, cols)) for cols in spans]
            if s == 0:
                scores[0] = add_corner(scores[0], [near_tiles(table_ref[0, h : h + 1, :]) for h in range(4)])
            for t, cols in enumerate(spans):
                peak = old[0][t]
                new_peak = jnp.maximum(peak, jnp.max(scores[t], axis=0, keepdims=True))
                rescale = jnp.exp(peak - new_peak)
                weights = jnp.exp(scores[t] - new_peak)
                summed = old[1][t] * rescale + jnp.sum(weights, axis=0, keepdims=True)
                acc = old[2][t] * rescale + dot(vp_turned, weights.astype(BF16))
                if s + 1 < earlier:
                    peak_ref[t], sum_ref[t], acc_ref[t] = new_peak, summed, acc
                else:
                    finish(o_ref, lse_ref, cols, new_peak, summed, acc)

        @pl.when(valid_ref[3 + s] == 0)
        def _(s=s, old=old):
            for t, cols in enumerate(spans):
                if s + 1 < earlier:
                    peak_ref[t], sum_ref[t], acc_ref[t] = old[0][t], old[1][t], old[2][t]
                else:
                    finish(o_ref, lse_ref, cols, old[0][t], old[1][t], old[2][t])


def placed_heads(block, cols):
    rows = []
    for h in range(4):
        pair = block[cols, (h // 2) * 2 * HEAD : (h // 2 + 1) * 2 * HEAD]
        rows.append(place_lanes(pair, h % 2, h // 2))
    return jnp.concatenate(rows, axis=0)


def row_of_heads(ref, cols):
    return jnp.concatenate([ref[0, h : h + 1, cols] for h in range(4)], axis=1)


def deltas(product, cols):
    return jnp.concatenate(
        [jnp.sum(product[h * HEAD : (h + 1) * HEAD, cols], axis=0, keepdims=True) for h in range(4)], axis=1
    )


def back_scores(scores, lse, d_prob, delta):
    prob = jnp.exp(scores - lse)
    d_score = prob * (d_prob - delta)
    return prob.astype(BF16), d_score.astype(BF16)


def query_rows(d_query):
    pieces = [
        d_query[(h // 2) * HEAD : (h // 2 + 1) * HEAD, h * TILE : (h + 1) * TILE] for h in range(4)
    ]
    return jnp.concatenate(pieces, axis=0).T.astype(BF16)


def self_backward_block(
    valid_ref, table_ref, q_ref, k_ref, v_ref, kp_ref, vp_ref, do_ref, o_ref, lse_ref,
    dq_ref, dk_ref, dv_ref, past_ref, db_ref, total_ref,
    near_sum, dq_sum, *, earlier,
):
    rows = q_ref.shape[0]
    steps = rows // TILE
    spans = [slice(t * TILE, (t + 1) * TILE) for t in range(steps)]
    k_turned = k_ref[...].T
    q_turned = q_ref[...].T
    do_turned = do_ref[...].T
    product = (do_ref[...].astype(F32) * o_ref[...].astype(F32)).T
    tiles = [near_tiles(table_ref[0, h : h + 1, :]) for h in range(4)]
    queries = [heads_of(q_turned, cols) for cols in spans]
    outs = [heads_of(do_turned, cols) for cols in spans]
    q_placed = [placed_heads(q_ref, cols) for cols in spans]
    do_placed = [placed_heads(do_ref, cols) for cols in spans]
    lses = [row_of_heads(lse_ref, cols) for cols in spans]
    delta = [deltas(product, cols) for cols in spans]

    for t, cols in enumerate(spans):
        seen = cols.stop
        scores = add_diagonal(dot(k_ref[:seen], queries[t]), tiles)
        prob, d_score = back_scores(scores, lses[t], dot(v_ref[:seen], outs[t]), delta[t])
        d_value = dot(prob, do_placed[t])
        d_key = dot(d_score, q_placed[t])
        if t == 0:
            dv_whole, dk_whole = d_value, d_key
        else:
            more = seen - dv_whole.shape[0]
            dv_whole = jnp.concatenate([dv_whole + d_value[: seen - more], d_value[seen - more :]], axis=0)
            dk_whole = jnp.concatenate([dk_whole + d_key[: seen - more], d_key[seen - more :]], axis=0)
        dq_sum[t] = dot(k_turned[:, :seen], d_score)
        d_wide = d_score.astype(F32)
        total = jnp.sum(d_wide, axis=0, keepdims=True)
        base = seen - TILE
        for h in range(4):
            left, right = slice(h * TILE, h * TILE + NEAR), slice(h * TILE + NEAR, (h + 1) * TILE)
            zero_part = d_wide[base : base + NEAR, left] + d_wide[base + NEAR :, right]
            one_part = d_wide[base : base + NEAR, right]
            if t > 0:
                one_part = one_part + d_wide[base - NEAR : base, left]
            both = jnp.concatenate([zero_part, one_part], axis=1)
            part = total[:, h * TILE : (h + 1) * TILE]
            if t == 0:
                near_sum[h] = both
                total_ref[0, h : h + 1, :] = part
            else:
                near_sum[h] += both
                total_ref[0, h : h + 1, :] += part
    dk_ref[...] = dk_whole.astype(BF16)
    dv_ref[...] = dv_whole.astype(BF16)

    for s in range(earlier):

        @pl.when(valid_ref[3 + s] > 0)
        def _(s=s):
            kp_turned = kp_ref[s].T
            for t in range(steps):
                scores = dot(kp_ref[s], queries[t])
                if s == 0 and t == 0:
                    scores = add_corner(scores, tiles)
                prob, d_score = back_scores(scores, lses[t], dot(vp_ref[s], outs[t]), delta[t])
                d_value = dot(prob, do_placed[t])
                d_key = dot(d_score, q_placed[t])
                dv_whole = d_value if t == 0 else dv_whole + d_value
                dk_whole = d_key if t == 0 else dk_whole + d_key
                dq_sum[t] += dot(kp_turned, d_score)
                d_wide = d_score.astype(F32)
                total = jnp.sum(d_wide, axis=0, keepdims=True)
                for h in range(4):
                    total_ref[0, h : h + 1, :] += total[:, h * TILE : (h + 1) * TILE]
                    if s == 0 and t == 0:
                        near_sum[h, :, NEAR:] += d_wide[rows - NEAR :, h * TILE : h * TILE + NEAR]
            past_ref[s, 0] = dk_whole.astype(BF16)
            past_ref[s, 1] = dv_whole.astype(BF16)

        @pl.when(valid_ref[3 + s] == 0)
        def _(s=s):
            past_ref[s] = jnp.zeros_like(past_ref[s])

    for t, cols in enumerate(spans):
        dq_ref[cols, :] = query_rows(dq_sum[t])
    for h in range(4):
        db_ref[0, h : h + 1, :] = by_distance(near_sum[h])
    db_ref[0, 4:, :] = jnp.zeros((4, 2 * NEAR), F32)
    total_ref[0, 4:, :] = jnp.zeros((4, 2 * NEAR), F32)


def cross_forward_block(q_ref, k_ref, v_ref, own_ref, o_ref, lse_ref, *, masked):
    rows = q_ref.shape[0]
    v_turned = v_ref[...].T
    q_turned = q_ref[...].T
    spans = [slice(t * TILE, (t + 1) * TILE) for t in range(rows // TILE)]
    scores = [dot(k_ref[...], heads_of(q_turned, cols)) for cols in spans]
    if masked:
        blocked = jnp.where(own_ref[...] > 0, 0.0, NEGATIVE)
        blocked = jnp.concatenate([blocked] * 4, axis=1)
        scores = [score + blocked for score in scores]
    for t, cols in enumerate(spans):
        peak, weights, summed = soft(scores[t])
        finish(o_ref, lse_ref, cols, peak, summed, dot(v_turned, weights))


def cross_backward_block(
    q_ref, k_ref, v_ref, own_ref, do_ref, o_ref, lse_ref, dq_ref, dk_ref, dv_ref, *, masked
):
    rows = q_ref.shape[0]
    k_turned = k_ref[...].T
    q_turned = q_ref[...].T
    do_turned = do_ref[...].T
    product = (do_ref[...].astype(F32) * o_ref[...].astype(F32)).T
    spans = [slice(t * TILE, (t + 1) * TILE) for t in range(rows // TILE)]
    dk_whole, dv_whole = 0.0, 0.0
    for t, cols in enumerate(spans):
        scores = dot(k_ref[...], heads_of(q_turned, cols))
        if masked:
            blocked = jnp.where(own_ref[...] > 0, 0.0, NEGATIVE)
            scores = scores + jnp.concatenate([blocked] * 4, axis=1)
        d_prob = dot(v_ref[...], heads_of(do_turned, cols))
        prob, d_score = back_scores(scores, row_of_heads(lse_ref, cols), d_prob, deltas(product, cols))
        dv_whole = dv_whole + dot(prob, placed_heads(do_ref, cols))
        dk_whole = dk_whole + dot(d_score, placed_heads(q_ref, cols))
        dq_ref[cols, :] = query_rows(dot(k_turned, d_score))
    dk_ref[...] = dk_whole.astype(BF16)
    dv_ref[...] = dv_whole.astype(BF16)


def wide_view(ref, p):
    return ref.at[:, pl.ds(p * 4 * HEAD, 4 * HEAD)]


def slim_view(ref, p):
    return ref.at[:, pl.ds(p * 2 * HEAD, 2 * HEAD)]


def past_view(ref, p):
    return ref.at[:, :, pl.ds(p * 2 * HEAD, 2 * HEAD)]


def page_view(ref, p):
    return ref.at[pl.ds(p, 1)]


def self_diagonal(place, table, q, k, v, fetch):
    rows, blocks = q.shape[0], k.shape[1] // (2 * HEAD)
    steps = rows // TILE

    def body(place_ref, arrays, weight, outs, scratch):
        table_ref, q_ref, k_ref, v_ref = arrays
        for p in range(blocks):
            self_diagonal_block(
                page_view(table_ref, p), wide_view(q_ref, p), slim_view(k_ref, p), slim_view(v_ref, p),
                *[ref.at[p] for ref in outs],
            )

    state = [(blocks, steps, 1, 4 * TILE), (blocks, steps, 1, 4 * TILE), (blocks, steps, 2 * HEAD, 4 * TILE)]
    return whole_kernel(body, place, [table, q, k, v], [], [shaped(shape, F32) for shape in state], "self_diagonal", fetch=fetch)


def self_past(place, table, q, kp, vp, peak, summed, acc, fetch):
    rows, blocks, earlier = q.shape[0], kp.shape[2] // (2 * HEAD), kp.shape[0]

    def body(place_ref, arrays, weight, outs, scratch):
        table_ref, q_ref, kp_ref, vp_ref, peak_ref, sum_ref, acc_ref = arrays
        for p in range(blocks):
            self_past_block(
                place_ref, page_view(table_ref, p), wide_view(q_ref, p), past_view(kp_ref, p), past_view(vp_ref, p),
                peak_ref.at[p], sum_ref.at[p], acc_ref.at[p], wide_view(outs[0], p), page_view(outs[1], p),
                *([ref.at[p] for ref in scratch] if earlier > 1 else [None] * 3), earlier=earlier,
            )

    return whole_kernel(
        body,
        place,
        [table, q, kp, vp, peak, summed, acc],
        [],
        [shaped(q.shape), shaped((blocks, 8, rows), F32)],
        "self_past",
        [pltpu.VMEM(a.shape, F32) for a in (peak, summed, acc)] if earlier > 1 else [],
        fetch=fetch,
    )


def self_backward(place, table, q, k, v, kp, vp, do, o, lse):
    rows, blocks, earlier = q.shape[0], k.shape[1] // (2 * HEAD), kp.shape[0]
    steps = rows // TILE

    def body(place_ref, arrays, weight, outs, scratch):
        table_ref, q_ref, k_ref, v_ref, kp_ref, vp_ref, do_ref, o_ref, lse_ref = arrays
        dq_ref, dk_ref, dv_ref, past_ref, db_ref, total_ref = outs
        for p in range(blocks):
            self_backward_block(
                place_ref, page_view(table_ref, p), wide_view(q_ref, p), slim_view(k_ref, p), slim_view(v_ref, p),
                past_view(kp_ref, p), past_view(vp_ref, p), wide_view(do_ref, p), wide_view(o_ref, p),
                page_view(lse_ref, p), wide_view(dq_ref, p), slim_view(dk_ref, p), slim_view(dv_ref, p),
                past_ref.at[:, :, :, pl.ds(p * 2 * HEAD, 2 * HEAD)], page_view(db_ref, p), page_view(total_ref, p),
                *[ref.at[p] for ref in scratch], earlier=earlier,
            )

    return whole_kernel(
        body,
        place,
        [table, q, k, v, kp, vp, do, o, lse],
        [],
        [
            shaped(q.shape),
            shaped(k.shape),
            shaped(k.shape),
            shaped((earlier, 2) + k.shape),
            shaped(table.shape, F32),
            shaped(table.shape, F32),
        ],
        "self_backward",
        [pltpu.VMEM((blocks, 4, NEAR, 2 * NEAR), F32), pltpu.VMEM((blocks, steps, 2 * HEAD, 4 * TILE), F32)],
    )


def cross_forward(place, q, k, v, own):
    rows, blocks = q.shape[0], k.shape[1] // (2 * HEAD)

    def body(place_ref, arrays, weight, outs, scratch):
        q_ref, k_ref, v_ref = arrays[:3]
        for p in range(blocks):
            cross_forward_block(
                wide_view(q_ref, p), slim_view(k_ref, p), slim_view(v_ref, p), arrays[-1], wide_view(outs[0], p),
                page_view(outs[1], p), masked=len(own) > 0,
            )

    outs = [shaped(q.shape), shaped((blocks, 8, rows), F32)]
    return whole_kernel(body, place, [q, k, v] + own, [], outs, "cross_forward")


def cross_backward(place, q, k, v, own, do, o, lse, fetch):
    blocks = k.shape[1] // (2 * HEAD)

    def body(place_ref, arrays, weight, outs, scratch):
        q_ref, k_ref, v_ref, do_ref, o_ref, lse_ref = arrays[:6]
        for p in range(blocks):
            cross_backward_block(
                wide_view(q_ref, p), slim_view(k_ref, p), slim_view(v_ref, p), arrays[-1], wide_view(do_ref, p),
                wide_view(o_ref, p), page_view(lse_ref, p), wide_view(outs[0], p), slim_view(outs[1], p),
                slim_view(outs[2], p), masked=len(own) > 0,
            )

    outs = [shaped(q.shape), shaped(k.shape), shaped(k.shape)]
    return whole_kernel(body, place, [q, k, v, do, o, lse] + own, [], outs, "cross_backward", fetch=fetch)


def project(place, own, peer, gain, wq, wk, wv):
    rows, model = own.shape
    wide, slim = wq.shape[1] // CORES, wk.shape[1] // CORES

    def body(place_ref, arrays, weight, outs, scratch):
        hidden = in_place_order(place_ref[1], arrays[0], arrays[1])
        low = norm_low(hidden, inverse_norm(hidden), arrays[2][...].astype(F32))
        outs[0][...] = low
        for at in range(3):
            outs[1 + at][...] = dot(low, weight(at)[...]).astype(BF16)

    return whole_kernel(
        body,
        place,
        [own, peer, gain],
        [(wq, 1, False), (wk, 1, False), (wv, 1, False)],
        [shaped((CORES * rows, n)) for n in (model, wide, slim, slim)],
        "project",
    )


def project_past(place, owns, peers, gain, wk, wv, fetch):
    rows, model = owns[0].shape
    earlier = len(owns)
    slim = wk.shape[1] // CORES

    def body(place_ref, arrays, weight, outs, scratch):
        own_refs, peer_refs = arrays[:earlier], arrays[earlier : 2 * earlier]
        gain_value = arrays[-1][...].astype(F32)
        for s in range(earlier):
            hidden = in_place_order(place_ref[1], own_refs[s], peer_refs[s])
            low = norm_low(hidden, inverse_norm(hidden), gain_value)
            outs[s][...] = low
            outs[earlier][s] = dot(low, weight(0)[...]).astype(BF16)
            outs[earlier + 1][s] = dot(low, weight(1)[...]).astype(BF16)

    made = whole_kernel(
        body,
        place,
        owns + peers + [gain],
        [(wk, 1, False), (wv, 1, False)],
        [shaped((CORES * rows, model))] * earlier + [shaped((earlier, CORES * rows, slim))] * 2,
        "project_past",
        fetch=fetch,
    )
    return made[:earlier], *made[earlier:]


def project_memory(place, mems, wk, wv):
    groups = len(mems)
    rows, model = mems[0].shape
    slim = wk.shape[1] // CORES

    def body(place_ref, arrays, weight, outs, scratch):
        for at, piece_ref in enumerate(arrays):
            block = jnp.bitwise_xor(place_ref[2], jnp.int32(at))
            outs[0][pl.ds(pl.multiple_of(block * rows, rows), rows)] = piece_ref[...]
        mem = outs[0][...]
        outs[1][...] = dot(mem, weight(0)[...]).astype(BF16)
        outs[2][...] = dot(mem, weight(1)[...]).astype(BF16)

    return whole_kernel(
        body,
        place,
        mems,
        [(wk, 1, False), (wv, 1, False)],
        [shaped((groups * rows, n)) for n in (model, slim, slim)],
        "project_memory",
        cost=8,
    )


def mid_forward(place, own, peer, att, att_peer, gain, wo, wo_peer, wq):
    rows, model = own.shape

    def body(place_ref, arrays, weight, outs, scratch):
        own_ref, peer_ref, att_ref, att_peer_ref, gain_ref = arrays
        hidden = in_place_order(place_ref[1], own_ref, peer_ref)
        hidden = hidden + dot(att_ref[...], weight(0)[...]) + dot(att_peer_ref[...], weight(1)[...])
        outs[0][...] = hidden.astype(BF16)
        low = norm_low(hidden, inverse_norm(hidden), gain_ref[...].astype(F32))
        outs[1][...] = low
        outs[2][...] = dot(low, weight(2)[...]).astype(BF16)

    return whole_kernel(
        body,
        place,
        [own, peer, att, att_peer, gain],
        [wo, wo_peer, wq],
        [shaped((CORES * rows, model))] * 2 + [shaped((CORES * rows, wq.shape[1]))],
        "mid_forward",
    )


def ffn(place, mid, crs, crs_peer, gain, cot, cot_peer, wc, wc_peer, wg, wu, wd):
    rows, model = mid.shape
    hidden_half = wd.shape[0]
    steps = [256] * (hidden_half // 256) + [hidden_half % 256] * (hidden_half % 256 > 0)
    scale = 0.7978845608028654

    def body(place_ref, arrays, weight, outs, scratch):
        mid_ref, crs_ref, crs_peer_ref, gain_ref, cot_ref, cot_peer_ref = arrays
        late_ref, low_ref, inner_ref, dg_ref, du_ref, dz_ref, cot_half_ref = outs
        cot_value = in_place_order(place_ref[1], cot_ref, cot_peer_ref).astype(BF16)
        cot_half_ref[...] = pick(place_ref[1], cot_value, 1)
        hidden = mid_ref[...].astype(F32) + dot(crs_ref[...], weight(0)[...]) + dot(crs_peer_ref[...], weight(1)[...])
        late_ref[...] = hidden.astype(BF16)
        low = norm_low(hidden, inverse_norm(hidden), gain_ref[...].astype(F32))
        low_ref[...] = low
        start = 0
        for width in steps:
            cols = slice(start, start + width)
            start += width
            gate = dot(low, weight(2)[:, cols])
            up = dot(low, weight(3)[:, cols])
            d_inner = dot_right(cot_value, weight(4)[cols]).astype(BF16).astype(F32)
            square = gate * gate
            bent = jnp.tanh(gate * (scale + (scale * 0.044715) * square))
            whole = 0.5 + 0.5 * bent
            slope = whole + (0.5 * gate) * (1.0 - bent * bent) * (scale + (3 * scale * 0.044715) * square)
            curve = gate * whole
            inner_ref[:, cols] = (curve * up).astype(BF16)
            dg_ref[:, cols] = (d_inner * up * slope).astype(BF16)
            du_ref[:, cols] = (d_inner * curve).astype(BF16)
        dz_ref[...] = (dot_right(dg_ref[...], weight(2)[...]) + dot_right(du_ref[...], weight(3)[...])).astype(BF16)

    return whole_kernel(
        body,
        place,
        [mid, crs, crs_peer, gain, cot, cot_peer],
        [wc, wc_peer, wg, wu, wd],
        [shaped((rows, model))] * 2
        + [shaped((rows, hidden_half))] * 3
        + [shaped((rows, model)), shaped((rows, model // CORES))],
        "ffn",
        room=16 * 1024 * 1024,
    )


def late_backward(place, dz, dz_peer, late, cot, cot_peer, gain, wc):
    rows, model = late.shape

    def body(place_ref, arrays, weight, outs, scratch):
        dz_ref, dz_peer_ref, late_ref, cot_ref, cot_peer_ref, gain_ref = arrays
        dz_value = dz_ref[...].astype(F32) + dz_peer_ref[...].astype(F32)
        hidden = late_ref[...].astype(F32)
        inverse = inverse_norm(hidden)
        outs[3][...] = jnp.sum(dz_value * hidden * inverse, axis=0, keepdims=True)
        grad = in_place_order(place_ref[1], cot_ref, cot_peer_ref)
        grad = grad + norm_back(hidden, inverse, gain_ref[...].astype(F32), dz_value)
        low = grad.astype(BF16)
        outs[0][...] = low
        outs[1][...] = pick(place_ref[1], low, 1)
        outs[2][...] = dot_right(low, weight(0)[...]).astype(BF16)

    return whole_kernel(
        body,
        place,
        [dz, dz_peer, late, cot, cot_peer, gain],
        [wc],
        [
            shaped((rows, model)),
            shaped((rows, model // CORES)),
            shaped((rows, wc.shape[0])),
            shaped((1, model), F32),
        ],
        "late_backward",
    )


def mid_backward(place, dq, dq_peer, mid, g_late, gain, wq, wq_peer, wo):
    rows, model = mid.shape

    def body(place_ref, arrays, weight, outs, scratch):
        dq_ref, dq_peer_ref, mid_ref, g_ref, gain_ref = arrays
        dz = dot_right(dq_ref[...], weight(0)[...]) + dot_right(dq_peer_ref[...], weight(1)[...])
        hidden = mid_ref[...].astype(F32)
        inverse = inverse_norm(hidden)
        outs[3][...] = jnp.sum(dz * hidden * inverse, axis=0, keepdims=True)
        grad = g_ref[...].astype(F32) + norm_back(hidden, inverse, gain_ref[...].astype(F32), dz)
        low = grad.astype(BF16)
        outs[0][...] = pick(place_ref[1], low, 0)
        outs[1][...] = pick(place_ref[1], low, 1)
        outs[2][...] = dot_right(low, weight(2)[...]).astype(BF16)

    return whole_kernel(
        body,
        place,
        [dq, dq_peer, mid, g_late, gain],
        [wq, wq_peer, wo],
        [
            shaped((rows // CORES, model)),
            shaped((rows, model // CORES)),
            shaped((rows, wo.shape[0])),
            shaped((1, model), F32),
        ],
        "mid_backward",
    )


def first_backward(place, dq, dk, dv, past, rider, wq, wk, wv):
    rows, model = dq.shape[0], wq.shape[0]
    slim = dk.shape[1]

    def body(place_ref, arrays, weight, outs, scratch):
        dq_ref, dk_ref, dv_ref = arrays[:3]
        dk_value, dv_value = dk_ref[...].astype(F32), dv_ref[...].astype(F32)
        if rider is not None:
            blocks = [
                arrays[3][rider[1] + at * rows : rider[1] + (at + 1) * rows].astype(F32)
                for at in range(2 * slim // LANES)
            ]
            dk_value = dk_value + jnp.concatenate(blocks[: slim // LANES], axis=1)
            dv_value = dv_value + jnp.concatenate(blocks[slim // LANES :], axis=1)
        else:
            for ref in arrays[3:]:
                dk_value = dk_value + ref[0].astype(F32)
                dv_value = dv_value + ref[1].astype(F32)
        dz = dot_right(dq_ref[...], weight(0)[...])
        dz = dz + dot_right(dk_value.astype(BF16), weight(1)[...]) + dot_right(dv_value.astype(BF16), weight(2)[...])
        outs[0][...] = pick(place_ref[1], dz, 0)
        outs[1][...] = pick(place_ref[1], dz, 0, True).astype(BF16)

    return whole_kernel(
        body,
        place,
        [dq, dk, dv] + (past if rider is None else [rider[0]]),
        [(wq, 1, False), (wk, 1, False), (wv, 1, False)],
        [shaped((rows // CORES, model), F32), shaped((rows // CORES, model))],
        "first_backward",
    )


def tokens_backward(place, dz, dz_got, tokens, g_mid, gain):
    def body(place_ref, arrays, weight, outs, scratch):
        dz_ref, dz_got_ref, tokens_ref, g_ref, gain_ref = arrays
        dz_value = dz_ref[...] + dz_got_ref[...].astype(F32)
        hidden = tokens_ref[...].astype(F32)
        inverse = inverse_norm(hidden)
        outs[1][...] = jnp.sum(dz_value * hidden * inverse, axis=0, keepdims=True)
        grad = g_ref[...].astype(F32) + norm_back(hidden, inverse, gain_ref[...].astype(F32), dz_value)
        outs[0][...] = grad.astype(BF16)

    outs = [shaped(tokens.shape), shaped((1, tokens.shape[1]), F32)]
    return whole_kernel(body, place, [dz, dz_got, tokens, g_mid, gain], [], outs, "tokens_backward")


def layer_output(place, late, inner, inner_peer, wd):
    rows, model = late.shape

    def body(place_ref, arrays, weight, outs, scratch):
        own, inner_own, inner_other = (pick(place_ref[1], ref[...], 0) for ref in arrays)
        total = own.astype(F32) + dot(inner_own, weight(0)[...]) + dot(inner_other, weight(1)[...])
        outs[0][...] = total.astype(BF16)

    return whole_kernel(
        body,
        place,
        [late, inner, inner_peer],
        [(wd, 0, False), (wd, 0, True)],
        [shaped((rows // CORES, model))],
        "layer_output",
    )[0]


def memory_backward(place, dk, dv, wk, wv):
    def body(place_ref, arrays, weight, outs, scratch):
        grad = dot_right(arrays[0][...], weight(0)[...]) + dot_right(arrays[1][...], weight(1)[...])
        outs[0][...] = grad.astype(BF16)

    weights = [(wk, 1, False), (wv, 1, False)]
    return whole_kernel(body, place, [dk, dv], weights, [shaped((dk.shape[0], wk.shape[0]))], "memory_backward")[0]


def small_sums(place, one, two, three, near, total, buckets, heads, devices):
    def body(place_ref, arrays, weight, outs, scratch):
        one_ref, two_ref, three_ref, near_ref, total_ref, bucket_ref = arrays
        core = place_ref[1]
        first = core == 0
        gains = [one_ref[...], jnp.where(first, two_ref[...], 0.0), jnp.where(first, three_ref[...], 0.0)]
        near = jnp.concatenate([near_ref[p, :4] for p in range(heads // 4)], axis=0)
        total = jnp.concatenate([total_ref[p, :4] for p in range(heads // 4)], axis=0)
        far = jnp.sum(total, axis=1, keepdims=True) - jnp.sum(near, axis=1, keepdims=True)
        last = lax.broadcasted_iota(jnp.int32, near.shape, 1) == near.shape[1] - 1
        near = near + jnp.where(last, far, 0.0)
        entries = BUCKETS * HEADS
        entry = lax.broadcasted_iota(jnp.int32, (near.shape[1], entries), 1)
        same = (lax.shift_right_logical(entry, jnp.int32(HEADS.bit_length() - 1)) == bucket_ref[...]).astype(F32)
        sums = jnp.dot(near, same, precision=lax.Precision.HIGHEST, preferred_element_type=F32)
        head = lax.broadcasted_iota(jnp.int32, sums.shape, 0) + core * heads
        of_entry = jnp.bitwise_and(lax.broadcasted_iota(jnp.int32, sums.shape, 1), jnp.int32(HEADS - 1))
        vectors = gains + [jnp.sum(jnp.where(head == of_entry, sums, 0.0), axis=0, keepdims=True)]
        for block in range(devices):
            rows = []
            for vector in vectors:
                size = vector.shape[1] // devices
                row = vector[:, block * size : (block + 1) * size]
                rows.append(jnp.concatenate([row, jnp.zeros((1, LANES - size), F32)], axis=1))
            outs[0][block] = jnp.concatenate(rows + [jnp.zeros((4, LANES), F32)], axis=0)

    return whole_kernel(
        body, place, [one, two, three, near, total, buckets], [], [shaped((devices, 8, LANES), F32)], "small_sums"
    )[0]


def gather_sums(place, parts, name):
    def body(place_ref, arrays, weight, outs, scratch):
        for array, out in zip(arrays, outs):
            total = array[0].astype(F32)
            for at in range(1, array.shape[0]):
                total = total + array[at].astype(F32)
            out[...] = total.astype(out.dtype)

    return whole_kernel(body, place, parts, [], [shaped(a.shape[1:], a.dtype) for a in parts], name)


def up_to(value, multiple):
    return (value + multiple - 1) // multiple * multiple


def array_of(y):
    return y[0] if isinstance(y, tuple) else y


class Flow:
    def __init__(self, name, pieces, order):
        self.name, self.pieces, self.order = name, pieces, order
        self.hops = [bit + 1 for bit in order]
        self.chips = 1 << len(order)
        self.layout = []
        start = 0
        for terms, rows in pieces:
            half = rows // self.chips // CORES
            padded = up_to(half, 8)
            width = array_of(terms[0][1]).shape[-1]
            self.layout.append((start, half, padded, width))
            start += CORES * padded * (width // LANES)
        self.rows = start
        self.keep = self.got = None

    def spread(self, x):
        half, padded = self.layout[0][1:3]
        if half == padded:
            return x
        chunks = x.reshape(x.shape[0], -1, half)
        return jnp.pad(chunks, ((0, 0), (0, 0), (0, padded - half))).reshape(x.shape[0], -1)


def chip_of(spot, order):
    number = 0
    for at, bit in enumerate(order):
        number |= (spot >> (len(order) - 1 - at) & 1) << bit
    return number


def sum_flow(flow, refs_of, place_ref, turned, free, send_ref, base, keep_ref):
    chip, core = place_ref[0], place_ref[1]
    half = flow.chips // 2
    for (terms, _), (start, _, padded, width) in zip(flow.pieces, flow.layout):
        chunk = CORES * padded
        lefts = []
        for xs, y in terms:
            key = (tuple(id(x) for x in xs), flow.order)
            if key not in turned:
                straight_ref, turned[key] = free.pop(0), free.pop(0)
                if len(xs) == 1:
                    straight_ref[...] = refs_of[id(xs[0])][...].T
                else:
                    size = straight_ref.shape[0] // CORES
                    for part, x in enumerate(xs):
                        at = (core if part == 0 else 1 - core) * size
                        straight_ref[pl.ds(pl.multiple_of(at, 16), size)] = refs_of[id(x)][...].T
                for spot in range(flow.chips):
                    at = jnp.bitwise_xor(jnp.int32(chip_of(spot, flow.order)), chip) * chunk
                    turned[key][spot * chunk : (spot + 1) * chunk] = straight_ref[pl.ds(pl.multiple_of(at, 16), chunk)]
            lefts.append(turned[key])
        count = max(1, min(flow.chips, 512 // chunk))
        while flow.chips % count:
            count -= 1
        for first in range(0, flow.chips, count):
            tile = None
            for left, (_, y) in zip(lefts, terms):
                y_ref = refs_of[id(array_of(y))]
                y_value = y_ref[y[1]] if isinstance(y, tuple) else y_ref[...]
                term = dot(left[first * chunk : (first + count) * chunk], y_value)
                tile = term if tile is None else tile + term
            tile = tile.astype(BF16)
            for inner in range(count):
                spot = first + inner
                for block in range(width // LANES):
                    value = tile[inner * chunk : (inner + 1) * chunk, block * LANES : (block + 1) * LANES]
                    at = start + block * chunk
                    if spot < half:
                        keep_ref[spot, at : at + chunk] = value
                    else:
                        at += base + (spot - half) * flow.rows
                        send_ref[at : at + chunk] = value


def add_flow(flow, old_ref, got_ref, got_at, send_ref, base, keep_ref):
    half = old_ref.shape[0] // 2
    for spot in range(2 * half):
        at = got_at + spot * flow.rows
        total = (old_ref[spot].astype(F32) + got_ref[at : at + flow.rows].astype(F32)).astype(BF16)
        if spot < half:
            keep_ref[spot] = total
        else:
            send_ref[base + (spot - half) * flow.rows : base + (spot - half + 1) * flow.rows] = total


def hop(place, swap, sums, adds, after, name, cost=0, rider=None):
    arrays, seen = [], {}

    def take(array):
        if id(array) not in seen:
            seen[id(array)] = len(arrays)
            arrays.append(array)

    for flow in sums:
        for terms, _ in flow.pieces:
            for xs, y in terms:
                for array in (*xs, array_of(y)):
                    take(array)
    for flow in adds:
        take(flow.keep)
        take(flow.got[0])
    bits, sends, keeps = {}, {}, {}
    for flow in sums + adds:
        half = (flow.chips if flow in sums else flow.keep.shape[0]) // 2
        bit = flow.hops[0]
        base = bits.setdefault(bit, 0)
        sends[flow.name] = (bit, base)
        bits[bit] = base + half * flow.rows
        keeps[flow.name] = shaped((half, flow.rows, LANES))
    if rider is not None:
        rider_array, rider_bit = rider
        take(rider_array)
        rider_at = bits.setdefault(rider_bit, 0)
        bits[rider_bit] = rider_at + rider_array.size // LANES
    order = list(bits)
    outs = [shaped((bits[bit], LANES)) for bit in order] + list(keeps.values())

    def body(place_ref, refs, weight, out_refs, scratch):
        refs_of = {key: refs[at] for key, at in seen.items()}
        turned, free = {}, list(scratch)
        for at, flow in enumerate(sums + adds):
            bit, base = sends[flow.name]
            send_ref, keep_ref = out_refs[order.index(bit)], out_refs[len(order) + at]
            if flow in sums:
                sum_flow(flow, refs_of, place_ref, turned, free, send_ref, base, keep_ref)
            else:
                add_flow(
                    flow, refs_of[id(flow.keep)], refs_of[id(flow.got[0])], flow.got[1], send_ref, base, keep_ref
                )
        if rider is not None:
            send_ref, at = out_refs[order.index(rider_bit)], rider_at
            _, pages, rows, width = rider_array.shape
            for page in range(pages):
                for block in range(width // LANES):
                    send_ref[at : at + rows] = refs_of[id(rider_array)][0, page, :, block * LANES : (block + 1) * LANES]
                    at += rows

    needed = {}
    for flow in sums:
        for terms, _ in flow.pieces:
            for xs, _ in terms:
                shape = (sum(x.shape[1] for x in xs), xs[0].shape[0])
                needed[(tuple(id(x) for x in xs), flow.order)] = [pltpu.VMEM(shape, BF16)] * 2
    scratch = sum(needed.values(), [])
    made = whole_kernel(body, place, follow(arrays, after), [], outs, name, scratch, cost=cost)
    moved = [swap(array, bit) for array, bit in zip(made, order)]
    for at, flow in enumerate(sums + adds):
        bit, base = sends[flow.name]
        flow.keep, flow.got, flow.hops = made[len(order) + at], (moved[order.index(bit)], base), flow.hops[1:]
    if rider is not None:
        return list(made), (moved[order.index(rider_bit)], rider_at)
    return list(made)


def last_hop(place, swap, flows, after, name):
    arrays, seen = [], {}
    for flow in flows:
        for array in (flow.keep, flow.got[0]):
            if id(array) not in seen:
                seen[id(array)] = len(arrays)
                arrays.append(array)
    blocks = []
    size = 0
    for f, flow in enumerate(flows):
        for piece, (start, half, padded, width) in enumerate(flow.layout):
            for block in range(width // LANES):
                blocks.append((f, piece, start + block * CORES * padded, padded, block, size))
                size += up_to(padded, 16)
    own_outs = [
        shaped((padded, width), F32) for flow in flows for _, _, padded, width in flow.layout
    ]
    first = [sum(len(flow.layout) for flow in flows[:f]) for f in range(len(flows))]

    def add_body(place_ref, refs, weight, outs, scratch):
        core = place_ref[1]
        for f, piece, at, padded, block, leave_at in blocks:
            flow = flows[f]
            got_at = flow.got[1] + at
            total = refs[seen[id(flow.keep)]][0, at : at + CORES * padded].astype(F32)
            total = total + refs[seen[id(flow.got[0])]][got_at : got_at + CORES * padded].astype(F32)
            own, leave = pick(core, total, 0), pick(core, total, 0, True)
            outs[1 + first[f] + piece][:, block * LANES : (block + 1) * LANES] = own
            full = up_to(padded, 16)
            if full > padded:
                leave = jnp.concatenate([leave, jnp.zeros((full - padded, LANES), F32)], axis=0)
            outs[0][leave_at : leave_at + full] = leave.astype(BF16)

    made = whole_kernel(add_body, place, follow(arrays, after), [], [shaped((size, LANES))] + own_outs, "last_" + name)
    got = swap(made[0], 0)

    def join_body(place_ref, refs, weight, outs, scratch):
        core = place_ref[1]
        for f, piece, _, padded, block, leave_at in blocks:
            at = first[f] + piece
            width = refs[1 + at].shape[1]
            own = refs[1 + at][:, block * LANES : (block + 1) * LANES]
            other = refs[0][leave_at : leave_at + up_to(padded, 16)].astype(F32)[:padded]
            low, high = slice(block * LANES, (block + 1) * LANES), slice(width + block * LANES, width + (block + 1) * LANES)
            outs[at][:, low] = jnp.where(core == 0, own, other)
            outs[at][:, high] = jnp.where(core == 0, other, own)

    joined = whole_kernel(
        join_body, place, [got] + list(made[1:]), [], [shaped((a.shape[0], CORES * a.shape[1]), F32) for a in own_outs],
        "join_" + name,
    )
    results = {}
    for f, flow in enumerate(flows):
        results[flow.name] = [
            joined[first[f] + piece][:half] for piece, (_, half, _, _) in enumerate(flow.layout)
        ]
    return results


def follow(value, after):
    return lax.optimization_barrier((value, after))[0]


def rel_bucket(distance):
    beyond = 16 + sum((distance >= border).astype(jnp.int32) for border in THRESHOLDS)
    return jnp.where(distance < 16, distance, beyond)


def shards(
    tokens, memory, cotangent, bucket, gain_self, self_query, self_key, self_value, self_out, rel_bias,
    gain_cross, cross_query, cross_key, cross_value, cross_out, gain_ffn, ffn_gate, ffn_up, ffn_down,
):
    groups = lax.axis_size("grp")
    dp_size = lax.axis_size("dp")
    n_chips = groups // CORES
    more = n_chips - 1
    chips = dp_size * n_chips
    devices = chips * CORES
    grp_at = lax.axis_index("grp")
    core = grp_at % CORES
    y_at = grp_at // CORES
    chip = lax.axis_index("dp") * n_chips + y_at
    rows, model = tokens.shape
    chip_rows = rows * CORES
    group_rows = chip_rows * n_chips
    hidden_units = ffn_down.shape[0]
    length = jnp.minimum(group_rows, jnp.maximum(SHORT, jnp.right_shift(jnp.int32(group_rows), bucket[0])))
    y_bits = n_chips.bit_length() - 1
    bits = chips.bit_length() - 1
    first_chip = y_at * chip_rows // length * length // chip_rows
    valid = [(y_at - s >= first_chip).astype(jnp.int32) for s in range(1, n_chips)]
    place = jnp.stack([chip, core, grp_at] + valid).astype(jnp.int32)

    def swap(v, bit):
        return lax.ppermute(v, ("dp", "grp"), [(i, i ^ (1 << bit)) for i in range(devices)])

    gain_one, gain_two, gain_three = (g.reshape(1, model) for g in (gain_self, gain_cross, gain_ffn))

    past_own = [
        lax.ppermute(tokens, "grp", [(g, g + CORES * s) for g in range(groups - CORES * s)]) for s in range(1, n_chips)
    ]
    tokens_peer = swap(tokens, 0)
    mems = [memory] + [
        lax.ppermute(memory, "grp", [(g, g ^ other) for g in range(groups)]) for other in range(1, groups)
    ]

    distances = jnp.arange(2 * NEAR, dtype=jnp.int32)
    buckets = rel_bucket(distances)[:, None]
    onehot = (buckets == jnp.arange(BUCKETS, dtype=jnp.int32)).astype(F32)
    heads = HEADS // CORES
    rel_local = lax.dynamic_slice_in_dim(rel_bias.astype(F32), core * heads, heads, 1)
    by_dist = jnp.dot(onehot, rel_local - rel_local[BUCKETS - 1 :], precision=lax.Precision.HIGHEST)
    table = jnp.pad(by_dist.T.reshape(heads // 4, 4, 2 * NEAR), ((0, 0), (0, 4), (0, 0)))

    low_one, q, k, v = project(place, tokens, tokens_peer, gain_one, self_query, self_key, self_value)
    *diagonal, w_gate, w_up = self_diagonal(place, table, q, k, v, [(ffn_gate, 1, False), (ffn_up, 1, False)])
    past_own = follow(past_own, diagonal)
    past_peer = [swap(own, 0) for own in past_own]
    cot_peer = swap(follow(cotangent, diagonal[0]), 0)
    low_past, k_past, v_past, w_down = project_past(
        place, past_own, past_peer, gain_one, self_key, self_value, [(ffn_down, 0, False)]
    )
    att, lse_self, w_out, w_out_peer, w_query, w_cross, w_cross_peer = self_past(
        place, table, q, k_past, v_past, *diagonal,
        [(self_out, 0, False), (self_out, 0, True), (cross_query, 1, False), (cross_out, 0, False), (cross_out, 0, True)],
    )
    att_peer = swap(att, 0)
    mem_all, km, vm = project_memory(place, follow(mems, att), cross_key, cross_value)
    att_peer = follow(att_peer, km)
    mid, low_two, cq = mid_forward(
        place, tokens, tokens_peer, att, att_peer, gain_two, w_out, w_out_peer, w_query
    )
    own_doc = []
    if group_rows > SHORT:
        mem_doc = jnp.arange(mem_all.shape[0], dtype=jnp.int32) // (length // RATIO)
        own = (mem_doc == y_at * chip_rows // length).astype(F32)
        own_doc = [jnp.broadcast_to(own[:, None], (mem_all.shape[0], TILE))]
    crs, lse_cross = cross_forward(place, cq, km, vm, own_doc)
    crs_peer = swap(crs, 0)
    late, low_three, inner, d_gate, d_up, dz, cot_half = ffn(
        place, mid, crs, crs_peer, gain_three, cotangent, cot_peer, w_cross, w_cross_peer, w_gate, w_up, w_down
    )

    axes = {
        "y": tuple(range(y_bits)),
        "x": (y_bits,),
        "z": (y_bits + 1,),
        "f": tuple(range(y_bits + 2, bits)),
    }

    def order_of(letters):
        return sum((axes[letter] for letter in letters), ())

    dz_peer = swap(dz, 0)
    inner_peer = swap(inner, 0)
    gate = Flow("gate", [([((low_three,), d_gate)], model)], order_of("xyzf"))
    up = Flow("up", [([((low_three,), d_up)], model)], order_of("yzfx"))
    last = hop(place, swap, [gate, up], [], place, "gate_up")
    down = Flow("down", [([((inner, inner_peer), cot_half)], hidden_units)], order_of("zxyf"))
    spread = (down.spread(inner), down.spread(inner_peer))
    down = Flow("down", [([(spread, cot_half)], hidden_units)], order_of("zxyf"))
    last = hop(place, swap, [down], [], last, "down")
    ffn_flows = [gate, up, down]

    g_late, late_half, d_crs, d_gain_three = late_backward(
        place, follow(dz, last), dz_peer, late, cotangent, cot_peer, gain_three, w_cross
    )
    dcq, dkm, dvm, w_query_peer = cross_backward(
        place, cq, km, vm, own_doc, d_crs, crs, lse_cross, [(cross_query, 1, True)]
    )
    dcq_peer = swap(dcq, 0)
    crs_mem = Flow(
        "crs_mem",
        [([((crs, crs_peer), late_half)], model), ([((mem_all,), dkm)], model), ([((mem_all,), dvm)], model)],
        order_of("zxyf"),
    )
    last = hop(place, swap, [crs_mem], [], dcq, "crs_mem", cost=5)
    g_mid, mid_half, d_att, d_gain_two = mid_backward(
        place, dcq, follow(dcq_peer, last), mid, g_late, gain_two, w_query, w_query_peer, w_out
    )
    att_cq = Flow("att_cq", [([((att, att_peer), mid_half)], model), ([((low_two,), dcq)], model)], order_of("xyzf"))
    last = hop(place, swap, [att_cq], [], d_att, "att_cq")
    dq, dk, dv, d_past, d_near, d_total = self_backward(
        place, table, q, k, v, k_past, v_past, follow(d_att, last), att, lse_self
    )
    past_moved, rider = [], None
    if n_chips == 2:
        last, rider = hop(place, swap, [], ffn_flows, dq, "ffn_1", rider=(d_past, 1))
    else:
        past_moved = [
            lax.ppermute(d_past[s - 1], "grp", [(g, g - CORES * s) for g in range(CORES * s, groups)])
            for s in range(1, n_chips)
        ]
        last = hop(place, swap, [], ffn_flows, dq, "ffn_1")
    mem_parts = memory_backward(place, follow(dkm, last), dvm, cross_key, cross_value)
    layer_out = layer_output(place, follow(late, mem_parts), inner, inner_peer, ffn_down)
    mem_parts = lax.all_to_all(mem_parts, "grp", split_axis=0, concat_axis=0, tiled=True)
    query = Flow("query", [([((low_one,), dq)], model)], order_of("xyzf"))
    kv = Flow(
        "kv",
        [
            ([((low_one,), d)] + [((low_past[s],), (d_past, (s, which))) for s in range(more)], model)
            for which, d in ((0, dk), (1, dv))
        ],
        order_of("yzxf"),
    )
    attention = [att_cq, crs_mem, query, kv]
    last = hop(place, swap, [query, kv], [att_cq, crs_mem], layer_out, "attention_1", cost=4)

    results = {}
    names = {"ffn": ffn_flows, "attention": attention}

    def step(label, after):
        flows = names[label]
        if label in results:
            return after
        moving = [flow for flow in flows if flow.hops]
        if moving:
            return hop(place, swap, [], moving, after, f"{label}_{len(moving[0].hops)}", cost=4)
        results[label] = last_hop(place, swap, flows, after, label)
        return after

    for label in ("ffn", "attention", "ffn"):
        last = step(label, last)
    dz_own, dz_leave = first_backward(
        place, follow(dq, last), dk, dv, past_moved, rider, self_query, self_key, self_value
    )
    dz_got = swap(dz_leave, 0)
    last = step("attention", dz_leave)
    grad_tokens, d_gain_one = tokens_backward(place, follow(dz_own, last), dz_got, tokens, g_mid, gain_one)
    small = small_sums(place, d_gain_one, d_gain_two, d_gain_three, d_near, d_total, buckets, heads, devices)
    last = small
    small = lax.all_to_all(small, ("dp", "grp"), split_axis=0, concat_axis=0, tiled=True)
    while len(results) < 2:
        for label in ("attention", "ffn"):
            last = step(label, last)
    grad_memory, small = gather_sums(
        place, [follow(mem_parts, last).reshape(groups, -1, model), small], "gather_sums"
    )
    share = model // devices
    rel_share = BUCKETS * HEADS // devices
    got = {**results["ffn"], **results["attention"]}
    return (
        layer_out,
        grad_tokens,
        grad_memory,
        small[0, :share],
        got["query"][0],
        got["kv"][0],
        got["kv"][1],
        got["att_cq"][0],
        small[3, :rel_share],
        small[1, :share],
        got["att_cq"][1],
        got["crs_mem"][1],
        got["crs_mem"][2],
        got["crs_mem"][0],
        small[2, :share],
        got["gate"][0],
        got["up"][0],
        got["down"][0],
    )


def solution(mesh):
    rows = P(("dp", "grp"), None)
    flat = P(("dp", "grp"))
    in_specs = (rows, rows, rows, P("dp")) + (P(),) * 15
    out_specs = (rows,) * 3 + (flat,) + (rows,) * 4 + (flat,) * 2 + (rows,) * 4 + (flat,) + (rows,) * 3
    return jax.shard_map(shards, mesh=mesh, in_specs=in_specs, out_specs=out_specs, check_vma=False)
```

```python
import functools

import jax
import jax.numpy as jnp
from jax import lax
from jax.experimental import pallas as pl
from jax.experimental.pallas import tpu as pltpu
from jax.sharding import PartitionSpec as P

SHORT = 1024
RATIO = 4
BUCKETS = 32
HEADS = 16
EPSILON = 1e-06
THRESHOLDS = (19, 21, 24, 27, 31, 35, 40, 46, 52, 59, 67, 77, 87, 99, 113)
CORES = 2
BF16 = jnp.bfloat16
F32 = jnp.float32
NEGATIVE = -1e30
HEAD = 64
TILE = 256
NEAR = 128
LANES = 128
ROOM = 16 * 1024 * 1024


def dot(a, b):
    return jnp.dot(a, b, preferred_element_type=F32)


def dot_right(a, b):
    return lax.dot_general(a, b, (((1,), (1,)), ((), ())), preferred_element_type=F32)


def shaped(shape, dtype=BF16):
    return jax.ShapeDtypeStruct(tuple(shape), dtype)


def half_shape(array, axis):
    shape = list(array.shape)
    shape[axis] //= CORES
    return tuple(shape)


def whole_kernel(body, place, arrays, weights, outs, name, scratch=(), room=ROOM, cost=0, fetch=()):
    ready = [w for w in weights if not isinstance(w, tuple)]
    far = [w for w in weights if isinstance(w, tuple)]
    n_a, n_r, n_w, n_o, n_f = len(arrays), len(ready), len(far), len(outs), len(fetch)
    buffers = [pltpu.VMEM(half_shape(array, axis), array.dtype) for array, axis, _ in far]
    fetched = [shaped(half_shape(array, axis), array.dtype) for array, axis, _ in fetch]

    def kernel(place_ref, *refs):
        array_refs, refs = refs[:n_a], refs[n_a:]
        ready_refs, refs = refs[:n_r], refs[n_r:]
        far_refs, refs = refs[: n_w + n_f], refs[n_w + n_f :]
        out_refs, refs = refs[:n_o], refs[n_o:]
        fetch_refs, refs = refs[:n_f], refs[n_f:]
        buffer_refs, refs = refs[:n_w], refs[n_w:]
        copies = []
        for at, (ref, buffer, (_, axis, other)) in enumerate(
            zip(far_refs, (*buffer_refs, *fetch_refs), (*far, *fetch))
        ):
            size = buffer.shape[axis]
            start = pl.multiple_of((1 - place_ref[1] if other else place_ref[1]) * size, size)
            source = ref.at[pl.ds(start, size)] if axis == 0 else ref.at[:, pl.ds(start, size)]
            copies.append(pltpu.make_async_copy(source, buffer, refs[0].at[at]))
        for copy in copies:
            copy.start()
        arrived = set()
        places = []
        for w in weights:
            places.append((isinstance(w, tuple), sum(isinstance(x, tuple) == isinstance(w, tuple) for x in weights[: len(places)])))

        def weight(at):
            distant, spot = places[at]
            if not distant:
                return ready_refs[spot]
            if spot not in arrived:
                copies[spot].wait()
                arrived.add(spot)
            return buffer_refs[spot]

        body(place_ref, array_refs, weight, out_refs, refs[1:] if n_w + n_f else refs)
        for copy in copies[n_w:]:
            copy.wait()

    inside = pl.BlockSpec(memory_space=pltpu.VMEM)
    scratch = buffers + ([pltpu.SemaphoreType.DMA((n_w + n_f,))] if n_w + n_f else []) + list(scratch)
    return pl.pallas_call(
        kernel,
        in_specs=[pl.BlockSpec(memory_space=pltpu.SMEM)]
        + [inside] * (n_a + n_r)
        + [pl.BlockSpec(memory_space=pltpu.HBM)] * (n_w + n_f),
        out_specs=[inside] * (n_o + n_f),
        out_shape=list(outs) + fetched,
        scratch_shapes=scratch,
        compiler_params=pltpu.CompilerParams(vmem_limit_bytes=room),
        cost_estimate=pl.CostEstimate(
            flops=int(1.15e9 * cost), bytes_accessed=int(3.69e6 * cost), transcendentals=0
        ),
        name=name,
    )(
        place,
        *arrays,
        *ready,
        *[pltpu.with_memory_space_constraint(array, pltpu.HBM) for array, _, _ in (*far, *fetch)],
    )


def inverse_norm(hidden):
    return lax.rsqrt(jnp.mean(hidden * hidden, axis=-1, keepdims=True) + EPSILON)


def norm_low(hidden, inverse, gain):
    return (hidden * inverse * gain).astype(BF16)


def norm_back(hidden, inverse, gain, dz):
    scaled = gain * dz
    inner = jnp.mean(scaled * hidden, axis=-1, keepdims=True)
    return inverse * scaled - hidden * (inverse * inverse * inverse) * inner


def pick(core, value, axis, other=False):
    half = value.shape[axis] // CORES
    low, high = lax.slice_in_dim(value, 0, half, axis=axis), lax.slice_in_dim(value, half, 2 * half, axis=axis)
    return jnp.where(core == (1 if other else 0), low, high)


def in_place_order(core, own_ref, peer_ref):
    own, peer = own_ref[...].astype(F32), peer_ref[...].astype(F32)
    return jnp.concatenate([jnp.where(core == 0, own, peer), jnp.where(core == 0, peer, own)], axis=0)


def place_rows(half, at):
    zero = jnp.zeros_like(half)
    return jnp.concatenate([half, zero] if at == 0 else [zero, half], axis=0)


def place_lanes(pair, source, at):
    lane = lax.broadcasted_iota(jnp.int32, pair.shape, 1)
    if source != at:
        pair = jnp.concatenate([pair[:, HEAD:], pair[:, :HEAD]], axis=1)
    return jnp.where((lane < HEAD) == (at == 0), pair, jnp.zeros_like(pair))


def near_tiles(table_row):
    skewed = pltpu.roll(jnp.broadcast_to(table_row, (NEAR, 2 * NEAR)), 0, 1, stride=1, stride_axis=0)
    key_at = lax.broadcasted_iota(jnp.int32, (NEAR, NEAR), 0)
    row_at = lax.broadcasted_iota(jnp.int32, (NEAR, NEAR), 1)
    return (jnp.where(key_at <= row_at, skewed[:, :NEAR], NEGATIVE), skewed[:, NEAR:])


def heads_of(pair_turned, cols):
    return jnp.concatenate(
        [place_rows(pair_turned[h * HEAD : (h + 1) * HEAD, cols], h // 2) for h in range(4)], axis=1
    )


def add_corner(scores, tiles):
    rows = scores.shape[0]
    last = scores[rows - NEAR :]
    pieces = []
    for h in range(4):
        pieces += [last[:, h * TILE : h * TILE + NEAR] + tiles[h][1], last[:, h * TILE + NEAR : (h + 1) * TILE]]
    return jnp.concatenate([scores[: rows - NEAR], jnp.concatenate(pieces, axis=1)], axis=0)


def add_diagonal(scores, tiles):
    rows = scores.shape[0]
    first = scores[rows - TILE : rows - NEAR]
    second = scores[rows - NEAR :]
    upper, lower = [], []
    for h in range(4):
        left, right = slice(h * TILE, h * TILE + NEAR), slice(h * TILE + NEAR, (h + 1) * TILE)
        upper += [first[:, left] + tiles[h][0], first[:, right] + tiles[h][1]]
        lower += [jnp.full((NEAR, NEAR), NEGATIVE, F32), second[:, right] + tiles[h][0]]
    last = [jnp.concatenate(upper, axis=1), jnp.concatenate(lower, axis=1)]
    if rows > TILE:
        last = [add_corner(scores[: rows - TILE], tiles)] + last
    return jnp.concatenate(last, axis=0)


def by_distance(near):
    level = near[:8]
    for first in range(8, NEAR, 8):
        level = level + pltpu.roll(near[first : first + 8], 2 * NEAR - first, 1)
    row = lax.broadcasted_iota(jnp.int32, level.shape, 0)
    for bit in (1, 2, 4):
        level = jnp.where(row & bit > 0, pltpu.roll(level, 2 * NEAR - bit, 1), level)
    return jnp.sum(level, axis=0, keepdims=True)


def soft(scores):
    peak = jnp.max(scores, axis=0, keepdims=True)
    weights = jnp.exp(scores - peak)
    return peak, weights.astype(BF16), jnp.sum(weights, axis=0, keepdims=True)


def finish(o_ref, lse_ref, cols, peak, summed, acc):
    out = acc / summed
    lse = peak + jnp.log(summed)
    pieces = []
    for h in range(4):
        e = h // 2
        lanes = slice(h * TILE, (h + 1) * TILE)
        pieces.append(out[e * HEAD : (e + 1) * HEAD, lanes])
        lse_ref[0, h : h + 1, cols] = lse[:, lanes]
    o_ref[cols, :] = jnp.concatenate(pieces, axis=0).T.astype(BF16)


def self_diagonal_block(table_ref, q_ref, k_ref, v_ref, peak_ref, sum_ref, acc_ref):
    rows = q_ref.shape[0]
    v_turned = v_ref[...].T
    q_turned = q_ref[...].T
    tiles = [near_tiles(table_ref[0, h : h + 1, :]) for h in range(4)]
    spans = [slice(t * TILE, (t + 1) * TILE) for t in range(rows // TILE)]
    scores = [add_diagonal(dot(k_ref[: cols.stop], heads_of(q_turned, cols)), tiles) for cols in spans]
    parts = [soft(score) for score in scores]
    for t, cols in enumerate(spans):
        peak_ref[t], sum_ref[t] = parts[t][0], parts[t][2]
        acc_ref[t] = dot(v_turned[:, : cols.stop], parts[t][1])


def self_past_block(
    valid_ref, table_ref, q_ref, kp_ref, vp_ref, peak_in, sum_in, acc_in, o_ref, lse_ref, peak_ref, sum_ref, acc_ref,
    *, earlier
):
    rows = q_ref.shape[0]
    steps = rows // TILE
    q_turned = q_ref[...].T
    spans = [slice(t * TILE, (t + 1) * TILE) for t in range(steps)]
    for s in range(earlier):
        old = (peak_in, sum_in, acc_in) if s == 0 else (peak_ref, sum_ref, acc_ref)

        @pl.when(valid_ref[3 + s] > 0)
        def _(s=s, old=old):
            vp_turned = vp_ref[s].T
            scores = [dot(kp_ref[s], heads_of(q_turned, cols)) for cols in spans]
            if s == 0:
                scores[0] = add_corner(scores[0], [near_tiles(table_ref[0, h : h + 1, :]) for h in range(4)])
            for t, cols in enumerate(spans):
                peak = old[0][t]
                new_peak = jnp.maximum(peak, jnp.max(scores[t], axis=0, keepdims=True))
                rescale = jnp.exp(peak - new_peak)
                weights = jnp.exp(scores[t] - new_peak)
                summed = old[1][t] * rescale + jnp.sum(weights, axis=0, keepdims=True)
                acc = old[2][t] * rescale + dot(vp_turned, weights.astype(BF16))
                if s + 1 < earlier:
                    peak_ref[t], sum_ref[t], acc_ref[t] = new_peak, summed, acc
                else:
                    finish(o_ref, lse_ref, cols, new_peak, summed, acc)

        @pl.when(valid_ref[3 + s] == 0)
        def _(s=s, old=old):
            for t, cols in enumerate(spans):
                if s + 1 < earlier:
                    peak_ref[t], sum_ref[t], acc_ref[t] = old[0][t], old[1][t], old[2][t]
                else:
                    finish(o_ref, lse_ref, cols, old[0][t], old[1][t], old[2][t])


def placed_heads(block, cols):
    rows = []
    for h in range(4):
        pair = block[cols, (h // 2) * 2 * HEAD : (h // 2 + 1) * 2 * HEAD]
        rows.append(place_lanes(pair, h % 2, h // 2))
    return jnp.concatenate(rows, axis=0)


def row_of_heads(ref, cols):
    return jnp.concatenate([ref[0, h : h + 1, cols] for h in range(4)], axis=1)


def deltas(product, cols):
    return jnp.concatenate(
        [jnp.sum(product[h * HEAD : (h + 1) * HEAD, cols], axis=0, keepdims=True) for h in range(4)], axis=1
    )


def back_scores(scores, lse, d_prob, delta):
    prob = jnp.exp(scores - lse)
    d_score = prob * (d_prob - delta)
    return prob.astype(BF16), d_score.astype(BF16)


def query_rows(d_query):
    pieces = [
        d_query[(h // 2) * HEAD : (h // 2 + 1) * HEAD, h * TILE : (h + 1) * TILE] for h in range(4)
    ]
    return jnp.concatenate(pieces, axis=0).T.astype(BF16)


def self_backward_block(
    valid_ref, table_ref, q_ref, k_ref, v_ref, kp_ref, vp_ref, do_ref, o_ref, lse_ref,
    dq_ref, dk_ref, dv_ref, past_ref, db_ref, total_ref,
    near_sum, dq_sum, *, earlier,
):
    rows = q_ref.shape[0]
    steps = rows // TILE
    spans = [slice(t * TILE, (t + 1) * TILE) for t in range(steps)]
    k_turned = k_ref[...].T
    q_turned = q_ref[...].T
    do_turned = do_ref[...].T
    product = (do_ref[...].astype(F32) * o_ref[...].astype(F32)).T
    tiles = [near_tiles(table_ref[0, h : h + 1, :]) for h in range(4)]
    queries = [heads_of(q_turned, cols) for cols in spans]
    outs = [heads_of(do_turned, cols) for cols in spans]
    q_placed = [placed_heads(q_ref, cols) for cols in spans]
    do_placed = [placed_heads(do_ref, cols) for cols in spans]
    lses = [row_of_heads(lse_ref, cols) for cols in spans]
    delta = [deltas(product, cols) for cols in spans]

    for t, cols in enumerate(spans):
        seen = cols.stop
        scores = add_diagonal(dot(k_ref[:seen], queries[t]), tiles)
        prob, d_score = back_scores(scores, lses[t], dot(v_ref[:seen], outs[t]), delta[t])
        d_value = dot(prob, do_placed[t])
        d_key = dot(d_score, q_placed[t])
        if t == 0:
            dv_whole, dk_whole = d_value, d_key
        else:
            more = seen - dv_whole.shape[0]
            dv_whole = jnp.concatenate([dv_whole + d_value[: seen - more], d_value[seen - more :]], axis=0)
            dk_whole = jnp.concatenate([dk_whole + d_key[: seen - more], d_key[seen - more :]], axis=0)
        dq_sum[t] = dot(k_turned[:, :seen], d_score)
        d_wide = d_score.astype(F32)
        total = jnp.sum(d_wide, axis=0, keepdims=True)
        base = seen - TILE
        for h in range(4):
            left, right = slice(h * TILE, h * TILE + NEAR), slice(h * TILE + NEAR, (h + 1) * TILE)
            zero_part = d_wide[base : base + NEAR, left] + d_wide[base + NEAR :, right]
            one_part = d_wide[base : base + NEAR, right]
            if t > 0:
                one_part = one_part + d_wide[base - NEAR : base, left]
            both = jnp.concatenate([zero_part, one_part], axis=1)
            part = total[:, h * TILE : (h + 1) * TILE]
            if t == 0:
                near_sum[h] = both
                total_ref[0, h : h + 1, :] = part
            else:
                near_sum[h] += both
                total_ref[0, h : h + 1, :] += part
    dk_ref[...] = dk_whole.astype(BF16)
    dv_ref[...] = dv_whole.astype(BF16)

    for s in range(earlier):

        @pl.when(valid_ref[3 + s] > 0)
        def _(s=s):
            kp_turned = kp_ref[s].T
            for t in range(steps):
                scores = dot(kp_ref[s], queries[t])
                if s == 0 and t == 0:
                    scores = add_corner(scores, tiles)
                prob, d_score = back_scores(scores, lses[t], dot(vp_ref[s], outs[t]), delta[t])
                d_value = dot(prob, do_placed[t])
                d_key = dot(d_score, q_placed[t])
                dv_whole = d_value if t == 0 else dv_whole + d_value
                dk_whole = d_key if t == 0 else dk_whole + d_key
                dq_sum[t] += dot(kp_turned, d_score)
                d_wide = d_score.astype(F32)
                total = jnp.sum(d_wide, axis=0, keepdims=True)
                for h in range(4):
                    total_ref[0, h : h + 1, :] += total[:, h * TILE : (h + 1) * TILE]
                    if s == 0 and t == 0:
                        near_sum[h, :, NEAR:] += d_wide[rows - NEAR :, h * TILE : h * TILE + NEAR]
            past_ref[s, 0] = dk_whole.astype(BF16)
            past_ref[s, 1] = dv_whole.astype(BF16)

        @pl.when(valid_ref[3 + s] == 0)
        def _(s=s):
            past_ref[s] = jnp.zeros_like(past_ref[s])

    for t, cols in enumerate(spans):
        dq_ref[cols, :] = query_rows(dq_sum[t])
    for h in range(4):
        db_ref[0, h : h + 1, :] = by_distance(near_sum[h])
    db_ref[0, 4:, :] = jnp.zeros((4, 2 * NEAR), F32)
    total_ref[0, 4:, :] = jnp.zeros((4, 2 * NEAR), F32)


def cross_forward_block(q_ref, k_ref, v_ref, own_ref, o_ref, lse_ref, *, masked):
    rows = q_ref.shape[0]
    v_turned = v_ref[...].T
    q_turned = q_ref[...].T
    spans = [slice(t * TILE, (t + 1) * TILE) for t in range(rows // TILE)]
    scores = [dot(k_ref[...], heads_of(q_turned, cols)) for cols in spans]
    if masked:
        blocked = jnp.where(own_ref[...] > 0, 0.0, NEGATIVE)
        blocked = jnp.concatenate([blocked] * 4, axis=1)
        scores = [score + blocked for score in scores]
    for t, cols in enumerate(spans):
        peak, weights, summed = soft(scores[t])
        finish(o_ref, lse_ref, cols, peak, summed, dot(v_turned, weights))


def cross_backward_block(
    q_ref, k_ref, v_ref, own_ref, do_ref, o_ref, lse_ref, dq_ref, dk_ref, dv_ref, *, masked
):
    rows = q_ref.shape[0]
    k_turned = k_ref[...].T
    q_turned = q_ref[...].T
    do_turned = do_ref[...].T
    product = (do_ref[...].astype(F32) * o_ref[...].astype(F32)).T
    spans = [slice(t * TILE, (t + 1) * TILE) for t in range(rows // TILE)]
    dk_whole, dv_whole = 0.0, 0.0
    for t, cols in enumerate(spans):
        scores = dot(k_ref[...], heads_of(q_turned, cols))
        if masked:
            blocked = jnp.where(own_ref[...] > 0, 0.0, NEGATIVE)
            scores = scores + jnp.concatenate([blocked] * 4, axis=1)
        d_prob = dot(v_ref[...], heads_of(do_turned, cols))
        prob, d_score = back_scores(scores, row_of_heads(lse_ref, cols), d_prob, deltas(product, cols))
        dv_whole = dv_whole + dot(prob, placed_heads(do_ref, cols))
        dk_whole = dk_whole + dot(d_score, placed_heads(q_ref, cols))
        dq_ref[cols, :] = query_rows(dot(k_turned, d_score))
    dk_ref[...] = dk_whole.astype(BF16)
    dv_ref[...] = dv_whole.astype(BF16)


def wide_view(ref, p):
    return ref.at[:, pl.ds(p * 4 * HEAD, 4 * HEAD)]


def slim_view(ref, p):
    return ref.at[:, pl.ds(p * 2 * HEAD, 2 * HEAD)]


def past_view(ref, p):
    return ref.at[:, :, pl.ds(p * 2 * HEAD, 2 * HEAD)]


def page_view(ref, p):
    return ref.at[pl.ds(p, 1)]


def self_diagonal(place, table, q, k, v, fetch):
    rows, blocks = q.shape[0], k.shape[1] // (2 * HEAD)
    steps = rows // TILE

    def body(place_ref, arrays, weight, outs, scratch):
        table_ref, q_ref, k_ref, v_ref = arrays
        for p in range(blocks):
            self_diagonal_block(
                page_view(table_ref, p), wide_view(q_ref, p), slim_view(k_ref, p), slim_view(v_ref, p),
                *[ref.at[p] for ref in outs],
            )

    state = [(blocks, steps, 1, 4 * TILE), (blocks, steps, 1, 4 * TILE), (blocks, steps, 2 * HEAD, 4 * TILE)]
    return whole_kernel(body, place, [table, q, k, v], [], [shaped(shape, F32) for shape in state], "self_diagonal", fetch=fetch)


def self_past(place, table, q, kp, vp, peak, summed, acc, fetch):
    rows, blocks, earlier = q.shape[0], kp.shape[2] // (2 * HEAD), kp.shape[0]

    def body(place_ref, arrays, weight, outs, scratch):
        table_ref, q_ref, kp_ref, vp_ref, peak_ref, sum_ref, acc_ref = arrays
        for p in range(blocks):
            self_past_block(
                place_ref, page_view(table_ref, p), wide_view(q_ref, p), past_view(kp_ref, p), past_view(vp_ref, p),
                peak_ref.at[p], sum_ref.at[p], acc_ref.at[p], wide_view(outs[0], p), page_view(outs[1], p),
                *([ref.at[p] for ref in scratch] if earlier > 1 else [None] * 3), earlier=earlier,
            )

    return whole_kernel(
        body,
        place,
        [table, q, kp, vp, peak, summed, acc],
        [],
        [shaped(q.shape), shaped((blocks, 8, rows), F32)],
        "self_past",
        [pltpu.VMEM(a.shape, F32) for a in (peak, summed, acc)] if earlier > 1 else [],
        fetch=fetch,
    )


def self_backward(place, table, q, k, v, kp, vp, do, o, lse):
    rows, blocks, earlier = q.shape[0], k.shape[1] // (2 * HEAD), kp.shape[0]
    steps = rows // TILE

    def body(place_ref, arrays, weight, outs, scratch):
        table_ref, q_ref, k_ref, v_ref, kp_ref, vp_ref, do_ref, o_ref, lse_ref = arrays
        dq_ref, dk_ref, dv_ref, past_ref, db_ref, total_ref = outs
        for p in range(blocks):
            self_backward_block(
                place_ref, page_view(table_ref, p), wide_view(q_ref, p), slim_view(k_ref, p), slim_view(v_ref, p),
                past_view(kp_ref, p), past_view(vp_ref, p), wide_view(do_ref, p), wide_view(o_ref, p),
                page_view(lse_ref, p), wide_view(dq_ref, p), slim_view(dk_ref, p), slim_view(dv_ref, p),
                past_ref.at[:, :, :, pl.ds(p * 2 * HEAD, 2 * HEAD)], page_view(db_ref, p), page_view(total_ref, p),
                *[ref.at[p] for ref in scratch], earlier=earlier,
            )

    return whole_kernel(
        body,
        place,
        [table, q, k, v, kp, vp, do, o, lse],
        [],
        [
            shaped(q.shape),
            shaped(k.shape),
            shaped(k.shape),
            shaped((earlier, 2) + k.shape),
            shaped(table.shape, F32),
            shaped(table.shape, F32),
        ],
        "self_backward",
        [pltpu.VMEM((blocks, 4, NEAR, 2 * NEAR), F32), pltpu.VMEM((blocks, steps, 2 * HEAD, 4 * TILE), F32)],
    )


def cross_forward(place, q, k, v, own):
    rows, blocks = q.shape[0], k.shape[1] // (2 * HEAD)

    def body(place_ref, arrays, weight, outs, scratch):
        q_ref, k_ref, v_ref = arrays[:3]
        for p in range(blocks):
            cross_forward_block(
                wide_view(q_ref, p), slim_view(k_ref, p), slim_view(v_ref, p), arrays[-1], wide_view(outs[0], p),
                page_view(outs[1], p), masked=len(own) > 0,
            )

    outs = [shaped(q.shape), shaped((blocks, 8, rows), F32)]
    return whole_kernel(body, place, [q, k, v] + own, [], outs, "cross_forward")


def cross_backward(place, q, k, v, own, do, o, lse, fetch):
    blocks = k.shape[1] // (2 * HEAD)

    def body(place_ref, arrays, weight, outs, scratch):
        q_ref, k_ref, v_ref, do_ref, o_ref, lse_ref = arrays[:6]
        for p in range(blocks):
            cross_backward_block(
                wide_view(q_ref, p), slim_view(k_ref, p), slim_view(v_ref, p), arrays[-1], wide_view(do_ref, p),
                wide_view(o_ref, p), page_view(lse_ref, p), wide_view(outs[0], p), slim_view(outs[1], p),
                slim_view(outs[2], p), masked=len(own) > 0,
            )

    outs = [shaped(q.shape), shaped(k.shape), shaped(k.shape)]
    return whole_kernel(body, place, [q, k, v, do, o, lse] + own, [], outs, "cross_backward", fetch=fetch)


def project(place, own, peer, gain, wq, wk, wv):
    rows, model = own.shape
    wide, slim = wq.shape[1] // CORES, wk.shape[1] // CORES

    def body(place_ref, arrays, weight, outs, scratch):
        hidden = in_place_order(place_ref[1], arrays[0], arrays[1])
        low = norm_low(hidden, inverse_norm(hidden), arrays[2][...].astype(F32))
        outs[0][...] = low
        for at in range(3):
            outs[1 + at][...] = dot(low, weight(at)[...]).astype(BF16)

    return whole_kernel(
        body,
        place,
        [own, peer, gain],
        [(wq, 1, False), (wk, 1, False), (wv, 1, False)],
        [shaped((CORES * rows, n)) for n in (model, wide, slim, slim)],
        "project",
    )


def project_past(place, owns, peers, gain, wk, wv, fetch):
    rows, model = owns[0].shape
    earlier = len(owns)
    slim = wk.shape[1] // CORES

    def body(place_ref, arrays, weight, outs, scratch):
        own_refs, peer_refs = arrays[:earlier], arrays[earlier : 2 * earlier]
        gain_value = arrays[-1][...].astype(F32)
        for s in range(earlier):
            hidden = in_place_order(place_ref[1], own_refs[s], peer_refs[s])
            low = norm_low(hidden, inverse_norm(hidden), gain_value)
            outs[s][...] = low
            outs[earlier][s] = dot(low, weight(0)[...]).astype(BF16)
            outs[earlier + 1][s] = dot(low, weight(1)[...]).astype(BF16)

    made = whole_kernel(
        body,
        place,
        owns + peers + [gain],
        [(wk, 1, False), (wv, 1, False)],
        [shaped((CORES * rows, model))] * earlier + [shaped((earlier, CORES * rows, slim))] * 2,
        "project_past",
        fetch=fetch,
    )
    return made[:earlier], *made[earlier:]


def project_memory(place, mems, wk, wv):
    groups = len(mems)
    rows, model = mems[0].shape
    slim = wk.shape[1] // CORES

    def body(place_ref, arrays, weight, outs, scratch):
        for at, piece_ref in enumerate(arrays):
            block = jnp.bitwise_xor(place_ref[2], jnp.int32(at))
            outs[0][pl.ds(pl.multiple_of(block * rows, rows), rows)] = piece_ref[...]
        mem = outs[0][...]
        outs[1][...] = dot(mem, weight(0)[...]).astype(BF16)
        outs[2][...] = dot(mem, weight(1)[...]).astype(BF16)

    return whole_kernel(
        body,
        place,
        mems,
        [(wk, 1, False), (wv, 1, False)],
        [shaped((groups * rows, n)) for n in (model, slim, slim)],
        "project_memory",
        cost=8,
    )


def mid_forward(place, own, peer, att, att_peer, gain, wo, wo_peer, wq):
    rows, model = own.shape

    def body(place_ref, arrays, weight, outs, scratch):
        own_ref, peer_ref, att_ref, att_peer_ref, gain_ref = arrays
        hidden = in_place_order(place_ref[1], own_ref, peer_ref)
        hidden = hidden + dot(att_ref[...], weight(0)[...]) + dot(att_peer_ref[...], weight(1)[...])
        outs[0][...] = hidden.astype(BF16)
        low = norm_low(hidden, inverse_norm(hidden), gain_ref[...].astype(F32))
        outs[1][...] = low
        outs[2][...] = dot(low, weight(2)[...]).astype(BF16)

    return whole_kernel(
        body,
        place,
        [own, peer, att, att_peer, gain],
        [wo, wo_peer, wq],
        [shaped((CORES * rows, model))] * 2 + [shaped((CORES * rows, wq.shape[1]))],
        "mid_forward",
    )


def ffn(place, mid, crs, crs_peer, gain, cot, cot_peer, wc, wc_peer, wg, wu, wd):
    rows, model = mid.shape
    hidden_half = wd.shape[0]
    steps = [256] * (hidden_half // 256) + [hidden_half % 256] * (hidden_half % 256 > 0)
    scale = 0.7978845608028654

    def body(place_ref, arrays, weight, outs, scratch):
        mid_ref, crs_ref, crs_peer_ref, gain_ref, cot_ref, cot_peer_ref = arrays
        late_ref, low_ref, inner_ref, dg_ref, du_ref, dz_ref, cot_half_ref = outs
        cot_value = in_place_order(place_ref[1], cot_ref, cot_peer_ref).astype(BF16)
        cot_half_ref[...] = pick(place_ref[1], cot_value, 1)
        hidden = mid_ref[...].astype(F32) + dot(crs_ref[...], weight(0)[...]) + dot(crs_peer_ref[...], weight(1)[...])
        late_ref[...] = hidden.astype(BF16)
        low = norm_low(hidden, inverse_norm(hidden), gain_ref[...].astype(F32))
        low_ref[...] = low
        start = 0
        for width in steps:
            cols = slice(start, start + width)
            start += width
            gate = dot(low, weight(2)[:, cols])
            up = dot(low, weight(3)[:, cols])
            d_inner = dot_right(cot_value, weight(4)[cols]).astype(BF16).astype(F32)
            square = gate * gate
            bent = jnp.tanh(gate * (scale + (scale * 0.044715) * square))
            whole = 0.5 + 0.5 * bent
            slope = whole + (0.5 * gate) * (1.0 - bent * bent) * (scale + (3 * scale * 0.044715) * square)
            curve = gate * whole
            inner_ref[:, cols] = (curve * up).astype(BF16)
            dg_ref[:, cols] = (d_inner * up * slope).astype(BF16)
            du_ref[:, cols] = (d_inner * curve).astype(BF16)
        dz_ref[...] = (dot_right(dg_ref[...], weight(2)[...]) + dot_right(du_ref[...], weight(3)[...])).astype(BF16)

    return whole_kernel(
        body,
        place,
        [mid, crs, crs_peer, gain, cot, cot_peer],
        [wc, wc_peer, wg, wu, wd],
        [shaped((rows, model))] * 2
        + [shaped((rows, hidden_half))] * 3
        + [shaped((rows, model)), shaped((rows, model // CORES))],
        "ffn",
        room=16 * 1024 * 1024,
    )


def late_backward(place, dz, dz_peer, late, cot, cot_peer, gain, wc):
    rows, model = late.shape

    def body(place_ref, arrays, weight, outs, scratch):
        dz_ref, dz_peer_ref, late_ref, cot_ref, cot_peer_ref, gain_ref = arrays
        dz_value = dz_ref[...].astype(F32) + dz_peer_ref[...].astype(F32)
        hidden = late_ref[...].astype(F32)
        inverse = inverse_norm(hidden)
        outs[3][...] = jnp.sum(dz_value * hidden * inverse, axis=0, keepdims=True)
        grad = in_place_order(place_ref[1], cot_ref, cot_peer_ref)
        grad = grad + norm_back(hidden, inverse, gain_ref[...].astype(F32), dz_value)
        low = grad.astype(BF16)
        outs[0][...] = low
        outs[1][...] = pick(place_ref[1], low, 1)
        outs[2][...] = dot_right(low, weight(0)[...]).astype(BF16)

    return whole_kernel(
        body,
        place,
        [dz, dz_peer, late, cot, cot_peer, gain],
        [wc],
        [
            shaped((rows, model)),
            shaped((rows, model // CORES)),
            shaped((rows, wc.shape[0])),
            shaped((1, model), F32),
        ],
        "late_backward",
    )


def mid_backward(place, dq, dq_peer, mid, g_late, gain, wq, wq_peer, wo):
    rows, model = mid.shape

    def body(place_ref, arrays, weight, outs, scratch):
        dq_ref, dq_peer_ref, mid_ref, g_ref, gain_ref = arrays
        dz = dot_right(dq_ref[...], weight(0)[...]) + dot_right(dq_peer_ref[...], weight(1)[...])
        hidden = mid_ref[...].astype(F32)
        inverse = inverse_norm(hidden)
        outs[3][...] = jnp.sum(dz * hidden * inverse, axis=0, keepdims=True)
        grad = g_ref[...].astype(F32) + norm_back(hidden, inverse, gain_ref[...].astype(F32), dz)
        low = grad.astype(BF16)
        outs[0][...] = pick(place_ref[1], low, 0)
        outs[1][...] = pick(place_ref[1], low, 1)
        outs[2][...] = dot_right(low, weight(2)[...]).astype(BF16)

    return whole_kernel(
        body,
        place,
        [dq, dq_peer, mid, g_late, gain],
        [wq, wq_peer, wo],
        [
            shaped((rows // CORES, model)),
            shaped((rows, model // CORES)),
            shaped((rows, wo.shape[0])),
            shaped((1, model), F32),
        ],
        "mid_backward",
    )


def first_backward(place, dq, dk, dv, past, rider, wq, wk, wv):
    rows, model = dq.shape[0], wq.shape[0]
    slim = dk.shape[1]

    def body(place_ref, arrays, weight, outs, scratch):
        dq_ref, dk_ref, dv_ref = arrays[:3]
        dk_value, dv_value = dk_ref[...].astype(F32), dv_ref[...].astype(F32)
        if rider is not None:
            blocks = [
                arrays[3][rider[1] + at * rows : rider[1] + (at + 1) * rows].astype(F32)
                for at in range(2 * slim // LANES)
            ]
            dk_value = dk_value + jnp.concatenate(blocks[: slim // LANES], axis=1)
            dv_value = dv_value + jnp.concatenate(blocks[slim // LANES :], axis=1)
        else:
            for ref in arrays[3:]:
                dk_value = dk_value + ref[0].astype(F32)
                dv_value = dv_value + ref[1].astype(F32)
        dz = dot_right(dq_ref[...], weight(0)[...])
        dz = dz + dot_right(dk_value.astype(BF16), weight(1)[...]) + dot_right(dv_value.astype(BF16), weight(2)[...])
        outs[0][...] = pick(place_ref[1], dz, 0)
        outs[1][...] = pick(place_ref[1], dz, 0, True).astype(BF16)

    return whole_kernel(
        body,
        place,
        [dq, dk, dv] + (past if rider is None else [rider[0]]),
        [(wq, 1, False), (wk, 1, False), (wv, 1, False)],
        [shaped((rows // CORES, model), F32), shaped((rows // CORES, model))],
        "first_backward",
    )


def tokens_backward(place, dz, dz_got, tokens, g_mid, gain):
    def body(place_ref, arrays, weight, outs, scratch):
        dz_ref, dz_got_ref, tokens_ref, g_ref, gain_ref = arrays
        dz_value = dz_ref[...] + dz_got_ref[...].astype(F32)
        hidden = tokens_ref[...].astype(F32)
        inverse = inverse_norm(hidden)
        outs[1][...] = jnp.sum(dz_value * hidden * inverse, axis=0, keepdims=True)
        grad = g_ref[...].astype(F32) + norm_back(hidden, inverse, gain_ref[...].astype(F32), dz_value)
        outs[0][...] = grad.astype(BF16)

    outs = [shaped(tokens.shape), shaped((1, tokens.shape[1]), F32)]
    return whole_kernel(body, place, [dz, dz_got, tokens, g_mid, gain], [], outs, "tokens_backward")


def layer_output(place, late, inner, inner_peer, wd):
    rows, model = late.shape

    def body(place_ref, arrays, weight, outs, scratch):
        own, inner_own, inner_other = (pick(place_ref[1], ref[...], 0) for ref in arrays)
        total = own.astype(F32) + dot(inner_own, weight(0)[...]) + dot(inner_other, weight(1)[...])
        outs[0][...] = total.astype(BF16)

    return whole_kernel(
        body,
        place,
        [late, inner, inner_peer],
        [(wd, 0, False), (wd, 0, True)],
        [shaped((rows // CORES, model))],
        "layer_output",
        cost=10,
    )[0]


def memory_backward(place, dk, dv, wk, wv):
    def body(place_ref, arrays, weight, outs, scratch):
        grad = dot_right(arrays[0][...], weight(0)[...]) + dot_right(arrays[1][...], weight(1)[...])
        outs[0][...] = grad.astype(BF16)

    weights = [(wk, 1, False), (wv, 1, False)]
    return whole_kernel(body, place, [dk, dv], weights, [shaped((dk.shape[0], wk.shape[0]))], "memory_backward")[0]


def small_sums(place, one, two, three, near, total, buckets, heads, devices):
    def body(place_ref, arrays, weight, outs, scratch):
        one_ref, two_ref, three_ref, near_ref, total_ref, bucket_ref = arrays
        core = place_ref[1]
        first = core == 0
        gains = [one_ref[...], jnp.where(first, two_ref[...], 0.0), jnp.where(first, three_ref[...], 0.0)]
        near = jnp.concatenate([near_ref[p, :4] for p in range(heads // 4)], axis=0)
        total = jnp.concatenate([total_ref[p, :4] for p in range(heads // 4)], axis=0)
        far = jnp.sum(total, axis=1, keepdims=True) - jnp.sum(near, axis=1, keepdims=True)
        last = lax.broadcasted_iota(jnp.int32, near.shape, 1) == near.shape[1] - 1
        near = near + jnp.where(last, far, 0.0)
        entries = BUCKETS * HEADS
        entry = lax.broadcasted_iota(jnp.int32, (near.shape[1], entries), 1)
        same = (lax.shift_right_logical(entry, jnp.int32(HEADS.bit_length() - 1)) == bucket_ref[...]).astype(F32)
        sums = jnp.dot(near, same, precision=lax.Precision.HIGHEST, preferred_element_type=F32)
        head = lax.broadcasted_iota(jnp.int32, sums.shape, 0) + core * heads
        of_entry = jnp.bitwise_and(lax.broadcasted_iota(jnp.int32, sums.shape, 1), jnp.int32(HEADS - 1))
        vectors = gains + [jnp.sum(jnp.where(head == of_entry, sums, 0.0), axis=0, keepdims=True)]
        for block in range(devices):
            rows = []
            for vector in vectors:
                size = vector.shape[1] // devices
                row = vector[:, block * size : (block + 1) * size]
                rows.append(jnp.concatenate([row, jnp.zeros((1, LANES - size), F32)], axis=1))
            outs[0][block] = jnp.concatenate(rows + [jnp.zeros((4, LANES), F32)], axis=0)

    return whole_kernel(
        body, place, [one, two, three, near, total, buckets], [], [shaped((devices, 8, LANES), F32)], "small_sums"
    )[0]


def gather_sums(place, parts, name):
    def body(place_ref, arrays, weight, outs, scratch):
        for array, out in zip(arrays, outs):
            total = array[0].astype(F32)
            for at in range(1, array.shape[0]):
                total = total + array[at].astype(F32)
            out[...] = total.astype(out.dtype)

    return whole_kernel(body, place, parts, [], [shaped(a.shape[1:], a.dtype) for a in parts], name)


def up_to(value, multiple):
    return (value + multiple - 1) // multiple * multiple


def array_of(y):
    return y[0] if isinstance(y, tuple) else y


class Flow:
    def __init__(self, name, pieces, order):
        self.name, self.pieces, self.order = name, pieces, order
        self.hops = [bit + 1 for bit in order]
        self.chips = 1 << len(order)
        self.layout = []
        start = 0
        for terms, rows in pieces:
            half = rows // self.chips // CORES
            padded = up_to(half, 8)
            width = array_of(terms[0][1]).shape[-1]
            self.layout.append((start, half, padded, width))
            start += CORES * padded * (width // LANES)
        self.rows = start
        self.keep = self.got = None

    def spread(self, x):
        half, padded = self.layout[0][1:3]
        if half == padded:
            return x
        chunks = x.reshape(x.shape[0], -1, half)
        return jnp.pad(chunks, ((0, 0), (0, 0), (0, padded - half))).reshape(x.shape[0], -1)


def chip_of(spot, order):
    number = 0
    for at, bit in enumerate(order):
        number |= (spot >> (len(order) - 1 - at) & 1) << bit
    return number


def sum_flow(flow, refs_of, place_ref, turned, free, send_ref, base, keep_ref):
    chip, core = place_ref[0], place_ref[1]
    half = flow.chips // 2
    for (terms, _), (start, _, padded, width) in zip(flow.pieces, flow.layout):
        chunk = CORES * padded
        lefts = []
        for xs, y in terms:
            key = (tuple(id(x) for x in xs), flow.order)
            if key not in turned:
                straight_ref, turned[key] = free.pop(0), free.pop(0)
                if len(xs) == 1:
                    straight_ref[...] = refs_of[id(xs[0])][...].T
                else:
                    size = straight_ref.shape[0] // CORES
                    for part, x in enumerate(xs):
                        at = (core if part == 0 else 1 - core) * size
                        straight_ref[pl.ds(pl.multiple_of(at, 16), size)] = refs_of[id(x)][...].T
                for spot in range(flow.chips):
                    at = jnp.bitwise_xor(jnp.int32(chip_of(spot, flow.order)), chip) * chunk
                    turned[key][spot * chunk : (spot + 1) * chunk] = straight_ref[pl.ds(pl.multiple_of(at, 16), chunk)]
            lefts.append(turned[key])
        count = max(1, min(flow.chips, 512 // chunk))
        while flow.chips % count:
            count -= 1
        for first in range(0, flow.chips, count):
            tile = None
            for left, (_, y) in zip(lefts, terms):
                y_ref = refs_of[id(array_of(y))]
                y_value = y_ref[y[1]] if isinstance(y, tuple) else y_ref[...]
                term = dot(left[first * chunk : (first + count) * chunk], y_value)
                tile = term if tile is None else tile + term
            tile = tile.astype(BF16)
            for inner in range(count):
                spot = first + inner
                for block in range(width // LANES):
                    value = tile[inner * chunk : (inner + 1) * chunk, block * LANES : (block + 1) * LANES]
                    at = start + block * chunk
                    if spot < half:
                        keep_ref[spot, at : at + chunk] = value
                    else:
                        at += base + (spot - half) * flow.rows
                        send_ref[at : at + chunk] = value


def add_flow(flow, old_ref, got_ref, got_at, send_ref, base, keep_ref):
    half = old_ref.shape[0] // 2
    for spot in range(2 * half):
        at = got_at + spot * flow.rows
        total = (old_ref[spot].astype(F32) + got_ref[at : at + flow.rows].astype(F32)).astype(BF16)
        if spot < half:
            keep_ref[spot] = total
        else:
            send_ref[base + (spot - half) * flow.rows : base + (spot - half + 1) * flow.rows] = total


def hop(place, swap, sums, adds, after, name, cost=0, rider=None):
    arrays, seen = [], {}

    def take(array):
        if id(array) not in seen:
            seen[id(array)] = len(arrays)
            arrays.append(array)

    for flow in sums:
        for terms, _ in flow.pieces:
            for xs, y in terms:
                for array in (*xs, array_of(y)):
                    take(array)
    for flow in adds:
        take(flow.keep)
        take(flow.got[0])
    bits, sends, keeps = {}, {}, {}
    for flow in sums + adds:
        half = (flow.chips if flow in sums else flow.keep.shape[0]) // 2
        bit = flow.hops[0]
        base = bits.setdefault(bit, 0)
        sends[flow.name] = (bit, base)
        bits[bit] = base + half * flow.rows
        keeps[flow.name] = shaped((half, flow.rows, LANES))
    if rider is not None:
        rider_array, rider_bit = rider
        take(rider_array)
        rider_at = bits.setdefault(rider_bit, 0)
        bits[rider_bit] = rider_at + rider_array.size // LANES
    order = list(bits)
    outs = [shaped((bits[bit], LANES)) for bit in order] + list(keeps.values())

    def body(place_ref, refs, weight, out_refs, scratch):
        refs_of = {key: refs[at] for key, at in seen.items()}
        turned, free = {}, list(scratch)
        for at, flow in enumerate(sums + adds):
            bit, base = sends[flow.name]
            send_ref, keep_ref = out_refs[order.index(bit)], out_refs[len(order) + at]
            if flow in sums:
                sum_flow(flow, refs_of, place_ref, turned, free, send_ref, base, keep_ref)
            else:
                add_flow(
                    flow, refs_of[id(flow.keep)], refs_of[id(flow.got[0])], flow.got[1], send_ref, base, keep_ref
                )
        if rider is not None:
            send_ref, at = out_refs[order.index(rider_bit)], rider_at
            _, pages, rows, width = rider_array.shape
            for page in range(pages):
                for block in range(width // LANES):
                    send_ref[at : at + rows] = refs_of[id(rider_array)][0, page, :, block * LANES : (block + 1) * LANES]
                    at += rows

    needed = {}
    for flow in sums:
        for terms, _ in flow.pieces:
            for xs, _ in terms:
                shape = (sum(x.shape[1] for x in xs), xs[0].shape[0])
                needed[(tuple(id(x) for x in xs), flow.order)] = [pltpu.VMEM(shape, BF16)] * 2
    scratch = sum(needed.values(), [])
    made = whole_kernel(body, place, follow(arrays, after), [], outs, name, scratch, cost=cost)
    moved = [swap(array, bit) for array, bit in zip(made, order)]
    for at, flow in enumerate(sums + adds):
        bit, base = sends[flow.name]
        flow.keep, flow.got, flow.hops = made[len(order) + at], (moved[order.index(bit)], base), flow.hops[1:]
    if rider is not None:
        return list(made), (moved[order.index(rider_bit)], rider_at)
    return list(made)


def last_hop(place, swap, flows, after, name):
    arrays, seen = [], {}
    for flow in flows:
        for array in (flow.keep, flow.got[0]):
            if id(array) not in seen:
                seen[id(array)] = len(arrays)
                arrays.append(array)
    blocks = []
    size = 0
    for f, flow in enumerate(flows):
        for piece, (start, half, padded, width) in enumerate(flow.layout):
            for block in range(width // LANES):
                blocks.append((f, piece, start + block * CORES * padded, padded, block, size))
                size += up_to(padded, 16)
    own_outs = [
        shaped((padded, width), F32) for flow in flows for _, _, padded, width in flow.layout
    ]
    first = [sum(len(flow.layout) for flow in flows[:f]) for f in range(len(flows))]

    def add_body(place_ref, refs, weight, outs, scratch):
        core = place_ref[1]
        for f, piece, at, padded, block, leave_at in blocks:
            flow = flows[f]
            got_at = flow.got[1] + at
            total = refs[seen[id(flow.keep)]][0, at : at + CORES * padded].astype(F32)
            total = total + refs[seen[id(flow.got[0])]][got_at : got_at + CORES * padded].astype(F32)
            own, leave = pick(core, total, 0), pick(core, total, 0, True)
            outs[1 + first[f] + piece][:, block * LANES : (block + 1) * LANES] = own
            full = up_to(padded, 16)
            if full > padded:
                leave = jnp.concatenate([leave, jnp.zeros((full - padded, LANES), F32)], axis=0)
            outs[0][leave_at : leave_at + full] = leave.astype(BF16)

    made = whole_kernel(add_body, place, follow(arrays, after), [], [shaped((size, LANES))] + own_outs, "last_" + name)
    got = swap(made[0], 0)

    def join_body(place_ref, refs, weight, outs, scratch):
        core = place_ref[1]
        for f, piece, _, padded, block, leave_at in blocks:
            at = first[f] + piece
            width = refs[1 + at].shape[1]
            own = refs[1 + at][:, block * LANES : (block + 1) * LANES]
            other = refs[0][leave_at : leave_at + up_to(padded, 16)].astype(F32)[:padded]
            low, high = slice(block * LANES, (block + 1) * LANES), slice(width + block * LANES, width + (block + 1) * LANES)
            outs[at][:, low] = jnp.where(core == 0, own, other)
            outs[at][:, high] = jnp.where(core == 0, other, own)

    joined = whole_kernel(
        join_body, place, [got] + list(made[1:]), [], [shaped((a.shape[0], CORES * a.shape[1]), F32) for a in own_outs],
        "join_" + name,
    )
    results = {}
    for f, flow in enumerate(flows):
        results[flow.name] = [
            joined[first[f] + piece][:half] for piece, (_, half, _, _) in enumerate(flow.layout)
        ]
    return results, list(made)


def follow(value, after):
    return lax.optimization_barrier((value, after))[0]


def rel_bucket(distance):
    beyond = 16 + sum((distance >= border).astype(jnp.int32) for border in THRESHOLDS)
    return jnp.where(distance < 16, distance, beyond)


def shards(
    tokens, memory, cotangent, bucket, gain_self, self_query, self_key, self_value, self_out, rel_bias,
    gain_cross, cross_query, cross_key, cross_value, cross_out, gain_ffn, ffn_gate, ffn_up, ffn_down,
):
    groups = lax.axis_size("grp")
    dp_size = lax.axis_size("dp")
    n_chips = groups // CORES
    more = n_chips - 1
    chips = dp_size * n_chips
    devices = chips * CORES
    grp_at = lax.axis_index("grp")
    core = grp_at % CORES
    y_at = grp_at // CORES
    chip = lax.axis_index("dp") * n_chips + y_at
    rows, model = tokens.shape
    chip_rows = rows * CORES
    group_rows = chip_rows * n_chips
    hidden_units = ffn_down.shape[0]
    length = jnp.minimum(group_rows, jnp.maximum(SHORT, jnp.right_shift(jnp.int32(group_rows), bucket[0])))
    y_bits = n_chips.bit_length() - 1
    bits = chips.bit_length() - 1
    first_chip = y_at * chip_rows // length * length // chip_rows
    valid = [(y_at - s >= first_chip).astype(jnp.int32) for s in range(1, n_chips)]
    place = jnp.stack([chip, core, grp_at] + valid).astype(jnp.int32)

    def swap(v, bit):
        return lax.ppermute(v, ("dp", "grp"), [(i, i ^ (1 << bit)) for i in range(devices)])

    gain_one, gain_two, gain_three = (g.reshape(1, model) for g in (gain_self, gain_cross, gain_ffn))

    past_own = [
        lax.ppermute(tokens, "grp", [(g, g + CORES * s) for g in range(groups - CORES * s)]) for s in range(1, n_chips)
    ]
    tokens_peer = swap(tokens, 0)
    mems = [memory] + [
        lax.ppermute(memory, "grp", [(g, g ^ other) for g in range(groups)]) for other in range(1, groups)
    ]

    distances = jnp.arange(2 * NEAR, dtype=jnp.int32)
    buckets = rel_bucket(distances)[:, None]
    onehot = (buckets == jnp.arange(BUCKETS, dtype=jnp.int32)).astype(F32)
    heads = HEADS // CORES
    rel_local = lax.dynamic_slice_in_dim(rel_bias.astype(F32), core * heads, heads, 1)
    by_dist = jnp.dot(onehot, rel_local - rel_local[BUCKETS - 1 :], precision=lax.Precision.HIGHEST)
    table = jnp.pad(by_dist.T.reshape(heads // 4, 4, 2 * NEAR), ((0, 0), (0, 4), (0, 0)))

    low_one, q, k, v = project(place, tokens, tokens_peer, gain_one, self_query, self_key, self_value)
    *diagonal, w_gate, w_up = self_diagonal(place, table, q, k, v, [(ffn_gate, 1, False), (ffn_up, 1, False)])
    past_own = follow(past_own, diagonal)
    past_peer = [swap(own, 0) for own in past_own]
    cot_peer = swap(follow(cotangent, diagonal[0]), 0)
    low_past, k_past, v_past, w_down = project_past(
        place, past_own, past_peer, gain_one, self_key, self_value, [(ffn_down, 0, False)]
    )
    att, lse_self, w_out, w_out_peer, w_query, w_cross, w_cross_peer = self_past(
        place, table, q, k_past, v_past, *diagonal,
        [(self_out, 0, False), (self_out, 0, True), (cross_query, 1, False), (cross_out, 0, False), (cross_out, 0, True)],
    )
    att_peer = swap(att, 0)
    mem_all, km, vm = project_memory(place, follow(mems, att), cross_key, cross_value)
    att_peer = follow(att_peer, km)
    mid, low_two, cq = mid_forward(
        place, tokens, tokens_peer, att, att_peer, gain_two, w_out, w_out_peer, w_query
    )
    own_doc = []
    if group_rows > SHORT:
        mem_doc = jnp.arange(mem_all.shape[0], dtype=jnp.int32) // (length // RATIO)
        own = (mem_doc == y_at * chip_rows // length).astype(F32)
        own_doc = [jnp.broadcast_to(own[:, None], (mem_all.shape[0], TILE))]
    crs, lse_cross = cross_forward(place, cq, km, vm, own_doc)
    crs_peer = swap(crs, 0)
    late, low_three, inner, d_gate, d_up, dz, cot_half = ffn(
        place, mid, crs, crs_peer, gain_three, cotangent, cot_peer, w_cross, w_cross_peer, w_gate, w_up, w_down
    )

    axes = {
        "y": tuple(range(y_bits)),
        "x": (y_bits,),
        "z": (y_bits + 1,),
        "f": tuple(range(y_bits + 2, bits)),
    }

    def order_of(letters):
        return sum((axes[letter] for letter in letters), ())

    dz_peer = swap(dz, 0)
    inner_peer = swap(inner, 0)
    gate = Flow("gate", [([((low_three,), d_gate)], model)], order_of("xyzf"))
    up = Flow("up", [([((low_three,), d_up)], model)], order_of("yzfx"))
    last = hop(place, swap, [gate, up], [], place, "gate_up")
    down = Flow("down", [([((inner, inner_peer), cot_half)], hidden_units)], order_of("zxyf"))
    spread = (down.spread(inner), down.spread(inner_peer))
    down = Flow("down", [([(spread, cot_half)], hidden_units)], order_of("zxyf"))
    last = hop(place, swap, [down], [], last, "down")
    ffn_flows = [gate, up, down]

    g_late, late_half, d_crs, d_gain_three = late_backward(
        place, follow(dz, last), dz_peer, late, cotangent, cot_peer, gain_three, w_cross
    )
    dcq, dkm, dvm, w_query_peer = cross_backward(
        place, cq, km, vm, own_doc, d_crs, crs, lse_cross, [(cross_query, 1, True)]
    )
    dcq_peer = swap(dcq, 0)
    crs_mem = Flow(
        "crs_mem",
        [([((crs, crs_peer), late_half)], model), ([((mem_all,), dkm)], model), ([((mem_all,), dvm)], model)],
        order_of("zxyf"),
    )
    last = hop(place, swap, [crs_mem], [], dcq, "crs_mem", cost=5)
    g_mid, mid_half, d_att, d_gain_two = mid_backward(
        place, dcq, follow(dcq_peer, last), mid, g_late, gain_two, w_query, w_query_peer, w_out
    )
    att_cq = Flow("att_cq", [([((att, att_peer), mid_half)], model), ([((low_two,), dcq)], model)], order_of("xyzf"))
    last = hop(place, swap, [att_cq], [], d_att, "att_cq")
    dq, dk, dv, d_past, d_near, d_total = self_backward(
        place, table, q, k, v, k_past, v_past, follow(d_att, last), att, lse_self
    )
    past_moved, rider = [], None
    if n_chips == 2:
        last, rider = hop(place, swap, [], ffn_flows, dq, "ffn_1", rider=(d_past, 1))
    else:
        past_moved = [
            lax.ppermute(d_past[s - 1], "grp", [(g, g - CORES * s) for g in range(CORES * s, groups)])
            for s in range(1, n_chips)
        ]
        last = hop(place, swap, [], ffn_flows, dq, "ffn_1")
    mem_parts = memory_backward(place, follow(dkm, last), dvm, cross_key, cross_value)
    query = Flow("query", [([((low_one,), dq)], model)], order_of("xyzf"))
    kv = Flow(
        "kv",
        [
            ([((low_one,), d)] + [((low_past[s],), (d_past, (s, which))) for s in range(more)], model)
            for which, d in ((0, dk), (1, dv))
        ],
        order_of("yzxf"),
    )
    attention = [att_cq, crs_mem, query, kv]
    last = hop(place, swap, [query, kv], [att_cq, crs_mem], mem_parts, "attention_1", cost=5)

    results = {}
    names = {"ffn": ffn_flows, "attention": attention}

    def step(label, after):
        flows = names[label]
        if label in results:
            return after
        moving = [flow for flow in flows if flow.hops]
        if moving:
            return hop(place, swap, [], moving, after, f"{label}_{len(moving[0].hops)}", cost=30)
        results[label], made = last_hop(place, swap, flows, after, label)
        return made

    for label in ("ffn", "attention", "ffn"):
        last = step(label, last)
    dz_own, dz_leave = first_backward(
        place, follow(dq, last), dk, dv, past_moved, rider, self_query, self_key, self_value
    )
    dz_got = swap(dz_leave, 0)
    layer_out = layer_output(place, follow(late, dz_leave), inner, inner_peer, ffn_down)
    dz_got = follow(dz_got, layer_out)
    grad_tokens, d_gain_one = tokens_backward(place, dz_own, dz_got, tokens, g_mid, gain_one)
    small = small_sums(place, d_gain_one, d_gain_two, d_gain_three, d_near, d_total, buckets, heads, devices)
    last = step("attention", small)
    small = lax.all_to_all(follow(small, last), ("dp", "grp"), split_axis=0, concat_axis=0, tiled=True)
    mem_parts = lax.all_to_all(follow(mem_parts, last), "grp", split_axis=0, concat_axis=0, tiled=True)
    while len(results) < 2:
        if "attention" not in results and not any(flow.hops for flow in attention):
            grad_memory, small = gather_sums(
                place, follow([mem_parts.reshape(groups, -1, model), small], last), "gather_sums"
            )
            last = [grad_memory] + last + sum(results.get("ffn", {}).values(), [])
        for label in ("ffn", "attention"):
            last = step(label, last)
    share = model // devices
    rel_share = BUCKETS * HEADS // devices
    got = {**results["ffn"], **results["attention"]}
    return (
        layer_out,
        grad_tokens,
        grad_memory,
        small[0, :share],
        got["query"][0],
        got["kv"][0],
        got["kv"][1],
        got["att_cq"][0],
        small[3, :rel_share],
        small[1, :share],
        got["att_cq"][1],
        got["crs_mem"][1],
        got["crs_mem"][2],
        got["crs_mem"][0],
        small[2, :share],
        got["gate"][0],
        got["up"][0],
        got["down"][0],
    )


def solution(mesh):
    rows = P(("dp", "grp"), None)
    flat = P(("dp", "grp"))
    in_specs = (rows, rows, rows, P("dp")) + (P(),) * 15
    out_specs = (rows,) * 3 + (flat,) + (rows,) * 4 + (flat,) * 2 + (rows,) * 4 + (flat,) + (rows,) * 3
    return jax.shard_map(shards, mesh=mesh, in_specs=in_specs, out_specs=out_specs, check_vma=False)
```

```python
import functools

import jax
import jax.numpy as jnp
from jax import lax
from jax.experimental import pallas as pl
from jax.experimental.pallas import tpu as pltpu
from jax.sharding import PartitionSpec as P

SHORT = 1024
RATIO = 4
BUCKETS = 32
HEADS = 16
EPSILON = 1e-06
THRESHOLDS = (19, 21, 24, 27, 31, 35, 40, 46, 52, 59, 67, 77, 87, 99, 113)
CORES = 2
BF16 = jnp.bfloat16
F32 = jnp.float32
NEGATIVE = -1e30
HEAD = 64
TILE = 256
NEAR = 128
LANES = 128
ROOM = 16 * 1024 * 1024


def dot(a, b):
    return jnp.dot(a, b, preferred_element_type=F32)


def dot_right(a, b):
    return lax.dot_general(a, b, (((1,), (1,)), ((), ())), preferred_element_type=F32)


def shaped(shape, dtype=BF16):
    return jax.ShapeDtypeStruct(tuple(shape), dtype)


def half_shape(array, axis):
    shape = list(array.shape)
    shape[axis] //= CORES
    return tuple(shape)


def whole_kernel(body, place, arrays, weights, outs, name, scratch=(), room=ROOM, cost=0, fetch=()):
    ready = [w for w in weights if not isinstance(w, tuple)]
    far = [w for w in weights if isinstance(w, tuple)]
    n_a, n_r, n_w, n_o, n_f = len(arrays), len(ready), len(far), len(outs), len(fetch)
    buffers = [pltpu.VMEM(half_shape(array, axis), array.dtype) for array, axis, _ in far]
    fetched = [shaped(half_shape(array, axis), array.dtype) for array, axis, _ in fetch]

    def kernel(place_ref, *refs):
        array_refs, refs = refs[:n_a], refs[n_a:]
        ready_refs, refs = refs[:n_r], refs[n_r:]
        far_refs, refs = refs[: n_w + n_f], refs[n_w + n_f :]
        out_refs, refs = refs[:n_o], refs[n_o:]
        fetch_refs, refs = refs[:n_f], refs[n_f:]
        buffer_refs, refs = refs[:n_w], refs[n_w:]
        copies = []
        for at, (ref, buffer, (_, axis, other)) in enumerate(
            zip(far_refs, (*buffer_refs, *fetch_refs), (*far, *fetch))
        ):
            size = buffer.shape[axis]
            start = pl.multiple_of((1 - place_ref[1] if other else place_ref[1]) * size, size)
            source = ref.at[pl.ds(start, size)] if axis == 0 else ref.at[:, pl.ds(start, size)]
            copies.append(pltpu.make_async_copy(source, buffer, refs[0].at[at]))
        for copy in copies:
            copy.start()
        arrived = set()
        places = []
        for w in weights:
            places.append((isinstance(w, tuple), sum(isinstance(x, tuple) == isinstance(w, tuple) for x in weights[: len(places)])))

        def weight(at):
            distant, spot = places[at]
            if not distant:
                return ready_refs[spot]
            if spot not in arrived:
                copies[spot].wait()
                arrived.add(spot)
            return buffer_refs[spot]

        body(place_ref, array_refs, weight, out_refs, refs[1:] if n_w + n_f else refs)
        for copy in copies[n_w:]:
            copy.wait()

    inside = pl.BlockSpec(memory_space=pltpu.VMEM)
    scratch = buffers + ([pltpu.SemaphoreType.DMA((n_w + n_f,))] if n_w + n_f else []) + list(scratch)
    return pl.pallas_call(
        kernel,
        in_specs=[pl.BlockSpec(memory_space=pltpu.SMEM)]
        + [inside] * (n_a + n_r)
        + [pl.BlockSpec(memory_space=pltpu.HBM)] * (n_w + n_f),
        out_specs=[inside] * (n_o + n_f),
        out_shape=list(outs) + fetched,
        scratch_shapes=scratch,
        compiler_params=pltpu.CompilerParams(vmem_limit_bytes=room),
        cost_estimate=pl.CostEstimate(
            flops=int(1.15e9 * cost), bytes_accessed=int(3.69e6 * cost), transcendentals=0
        ),
        name=name,
    )(
        place,
        *arrays,
        *ready,
        *[pltpu.with_memory_space_constraint(array, pltpu.HBM) for array, _, _ in (*far, *fetch)],
    )


def inverse_norm(hidden):
    return lax.rsqrt(jnp.mean(hidden * hidden, axis=-1, keepdims=True) + EPSILON)


def norm_low(hidden, inverse, gain):
    return (hidden * inverse * gain).astype(BF16)


def norm_back(hidden, inverse, gain, dz):
    scaled = gain * dz
    inner = jnp.mean(scaled * hidden, axis=-1, keepdims=True)
    return inverse * scaled - hidden * (inverse * inverse * inverse) * inner


def pick(core, value, axis, other=False):
    half = value.shape[axis] // CORES
    low, high = lax.slice_in_dim(value, 0, half, axis=axis), lax.slice_in_dim(value, half, 2 * half, axis=axis)
    return jnp.where(core == (1 if other else 0), low, high)


def in_place_order(core, own_ref, peer_ref):
    own, peer = own_ref[...].astype(F32), peer_ref[...].astype(F32)
    return jnp.concatenate([jnp.where(core == 0, own, peer), jnp.where(core == 0, peer, own)], axis=0)


def place_rows(half, at):
    zero = jnp.zeros_like(half)
    return jnp.concatenate([half, zero] if at == 0 else [zero, half], axis=0)


def place_lanes(pair, source, at):
    lane = lax.broadcasted_iota(jnp.int32, pair.shape, 1)
    if source != at:
        pair = jnp.concatenate([pair[:, HEAD:], pair[:, :HEAD]], axis=1)
    return jnp.where((lane < HEAD) == (at == 0), pair, jnp.zeros_like(pair))


def near_tiles(table_row):
    skewed = pltpu.roll(jnp.broadcast_to(table_row, (NEAR, 2 * NEAR)), 0, 1, stride=1, stride_axis=0)
    key_at = lax.broadcasted_iota(jnp.int32, (NEAR, NEAR), 0)
    row_at = lax.broadcasted_iota(jnp.int32, (NEAR, NEAR), 1)
    return (jnp.where(key_at <= row_at, skewed[:, :NEAR], NEGATIVE), skewed[:, NEAR:])


def heads_of(pair_turned, cols):
    return jnp.concatenate(
        [place_rows(pair_turned[h * HEAD : (h + 1) * HEAD, cols], h // 2) for h in range(4)], axis=1
    )


def add_corner(scores, tiles):
    rows = scores.shape[0]
    last = scores[rows - NEAR :]
    pieces = []
    for h in range(4):
        pieces += [last[:, h * TILE : h * TILE + NEAR] + tiles[h][1], last[:, h * TILE + NEAR : (h + 1) * TILE]]
    return jnp.concatenate([scores[: rows - NEAR], jnp.concatenate(pieces, axis=1)], axis=0)


def add_diagonal(scores, tiles):
    rows = scores.shape[0]
    first = scores[rows - TILE : rows - NEAR]
    second = scores[rows - NEAR :]
    upper, lower = [], []
    for h in range(4):
        left, right = slice(h * TILE, h * TILE + NEAR), slice(h * TILE + NEAR, (h + 1) * TILE)
        upper += [first[:, left] + tiles[h][0], first[:, right] + tiles[h][1]]
        lower += [jnp.full((NEAR, NEAR), NEGATIVE, F32), second[:, right] + tiles[h][0]]
    last = [jnp.concatenate(upper, axis=1), jnp.concatenate(lower, axis=1)]
    if rows > TILE:
        last = [add_corner(scores[: rows - TILE], tiles)] + last
    return jnp.concatenate(last, axis=0)


def by_distance(near):
    level = near[:8]
    for first in range(8, NEAR, 8):
        level = level + pltpu.roll(near[first : first + 8], 2 * NEAR - first, 1)
    row = lax.broadcasted_iota(jnp.int32, level.shape, 0)
    for bit in (1, 2, 4):
        level = jnp.where(row & bit > 0, pltpu.roll(level, 2 * NEAR - bit, 1), level)
    return jnp.sum(level, axis=0, keepdims=True)


def soft(scores):
    peak = jnp.max(scores, axis=0, keepdims=True)
    weights = jnp.exp(scores - peak)
    return peak, weights.astype(BF16), jnp.sum(weights, axis=0, keepdims=True)


def finish(o_ref, lse_ref, cols, peak, summed, acc):
    out = acc / summed
    lse = peak + jnp.log(summed)
    pieces = []
    for h in range(4):
        e = h // 2
        lanes = slice(h * TILE, (h + 1) * TILE)
        pieces.append(out[e * HEAD : (e + 1) * HEAD, lanes])
        lse_ref[0, h : h + 1, cols] = lse[:, lanes]
    o_ref[cols, :] = jnp.concatenate(pieces, axis=0).T.astype(BF16)


def self_diagonal_block(table_ref, q_ref, k_ref, v_ref, peak_ref, sum_ref, acc_ref):
    rows = q_ref.shape[0]
    v_turned = v_ref[...].T
    q_turned = q_ref[...].T
    tiles = [near_tiles(table_ref[0, h : h + 1, :]) for h in range(4)]
    spans = [slice(t * TILE, (t + 1) * TILE) for t in range(rows // TILE)]
    scores = [add_diagonal(dot(k_ref[: cols.stop], heads_of(q_turned, cols)), tiles) for cols in spans]
    parts = [soft(score) for score in scores]
    for t, cols in enumerate(spans):
        peak_ref[t], sum_ref[t] = parts[t][0], parts[t][2]
        acc_ref[t] = dot(v_turned[:, : cols.stop], parts[t][1])


def self_past_blocks(valid_ref, blocks, *, earlier):
    steps = blocks[0][1].shape[0] // TILE
    spans = [slice(t * TILE, (t + 1) * TILE) for t in range(steps)]
    units = [(p, t) for p in range(len(blocks)) for t in range(steps)]
    for s in range(earlier):

        @pl.when(valid_ref[3 + s] > 0)
        def _(s=s):
            turned = [block[1][...].T for block in blocks]
            values = [block[3][s].T for block in blocks]

            def scores_of(p, t):
                scores = dot(blocks[p][2][s], heads_of(turned[p], spans[t]))
                if s == 0 and t == 0:
                    table_ref = blocks[p][0]
                    scores = add_corner(scores, [near_tiles(table_ref[0, h : h + 1, :]) for h in range(4)])
                return scores

            ready = scores_of(*units[0])
            for at, (p, t) in enumerate(units):
                scores = ready
                if at + 1 < len(units):
                    ready = scores_of(*units[at + 1])
                _, _, _, _, peak_in, sum_in, acc_in, o_ref, lse_ref, peak_ref, sum_ref, acc_ref = blocks[p]
                old = (peak_in, sum_in, acc_in) if s == 0 else (peak_ref, sum_ref, acc_ref)
                peak = old[0][t]
                new_peak = jnp.maximum(peak, jnp.max(scores, axis=0, keepdims=True))
                rescale = jnp.exp(peak - new_peak)
                weights = jnp.exp(scores - new_peak)
                summed = old[1][t] * rescale + jnp.sum(weights, axis=0, keepdims=True)
                acc = old[2][t] * rescale + dot(values[p], weights.astype(BF16))
                if s + 1 < earlier:
                    peak_ref[t], sum_ref[t], acc_ref[t] = new_peak, summed, acc
                else:
                    finish(o_ref, lse_ref, spans[t], new_peak, summed, acc)

        @pl.when(valid_ref[3 + s] == 0)
        def _(s=s):
            for p, t in units:
                _, _, _, _, peak_in, sum_in, acc_in, o_ref, lse_ref, peak_ref, sum_ref, acc_ref = blocks[p]
                old = (peak_in, sum_in, acc_in) if s == 0 else (peak_ref, sum_ref, acc_ref)
                if s + 1 < earlier:
                    peak_ref[t], sum_ref[t], acc_ref[t] = old[0][t], old[1][t], old[2][t]
                else:
                    finish(o_ref, lse_ref, spans[t], old[0][t], old[1][t], old[2][t])


def placed_heads(block, cols):
    rows = []
    for h in range(4):
        pair = block[cols, (h // 2) * 2 * HEAD : (h // 2 + 1) * 2 * HEAD]
        rows.append(place_lanes(pair, h % 2, h // 2))
    return jnp.concatenate(rows, axis=0)


def row_of_heads(ref, cols):
    return jnp.concatenate([ref[0, h : h + 1, cols] for h in range(4)], axis=1)


def deltas(product, cols):
    return jnp.concatenate(
        [jnp.sum(product[h * HEAD : (h + 1) * HEAD, cols], axis=0, keepdims=True) for h in range(4)], axis=1
    )


def back_scores(scores, lse, d_prob, delta):
    prob = jnp.exp(scores - lse)
    d_score = prob * (d_prob - delta)
    return prob.astype(BF16), d_score.astype(BF16)


def query_rows(d_query):
    pieces = [
        d_query[(h // 2) * HEAD : (h // 2 + 1) * HEAD, h * TILE : (h + 1) * TILE] for h in range(4)
    ]
    return jnp.concatenate(pieces, axis=0).T.astype(BF16)


def self_backward_block(
    valid_ref, table_ref, q_ref, k_ref, v_ref, kp_ref, vp_ref, do_ref, o_ref, lse_ref,
    dq_ref, dk_ref, dv_ref, past_ref, db_ref, total_ref,
    near_sum, dq_sum, *, earlier,
):
    rows = q_ref.shape[0]
    steps = rows // TILE
    spans = [slice(t * TILE, (t + 1) * TILE) for t in range(steps)]
    k_turned = k_ref[...].T
    q_turned = q_ref[...].T
    do_turned = do_ref[...].T
    product = (do_ref[...].astype(F32) * o_ref[...].astype(F32)).T
    tiles = [near_tiles(table_ref[0, h : h + 1, :]) for h in range(4)]
    queries = [heads_of(q_turned, cols) for cols in spans]
    outs = [heads_of(do_turned, cols) for cols in spans]
    q_placed = [placed_heads(q_ref, cols) for cols in spans]
    do_placed = [placed_heads(do_ref, cols) for cols in spans]
    lses = [row_of_heads(lse_ref, cols) for cols in spans]
    delta = [deltas(product, cols) for cols in spans]

    for t, cols in enumerate(spans):
        seen = cols.stop
        scores = add_diagonal(dot(k_ref[:seen], queries[t]), tiles)
        prob, d_score = back_scores(scores, lses[t], dot(v_ref[:seen], outs[t]), delta[t])
        d_value = dot(prob, do_placed[t])
        d_key = dot(d_score, q_placed[t])
        if t == 0:
            dv_whole, dk_whole = d_value, d_key
        else:
            more = seen - dv_whole.shape[0]
            dv_whole = jnp.concatenate([dv_whole + d_value[: seen - more], d_value[seen - more :]], axis=0)
            dk_whole = jnp.concatenate([dk_whole + d_key[: seen - more], d_key[seen - more :]], axis=0)
        dq_sum[t] = dot(k_turned[:, :seen], d_score)
        d_wide = d_score.astype(F32)
        total = jnp.sum(d_wide, axis=0, keepdims=True)
        base = seen - TILE
        for h in range(4):
            left, right = slice(h * TILE, h * TILE + NEAR), slice(h * TILE + NEAR, (h + 1) * TILE)
            zero_part = d_wide[base : base + NEAR, left] + d_wide[base + NEAR :, right]
            one_part = d_wide[base : base + NEAR, right]
            if t > 0:
                one_part = one_part + d_wide[base - NEAR : base, left]
            both = jnp.concatenate([zero_part, one_part], axis=1)
            part = total[:, h * TILE : (h + 1) * TILE]
            if t == 0:
                near_sum[h] = both
                total_ref[0, h : h + 1, :] = part
            else:
                near_sum[h] += both
                total_ref[0, h : h + 1, :] += part
    dk_ref[...] = dk_whole.astype(BF16)
    dv_ref[...] = dv_whole.astype(BF16)

    for s in range(earlier):

        @pl.when(valid_ref[3 + s] > 0)
        def _(s=s):
            kp_turned = kp_ref[s].T
            for t in range(steps):
                scores = dot(kp_ref[s], queries[t])
                if s == 0 and t == 0:
                    scores = add_corner(scores, tiles)
                prob, d_score = back_scores(scores, lses[t], dot(vp_ref[s], outs[t]), delta[t])
                d_value = dot(prob, do_placed[t])
                d_key = dot(d_score, q_placed[t])
                dv_whole = d_value if t == 0 else dv_whole + d_value
                dk_whole = d_key if t == 0 else dk_whole + d_key
                dq_sum[t] += dot(kp_turned, d_score)
                d_wide = d_score.astype(F32)
                total = jnp.sum(d_wide, axis=0, keepdims=True)
                for h in range(4):
                    total_ref[0, h : h + 1, :] += total[:, h * TILE : (h + 1) * TILE]
                    if s == 0 and t == 0:
                        near_sum[h, :, NEAR:] += d_wide[rows - NEAR :, h * TILE : h * TILE + NEAR]
            past_ref[s, 0] = dk_whole.astype(BF16)
            past_ref[s, 1] = dv_whole.astype(BF16)

        @pl.when(valid_ref[3 + s] == 0)
        def _(s=s):
            past_ref[s] = jnp.zeros_like(past_ref[s])

    for t, cols in enumerate(spans):
        dq_ref[cols, :] = query_rows(dq_sum[t])
    for h in range(4):
        db_ref[0, h : h + 1, :] = by_distance(near_sum[h])
    db_ref[0, 4:, :] = jnp.zeros((4, 2 * NEAR), F32)
    total_ref[0, 4:, :] = jnp.zeros((4, 2 * NEAR), F32)


def cross_forward_block(q_ref, k_ref, v_ref, own_ref, o_ref, lse_ref, *, masked):
    rows = q_ref.shape[0]
    v_turned = v_ref[...].T
    q_turned = q_ref[...].T
    spans = [slice(t * TILE, (t + 1) * TILE) for t in range(rows // TILE)]
    scores = [dot(k_ref[...], heads_of(q_turned, cols)) for cols in spans]
    if masked:
        blocked = jnp.where(own_ref[...] > 0, 0.0, NEGATIVE)
        blocked = jnp.concatenate([blocked] * 4, axis=1)
        scores = [score + blocked for score in scores]
    for t, cols in enumerate(spans):
        peak, weights, summed = soft(scores[t])
        finish(o_ref, lse_ref, cols, peak, summed, dot(v_turned, weights))


def cross_backward_block(
    q_ref, k_ref, v_ref, own_ref, do_ref, o_ref, lse_ref, dq_ref, dk_ref, dv_ref, *, masked
):
    rows = q_ref.shape[0]
    k_turned = k_ref[...].T
    q_turned = q_ref[...].T
    do_turned = do_ref[...].T
    product = (do_ref[...].astype(F32) * o_ref[...].astype(F32)).T
    spans = [slice(t * TILE, (t + 1) * TILE) for t in range(rows // TILE)]
    dk_whole, dv_whole = 0.0, 0.0
    for t, cols in enumerate(spans):
        scores = dot(k_ref[...], heads_of(q_turned, cols))
        if masked:
            blocked = jnp.where(own_ref[...] > 0, 0.0, NEGATIVE)
            scores = scores + jnp.concatenate([blocked] * 4, axis=1)
        d_prob = dot(v_ref[...], heads_of(do_turned, cols))
        prob, d_score = back_scores(scores, row_of_heads(lse_ref, cols), d_prob, deltas(product, cols))
        dv_whole = dv_whole + dot(prob, placed_heads(do_ref, cols))
        dk_whole = dk_whole + dot(d_score, placed_heads(q_ref, cols))
        dq_ref[cols, :] = query_rows(dot(k_turned, d_score))
    dk_ref[...] = dk_whole.astype(BF16)
    dv_ref[...] = dv_whole.astype(BF16)


def wide_view(ref, p):
    return ref.at[:, pl.ds(p * 4 * HEAD, 4 * HEAD)]


def slim_view(ref, p):
    return ref.at[:, pl.ds(p * 2 * HEAD, 2 * HEAD)]


def past_view(ref, p):
    return ref.at[:, :, pl.ds(p * 2 * HEAD, 2 * HEAD)]


def page_view(ref, p):
    return ref.at[pl.ds(p, 1)]


def self_diagonal(place, table, q, k, v, fetch):
    rows, blocks = q.shape[0], k.shape[1] // (2 * HEAD)
    steps = rows // TILE

    def body(place_ref, arrays, weight, outs, scratch):
        table_ref, q_ref, k_ref, v_ref = arrays
        for p in range(blocks):
            self_diagonal_block(
                page_view(table_ref, p), wide_view(q_ref, p), slim_view(k_ref, p), slim_view(v_ref, p),
                *[ref.at[p] for ref in outs],
            )

    state = [(blocks, steps, 1, 4 * TILE), (blocks, steps, 1, 4 * TILE), (blocks, steps, 2 * HEAD, 4 * TILE)]
    return whole_kernel(body, place, [table, q, k, v], [], [shaped(shape, F32) for shape in state], "self_diagonal", fetch=fetch)


def self_past(place, table, q, kp, vp, peak, summed, acc, fetch):
    rows, blocks, earlier = q.shape[0], kp.shape[2] // (2 * HEAD), kp.shape[0]

    def body(place_ref, arrays, weight, outs, scratch):
        table_ref, q_ref, kp_ref, vp_ref, peak_ref, sum_ref, acc_ref = arrays
        views = [
            (
                page_view(table_ref, p), wide_view(q_ref, p), past_view(kp_ref, p), past_view(vp_ref, p),
                peak_ref.at[p], sum_ref.at[p], acc_ref.at[p], wide_view(outs[0], p), page_view(outs[1], p),
                *([ref.at[p] for ref in scratch] if earlier > 1 else [None] * 3),
            )
            for p in range(blocks)
        ]
        self_past_blocks(place_ref, views, earlier=earlier)

    return whole_kernel(
        body,
        place,
        [table, q, kp, vp, peak, summed, acc],
        [],
        [shaped(q.shape), shaped((blocks, 8, rows), F32)],
        "self_past",
        [pltpu.VMEM(a.shape, F32) for a in (peak, summed, acc)] if earlier > 1 else [],
        fetch=fetch,
    )


def self_backward(place, table, q, k, v, kp, vp, do, o, lse, fetch):
    rows, blocks, earlier = q.shape[0], k.shape[1] // (2 * HEAD), kp.shape[0]
    steps = rows // TILE

    def body(place_ref, arrays, weight, outs, scratch):
        table_ref, q_ref, k_ref, v_ref, kp_ref, vp_ref, do_ref, o_ref, lse_ref = arrays
        dq_ref, dk_ref, dv_ref, past_ref, db_ref, total_ref = outs
        for p in range(blocks):
            self_backward_block(
                place_ref, page_view(table_ref, p), wide_view(q_ref, p), slim_view(k_ref, p), slim_view(v_ref, p),
                past_view(kp_ref, p), past_view(vp_ref, p), wide_view(do_ref, p), wide_view(o_ref, p),
                page_view(lse_ref, p), wide_view(dq_ref, p), slim_view(dk_ref, p), slim_view(dv_ref, p),
                past_ref.at[:, :, :, pl.ds(p * 2 * HEAD, 2 * HEAD)], page_view(db_ref, p), page_view(total_ref, p),
                *[ref.at[p] for ref in scratch], earlier=earlier,
            )

    return whole_kernel(
        body,
        place,
        [table, q, k, v, kp, vp, do, o, lse],
        [],
        [
            shaped(q.shape),
            shaped(k.shape),
            shaped(k.shape),
            shaped((earlier, 2) + k.shape),
            shaped(table.shape, F32),
            shaped(table.shape, F32),
        ],
        "self_backward",
        [pltpu.VMEM((blocks, 4, NEAR, 2 * NEAR), F32), pltpu.VMEM((blocks, steps, 2 * HEAD, 4 * TILE), F32)],
        fetch=fetch,
    )


def cross_forward(place, q, k, v, own):
    rows, blocks = q.shape[0], k.shape[1] // (2 * HEAD)

    def body(place_ref, arrays, weight, outs, scratch):
        q_ref, k_ref, v_ref = arrays[:3]
        for p in range(blocks):
            cross_forward_block(
                wide_view(q_ref, p), slim_view(k_ref, p), slim_view(v_ref, p), arrays[-1], wide_view(outs[0], p),
                page_view(outs[1], p), masked=len(own) > 0,
            )

    outs = [shaped(q.shape), shaped((blocks, 8, rows), F32)]
    return whole_kernel(body, place, [q, k, v] + own, [], outs, "cross_forward")


def cross_backward(place, q, k, v, own, do, o, lse, fetch):
    blocks = k.shape[1] // (2 * HEAD)

    def body(place_ref, arrays, weight, outs, scratch):
        q_ref, k_ref, v_ref, do_ref, o_ref, lse_ref = arrays[:6]
        for p in range(blocks):
            cross_backward_block(
                wide_view(q_ref, p), slim_view(k_ref, p), slim_view(v_ref, p), arrays[-1], wide_view(do_ref, p),
                wide_view(o_ref, p), page_view(lse_ref, p), wide_view(outs[0], p), slim_view(outs[1], p),
                slim_view(outs[2], p), masked=len(own) > 0,
            )

    outs = [shaped(q.shape), shaped(k.shape), shaped(k.shape)]
    return whole_kernel(body, place, [q, k, v, do, o, lse] + own, [], outs, "cross_backward", fetch=fetch)


def project(place, own, peer, gain, wq, wk, wv):
    rows, model = own.shape
    wide, slim = wq.shape[1] // CORES, wk.shape[1] // CORES

    def body(place_ref, arrays, weight, outs, scratch):
        hidden = in_place_order(place_ref[1], arrays[0], arrays[1])
        low = norm_low(hidden, inverse_norm(hidden), arrays[2][...].astype(F32))
        outs[0][...] = low
        for at in range(3):
            outs[1 + at][...] = dot(low, weight(at)[...]).astype(BF16)

    return whole_kernel(
        body,
        place,
        [own, peer, gain],
        [(wq, 1, False), (wk, 1, False), (wv, 1, False)],
        [shaped((CORES * rows, n)) for n in (model, wide, slim, slim)],
        "project",
    )


def project_past(place, owns, peers, gain, wk, wv, fetch):
    rows, model = owns[0].shape
    earlier = len(owns)
    slim = wk.shape[1] // CORES

    def body(place_ref, arrays, weight, outs, scratch):
        own_refs, peer_refs = arrays[:earlier], arrays[earlier : 2 * earlier]
        gain_value = arrays[-1][...].astype(F32)
        for s in range(earlier):
            hidden = in_place_order(place_ref[1], own_refs[s], peer_refs[s])
            low = norm_low(hidden, inverse_norm(hidden), gain_value)
            outs[s][...] = low
            outs[earlier][s] = dot(low, weight(0)[...]).astype(BF16)
            outs[earlier + 1][s] = dot(low, weight(1)[...]).astype(BF16)

    made = whole_kernel(
        body,
        place,
        owns + peers + [gain],
        [(wk, 1, False), (wv, 1, False)],
        [shaped((CORES * rows, model))] * earlier + [shaped((earlier, CORES * rows, slim))] * 2,
        "project_past",
        fetch=fetch,
    )
    return made[:earlier], *made[earlier:]


def project_memory(place, mems, wk, wv):
    groups = len(mems)
    rows, model = mems[0].shape
    slim = wk.shape[1] // CORES

    def body(place_ref, arrays, weight, outs, scratch):
        for at, piece_ref in enumerate(arrays):
            block = jnp.bitwise_xor(place_ref[2], jnp.int32(at))
            outs[0][pl.ds(pl.multiple_of(block * rows, rows), rows)] = piece_ref[...]
        mem = outs[0][...]
        outs[1][...] = dot(mem, weight(0)[...]).astype(BF16)
        outs[2][...] = dot(mem, weight(1)[...]).astype(BF16)

    return whole_kernel(
        body,
        place,
        mems,
        [(wk, 1, False), (wv, 1, False)],
        [shaped((groups * rows, n)) for n in (model, slim, slim)],
        "project_memory",
        cost=8,
    )


def mid_forward(place, own, peer, att, att_peer, gain, wo, wo_peer, wq):
    rows, model = own.shape

    def body(place_ref, arrays, weight, outs, scratch):
        own_ref, peer_ref, att_ref, att_peer_ref, gain_ref = arrays
        hidden = in_place_order(place_ref[1], own_ref, peer_ref)
        hidden = hidden + dot(att_ref[...], weight(0)[...]) + dot(att_peer_ref[...], weight(1)[...])
        outs[0][...] = hidden.astype(BF16)
        low = norm_low(hidden, inverse_norm(hidden), gain_ref[...].astype(F32))
        outs[1][...] = low
        outs[2][...] = dot(low, weight(2)[...]).astype(BF16)

    return whole_kernel(
        body,
        place,
        [own, peer, att, att_peer, gain],
        [wo, wo_peer, wq],
        [shaped((CORES * rows, model))] * 2 + [shaped((CORES * rows, wq.shape[1]))],
        "mid_forward",
    )


def cotangent_inner(place, cot, cot_peer, wd):
    rows, model = cot.shape

    def body(place_ref, arrays, weight, outs, scratch):
        value = in_place_order(place_ref[1], arrays[0], arrays[1]).astype(BF16)
        outs[0][...] = pick(place_ref[1], value, 1)
        outs[1][...] = dot_right(value, weight(0)[...]).astype(BF16)

    outs = [shaped((CORES * rows, model // CORES)), shaped((CORES * rows, wd.shape[0]))]
    return whole_kernel(body, place, [cot, cot_peer], [wd], outs, "cotangent_inner", cost=8)


def ffn(place, mid, crs, crs_peer, gain, d_inner, wc, wc_peer, wg, wu):
    rows, model = mid.shape
    hidden_half = wg.shape[1]
    steps = [256] * (hidden_half // 256) + [hidden_half % 256] * (hidden_half % 256 > 0)
    scale = 0.7978845608028654

    def body(place_ref, arrays, weight, outs, scratch):
        mid_ref, crs_ref, crs_peer_ref, gain_ref, d_inner_ref = arrays
        late_ref, low_ref, inner_ref, dg_ref, du_ref, dz_ref = outs
        hidden = mid_ref[...].astype(F32) + dot(crs_ref[...], weight(0)[...]) + dot(crs_peer_ref[...], weight(1)[...])
        late_ref[...] = hidden.astype(BF16)
        low = norm_low(hidden, inverse_norm(hidden), gain_ref[...].astype(F32))
        low_ref[...] = low
        start = 0
        for width in steps:
            cols = slice(start, start + width)
            start += width
            gate = dot(low, weight(2)[:, cols])
            up = dot(low, weight(3)[:, cols])
            d_inner = d_inner_ref[:, cols].astype(F32)
            square = gate * gate
            bent = jnp.tanh(gate * (scale + (scale * 0.044715) * square))
            whole = 0.5 + 0.5 * bent
            slope = whole + (0.5 * gate) * (1.0 - bent * bent) * (scale + (3 * scale * 0.044715) * square)
            curve = gate * whole
            inner_ref[:, cols] = (curve * up).astype(BF16)
            dg_ref[:, cols] = (d_inner * up * slope).astype(BF16)
            du_ref[:, cols] = (d_inner * curve).astype(BF16)
        dz_ref[...] = (dot_right(dg_ref[...], weight(2)[...]) + dot_right(du_ref[...], weight(3)[...])).astype(BF16)

    return whole_kernel(
        body,
        place,
        [mid, crs, crs_peer, gain, d_inner],
        [wc, wc_peer, wg, wu],
        [shaped((rows, model))] * 2
        + [shaped((rows, hidden_half))] * 3
        + [shaped((rows, model))],
        "ffn",
        room=16 * 1024 * 1024,
    )


def late_backward(place, dz, dz_peer, late, cot, cot_peer, gain, wc):
    rows, model = late.shape

    def body(place_ref, arrays, weight, outs, scratch):
        dz_ref, dz_peer_ref, late_ref, cot_ref, cot_peer_ref, gain_ref = arrays
        dz_value = dz_ref[...].astype(F32) + dz_peer_ref[...].astype(F32)
        hidden = late_ref[...].astype(F32)
        inverse = inverse_norm(hidden)
        outs[3][...] = jnp.sum(dz_value * hidden * inverse, axis=0, keepdims=True)
        grad = in_place_order(place_ref[1], cot_ref, cot_peer_ref)
        grad = grad + norm_back(hidden, inverse, gain_ref[...].astype(F32), dz_value)
        low = grad.astype(BF16)
        outs[0][...] = low
        outs[1][...] = pick(place_ref[1], low, 1)
        outs[2][...] = dot_right(low, weight(0)[...]).astype(BF16)

    return whole_kernel(
        body,
        place,
        [dz, dz_peer, late, cot, cot_peer, gain],
        [wc],
        [
            shaped((rows, model)),
            shaped((rows, model // CORES)),
            shaped((rows, wc.shape[0])),
            shaped((1, model), F32),
        ],
        "late_backward",
    )


def mid_backward(place, dq, dq_peer, mid, g_late, gain, wq, wq_peer, wo):
    rows, model = mid.shape

    def body(place_ref, arrays, weight, outs, scratch):
        dq_ref, dq_peer_ref, mid_ref, g_ref, gain_ref = arrays
        dz = dot_right(dq_ref[...], weight(0)[...]) + dot_right(dq_peer_ref[...], weight(1)[...])
        hidden = mid_ref[...].astype(F32)
        inverse = inverse_norm(hidden)
        outs[3][...] = jnp.sum(dz * hidden * inverse, axis=0, keepdims=True)
        grad = g_ref[...].astype(F32) + norm_back(hidden, inverse, gain_ref[...].astype(F32), dz)
        low = grad.astype(BF16)
        outs[0][...] = pick(place_ref[1], low, 0)
        outs[1][...] = pick(place_ref[1], low, 1)
        outs[2][...] = dot_right(low, weight(2)[...]).astype(BF16)

    return whole_kernel(
        body,
        place,
        [dq, dq_peer, mid, g_late, gain],
        [wq, wq_peer, wo],
        [
            shaped((rows // CORES, model)),
            shaped((rows, model // CORES)),
            shaped((rows, wo.shape[0])),
            shaped((1, model), F32),
        ],
        "mid_backward",
    )


def first_backward(place, dz, past, riders, mem_parts, wk, wv):
    rows, model = dz.shape
    slim = wk.shape[1]
    own_rows = rows // CORES
    joint = riders is not None
    mem_rows = mem_parts.shape[0] // (CORES * CORES) if joint else 0

    def body(place_ref, arrays, weight, outs, scratch):
        core = place_ref[1]
        pairs = []
        if joint:
            got_ref, past_at, mem_at = arrays[1], *riders[1:]
            blocks = [got_ref[past_at + at * rows : past_at + (at + 1) * rows] for at in range(2 * slim // LANES)]
            pairs.append((jnp.concatenate(blocks[: slim // LANES], 1), jnp.concatenate(blocks[slim // LANES :], 1)))
        else:
            pairs += [(ref[0], ref[1]) for ref in arrays[1:]]
        total = arrays[0][...].astype(F32)
        for dk, dv in pairs:
            total = total + dot_right(dk, weight(0)[...]) + dot_right(dv, weight(1)[...])
        outs[0][...] = pick(core, total, 0)
        outs[1][:own_rows] = pick(core, total, 0, True).astype(BF16)
        if joint:
            half = CORES * mem_rows
            mine = pick(place_ref[2] // CORES, arrays[2][...].astype(F32), 0)
            got = [got_ref[mem_at + at * half : mem_at + (at + 1) * half].astype(F32) for at in range(model // LANES)]
            mine = mine + jnp.concatenate(got, axis=1)
            outs[2][...] = pick(core, mine, 0)
            outs[1][own_rows:] = pick(core, mine, 0, True).astype(BF16)

    outs = [shaped((own_rows, model), F32), shaped((own_rows + mem_rows, model))]
    if joint:
        outs.append(shaped((mem_rows, model), F32))
    return whole_kernel(
        body, place, [dz] + ([riders[0], mem_parts] if joint else past), [wk, wv], outs, "first_backward"
    )


def tokens_backward(place, dz, dz_got, mem, tokens, g_mid, gain):
    rows = tokens.shape[0]

    def body(place_ref, arrays, weight, outs, scratch):
        dz_ref, dz_got_ref, tokens_ref, g_ref, gain_ref = arrays[:5]
        dz_value = dz_ref[...] + dz_got_ref[:rows].astype(F32)
        hidden = tokens_ref[...].astype(F32)
        grad = norm_back(hidden, inverse_norm(hidden), gain_ref[...].astype(F32), dz_value)
        outs[0][...] = (g_ref[...].astype(F32) + grad).astype(BF16)
        if mem:
            outs[1][...] = (arrays[5][...] + dz_got_ref[rows:].astype(F32)).astype(BF16)

    outs = [shaped(tokens.shape)] + [shaped(m.shape) for m in mem]
    return whole_kernel(body, place, [dz, dz_got, tokens, g_mid, gain] + mem, [], outs, "tokens_backward")


def layer_output(place, late, inner, inner_peer, wd):
    rows, model = late.shape

    def body(place_ref, arrays, weight, outs, scratch):
        own, inner_own, inner_other = (pick(place_ref[1], ref[...], 0) for ref in arrays)
        total = own.astype(F32) + dot(inner_own, weight(0)[...]) + dot(inner_other, weight(1)[...])
        outs[0][...] = total.astype(BF16)

    return whole_kernel(
        body,
        place,
        [late, inner, inner_peer],
        [(wd, 0, False), (wd, 0, True)],
        [shaped((rows // CORES, model))],
        "layer_output",
        cost=10,
    )[0]


def memory_backward(place, dk, dv, wk, wv):
    def body(place_ref, arrays, weight, outs, scratch):
        grad = dot_right(arrays[0][...], weight(0)[...]) + dot_right(arrays[1][...], weight(1)[...])
        outs[0][...] = grad.astype(BF16)

    weights = [(wk, 1, False), (wv, 1, False)]
    return whole_kernel(body, place, [dk, dv], weights, [shaped((dk.shape[0], wk.shape[0]))], "memory_backward")[0]


def small_sums(place, dq, dk, dv, d_past, own, peer, past_own, past_peer, two, three, near, total, buckets, weights, chips):
    rows, model = dq.shape[0], own.shape[1]
    earlier = len(past_own)
    heads = HEADS // CORES

    def body(place_ref, arrays, weight, outs, scratch):
        dq_ref, dk_ref, dv_ref, past_ref, own_ref, peer_ref = arrays[:6]
        past_own_refs, past_peer_refs = arrays[6 : 6 + earlier], arrays[6 + earlier : 6 + 2 * earlier]
        two_ref, three_ref, near_ref, total_ref, bucket_ref = arrays[6 + 2 * earlier :]
        core = place_ref[1]
        first = core == 0

        def gain_part(dz, own_ref, peer_ref):
            hidden = in_place_order(core, own_ref, peer_ref)
            return jnp.sum(dz * (hidden * inverse_norm(hidden)), axis=0, keepdims=True)

        dz = dot_right(dq_ref[...], weight(0)[...])
        dz = dz + dot_right(dk_ref[...], weight(1)[...]) + dot_right(dv_ref[...], weight(2)[...])
        outs[0][...] = dz.astype(BF16)
        one = gain_part(dz, own_ref, peer_ref)
        for s in range(earlier):
            dz = dot_right(past_ref[s, 0], weight(1)[...]) + dot_right(past_ref[s, 1], weight(2)[...])
            one = one + gain_part(dz, past_own_refs[s], past_peer_refs[s])
        gains = [one, jnp.where(first, two_ref[...], 0.0), jnp.where(first, three_ref[...], 0.0)]
        near = jnp.concatenate([near_ref[p, :4] for p in range(heads // 4)], axis=0)
        total = jnp.concatenate([total_ref[p, :4] for p in range(heads // 4)], axis=0)
        far = jnp.sum(total, axis=1, keepdims=True) - jnp.sum(near, axis=1, keepdims=True)
        last = lax.broadcasted_iota(jnp.int32, near.shape, 1) == near.shape[1] - 1
        near = near + jnp.where(last, far, 0.0)
        entries = BUCKETS * HEADS
        entry = lax.broadcasted_iota(jnp.int32, (near.shape[1], entries), 1)
        same = (lax.shift_right_logical(entry, jnp.int32(HEADS.bit_length() - 1)) == bucket_ref[...]).astype(F32)
        sums = jnp.dot(near, same, precision=lax.Precision.HIGHEST, preferred_element_type=F32)
        head = lax.broadcasted_iota(jnp.int32, sums.shape, 0) + core * heads
        of_entry = jnp.bitwise_and(lax.broadcasted_iota(jnp.int32, sums.shape, 1), jnp.int32(HEADS - 1))
        vectors = gains + [jnp.sum(jnp.where(head == of_entry, sums, 0.0), axis=0, keepdims=True)]
        for block in range(chips):
            lines = []
            for vector in vectors:
                size = vector.shape[1] // chips
                line = vector[:, block * size : (block + 1) * size]
                lines.append(jnp.concatenate([line, jnp.zeros((1, LANES - size), F32)], axis=1))
            lines.append(jnp.zeros((12, LANES), F32))
            outs[1][block * 16 : (block + 1) * 16] = jnp.concatenate(lines, axis=0).astype(BF16)

    arrays = [dq, dk, dv, d_past, own, peer] + past_own + past_peer + [two, three, near, total, buckets]
    return whole_kernel(
        body, place, arrays, weights, [shaped((rows, model)), shaped((chips * 16, LANES))], "small_sums"
    )


def gather_sums(place, parts, name):
    def body(place_ref, arrays, weight, outs, scratch):
        for array, out in zip(arrays, outs):
            total = array[0].astype(F32)
            for at in range(1, array.shape[0]):
                total = total + array[at].astype(F32)
            out[...] = total.astype(out.dtype)

    return whole_kernel(body, place, parts, [], [shaped(a.shape[1:], a.dtype) for a in parts], name)


def up_to(value, multiple):
    return (value + multiple - 1) // multiple * multiple


def array_of(y):
    return y[0] if isinstance(y, tuple) else y


class Flow:
    def __init__(self, name, pieces, order, extra=None):
        self.name, self.pieces, self.order, self.extra = name, pieces, order, extra
        self.hops = [bit + 1 for bit in order]
        self.chips = 1 << len(order)
        self.layout = []
        start = 0
        for terms, rows in pieces:
            half = rows // self.chips // CORES
            padded = up_to(half, 8)
            width = array_of(terms[0][1]).shape[-1]
            self.layout.append((start, half, padded, width))
            start += CORES * padded * (width // LANES)
        self.extra_at = start
        self.rows = start + (16 if extra is not None else 0)
        self.keep = self.got = None

    def spread(self, x):
        half, padded = self.layout[0][1:3]
        if half == padded:
            return x
        chunks = x.reshape(x.shape[0], -1, half)
        return jnp.pad(chunks, ((0, 0), (0, 0), (0, padded - half))).reshape(x.shape[0], -1)


def chip_of(spot, order):
    number = 0
    for at, bit in enumerate(order):
        number |= (spot >> (len(order) - 1 - at) & 1) << bit
    return number


def sum_flow(flow, refs_of, place_ref, turned, free, send_ref, base, keep_ref):
    chip, core = place_ref[0], place_ref[1]
    half = flow.chips // 2
    for (terms, _), (start, _, padded, width) in zip(flow.pieces, flow.layout):
        chunk = CORES * padded
        lefts = []
        for xs, y in terms:
            key = (tuple(id(x) for x in xs), flow.order)
            if key not in turned:
                straight_ref, turned[key] = free.pop(0), free.pop(0)
                if len(xs) == 1:
                    straight_ref[...] = refs_of[id(xs[0])][...].T
                else:
                    size = straight_ref.shape[0] // CORES
                    for part, x in enumerate(xs):
                        at = (core if part == 0 else 1 - core) * size
                        straight_ref[pl.ds(pl.multiple_of(at, 16), size)] = refs_of[id(x)][...].T
                for spot in range(flow.chips):
                    at = jnp.bitwise_xor(jnp.int32(chip_of(spot, flow.order)), chip) * chunk
                    turned[key][spot * chunk : (spot + 1) * chunk] = straight_ref[pl.ds(pl.multiple_of(at, 16), chunk)]
            lefts.append(turned[key])
        count = max(1, min(flow.chips, 512 // chunk))
        while flow.chips % count:
            count -= 1
        for first in range(0, flow.chips, count):
            tile = None
            for left, (_, y) in zip(lefts, terms):
                y_ref = refs_of[id(array_of(y))]
                y_value = y_ref[y[1]] if isinstance(y, tuple) else y_ref[...]
                term = dot(left[first * chunk : (first + count) * chunk], y_value)
                tile = term if tile is None else tile + term
            tile = tile.astype(BF16)
            for inner in range(count):
                spot = first + inner
                for block in range(width // LANES):
                    value = tile[inner * chunk : (inner + 1) * chunk, block * LANES : (block + 1) * LANES]
                    at = start + block * chunk
                    if spot < half:
                        keep_ref[spot, at : at + chunk] = value
                    else:
                        at += base + (spot - half) * flow.rows
                        send_ref[at : at + chunk] = value


def copy_extra(flow, extra_ref, place_ref, send_ref, base, keep_ref):
    half = flow.chips // 2
    for spot in range(flow.chips):
        at = jnp.bitwise_xor(jnp.int32(chip_of(spot, flow.order)), place_ref[0]) * 16
        value = extra_ref[pl.ds(pl.multiple_of(at, 16), 16)]
        if spot < half:
            keep_ref[spot, flow.extra_at : flow.extra_at + 16] = value
        else:
            to = base + (spot - half) * flow.rows + flow.extra_at
            send_ref[to : to + 16] = value


def add_flow(flow, old_ref, got_ref, got_at, send_ref, base, keep_ref):
    half = old_ref.shape[0] // 2
    for spot in range(2 * half):
        at = got_at + spot * flow.rows
        total = (old_ref[spot].astype(F32) + got_ref[at : at + flow.rows].astype(F32)).astype(BF16)
        if spot < half:
            keep_ref[spot] = total
        else:
            send_ref[base + (spot - half) * flow.rows : base + (spot - half + 1) * flow.rows] = total


def hop(place, swap, sums, adds, after, name, cost=0, riders=()):
    arrays, seen = [], {}

    def take(array):
        if id(array) not in seen:
            seen[id(array)] = len(arrays)
            arrays.append(array)

    for flow in sums:
        for terms, _ in flow.pieces:
            for xs, y in terms:
                for array in (*xs, array_of(y)):
                    take(array)
        if flow.extra is not None:
            take(flow.extra)
    for flow in adds:
        take(flow.keep)
        take(flow.got[0])
    bits, sends, keeps = {}, {}, {}
    for flow in sums + adds:
        half = (flow.chips if flow in sums else flow.keep.shape[0]) // 2
        bit = flow.hops[0]
        base = bits.setdefault(bit, 0)
        sends[flow.name] = (bit, base)
        bits[bit] = base + half * flow.rows
        keeps[flow.name] = shaped((half, flow.rows, LANES))
    rider_at = []
    for rider, bit, size, _ in riders:
        take(rider)
        rider_at.append(bits.setdefault(bit, 0))
        bits[bit] = rider_at[-1] + size
    order = list(bits)
    outs = [shaped((bits[bit], LANES)) for bit in order] + list(keeps.values())

    def body(place_ref, refs, weight, out_refs, scratch):
        refs_of = {key: refs[at] for key, at in seen.items()}
        turned, free = {}, list(scratch)
        for at, flow in enumerate(sums + adds):
            bit, base = sends[flow.name]
            send_ref, keep_ref = out_refs[order.index(bit)], out_refs[len(order) + at]
            if flow in sums:
                sum_flow(flow, refs_of, place_ref, turned, free, send_ref, base, keep_ref)
                if flow.extra is not None:
                    copy_extra(flow, refs_of[id(flow.extra)], place_ref, send_ref, base, keep_ref)
            else:
                add_flow(
                    flow, refs_of[id(flow.keep)], refs_of[id(flow.got[0])], flow.got[1], send_ref, base, keep_ref
                )
        for (rider, bit, _, write), at in zip(riders, rider_at):
            write(refs_of[id(rider)], out_refs[order.index(bit)], at, place_ref)

    needed = {}
    for flow in sums:
        for terms, _ in flow.pieces:
            for xs, _ in terms:
                shape = (sum(x.shape[1] for x in xs), xs[0].shape[0])
                needed[(tuple(id(x) for x in xs), flow.order)] = [pltpu.VMEM(shape, BF16)] * 2
    scratch = sum(needed.values(), [])
    made = whole_kernel(body, place, follow(arrays, after), [], outs, name, scratch, cost=cost)
    moved = [swap(array, bit) for array, bit in zip(made, order)]
    for at, flow in enumerate(sums + adds):
        bit, base = sends[flow.name]
        flow.keep, flow.got, flow.hops = made[len(order) + at], (moved[order.index(bit)], base), flow.hops[1:]
    if riders:
        return list(made), (moved[order.index(riders[0][1])], *rider_at)
    return list(made)


def write_past(past_ref, send_ref, at, place_ref):
    _, pages, rows, width = past_ref.shape
    for page in range(pages):
        for block in range(width // LANES):
            send_ref[at : at + rows] = past_ref[0, page, :, block * LANES : (block + 1) * LANES]
            at += rows


def write_memory(mem_ref, send_ref, at, place_ref):
    rows = mem_ref.shape[0] // CORES
    there = pl.ds(pl.multiple_of((1 - place_ref[2] // CORES) * rows, rows), rows)
    for block in range(mem_ref.shape[1] // LANES):
        send_ref[at : at + rows] = mem_ref[there, block * LANES : (block + 1) * LANES]
        at += rows


def last_hop(place, swap, flows, after, name, shares=()):
    arrays, seen = [], {}
    for flow in flows:
        for array in (flow.keep, flow.got[0]):
            if id(array) not in seen:
                seen[id(array)] = len(arrays)
                arrays.append(array)
    blocks = []
    size = 0
    for f, flow in enumerate(flows):
        for piece, (start, half, padded, width) in enumerate(flow.layout):
            for block in range(width // LANES):
                blocks.append((f, piece, start + block * CORES * padded, padded, block, size))
                size += up_to(padded, 16)
    extras = [(f, flow.extra_at, size + 16 * sum(x.extra is not None for x in flows[:f])) for f, flow in enumerate(flows) if flow.extra is not None]
    size += 16 * len(extras)
    own_outs = [
        shaped((padded, width), F32) for flow in flows for _, _, padded, width in flow.layout
    ]
    own_outs += [shaped((16, LANES), F32) for _ in extras]
    n_pieces = len(own_outs) - len(extras)
    first = [sum(len(flow.layout) for flow in flows[:f]) for f in range(len(flows))]

    def add_body(place_ref, refs, weight, outs, scratch):
        core = place_ref[1]
        for f, piece, at, padded, block, leave_at in blocks:
            flow = flows[f]
            got_at = flow.got[1] + at
            total = refs[seen[id(flow.keep)]][0, at : at + CORES * padded].astype(F32)
            total = total + refs[seen[id(flow.got[0])]][got_at : got_at + CORES * padded].astype(F32)
            own, leave = pick(core, total, 0), pick(core, total, 0, True)
            outs[1 + first[f] + piece][:, block * LANES : (block + 1) * LANES] = own
            full = up_to(padded, 16)
            if full > padded:
                leave = jnp.concatenate([leave, jnp.zeros((full - padded, LANES), F32)], axis=0)
            outs[0][leave_at : leave_at + full] = leave.astype(BF16)
        for at, (f, start, leave_at) in enumerate(extras):
            flow = flows[f]
            got_at = flow.got[1] + start
            total = refs[seen[id(flow.keep)]][0, start : start + 16].astype(F32)
            total = total + refs[seen[id(flow.got[0])]][got_at : got_at + 16].astype(F32)
            outs[1 + n_pieces + at][...] = total
            outs[0][leave_at : leave_at + 16] = total.astype(BF16)

    made = whole_kernel(add_body, place, follow(arrays, after), [], [shaped((size, LANES))] + own_outs, "last_" + name)
    got = swap(made[0], 0)

    def join_body(place_ref, refs, weight, outs, scratch):
        core = place_ref[1]
        for f, piece, _, padded, block, leave_at in blocks:
            at = first[f] + piece
            width = refs[1 + at].shape[1]
            own = refs[1 + at][:, block * LANES : (block + 1) * LANES]
            other = refs[0][leave_at : leave_at + up_to(padded, 16)].astype(F32)[:padded]
            low, high = slice(block * LANES, (block + 1) * LANES), slice(width + block * LANES, width + (block + 1) * LANES)
            outs[at][:, low] = jnp.where(core == 0, own, other)
            outs[at][:, high] = jnp.where(core == 0, other, own)
        for at, (_, _, leave_at) in enumerate(extras):
            total = refs[1 + n_pieces + at][...] + refs[0][leave_at : leave_at + 16].astype(F32)
            for line, (out, share) in enumerate(zip(outs[n_pieces:], shares)):
                out[...] = jnp.where(core == 0, total[line, :share], total[line, share : 2 * share])

    joined = whole_kernel(
        join_body,
        place,
        [got] + list(made[1:]),
        [],
        [shaped((a.shape[0], CORES * a.shape[1]), F32) for a in own_outs[:n_pieces]]
        + [shaped((share,), F32) for _ in extras for share in shares],
        "join_" + name,
    )
    results = {}
    for f, flow in enumerate(flows):
        results[flow.name] = [
            joined[first[f] + piece][:half] for piece, (_, half, _, _) in enumerate(flow.layout)
        ]
    if extras:
        results["small"] = joined[n_pieces:]
    return results, list(made)


def follow(value, after):
    return lax.optimization_barrier((value, after))[0]


def rel_bucket(distance):
    beyond = 16 + sum((distance >= border).astype(jnp.int32) for border in THRESHOLDS)
    return jnp.where(distance < 16, distance, beyond)


def shards(
    tokens, memory, cotangent, bucket, gain_self, self_query, self_key, self_value, self_out, rel_bias,
    gain_cross, cross_query, cross_key, cross_value, cross_out, gain_ffn, ffn_gate, ffn_up, ffn_down,
):
    groups = lax.axis_size("grp")
    dp_size = lax.axis_size("dp")
    n_chips = groups // CORES
    more = n_chips - 1
    chips = dp_size * n_chips
    devices = chips * CORES
    grp_at = lax.axis_index("grp")
    core = grp_at % CORES
    y_at = grp_at // CORES
    chip = lax.axis_index("dp") * n_chips + y_at
    rows, model = tokens.shape
    chip_rows = rows * CORES
    group_rows = chip_rows * n_chips
    hidden_units = ffn_down.shape[0]
    length = jnp.minimum(group_rows, jnp.maximum(SHORT, jnp.right_shift(jnp.int32(group_rows), bucket[0])))
    y_bits = n_chips.bit_length() - 1
    bits = chips.bit_length() - 1
    first_chip = y_at * chip_rows // length * length // chip_rows
    valid = [(y_at - s >= first_chip).astype(jnp.int32) for s in range(1, n_chips)]
    place = jnp.stack([chip, core, grp_at] + valid).astype(jnp.int32)

    def swap(v, bit):
        return lax.ppermute(v, ("dp", "grp"), [(i, i ^ (1 << bit)) for i in range(devices)])

    gain_one, gain_two, gain_three = (g.reshape(1, model) for g in (gain_self, gain_cross, gain_ffn))

    past_own = [
        lax.ppermute(tokens, "grp", [(g, g + CORES * s) for g in range(groups - CORES * s)]) for s in range(1, n_chips)
    ]
    tokens_peer = swap(tokens, 0)
    mems = [memory] + [
        lax.ppermute(memory, "grp", [(g, g ^ other) for g in range(groups)]) for other in range(1, groups)
    ]

    distances = jnp.arange(2 * NEAR, dtype=jnp.int32)
    buckets = rel_bucket(distances)[:, None]
    onehot = (buckets == jnp.arange(BUCKETS, dtype=jnp.int32)).astype(F32)
    heads = HEADS // CORES
    rel_local = lax.dynamic_slice_in_dim(rel_bias.astype(F32), core * heads, heads, 1)
    by_dist = jnp.dot(onehot, rel_local - rel_local[BUCKETS - 1 :], precision=lax.Precision.HIGHEST)
    table = jnp.pad(by_dist.T.reshape(heads // 4, 4, 2 * NEAR), ((0, 0), (0, 4), (0, 0)))

    low_one, q, k, v = project(place, tokens, tokens_peer, gain_one, self_query, self_key, self_value)
    *diagonal, w_gate, w_up = self_diagonal(place, table, q, k, v, [(ffn_gate, 1, False), (ffn_up, 1, False)])
    past_own = follow(past_own, diagonal)
    past_peer = [swap(own, 0) for own in past_own]
    cot_peer = swap(follow(cotangent, diagonal[0]), 0)
    low_past, k_past, v_past, w_down = project_past(
        place, past_own, past_peer, gain_one, self_key, self_value, [(ffn_down, 0, False)]
    )
    att, lse_self, w_out, w_out_peer, w_query, w_cross, w_cross_peer = self_past(
        place, table, q, k_past, v_past, *diagonal,
        [(self_out, 0, False), (self_out, 0, True), (cross_query, 1, False), (cross_out, 0, False), (cross_out, 0, True)],
    )
    att_peer = swap(att, 0)
    mem_all, km, vm = project_memory(place, follow(mems, att), cross_key, cross_value)
    att_peer = follow(att_peer, km)
    mid, low_two, cq = mid_forward(
        place, tokens, tokens_peer, att, att_peer, gain_two, w_out, w_out_peer, w_query
    )
    own_doc = []
    if group_rows > SHORT:
        mem_doc = jnp.arange(mem_all.shape[0], dtype=jnp.int32) // (length // RATIO)
        own = (mem_doc == y_at * chip_rows // length).astype(F32)
        own_doc = [jnp.broadcast_to(own[:, None], (mem_all.shape[0], TILE))]
    crs, lse_cross = cross_forward(place, cq, km, vm, own_doc)
    crs_peer = swap(crs, 0)
    cot_half, d_inner = cotangent_inner(place, follow(cotangent, crs), cot_peer, w_down)
    crs_peer = follow(crs_peer, d_inner)
    late, low_three, inner, d_gate, d_up, dz = ffn(
        place, mid, crs, crs_peer, gain_three, d_inner, w_cross, w_cross_peer, w_gate, w_up
    )

    axes = {
        "y": tuple(range(y_bits)),
        "x": (y_bits,),
        "z": (y_bits + 1,),
        "f": tuple(range(y_bits + 2, bits)),
    }

    def order_of(letters):
        return sum((axes[letter] for letter in letters), ())

    dz_peer = swap(dz, 0)
    inner_peer = swap(inner, 0)
    gate = Flow("gate", [([((low_three,), d_gate)], model)], order_of("xyzf"))
    up = Flow("up", [([((low_three,), d_up)], model)], order_of("yzfx"))
    last = hop(place, swap, [gate], [], place, "gate")
    last = hop(place, swap, [up], [], last, "up")
    down = Flow("down", [([((inner, inner_peer), cot_half)], hidden_units)], order_of("zxyf"))
    spread = (down.spread(inner), down.spread(inner_peer))
    down = Flow("down", [([(spread, cot_half)], hidden_units)], order_of("zxyf"))
    last = hop(place, swap, [down], [], last, "down")
    ffn_flows = [gate, up, down]

    g_late, late_half, d_crs, d_gain_three = late_backward(
        place, follow(dz, last), dz_peer, late, cotangent, cot_peer, gain_three, w_cross
    )
    dcq, dkm, dvm, w_query_peer = cross_backward(
        place, cq, km, vm, own_doc, d_crs, crs, lse_cross, [(cross_query, 1, True)]
    )
    dcq_peer = swap(dcq, 0)
    crs_mem = Flow(
        "crs_mem",
        [([((crs, crs_peer), late_half)], model), ([((mem_all,), dkm)], model), ([((mem_all,), dvm)], model)],
        order_of("zxyf"),
    )
    last = hop(place, swap, [crs_mem], [], dcq, "crs_mem", cost=5)
    g_mid, mid_half, d_att, d_gain_two = mid_backward(
        place, dcq, follow(dcq_peer, last), mid, g_late, gain_two, w_query, w_query_peer, w_out
    )
    att_cq = Flow("att_cq", [([((att, att_peer), mid_half)], model), ([((low_two,), dcq)], model)], order_of("xyzf"))
    last = hop(place, swap, [att_cq], [], d_att, "att_cq")
    dq, dk, dv, d_past, d_near, d_total, *w_first = self_backward(
        place, table, q, k, v, k_past, v_past, follow(d_att, last), att, lse_self,
        [(self_query, 1, False), (self_key, 1, False), (self_value, 1, False)],
    )
    mem_parts = memory_backward(place, follow(dkm, dq), dvm, cross_key, cross_value)
    past_moved, riders = [], None
    if n_chips == 2:
        y_bit = 1
        last, riders = hop(
            place, swap, [], ffn_flows, mem_parts, "ffn_1",
            riders=[
                (d_past, y_bit, d_past.size // LANES, write_past),
                (mem_parts, y_bit, mem_parts.size // CORES // LANES, write_memory),
            ],
        )
    else:
        past_moved = [
            lax.ppermute(d_past[s - 1], "grp", [(g, g - CORES * s) for g in range(CORES * s, groups)])
            for s in range(1, n_chips)
        ]
        last = hop(place, swap, [], ffn_flows, mem_parts, "ffn_1")
    dz, small = small_sums(
        place, follow(dq, last), dk, dv, d_past, tokens, tokens_peer, past_own, past_peer, d_gain_two, d_gain_three,
        d_near, d_total, buckets, w_first, chips,
    )
    query = Flow("query", [([((low_one,), dq)], model)], order_of("xyzf"), small)
    kv = Flow(
        "kv",
        [
            ([((low_one,), d)] + [((low_past[s],), (d_past, (s, which))) for s in range(more)], model)
            for which, d in ((0, dk), (1, dv))
        ],
        order_of("yxzf"),
    )
    attention = [att_cq, crs_mem, query, kv]
    last = hop(place, swap, [query, kv], [att_cq, crs_mem], dz, "attention_1", cost=5)

    results = {}
    names = {"ffn": ffn_flows, "attention": attention}

    def step(label, after):
        flows = names[label]
        if label in results:
            return after
        moving = [flow for flow in flows if flow.hops]
        if moving:
            return hop(place, swap, [], moving, after, f"{label}_{len(moving[0].hops)}", cost=30)
        results[label], made = last_hop(place, swap, flows, after, label, [model // devices] * 3 + [BUCKETS * HEADS // devices])
        return made

    for label in ("ffn", "attention", "ffn", "attention"):
        last = step(label, last)
    dz_own, dz_leave, *mem_own = first_backward(place, follow(dz, last), past_moved, riders, mem_parts, *w_first[1:])
    dz_got = swap(dz_leave, 0)
    layer_out = layer_output(place, follow(late, dz_leave), inner, inner_peer, ffn_down)
    dz_got = follow(dz_got, layer_out)
    grad_tokens, *grad_memory = tokens_backward(place, dz_own, dz_got, mem_own, tokens, g_mid, gain_one)
    if not grad_memory:
        parts = lax.all_to_all(mem_parts, "grp", split_axis=0, concat_axis=0, tiled=True)
        grad_memory = gather_sums(place, [parts.reshape(groups, -1, model)], "memory_sums")
    last = [grad_tokens]
    while len(results) < 2:
        if "attention" not in results and not any(flow.hops for flow in attention):
            last = last + sum(results.get("ffn", {}).values(), [])
        for label in ("ffn", "attention"):
            last = step(label, last)
    got = {**results["ffn"], **results["attention"]}
    *gains, relative = got["small"]
    return (
        layer_out,
        grad_tokens,
        grad_memory[0],
        gains[0],
        got["query"][0],
        got["kv"][0],
        got["kv"][1],
        got["att_cq"][0],
        relative,
        gains[1],
        got["att_cq"][1],
        got["crs_mem"][1],
        got["crs_mem"][2],
        got["crs_mem"][0],
        gains[2],
        got["gate"][0],
        got["up"][0],
        got["down"][0],
    )


def solution(mesh):
    rows = P(("dp", "grp"), None)
    flat = P(("dp", "grp"))
    in_specs = (rows, rows, rows, P("dp")) + (P(),) * 15
    out_specs = (rows,) * 3 + (flat,) + (rows,) * 4 + (flat,) * 2 + (rows,) * 4 + (flat,) + (rows,) * 3
    return jax.shard_map(shards, mesh=mesh, in_specs=in_specs, out_specs=out_specs, check_vma=False)
```

```python
import functools

import jax
import jax.numpy as jnp
from jax import lax
from jax.experimental import pallas as pl
from jax.experimental.pallas import tpu as pltpu
from jax.sharding import PartitionSpec as P

SHORT = 1024
RATIO = 4
BUCKETS = 32
HEADS = 16
EPSILON = 1e-06
THRESHOLDS = (19, 21, 24, 27, 31, 35, 40, 46, 52, 59, 67, 77, 87, 99, 113)
CORES = 2
BF16 = jnp.bfloat16
F32 = jnp.float32
NEGATIVE = -1e30
HEAD = 64
TILE = 256
NEAR = 128
LANES = 128
ROOM = 16 * 1024 * 1024


def dot(a, b):
    return jnp.dot(a, b, preferred_element_type=F32)


def dot_right(a, b):
    return lax.dot_general(a, b, (((1,), (1,)), ((), ())), preferred_element_type=F32)


def shaped(shape, dtype=BF16):
    return jax.ShapeDtypeStruct(tuple(shape), dtype)


def half_shape(array, axis):
    shape = list(array.shape)
    shape[axis] //= CORES
    return tuple(shape)


def whole_kernel(body, place, arrays, weights, outs, name, scratch=(), room=ROOM, cost=0, fetch=()):
    ready = [w for w in weights if not isinstance(w, tuple)]
    far = [w for w in weights if isinstance(w, tuple)]
    n_a, n_r, n_w, n_o, n_f = len(arrays), len(ready), len(far), len(outs), len(fetch)
    buffers = [pltpu.VMEM(half_shape(array, axis), array.dtype) for array, axis, _ in far]
    fetched = [shaped(half_shape(array, axis), array.dtype) for array, axis, _ in fetch]

    def kernel(place_ref, *refs):
        array_refs, refs = refs[:n_a], refs[n_a:]
        ready_refs, refs = refs[:n_r], refs[n_r:]
        far_refs, refs = refs[: n_w + n_f], refs[n_w + n_f :]
        out_refs, refs = refs[:n_o], refs[n_o:]
        fetch_refs, refs = refs[:n_f], refs[n_f:]
        buffer_refs, refs = refs[:n_w], refs[n_w:]
        copies = []
        for at, (ref, buffer, (_, axis, other)) in enumerate(
            zip(far_refs, (*buffer_refs, *fetch_refs), (*far, *fetch))
        ):
            size = buffer.shape[axis]
            start = pl.multiple_of((1 - place_ref[1] if other else place_ref[1]) * size, size)
            source = ref.at[pl.ds(start, size)] if axis == 0 else ref.at[:, pl.ds(start, size)]
            copies.append(pltpu.make_async_copy(source, buffer, refs[0].at[at]))
        for copy in copies:
            copy.start()
        arrived = set()
        places = []
        for w in weights:
            places.append((isinstance(w, tuple), sum(isinstance(x, tuple) == isinstance(w, tuple) for x in weights[: len(places)])))

        def weight(at):
            distant, spot = places[at]
            if not distant:
                return ready_refs[spot]
            if spot not in arrived:
                copies[spot].wait()
                arrived.add(spot)
            return buffer_refs[spot]

        body(place_ref, array_refs, weight, out_refs, refs[1:] if n_w + n_f else refs)
        for copy in copies[n_w:]:
            copy.wait()

    inside = pl.BlockSpec(memory_space=pltpu.VMEM)
    scratch = buffers + ([pltpu.SemaphoreType.DMA((n_w + n_f,))] if n_w + n_f else []) + list(scratch)
    return pl.pallas_call(
        kernel,
        in_specs=[pl.BlockSpec(memory_space=pltpu.SMEM)]
        + [inside] * (n_a + n_r)
        + [pl.BlockSpec(memory_space=pltpu.HBM)] * (n_w + n_f),
        out_specs=[inside] * (n_o + n_f),
        out_shape=list(outs) + fetched,
        scratch_shapes=scratch,
        compiler_params=pltpu.CompilerParams(vmem_limit_bytes=room),
        cost_estimate=pl.CostEstimate(
            flops=int(1.15e9 * cost), bytes_accessed=int(3.69e6 * cost), transcendentals=0
        ),
        name=name,
    )(
        place,
        *arrays,
        *ready,
        *[pltpu.with_memory_space_constraint(array, pltpu.HBM) for array, _, _ in (*far, *fetch)],
    )


def inverse_norm(hidden):
    return lax.rsqrt(jnp.mean(hidden * hidden, axis=-1, keepdims=True) + EPSILON)


def norm_low(hidden, inverse, gain):
    return (hidden * inverse * gain).astype(BF16)


def norm_back(hidden, inverse, gain, dz):
    scaled = gain * dz
    inner = jnp.mean(scaled * hidden, axis=-1, keepdims=True)
    return inverse * scaled - hidden * (inverse * inverse * inverse) * inner


def pick(core, value, axis, other=False):
    half = value.shape[axis] // CORES
    low, high = lax.slice_in_dim(value, 0, half, axis=axis), lax.slice_in_dim(value, half, 2 * half, axis=axis)
    return jnp.where(core == (1 if other else 0), low, high)


def in_place_order(core, own_ref, peer_ref):
    own, peer = own_ref[...].astype(F32), peer_ref[...].astype(F32)
    return jnp.concatenate([jnp.where(core == 0, own, peer), jnp.where(core == 0, peer, own)], axis=0)


def place_rows(half, at):
    zero = jnp.zeros_like(half)
    return jnp.concatenate([half, zero] if at == 0 else [zero, half], axis=0)


def place_lanes(pair, source, at):
    lane = lax.broadcasted_iota(jnp.int32, pair.shape, 1)
    if source != at:
        pair = jnp.concatenate([pair[:, HEAD:], pair[:, :HEAD]], axis=1)
    return jnp.where((lane < HEAD) == (at == 0), pair, jnp.zeros_like(pair))


def near_tiles(table_row):
    skewed = pltpu.roll(jnp.broadcast_to(table_row, (NEAR, 2 * NEAR)), 0, 1, stride=1, stride_axis=0)
    key_at = lax.broadcasted_iota(jnp.int32, (NEAR, NEAR), 0)
    row_at = lax.broadcasted_iota(jnp.int32, (NEAR, NEAR), 1)
    return (jnp.where(key_at <= row_at, skewed[:, :NEAR], NEGATIVE), skewed[:, NEAR:])


def heads_of(pair_turned, cols):
    return jnp.concatenate(
        [place_rows(pair_turned[h * HEAD : (h + 1) * HEAD, cols], h // 2) for h in range(4)], axis=1
    )


def add_corner(scores, tiles):
    rows = scores.shape[0]
    last = scores[rows - NEAR :]
    pieces = []
    for h in range(4):
        pieces += [last[:, h * TILE : h * TILE + NEAR] + tiles[h][1], last[:, h * TILE + NEAR : (h + 1) * TILE]]
    return jnp.concatenate([scores[: rows - NEAR], jnp.concatenate(pieces, axis=1)], axis=0)


def add_diagonal(scores, tiles):
    rows = scores.shape[0]
    first = scores[rows - TILE : rows - NEAR]
    second = scores[rows - NEAR :]
    upper, lower = [], []
    for h in range(4):
        left, right = slice(h * TILE, h * TILE + NEAR), slice(h * TILE + NEAR, (h + 1) * TILE)
        upper += [first[:, left] + tiles[h][0], first[:, right] + tiles[h][1]]
        lower += [jnp.full((NEAR, NEAR), NEGATIVE, F32), second[:, right] + tiles[h][0]]
    last = [jnp.concatenate(upper, axis=1), jnp.concatenate(lower, axis=1)]
    if rows > TILE:
        last = [add_corner(scores[: rows - TILE], tiles)] + last
    return jnp.concatenate(last, axis=0)


def by_distance(near):
    level = near[:8]
    for first in range(8, NEAR, 8):
        level = level + pltpu.roll(near[first : first + 8], 2 * NEAR - first, 1)
    row = lax.broadcasted_iota(jnp.int32, level.shape, 0)
    for bit in (1, 2, 4):
        level = jnp.where(row & bit > 0, pltpu.roll(level, 2 * NEAR - bit, 1), level)
    return jnp.sum(level, axis=0, keepdims=True)


def soft(scores):
    peak = jnp.max(scores, axis=0, keepdims=True)
    weights = jnp.exp(scores - peak)
    return peak, weights.astype(BF16), jnp.sum(weights, axis=0, keepdims=True)


def finish(o_ref, lse_ref, cols, peak, summed, acc):
    out = acc / summed
    lse = peak + jnp.log(summed)
    pieces = []
    for h in range(4):
        e = h // 2
        lanes = slice(h * TILE, (h + 1) * TILE)
        pieces.append(out[e * HEAD : (e + 1) * HEAD, lanes])
        lse_ref[0, h : h + 1, cols] = lse[:, lanes]
    o_ref[cols, :] = jnp.concatenate(pieces, axis=0).T.astype(BF16)


def self_diagonal_block(table_ref, q_ref, k_ref, v_ref, peak_ref, sum_ref, acc_ref):
    rows = q_ref.shape[0]
    v_turned = v_ref[...].T
    q_turned = q_ref[...].T
    tiles = [near_tiles(table_ref[0, h : h + 1, :]) for h in range(4)]
    spans = [slice(t * TILE, (t + 1) * TILE) for t in range(rows // TILE)]
    scores = [add_diagonal(dot(k_ref[: cols.stop], heads_of(q_turned, cols)), tiles) for cols in spans]
    parts = [soft(score) for score in scores]
    for t, cols in enumerate(spans):
        peak_ref[t], sum_ref[t] = parts[t][0], parts[t][2]
        acc_ref[t] = dot(v_turned[:, : cols.stop], parts[t][1])


def self_past_blocks(valid_ref, blocks, *, earlier):
    steps = blocks[0][1].shape[0] // TILE
    spans = [slice(t * TILE, (t + 1) * TILE) for t in range(steps)]
    units = [(p, t) for p in range(len(blocks)) for t in range(steps)]
    for s in range(earlier):

        @pl.when(valid_ref[3 + s] > 0)
        def _(s=s):
            turned = [block[1][...].T for block in blocks]
            values = [block[3][s].T for block in blocks]

            def scores_of(p, t):
                scores = dot(blocks[p][2][s], heads_of(turned[p], spans[t]))
                if s == 0 and t == 0:
                    table_ref = blocks[p][0]
                    scores = add_corner(scores, [near_tiles(table_ref[0, h : h + 1, :]) for h in range(4)])
                return scores

            ready = scores_of(*units[0])
            for at, (p, t) in enumerate(units):
                scores = ready
                if at + 1 < len(units):
                    ready = scores_of(*units[at + 1])
                _, _, _, _, peak_in, sum_in, acc_in, o_ref, lse_ref, peak_ref, sum_ref, acc_ref = blocks[p]
                old = (peak_in, sum_in, acc_in) if s == 0 else (peak_ref, sum_ref, acc_ref)
                peak = old[0][t]
                new_peak = jnp.maximum(peak, jnp.max(scores, axis=0, keepdims=True))
                rescale = jnp.exp(peak - new_peak)
                weights = jnp.exp(scores - new_peak)
                summed = old[1][t] * rescale + jnp.sum(weights, axis=0, keepdims=True)
                acc = old[2][t] * rescale + dot(values[p], weights.astype(BF16))
                if s + 1 < earlier:
                    peak_ref[t], sum_ref[t], acc_ref[t] = new_peak, summed, acc
                else:
                    finish(o_ref, lse_ref, spans[t], new_peak, summed, acc)

        @pl.when(valid_ref[3 + s] == 0)
        def _(s=s):
            for p, t in units:
                _, _, _, _, peak_in, sum_in, acc_in, o_ref, lse_ref, peak_ref, sum_ref, acc_ref = blocks[p]
                old = (peak_in, sum_in, acc_in) if s == 0 else (peak_ref, sum_ref, acc_ref)
                if s + 1 < earlier:
                    peak_ref[t], sum_ref[t], acc_ref[t] = old[0][t], old[1][t], old[2][t]
                else:
                    finish(o_ref, lse_ref, spans[t], old[0][t], old[1][t], old[2][t])


def placed_heads(block, cols):
    rows = []
    for h in range(4):
        pair = block[cols, (h // 2) * 2 * HEAD : (h // 2 + 1) * 2 * HEAD]
        rows.append(place_lanes(pair, h % 2, h // 2))
    return jnp.concatenate(rows, axis=0)


def row_of_heads(ref, cols):
    return jnp.concatenate([ref[0, h : h + 1, cols] for h in range(4)], axis=1)


def deltas(product, cols):
    return jnp.concatenate(
        [jnp.sum(product[h * HEAD : (h + 1) * HEAD, cols], axis=0, keepdims=True) for h in range(4)], axis=1
    )


def back_scores(scores, lse, d_prob, delta):
    prob = jnp.exp(scores - lse)
    d_score = prob * (d_prob - delta)
    return prob.astype(BF16), d_score.astype(BF16)


def query_rows(d_query):
    pieces = [
        d_query[(h // 2) * HEAD : (h // 2 + 1) * HEAD, h * TILE : (h + 1) * TILE] for h in range(4)
    ]
    return jnp.concatenate(pieces, axis=0).T.astype(BF16)


def self_backward_block(
    valid_ref, table_ref, q_ref, k_ref, v_ref, kp_ref, vp_ref, do_ref, o_ref, lse_ref,
    dq_ref, dk_ref, dv_ref, past_ref, db_ref, total_ref,
    near_sum, dq_sum, *, earlier,
):
    rows = q_ref.shape[0]
    steps = rows // TILE
    spans = [slice(t * TILE, (t + 1) * TILE) for t in range(steps)]
    k_turned = k_ref[...].T
    q_turned = q_ref[...].T
    do_turned = do_ref[...].T
    product = (do_ref[...].astype(F32) * o_ref[...].astype(F32)).T
    tiles = [near_tiles(table_ref[0, h : h + 1, :]) for h in range(4)]
    queries = [heads_of(q_turned, cols) for cols in spans]
    outs = [heads_of(do_turned, cols) for cols in spans]
    q_placed = [placed_heads(q_ref, cols) for cols in spans]
    do_placed = [placed_heads(do_ref, cols) for cols in spans]
    lses = [row_of_heads(lse_ref, cols) for cols in spans]
    delta = [deltas(product, cols) for cols in spans]

    for t, cols in enumerate(spans):
        seen = cols.stop
        scores = add_diagonal(dot(k_ref[:seen], queries[t]), tiles)
        prob, d_score = back_scores(scores, lses[t], dot(v_ref[:seen], outs[t]), delta[t])
        d_value = dot(prob, do_placed[t])
        d_key = dot(d_score, q_placed[t])
        if t == 0:
            dv_whole, dk_whole = d_value, d_key
        else:
            more = seen - dv_whole.shape[0]
            dv_whole = jnp.concatenate([dv_whole + d_value[: seen - more], d_value[seen - more :]], axis=0)
            dk_whole = jnp.concatenate([dk_whole + d_key[: seen - more], d_key[seen - more :]], axis=0)
        dq_sum[t] = dot(k_turned[:, :seen], d_score)
        d_wide = d_score.astype(F32)
        total = jnp.sum(d_wide, axis=0, keepdims=True)
        base = seen - TILE
        for h in range(4):
            left, right = slice(h * TILE, h * TILE + NEAR), slice(h * TILE + NEAR, (h + 1) * TILE)
            zero_part = d_wide[base : base + NEAR, left] + d_wide[base + NEAR :, right]
            one_part = d_wide[base : base + NEAR, right]
            if t > 0:
                one_part = one_part + d_wide[base - NEAR : base, left]
            both = jnp.concatenate([zero_part, one_part], axis=1)
            part = total[:, h * TILE : (h + 1) * TILE]
            if t == 0:
                near_sum[h] = both
                total_ref[0, h : h + 1, :] = part
            else:
                near_sum[h] += both
                total_ref[0, h : h + 1, :] += part
    dk_ref[...] = dk_whole.astype(BF16)
    dv_ref[...] = dv_whole.astype(BF16)

    for s in range(earlier):

        @pl.when(valid_ref[3 + s] > 0)
        def _(s=s):
            kp_turned = kp_ref[s].T
            for t in range(steps):
                scores = dot(kp_ref[s], queries[t])
                if s == 0 and t == 0:
                    scores = add_corner(scores, tiles)
                prob, d_score = back_scores(scores, lses[t], dot(vp_ref[s], outs[t]), delta[t])
                d_value = dot(prob, do_placed[t])
                d_key = dot(d_score, q_placed[t])
                dv_whole = d_value if t == 0 else dv_whole + d_value
                dk_whole = d_key if t == 0 else dk_whole + d_key
                dq_sum[t] += dot(kp_turned, d_score)
                d_wide = d_score.astype(F32)
                total = jnp.sum(d_wide, axis=0, keepdims=True)
                for h in range(4):
                    total_ref[0, h : h + 1, :] += total[:, h * TILE : (h + 1) * TILE]
                    if s == 0 and t == 0:
                        near_sum[h, :, NEAR:] += d_wide[rows - NEAR :, h * TILE : h * TILE + NEAR]
            past_ref[s, 0] = dk_whole.astype(BF16)
            past_ref[s, 1] = dv_whole.astype(BF16)

        @pl.when(valid_ref[3 + s] == 0)
        def _(s=s):
            past_ref[s] = jnp.zeros_like(past_ref[s])

    for t, cols in enumerate(spans):
        dq_ref[cols, :] = query_rows(dq_sum[t])
    for h in range(4):
        db_ref[0, h : h + 1, :] = by_distance(near_sum[h])
    db_ref[0, 4:, :] = jnp.zeros((4, 2 * NEAR), F32)
    total_ref[0, 4:, :] = jnp.zeros((4, 2 * NEAR), F32)


def cross_forward_block(q_ref, k_ref, v_ref, own_ref, o_ref, lse_ref, *, masked):
    rows = q_ref.shape[0]
    v_turned = v_ref[...].T
    q_turned = q_ref[...].T
    spans = [slice(t * TILE, (t + 1) * TILE) for t in range(rows // TILE)]
    scores = [dot(k_ref[...], heads_of(q_turned, cols)) for cols in spans]
    if masked:
        blocked = jnp.where(own_ref[...] > 0, 0.0, NEGATIVE)
        blocked = jnp.concatenate([blocked] * 4, axis=1)
        scores = [score + blocked for score in scores]
    for t, cols in enumerate(spans):
        peak, weights, summed = soft(scores[t])
        finish(o_ref, lse_ref, cols, peak, summed, dot(v_turned, weights))


def cross_backward_block(
    q_ref, k_ref, v_ref, own_ref, do_ref, o_ref, lse_ref, dq_ref, dk_ref, dv_ref, *, masked
):
    rows = q_ref.shape[0]
    k_turned = k_ref[...].T
    q_turned = q_ref[...].T
    do_turned = do_ref[...].T
    product = (do_ref[...].astype(F32) * o_ref[...].astype(F32)).T
    spans = [slice(t * TILE, (t + 1) * TILE) for t in range(rows // TILE)]
    dk_whole, dv_whole = 0.0, 0.0
    for t, cols in enumerate(spans):
        scores = dot(k_ref[...], heads_of(q_turned, cols))
        if masked:
            blocked = jnp.where(own_ref[...] > 0, 0.0, NEGATIVE)
            scores = scores + jnp.concatenate([blocked] * 4, axis=1)
        d_prob = dot(v_ref[...], heads_of(do_turned, cols))
        prob, d_score = back_scores(scores, row_of_heads(lse_ref, cols), d_prob, deltas(product, cols))
        dv_whole = dv_whole + dot(prob, placed_heads(do_ref, cols))
        dk_whole = dk_whole + dot(d_score, placed_heads(q_ref, cols))
        dq_ref[cols, :] = query_rows(dot(k_turned, d_score))
    dk_ref[...] = dk_whole.astype(BF16)
    dv_ref[...] = dv_whole.astype(BF16)


def wide_view(ref, p):
    return ref.at[:, pl.ds(p * 4 * HEAD, 4 * HEAD)]


def slim_view(ref, p):
    return ref.at[:, pl.ds(p * 2 * HEAD, 2 * HEAD)]


def past_view(ref, p):
    return ref.at[:, :, pl.ds(p * 2 * HEAD, 2 * HEAD)]


def page_view(ref, p):
    return ref.at[pl.ds(p, 1)]


def self_diagonal(place, table, q, k, v, fetch):
    rows, blocks = q.shape[0], k.shape[1] // (2 * HEAD)
    steps = rows // TILE

    def body(place_ref, arrays, weight, outs, scratch):
        table_ref, q_ref, k_ref, v_ref = arrays
        for p in range(blocks):
            self_diagonal_block(
                page_view(table_ref, p), wide_view(q_ref, p), slim_view(k_ref, p), slim_view(v_ref, p),
                *[ref.at[p] for ref in outs],
            )

    state = [(blocks, steps, 1, 4 * TILE), (blocks, steps, 1, 4 * TILE), (blocks, steps, 2 * HEAD, 4 * TILE)]
    return whole_kernel(body, place, [table, q, k, v], [], [shaped(shape, F32) for shape in state], "self_diagonal", fetch=fetch)


def self_past(place, table, q, kp, vp, peak, summed, acc, fetch):
    rows, blocks, earlier = q.shape[0], kp.shape[2] // (2 * HEAD), kp.shape[0]

    def body(place_ref, arrays, weight, outs, scratch):
        table_ref, q_ref, kp_ref, vp_ref, peak_ref, sum_ref, acc_ref = arrays
        views = [
            (
                page_view(table_ref, p), wide_view(q_ref, p), past_view(kp_ref, p), past_view(vp_ref, p),
                peak_ref.at[p], sum_ref.at[p], acc_ref.at[p], wide_view(outs[0], p), page_view(outs[1], p),
                *([ref.at[p] for ref in scratch] if earlier > 1 else [None] * 3),
            )
            for p in range(blocks)
        ]
        self_past_blocks(place_ref, views, earlier=earlier)

    return whole_kernel(
        body,
        place,
        [table, q, kp, vp, peak, summed, acc],
        [],
        [shaped(q.shape), shaped((blocks, 8, rows), F32)],
        "self_past",
        [pltpu.VMEM(a.shape, F32) for a in (peak, summed, acc)] if earlier > 1 else [],
        fetch=fetch,
    )


def self_backward(place, table, q, k, v, kp, vp, do, o, lse, fetch):
    rows, blocks, earlier = q.shape[0], k.shape[1] // (2 * HEAD), kp.shape[0]
    steps = rows // TILE

    def body(place_ref, arrays, weight, outs, scratch):
        table_ref, q_ref, k_ref, v_ref, kp_ref, vp_ref, do_ref, o_ref, lse_ref = arrays
        dq_ref, dk_ref, dv_ref, past_ref, db_ref, total_ref = outs
        for p in range(blocks):
            self_backward_block(
                place_ref, page_view(table_ref, p), wide_view(q_ref, p), slim_view(k_ref, p), slim_view(v_ref, p),
                past_view(kp_ref, p), past_view(vp_ref, p), wide_view(do_ref, p), wide_view(o_ref, p),
                page_view(lse_ref, p), wide_view(dq_ref, p), slim_view(dk_ref, p), slim_view(dv_ref, p),
                past_ref.at[:, :, :, pl.ds(p * 2 * HEAD, 2 * HEAD)], page_view(db_ref, p), page_view(total_ref, p),
                *[ref.at[p] for ref in scratch], earlier=earlier,
            )

    return whole_kernel(
        body,
        place,
        [table, q, k, v, kp, vp, do, o, lse],
        [],
        [
            shaped(q.shape),
            shaped(k.shape),
            shaped(k.shape),
            shaped((earlier, 2) + k.shape),
            shaped(table.shape, F32),
            shaped(table.shape, F32),
        ],
        "self_backward",
        [pltpu.VMEM((blocks, 4, NEAR, 2 * NEAR), F32), pltpu.VMEM((blocks, steps, 2 * HEAD, 4 * TILE), F32)],
        fetch=fetch,
    )


def cross_forward(place, q, k, v, own):
    rows, blocks = q.shape[0], k.shape[1] // (2 * HEAD)

    def body(place_ref, arrays, weight, outs, scratch):
        q_ref, k_ref, v_ref = arrays[:3]
        for p in range(blocks):
            cross_forward_block(
                wide_view(q_ref, p), slim_view(k_ref, p), slim_view(v_ref, p), arrays[-1], wide_view(outs[0], p),
                page_view(outs[1], p), masked=len(own) > 0,
            )

    outs = [shaped(q.shape), shaped((blocks, 8, rows), F32)]
    return whole_kernel(body, place, [q, k, v] + own, [], outs, "cross_forward")


def cross_backward(place, q, k, v, own, do, o, lse, fetch):
    blocks = k.shape[1] // (2 * HEAD)

    def body(place_ref, arrays, weight, outs, scratch):
        q_ref, k_ref, v_ref, do_ref, o_ref, lse_ref = arrays[:6]
        for p in range(blocks):
            cross_backward_block(
                wide_view(q_ref, p), slim_view(k_ref, p), slim_view(v_ref, p), arrays[-1], wide_view(do_ref, p),
                wide_view(o_ref, p), page_view(lse_ref, p), wide_view(outs[0], p), slim_view(outs[1], p),
                slim_view(outs[2], p), masked=len(own) > 0,
            )

    outs = [shaped(q.shape), shaped(k.shape), shaped(k.shape)]
    return whole_kernel(body, place, [q, k, v, do, o, lse] + own, [], outs, "cross_backward", fetch=fetch)


def project(place, own, peer, gain, wq, wk, wv):
    rows, model = own.shape
    wide, slim = wq.shape[1] // CORES, wk.shape[1] // CORES

    def body(place_ref, arrays, weight, outs, scratch):
        hidden = in_place_order(place_ref[1], arrays[0], arrays[1])
        low = norm_low(hidden, inverse_norm(hidden), arrays[2][...].astype(F32))
        outs[0][...] = low
        for at in range(3):
            outs[1 + at][...] = dot(low, weight(at)[...]).astype(BF16)

    return whole_kernel(
        body,
        place,
        [own, peer, gain],
        [(wq, 1, False), (wk, 1, False), (wv, 1, False)],
        [shaped((CORES * rows, n)) for n in (model, wide, slim, slim)],
        "project",
    )


def project_past(place, owns, peers, gain, wk, wv, fetch):
    rows, model = owns[0].shape
    earlier = len(owns)
    slim = wk.shape[1] // CORES

    def body(place_ref, arrays, weight, outs, scratch):
        own_refs, peer_refs = arrays[:earlier], arrays[earlier : 2 * earlier]
        gain_value = arrays[-1][...].astype(F32)
        for s in range(earlier):
            hidden = in_place_order(place_ref[1], own_refs[s], peer_refs[s])
            low = norm_low(hidden, inverse_norm(hidden), gain_value)
            outs[s][...] = low
            outs[earlier][s] = dot(low, weight(0)[...]).astype(BF16)
            outs[earlier + 1][s] = dot(low, weight(1)[...]).astype(BF16)

    made = whole_kernel(
        body,
        place,
        owns + peers + [gain],
        [(wk, 1, False), (wv, 1, False)],
        [shaped((CORES * rows, model))] * earlier + [shaped((earlier, CORES * rows, slim))] * 2,
        "project_past",
        fetch=fetch,
    )
    return made[:earlier], *made[earlier:]


def project_memory(place, mems, wk, wv):
    groups = len(mems)
    rows, model = mems[0].shape
    slim = wk.shape[1] // CORES

    def body(place_ref, arrays, weight, outs, scratch):
        for at, piece_ref in enumerate(arrays):
            block = jnp.bitwise_xor(place_ref[2], jnp.int32(at))
            outs[0][pl.ds(pl.multiple_of(block * rows, rows), rows)] = piece_ref[...]
        mem = outs[0][...]
        outs[1][...] = dot(mem, weight(0)[...]).astype(BF16)
        outs[2][...] = dot(mem, weight(1)[...]).astype(BF16)

    return whole_kernel(
        body,
        place,
        mems,
        [(wk, 1, False), (wv, 1, False)],
        [shaped((groups * rows, n)) for n in (model, slim, slim)],
        "project_memory",
        cost=8,
    )


def mid_forward(place, own, peer, att, att_peer, gain, wo, wo_peer, wq):
    rows, model = own.shape

    def body(place_ref, arrays, weight, outs, scratch):
        own_ref, peer_ref, att_ref, att_peer_ref, gain_ref = arrays
        hidden = in_place_order(place_ref[1], own_ref, peer_ref)
        hidden = hidden + dot(att_ref[...], weight(0)[...]) + dot(att_peer_ref[...], weight(1)[...])
        outs[0][...] = hidden.astype(BF16)
        low = norm_low(hidden, inverse_norm(hidden), gain_ref[...].astype(F32))
        outs[1][...] = low
        outs[2][...] = dot(low, weight(2)[...]).astype(BF16)

    return whole_kernel(
        body,
        place,
        [own, peer, att, att_peer, gain],
        [wo, wo_peer, wq],
        [shaped((CORES * rows, model))] * 2 + [shaped((CORES * rows, wq.shape[1]))],
        "mid_forward",
    )


def cotangent_inner(place, cot, cot_peer, wd):
    rows, model = cot.shape

    def body(place_ref, arrays, weight, outs, scratch):
        value = in_place_order(place_ref[1], arrays[0], arrays[1]).astype(BF16)
        outs[0][...] = pick(place_ref[1], value, 1)
        outs[1][...] = dot_right(value, weight(0)[...]).astype(BF16)

    outs = [shaped((CORES * rows, model // CORES)), shaped((CORES * rows, wd.shape[0]))]
    return whole_kernel(body, place, [cot, cot_peer], [wd], outs, "cotangent_inner", cost=8)


def ffn(place, mid, crs, crs_peer, gain, d_inner, wc, wc_peer, wg, wu):
    rows, model = mid.shape
    hidden_half = wg.shape[1]
    steps = [256] * (hidden_half // 256) + [hidden_half % 256] * (hidden_half % 256 > 0)
    scale = 0.7978845608028654

    def body(place_ref, arrays, weight, outs, scratch):
        mid_ref, crs_ref, crs_peer_ref, gain_ref, d_inner_ref = arrays
        late_ref, low_ref, inner_ref, dg_ref, du_ref, dz_ref = outs
        hidden = mid_ref[...].astype(F32) + dot(crs_ref[...], weight(0)[...]) + dot(crs_peer_ref[...], weight(1)[...])
        late_ref[...] = hidden.astype(BF16)
        low = norm_low(hidden, inverse_norm(hidden), gain_ref[...].astype(F32))
        low_ref[...] = low
        start = 0
        for width in steps:
            cols = slice(start, start + width)
            start += width
            gate = dot(low, weight(2)[:, cols])
            up = dot(low, weight(3)[:, cols])
            d_inner = d_inner_ref[:, cols].astype(F32)
            square = gate * gate
            bent = jnp.tanh(gate * (scale + (scale * 0.044715) * square))
            whole = 0.5 + 0.5 * bent
            slope = whole + (0.5 * gate) * (1.0 - bent * bent) * (scale + (3 * scale * 0.044715) * square)
            curve = gate * whole
            inner_ref[:, cols] = (curve * up).astype(BF16)
            dg_ref[:, cols] = (d_inner * up * slope).astype(BF16)
            du_ref[:, cols] = (d_inner * curve).astype(BF16)
        dz_ref[...] = (dot_right(dg_ref[...], weight(2)[...]) + dot_right(du_ref[...], weight(3)[...])).astype(BF16)

    return whole_kernel(
        body,
        place,
        [mid, crs, crs_peer, gain, d_inner],
        [wc, wc_peer, wg, wu],
        [shaped((rows, model))] * 2
        + [shaped((rows, hidden_half))] * 3
        + [shaped((rows, model))],
        "ffn",
        room=16 * 1024 * 1024,
    )


def late_backward(place, dz, dz_peer, late, cot, cot_peer, gain, wc):
    rows, model = late.shape

    def body(place_ref, arrays, weight, outs, scratch):
        dz_ref, dz_peer_ref, late_ref, cot_ref, cot_peer_ref, gain_ref = arrays
        dz_value = dz_ref[...].astype(F32) + dz_peer_ref[...].astype(F32)
        hidden = late_ref[...].astype(F32)
        inverse = inverse_norm(hidden)
        outs[3][...] = jnp.sum(dz_value * hidden * inverse, axis=0, keepdims=True)
        grad = in_place_order(place_ref[1], cot_ref, cot_peer_ref)
        grad = grad + norm_back(hidden, inverse, gain_ref[...].astype(F32), dz_value)
        low = grad.astype(BF16)
        outs[0][...] = low
        outs[1][...] = pick(place_ref[1], low, 1)
        outs[2][...] = dot_right(low, weight(0)[...]).astype(BF16)

    return whole_kernel(
        body,
        place,
        [dz, dz_peer, late, cot, cot_peer, gain],
        [wc],
        [
            shaped((rows, model)),
            shaped((rows, model // CORES)),
            shaped((rows, wc.shape[0])),
            shaped((1, model), F32),
        ],
        "late_backward",
    )


def mid_backward(place, dq, dq_peer, mid, g_late, gain, wq, wq_peer, wo):
    rows, model = mid.shape

    def body(place_ref, arrays, weight, outs, scratch):
        dq_ref, dq_peer_ref, mid_ref, g_ref, gain_ref = arrays
        dz = dot_right(dq_ref[...], weight(0)[...]) + dot_right(dq_peer_ref[...], weight(1)[...])
        hidden = mid_ref[...].astype(F32)
        inverse = inverse_norm(hidden)
        outs[3][...] = jnp.sum(dz * hidden * inverse, axis=0, keepdims=True)
        grad = g_ref[...].astype(F32) + norm_back(hidden, inverse, gain_ref[...].astype(F32), dz)
        low = grad.astype(BF16)
        outs[0][...] = pick(place_ref[1], low, 0)
        outs[1][...] = pick(place_ref[1], low, 1)
        outs[2][...] = dot_right(low, weight(2)[...]).astype(BF16)

    return whole_kernel(
        body,
        place,
        [dq, dq_peer, mid, g_late, gain],
        [wq, wq_peer, wo],
        [
            shaped((rows // CORES, model)),
            shaped((rows, model // CORES)),
            shaped((rows, wo.shape[0])),
            shaped((1, model), F32),
        ],
        "mid_backward",
    )


def first_backward(place, dz, past, riders, mem_parts, wk, wv):
    rows, model = dz.shape
    slim = wk.shape[1]
    own_rows = rows // CORES
    joint = riders is not None
    mem_rows = mem_parts.shape[0] // (CORES * CORES) if joint else 0

    def body(place_ref, arrays, weight, outs, scratch):
        core = place_ref[1]
        pairs = []
        if joint:
            past_at, mem_at = past[0][1], riders[0][1]
            blocks = [arrays[1][past_at + at * rows : past_at + (at + 1) * rows] for at in range(2 * slim // LANES)]
            pairs.append((jnp.concatenate(blocks[: slim // LANES], 1), jnp.concatenate(blocks[slim // LANES :], 1)))
        else:
            pairs += [(ref[0], ref[1]) for ref in arrays[1:]]
        total = arrays[0][...].astype(F32)
        for dk, dv in pairs:
            total = total + dot_right(dk, weight(0)[...]) + dot_right(dv, weight(1)[...])
        outs[0][...] = pick(core, total, 0)
        outs[1][:own_rows] = pick(core, total, 0, True).astype(BF16)
        if joint:
            half = CORES * mem_rows
            mine = pick(place_ref[2] // CORES, arrays[3][...].astype(F32), 0)
            got = [arrays[2][mem_at + at * half : mem_at + (at + 1) * half].astype(F32) for at in range(model // LANES)]
            mine = mine + jnp.concatenate(got, axis=1)
            outs[2][...] = pick(core, mine, 0)
            outs[1][own_rows:] = pick(core, mine, 0, True).astype(BF16)

    outs = [shaped((own_rows, model), F32), shaped((own_rows + mem_rows, model))]
    if joint:
        outs.append(shaped((mem_rows, model), F32))
    return whole_kernel(
        body, place, [dz] + ([past[0][0], riders[0][0], mem_parts] if joint else past), [wk, wv], outs, "first_backward"
    )


def tokens_backward(place, dz, dz_got, mem, tokens, g_mid, gain):
    rows = tokens.shape[0]

    def body(place_ref, arrays, weight, outs, scratch):
        dz_ref, dz_got_ref, tokens_ref, g_ref, gain_ref = arrays[:5]
        dz_value = dz_ref[...] + dz_got_ref[:rows].astype(F32)
        hidden = tokens_ref[...].astype(F32)
        grad = norm_back(hidden, inverse_norm(hidden), gain_ref[...].astype(F32), dz_value)
        outs[0][...] = (g_ref[...].astype(F32) + grad).astype(BF16)
        if mem:
            outs[1][...] = (arrays[5][...] + dz_got_ref[rows:].astype(F32)).astype(BF16)

    outs = [shaped(tokens.shape)] + [shaped(m.shape) for m in mem]
    return whole_kernel(body, place, [dz, dz_got, tokens, g_mid, gain] + mem, [], outs, "tokens_backward")


def layer_output(place, late, inner, inner_peer, wd):
    rows, model = late.shape

    def body(place_ref, arrays, weight, outs, scratch):
        own, inner_own, inner_other = (pick(place_ref[1], ref[...], 0) for ref in arrays)
        total = own.astype(F32) + dot(inner_own, weight(0)[...]) + dot(inner_other, weight(1)[...])
        outs[0][...] = total.astype(BF16)

    return whole_kernel(
        body,
        place,
        [late, inner, inner_peer],
        [(wd, 0, False), (wd, 0, True)],
        [shaped((rows // CORES, model))],
        "layer_output",
        cost=10,
    )[0]


def memory_backward(place, dk, dv, wk, wv):
    def body(place_ref, arrays, weight, outs, scratch):
        grad = dot_right(arrays[0][...], weight(0)[...]) + dot_right(arrays[1][...], weight(1)[...])
        outs[0][...] = grad.astype(BF16)

    weights = [(wk, 1, False), (wv, 1, False)]
    return whole_kernel(body, place, [dk, dv], weights, [shaped((dk.shape[0], wk.shape[0]))], "memory_backward")[0]


def small_sums(place, dq, dk, dv, d_past, own, peer, past_own, past_peer, two, three, near, total, buckets, weights, chips):
    rows, model = dq.shape[0], own.shape[1]
    earlier = len(past_own)
    heads = HEADS // CORES

    def body(place_ref, arrays, weight, outs, scratch):
        dq_ref, dk_ref, dv_ref, past_ref, own_ref, peer_ref = arrays[:6]
        past_own_refs, past_peer_refs = arrays[6 : 6 + earlier], arrays[6 + earlier : 6 + 2 * earlier]
        two_ref, three_ref, near_ref, total_ref, bucket_ref = arrays[6 + 2 * earlier :]
        core = place_ref[1]
        first = core == 0

        def gain_part(dz, own_ref, peer_ref):
            hidden = in_place_order(core, own_ref, peer_ref)
            return jnp.sum(dz * (hidden * inverse_norm(hidden)), axis=0, keepdims=True)

        dz = dot_right(dq_ref[...], weight(0)[...])
        dz = dz + dot_right(dk_ref[...], weight(1)[...]) + dot_right(dv_ref[...], weight(2)[...])
        outs[0][...] = dz.astype(BF16)
        one = gain_part(dz, own_ref, peer_ref)
        for s in range(earlier):
            dz = dot_right(past_ref[s, 0], weight(1)[...]) + dot_right(past_ref[s, 1], weight(2)[...])
            one = one + gain_part(dz, past_own_refs[s], past_peer_refs[s])
        gains = [one, jnp.where(first, two_ref[...], 0.0), jnp.where(first, three_ref[...], 0.0)]
        near = jnp.concatenate([near_ref[p, :4] for p in range(heads // 4)], axis=0)
        total = jnp.concatenate([total_ref[p, :4] for p in range(heads // 4)], axis=0)
        far = jnp.sum(total, axis=1, keepdims=True) - jnp.sum(near, axis=1, keepdims=True)
        last = lax.broadcasted_iota(jnp.int32, near.shape, 1) == near.shape[1] - 1
        near = near + jnp.where(last, far, 0.0)
        entries = BUCKETS * HEADS
        entry = lax.broadcasted_iota(jnp.int32, (near.shape[1], entries), 1)
        same = (lax.shift_right_logical(entry, jnp.int32(HEADS.bit_length() - 1)) == bucket_ref[...]).astype(F32)
        sums = jnp.dot(near, same, precision=lax.Precision.HIGHEST, preferred_element_type=F32)
        head = lax.broadcasted_iota(jnp.int32, sums.shape, 0) + core * heads
        of_entry = jnp.bitwise_and(lax.broadcasted_iota(jnp.int32, sums.shape, 1), jnp.int32(HEADS - 1))
        vectors = gains + [jnp.sum(jnp.where(head == of_entry, sums, 0.0), axis=0, keepdims=True)]
        for block in range(chips):
            lines = []
            for vector in vectors:
                size = vector.shape[1] // chips
                line = vector[:, block * size : (block + 1) * size]
                lines.append(jnp.concatenate([line, jnp.zeros((1, LANES - size), F32)], axis=1))
            lines.append(jnp.zeros((12, LANES), F32))
            outs[1][block * 16 : (block + 1) * 16] = jnp.concatenate(lines, axis=0).astype(BF16)

    arrays = [dq, dk, dv, d_past, own, peer] + past_own + past_peer + [two, three, near, total, buckets]
    return whole_kernel(
        body, place, arrays, weights, [shaped((rows, model)), shaped((chips * 16, LANES))], "small_sums"
    )


def gather_sums(place, parts, name):
    def body(place_ref, arrays, weight, outs, scratch):
        for array, out in zip(arrays, outs):
            total = array[0].astype(F32)
            for at in range(1, array.shape[0]):
                total = total + array[at].astype(F32)
            out[...] = total.astype(out.dtype)

    return whole_kernel(body, place, parts, [], [shaped(a.shape[1:], a.dtype) for a in parts], name)


def up_to(value, multiple):
    return (value + multiple - 1) // multiple * multiple


def array_of(y):
    return y[0] if isinstance(y, tuple) else y


class Flow:
    def __init__(self, name, pieces, order, extra=None):
        self.name, self.pieces, self.order, self.extra = name, pieces, order, extra
        self.hops = [bit + 1 for bit in order]
        self.chips = 1 << len(order)
        self.layout = []
        start = 0
        for terms, rows in pieces:
            half = rows // self.chips // CORES
            padded = up_to(half, 8)
            width = array_of(terms[0][1]).shape[-1]
            self.layout.append((start, half, padded, width))
            start += CORES * padded * (width // LANES)
        self.extra_at = start
        self.rows = start + (16 if extra is not None else 0)
        self.keep = self.got = None

    def spread(self, x):
        half, padded = self.layout[0][1:3]
        if half == padded:
            return x
        chunks = x.reshape(x.shape[0], -1, half)
        return jnp.pad(chunks, ((0, 0), (0, 0), (0, padded - half))).reshape(x.shape[0], -1)


def chip_of(spot, order):
    number = 0
    for at, bit in enumerate(order):
        number |= (spot >> (len(order) - 1 - at) & 1) << bit
    return number


def sum_flow(flow, refs_of, place_ref, turned, free, send_ref, base, keep_ref):
    chip, core = place_ref[0], place_ref[1]
    half = flow.chips // 2
    for (terms, _), (start, _, padded, width) in zip(flow.pieces, flow.layout):
        chunk = CORES * padded
        lefts = []
        for xs, y in terms:
            key = (tuple(id(x) for x in xs), flow.order)
            if key not in turned:
                straight_ref, turned[key] = free.pop(0), free.pop(0)
                if len(xs) == 1:
                    straight_ref[...] = refs_of[id(xs[0])][...].T
                else:
                    size = straight_ref.shape[0] // CORES
                    for part, x in enumerate(xs):
                        at = (core if part == 0 else 1 - core) * size
                        straight_ref[pl.ds(pl.multiple_of(at, 16), size)] = refs_of[id(x)][...].T
                for spot in range(flow.chips):
                    at = jnp.bitwise_xor(jnp.int32(chip_of(spot, flow.order)), chip) * chunk
                    turned[key][spot * chunk : (spot + 1) * chunk] = straight_ref[pl.ds(pl.multiple_of(at, 16), chunk)]
            lefts.append(turned[key])
        count = max(1, min(flow.chips, 512 // chunk))
        while flow.chips % count:
            count -= 1
        for first in range(0, flow.chips, count):
            tile = None
            for left, (_, y) in zip(lefts, terms):
                y_ref = refs_of[id(array_of(y))]
                y_value = y_ref[y[1]] if isinstance(y, tuple) else y_ref[...]
                term = dot(left[first * chunk : (first + count) * chunk], y_value)
                tile = term if tile is None else tile + term
            tile = tile.astype(BF16)
            for inner in range(count):
                spot = first + inner
                for block in range(width // LANES):
                    value = tile[inner * chunk : (inner + 1) * chunk, block * LANES : (block + 1) * LANES]
                    at = start + block * chunk
                    if spot < half:
                        keep_ref[spot, at : at + chunk] = value
                    else:
                        at += base + (spot - half) * flow.rows
                        send_ref[at : at + chunk] = value


def copy_extra(flow, extra_ref, place_ref, send_ref, base, keep_ref):
    half = flow.chips // 2
    for spot in range(flow.chips):
        at = jnp.bitwise_xor(jnp.int32(chip_of(spot, flow.order)), place_ref[0]) * 16
        value = extra_ref[pl.ds(pl.multiple_of(at, 16), 16)]
        if spot < half:
            keep_ref[spot, flow.extra_at : flow.extra_at + 16] = value
        else:
            to = base + (spot - half) * flow.rows + flow.extra_at
            send_ref[to : to + 16] = value


def add_flow(flow, old_ref, got_ref, got_at, send_ref, base, keep_ref):
    half = old_ref.shape[0] // 2
    for spot in range(2 * half):
        at = got_at + spot * flow.rows
        total = (old_ref[spot].astype(F32) + got_ref[at : at + flow.rows].astype(F32)).astype(BF16)
        if spot < half:
            keep_ref[spot] = total
        else:
            send_ref[base + (spot - half) * flow.rows : base + (spot - half + 1) * flow.rows] = total


def hop(place, swap, sums, adds, after, name, cost=0, riders=()):
    arrays, seen = [], {}

    def take(array):
        if id(array) not in seen:
            seen[id(array)] = len(arrays)
            arrays.append(array)

    for flow in sums:
        for terms, _ in flow.pieces:
            for xs, y in terms:
                for array in (*xs, array_of(y)):
                    take(array)
        if flow.extra is not None:
            take(flow.extra)
    for flow in adds:
        take(flow.keep)
        take(flow.got[0])
    bits, sends, keeps = {}, {}, {}
    for flow in sums + adds:
        half = (flow.chips if flow in sums else flow.keep.shape[0]) // 2
        bit = flow.hops[0]
        base = bits.setdefault(bit, 0)
        sends[flow.name] = (bit, base)
        bits[bit] = base + half * flow.rows
        keeps[flow.name] = shaped((half, flow.rows, LANES))
    rider_at = []
    for rider, bit, size, _ in riders:
        take(rider)
        rider_at.append(bits.setdefault(bit, 0))
        bits[bit] = rider_at[-1] + size
    order = list(bits)
    outs = [shaped((bits[bit], LANES)) for bit in order] + list(keeps.values())

    def body(place_ref, refs, weight, out_refs, scratch):
        refs_of = {key: refs[at] for key, at in seen.items()}
        turned, free = {}, list(scratch)
        for at, flow in enumerate(sums + adds):
            bit, base = sends[flow.name]
            send_ref, keep_ref = out_refs[order.index(bit)], out_refs[len(order) + at]
            if flow in sums:
                sum_flow(flow, refs_of, place_ref, turned, free, send_ref, base, keep_ref)
                if flow.extra is not None:
                    copy_extra(flow, refs_of[id(flow.extra)], place_ref, send_ref, base, keep_ref)
            else:
                add_flow(
                    flow, refs_of[id(flow.keep)], refs_of[id(flow.got[0])], flow.got[1], send_ref, base, keep_ref
                )
        for (rider, bit, _, write), at in zip(riders, rider_at):
            write(refs_of[id(rider)], out_refs[order.index(bit)], at, place_ref)

    needed = {}
    for flow in sums:
        for terms, _ in flow.pieces:
            for xs, _ in terms:
                shape = (sum(x.shape[1] for x in xs), xs[0].shape[0])
                needed[(tuple(id(x) for x in xs), flow.order)] = [pltpu.VMEM(shape, BF16)] * 2
    scratch = sum(needed.values(), [])
    made = whole_kernel(body, place, follow(arrays, after), [], outs, name, scratch, cost=cost)
    moved = [swap(array, bit) for array, bit in zip(made, order)]
    for at, flow in enumerate(sums + adds):
        bit, base = sends[flow.name]
        flow.keep, flow.got, flow.hops = made[len(order) + at], (moved[order.index(bit)], base), flow.hops[1:]
    if riders:
        return list(made), (moved[order.index(riders[0][1])], *rider_at)
    return list(made)


def write_past(past_ref, send_ref, at, place_ref):
    _, pages, rows, width = past_ref.shape
    for page in range(pages):
        for block in range(width // LANES):
            send_ref[at : at + rows] = past_ref[0, page, :, block * LANES : (block + 1) * LANES]
            at += rows


def write_memory(mem_ref, send_ref, at, place_ref):
    rows = mem_ref.shape[0] // CORES
    there = pl.ds(pl.multiple_of((1 - place_ref[2] // CORES) * rows, rows), rows)
    for block in range(mem_ref.shape[1] // LANES):
        send_ref[at : at + rows] = mem_ref[there, block * LANES : (block + 1) * LANES]
        at += rows


def last_hop(place, swap, flows, after, name, shares=()):
    arrays, seen = [], {}
    for flow in flows:
        for array in (flow.keep, flow.got[0]):
            if id(array) not in seen:
                seen[id(array)] = len(arrays)
                arrays.append(array)
    blocks = []
    size = 0
    for f, flow in enumerate(flows):
        for piece, (start, half, padded, width) in enumerate(flow.layout):
            for block in range(width // LANES):
                blocks.append((f, piece, start + block * CORES * padded, padded, block, size))
                size += up_to(padded, 16)
    extras = [(f, flow.extra_at, size + 16 * sum(x.extra is not None for x in flows[:f])) for f, flow in enumerate(flows) if flow.extra is not None]
    size += 16 * len(extras)
    own_outs = [
        shaped((padded, width), F32) for flow in flows for _, _, padded, width in flow.layout
    ]
    own_outs += [shaped((16, LANES), F32) for _ in extras]
    n_pieces = len(own_outs) - len(extras)
    first = [sum(len(flow.layout) for flow in flows[:f]) for f in range(len(flows))]

    def add_body(place_ref, refs, weight, outs, scratch):
        core = place_ref[1]
        for f, piece, at, padded, block, leave_at in blocks:
            flow = flows[f]
            got_at = flow.got[1] + at
            total = refs[seen[id(flow.keep)]][0, at : at + CORES * padded].astype(F32)
            total = total + refs[seen[id(flow.got[0])]][got_at : got_at + CORES * padded].astype(F32)
            own, leave = pick(core, total, 0), pick(core, total, 0, True)
            outs[1 + first[f] + piece][:, block * LANES : (block + 1) * LANES] = own
            full = up_to(padded, 16)
            if full > padded:
                leave = jnp.concatenate([leave, jnp.zeros((full - padded, LANES), F32)], axis=0)
            outs[0][leave_at : leave_at + full] = leave.astype(BF16)
        for at, (f, start, leave_at) in enumerate(extras):
            flow = flows[f]
            got_at = flow.got[1] + start
            total = refs[seen[id(flow.keep)]][0, start : start + 16].astype(F32)
            total = total + refs[seen[id(flow.got[0])]][got_at : got_at + 16].astype(F32)
            outs[1 + n_pieces + at][...] = total
            outs[0][leave_at : leave_at + 16] = total.astype(BF16)

    made = whole_kernel(add_body, place, follow(arrays, after), [], [shaped((size, LANES))] + own_outs, "last_" + name)
    got = swap(made[0], 0)

    def join_body(place_ref, refs, weight, outs, scratch):
        core = place_ref[1]
        for f, piece, _, padded, block, leave_at in blocks:
            at = first[f] + piece
            width = refs[1 + at].shape[1]
            own = refs[1 + at][:, block * LANES : (block + 1) * LANES]
            other = refs[0][leave_at : leave_at + up_to(padded, 16)].astype(F32)[:padded]
            low, high = slice(block * LANES, (block + 1) * LANES), slice(width + block * LANES, width + (block + 1) * LANES)
            outs[at][:, low] = jnp.where(core == 0, own, other)
            outs[at][:, high] = jnp.where(core == 0, other, own)
        for at, (_, _, leave_at) in enumerate(extras):
            total = refs[1 + n_pieces + at][...] + refs[0][leave_at : leave_at + 16].astype(F32)
            for line, (out, share) in enumerate(zip(outs[n_pieces:], shares)):
                out[...] = jnp.where(core == 0, total[line, :share], total[line, share : 2 * share])

    joined = whole_kernel(
        join_body,
        place,
        [got] + list(made[1:]),
        [],
        [shaped((a.shape[0], CORES * a.shape[1]), F32) for a in own_outs[:n_pieces]]
        + [shaped((share,), F32) for _ in extras for share in shares],
        "join_" + name,
    )
    results = {}
    for f, flow in enumerate(flows):
        results[flow.name] = [
            joined[first[f] + piece][:half] for piece, (_, half, _, _) in enumerate(flow.layout)
        ]
    if extras:
        results["small"] = joined[n_pieces:]
    return results, list(made)


def follow(value, after):
    return lax.optimization_barrier((value, after))[0]


def rel_bucket(distance):
    beyond = 16 + sum((distance >= border).astype(jnp.int32) for border in THRESHOLDS)
    return jnp.where(distance < 16, distance, beyond)


def shards(
    tokens, memory, cotangent, bucket, gain_self, self_query, self_key, self_value, self_out, rel_bias,
    gain_cross, cross_query, cross_key, cross_value, cross_out, gain_ffn, ffn_gate, ffn_up, ffn_down,
):
    groups = lax.axis_size("grp")
    dp_size = lax.axis_size("dp")
    n_chips = groups // CORES
    more = n_chips - 1
    chips = dp_size * n_chips
    devices = chips * CORES
    grp_at = lax.axis_index("grp")
    core = grp_at % CORES
    y_at = grp_at // CORES
    chip = lax.axis_index("dp") * n_chips + y_at
    rows, model = tokens.shape
    chip_rows = rows * CORES
    group_rows = chip_rows * n_chips
    hidden_units = ffn_down.shape[0]
    length = jnp.minimum(group_rows, jnp.maximum(SHORT, jnp.right_shift(jnp.int32(group_rows), bucket[0])))
    y_bits = n_chips.bit_length() - 1
    bits = chips.bit_length() - 1
    first_chip = y_at * chip_rows // length * length // chip_rows
    valid = [(y_at - s >= first_chip).astype(jnp.int32) for s in range(1, n_chips)]
    place = jnp.stack([chip, core, grp_at] + valid).astype(jnp.int32)

    def swap(v, bit):
        return lax.ppermute(v, ("dp", "grp"), [(i, i ^ (1 << bit)) for i in range(devices)])

    gain_one, gain_two, gain_three = (g.reshape(1, model) for g in (gain_self, gain_cross, gain_ffn))

    past_own = [
        lax.ppermute(tokens, "grp", [(g, g + CORES * s) for g in range(groups - CORES * s)]) for s in range(1, n_chips)
    ]
    tokens_peer = swap(tokens, 0)
    mems = [memory] + [
        lax.ppermute(memory, "grp", [(g, g ^ other) for g in range(groups)]) for other in range(1, groups)
    ]

    distances = jnp.arange(2 * NEAR, dtype=jnp.int32)
    buckets = rel_bucket(distances)[:, None]
    onehot = (buckets == jnp.arange(BUCKETS, dtype=jnp.int32)).astype(F32)
    heads = HEADS // CORES
    rel_local = lax.dynamic_slice_in_dim(rel_bias.astype(F32), core * heads, heads, 1)
    by_dist = jnp.dot(onehot, rel_local - rel_local[BUCKETS - 1 :], precision=lax.Precision.HIGHEST)
    table = jnp.pad(by_dist.T.reshape(heads // 4, 4, 2 * NEAR), ((0, 0), (0, 4), (0, 0)))

    low_one, q, k, v = project(place, tokens, tokens_peer, gain_one, self_query, self_key, self_value)
    *diagonal, w_gate, w_up = self_diagonal(place, table, q, k, v, [(ffn_gate, 1, False), (ffn_up, 1, False)])
    past_own = follow(past_own, diagonal)
    past_peer = [swap(own, 0) for own in past_own]
    cot_peer = swap(follow(cotangent, diagonal[0]), 0)
    low_past, k_past, v_past, w_down = project_past(
        place, past_own, past_peer, gain_one, self_key, self_value, [(ffn_down, 0, False)]
    )
    att, lse_self, w_out, w_out_peer, w_query, w_cross, w_cross_peer = self_past(
        place, table, q, k_past, v_past, *diagonal,
        [(self_out, 0, False), (self_out, 0, True), (cross_query, 1, False), (cross_out, 0, False), (cross_out, 0, True)],
    )
    att_peer = swap(att, 0)
    mem_all, km, vm = project_memory(place, follow(mems, att), cross_key, cross_value)
    att_peer = follow(att_peer, km)
    mid, low_two, cq = mid_forward(
        place, tokens, tokens_peer, att, att_peer, gain_two, w_out, w_out_peer, w_query
    )
    own_doc = []
    if group_rows > SHORT:
        mem_doc = jnp.arange(mem_all.shape[0], dtype=jnp.int32) // (length // RATIO)
        own = (mem_doc == y_at * chip_rows // length).astype(F32)
        own_doc = [jnp.broadcast_to(own[:, None], (mem_all.shape[0], TILE))]
    crs, lse_cross = cross_forward(place, cq, km, vm, own_doc)
    crs_peer = swap(crs, 0)
    cot_half, d_inner = cotangent_inner(place, follow(cotangent, crs), cot_peer, w_down)
    crs_peer = follow(crs_peer, d_inner)
    late, low_three, inner, d_gate, d_up, dz = ffn(
        place, mid, crs, crs_peer, gain_three, d_inner, w_cross, w_cross_peer, w_gate, w_up
    )

    axes = {
        "y": tuple(range(y_bits)),
        "x": (y_bits,),
        "z": (y_bits + 1,),
        "f": tuple(range(y_bits + 2, bits)),
    }

    def order_of(letters):
        return sum((axes[letter] for letter in letters), ())

    dz_peer = swap(dz, 0)
    inner_peer = swap(inner, 0)
    gate = Flow("gate", [([((low_three,), d_gate)], model)], order_of("xyzf"))
    up = Flow("up", [([((low_three,), d_up)], model)], order_of("yzfx"))
    last = hop(place, swap, [gate], [], place, "gate")
    last = hop(place, swap, [up], [], last, "up")
    down = Flow("down", [([((inner, inner_peer), cot_half)], hidden_units)], order_of("zxyf"))
    spread = (down.spread(inner), down.spread(inner_peer))
    down = Flow("down", [([(spread, cot_half)], hidden_units)], order_of("zxyf"))
    last = hop(place, swap, [down], [], last, "down")
    ffn_flows = [gate, up, down]

    g_late, late_half, d_crs, d_gain_three = late_backward(
        place, follow(dz, last), dz_peer, late, cotangent, cot_peer, gain_three, w_cross
    )
    dcq, dkm, dvm, w_query_peer = cross_backward(
        place, cq, km, vm, own_doc, d_crs, crs, lse_cross, [(cross_query, 1, True)]
    )
    dcq_peer = swap(dcq, 0)
    crs_mem = Flow(
        "crs_mem",
        [([((crs, crs_peer), late_half)], model), ([((mem_all,), dkm)], model), ([((mem_all,), dvm)], model)],
        order_of("zxyf"),
    )
    last = hop(place, swap, [crs_mem], [], dcq, "crs_mem", cost=5)
    g_mid, mid_half, d_att, d_gain_two = mid_backward(
        place, dcq, follow(dcq_peer, last), mid, g_late, gain_two, w_query, w_query_peer, w_out
    )
    att_cq = Flow("att_cq", [([((att, att_peer), mid_half)], model), ([((low_two,), dcq)], model)], order_of("xyzf"))
    last = hop(place, swap, [att_cq], [], d_att, "att_cq")
    dq, dk, dv, d_past, d_near, d_total, *w_first = self_backward(
        place, table, q, k, v, k_past, v_past, follow(d_att, last), att, lse_self,
        [(self_query, 1, False), (self_key, 1, False), (self_value, 1, False)],
    )
    mem_parts = memory_backward(place, follow(dkm, dq), dvm, cross_key, cross_value)
    past_moved, riders = [], None
    if n_chips == 2:
        y_bit = 1
        last, riders = hop(
            place, swap, [], ffn_flows, mem_parts, "ffn_1",
            riders=[(mem_parts, y_bit, mem_parts.size // CORES // LANES, write_memory)],
        )
    else:
        past_moved = [
            lax.ppermute(d_past[s - 1], "grp", [(g, g - CORES * s) for g in range(CORES * s, groups)])
            for s in range(1, n_chips)
        ]
        last = hop(place, swap, [], ffn_flows, mem_parts, "ffn_1")
    dz, small = small_sums(
        place, follow(dq, last), dk, dv, d_past, tokens, tokens_peer, past_own, past_peer, d_gain_two, d_gain_three,
        d_near, d_total, buckets, w_first, chips,
    )
    query = Flow("query", [([((low_one,), dq)], model)], order_of("xyzf"), small)
    kv = Flow(
        "kv",
        [
            ([((low_one,), d)] + [((low_past[s],), (d_past, (s, which))) for s in range(more)], model)
            for which, d in ((0, dk), (1, dv))
        ],
        order_of("yxzf"),
    )
    attention = [att_cq, crs_mem, query, kv]
    last = hop(place, swap, [query, kv], [att_cq, crs_mem], dz, "attention_1", cost=5)

    results = {}
    names = {"ffn": ffn_flows, "attention": attention}

    def step(label, after, riders=()):
        flows = names[label]
        if label in results:
            return after
        moving = [flow for flow in flows if flow.hops]
        if moving:
            return hop(place, swap, [], moving, after, f"{label}_{len(moving[0].hops)}", cost=30, riders=riders)
        results[label], made = last_hop(place, swap, flows, after, label, [model // devices] * 3 + [BUCKETS * HEADS // devices])
        return made

    for label in ("ffn", "attention", "ffn"):
        last = step(label, last)
    if n_chips == 2:
        last, past_rider = step("attention", last, [(d_past, y_bit, d_past.size // LANES, write_past)])
        past_moved, riders = [past_rider], [riders]
    else:
        last = step("attention", last)
    waiting = True
    while len(results) < 2:
        if "attention" not in results and not any(flow.hops for flow in attention):
            last = last + sum(results.get("ffn", {}).values(), [])
        last = step("ffn", last)
        if waiting and not any(flow.hops for flow in attention):
            waiting = False
            dz_own, dz_leave, *mem_own = first_backward(
                place, follow(dz, last), past_moved, riders, mem_parts, *w_first[1:]
            )
            dz_got = swap(dz_leave, 0)
            layer_out = layer_output(place, follow(late, dz_leave), inner, inner_peer, ffn_down)
            dz_got = follow(dz_got, layer_out)
            grad_tokens, *grad_memory = tokens_backward(place, dz_own, dz_got, mem_own, tokens, g_mid, gain_one)
            if not grad_memory:
                parts = lax.all_to_all(mem_parts, "grp", split_axis=0, concat_axis=0, tiled=True)
                grad_memory = gather_sums(place, [parts.reshape(groups, -1, model)], "memory_sums")
            last = last + [grad_tokens]
        last = step("attention", last)
    got = {**results["ffn"], **results["attention"]}
    *gains, relative = got["small"]
    return (
        layer_out,
        grad_tokens,
        grad_memory[0],
        gains[0],
        got["query"][0],
        got["kv"][0],
        got["kv"][1],
        got["att_cq"][0],
        relative,
        gains[1],
        got["att_cq"][1],
        got["crs_mem"][1],
        got["crs_mem"][2],
        got["crs_mem"][0],
        gains[2],
        got["gate"][0],
        got["up"][0],
        got["down"][0],
    )


def solution(mesh):
    rows = P(("dp", "grp"), None)
    flat = P(("dp", "grp"))
    in_specs = (rows, rows, rows, P("dp")) + (P(),) * 15
    out_specs = (rows,) * 3 + (flat,) + (rows,) * 4 + (flat,) * 2 + (rows,) * 4 + (flat,) + (rows,) * 3
    return jax.shard_map(shards, mesh=mesh, in_specs=in_specs, out_specs=out_specs, check_vma=False)
```

```python
import functools

import jax
import jax.numpy as jnp
from jax import lax
from jax.experimental import pallas as pl
from jax.experimental.pallas import tpu as pltpu
from jax.sharding import PartitionSpec as P

SHORT = 1024
RATIO = 4
BUCKETS = 32
HEADS = 16
EPSILON = 1e-06
THRESHOLDS = (19, 21, 24, 27, 31, 35, 40, 46, 52, 59, 67, 77, 87, 99, 113)
CORES = 2
BF16 = jnp.bfloat16
F32 = jnp.float32
NEGATIVE = -1e30
HEAD = 64
TILE = 256
NEAR = 128
LANES = 128
ROOM = 16 * 1024 * 1024


def dot(a, b):
    return jnp.dot(a, b, preferred_element_type=F32)


def dot_right(a, b):
    return lax.dot_general(a, b, (((1,), (1,)), ((), ())), preferred_element_type=F32)


def shaped(shape, dtype=BF16):
    return jax.ShapeDtypeStruct(tuple(shape), dtype)


def half_shape(array, axis):
    shape = list(array.shape)
    shape[axis] //= CORES
    return tuple(shape)


def whole_kernel(body, place, arrays, weights, outs, name, scratch=(), room=ROOM, cost=0, fetch=()):
    ready = [w for w in weights if not isinstance(w, tuple)]
    far = [w for w in weights if isinstance(w, tuple)]
    n_a, n_r, n_w, n_o, n_f = len(arrays), len(ready), len(far), len(outs), len(fetch)
    buffers = [pltpu.VMEM(half_shape(array, axis), array.dtype) for array, axis, _ in far]
    fetched = [shaped(half_shape(array, axis), array.dtype) for array, axis, _ in fetch]

    def kernel(place_ref, *refs):
        array_refs, refs = refs[:n_a], refs[n_a:]
        ready_refs, refs = refs[:n_r], refs[n_r:]
        far_refs, refs = refs[: n_w + n_f], refs[n_w + n_f :]
        out_refs, refs = refs[:n_o], refs[n_o:]
        fetch_refs, refs = refs[:n_f], refs[n_f:]
        buffer_refs, refs = refs[:n_w], refs[n_w:]
        copies = []
        for at, (ref, buffer, (_, axis, other)) in enumerate(
            zip(far_refs, (*buffer_refs, *fetch_refs), (*far, *fetch))
        ):
            size = buffer.shape[axis]
            start = pl.multiple_of((1 - place_ref[1] if other else place_ref[1]) * size, size)
            source = ref.at[pl.ds(start, size)] if axis == 0 else ref.at[:, pl.ds(start, size)]
            copies.append(pltpu.make_async_copy(source, buffer, refs[0].at[at]))
        for copy in copies:
            copy.start()
        arrived = set()
        places = []
        for w in weights:
            places.append((isinstance(w, tuple), sum(isinstance(x, tuple) == isinstance(w, tuple) for x in weights[: len(places)])))

        def weight(at):
            distant, spot = places[at]
            if not distant:
                return ready_refs[spot]
            if spot not in arrived:
                copies[spot].wait()
                arrived.add(spot)
            return buffer_refs[spot]

        body(place_ref, array_refs, weight, out_refs, refs[1:] if n_w + n_f else refs)
        for copy in copies[n_w:]:
            copy.wait()

    inside = pl.BlockSpec(memory_space=pltpu.VMEM)
    scratch = buffers + ([pltpu.SemaphoreType.DMA((n_w + n_f,))] if n_w + n_f else []) + list(scratch)
    return pl.pallas_call(
        kernel,
        in_specs=[pl.BlockSpec(memory_space=pltpu.SMEM)]
        + [inside] * (n_a + n_r)
        + [pl.BlockSpec(memory_space=pltpu.HBM)] * (n_w + n_f),
        out_specs=[inside] * (n_o + n_f),
        out_shape=list(outs) + fetched,
        scratch_shapes=scratch,
        compiler_params=pltpu.CompilerParams(vmem_limit_bytes=room),
        cost_estimate=pl.CostEstimate(
            flops=int(1.15e9 * cost), bytes_accessed=int(3.69e6 * cost), transcendentals=0
        ),
        name=name,
    )(
        place,
        *arrays,
        *ready,
        *[pltpu.with_memory_space_constraint(array, pltpu.HBM) for array, _, _ in (*far, *fetch)],
    )


def inverse_norm(hidden):
    return lax.rsqrt(jnp.mean(hidden * hidden, axis=-1, keepdims=True) + EPSILON)


def norm_low(hidden, inverse, gain):
    return (hidden * inverse * gain).astype(BF16)


def norm_back(hidden, inverse, gain, dz):
    scaled = gain * dz
    inner = jnp.mean(scaled * hidden, axis=-1, keepdims=True)
    return inverse * scaled - hidden * (inverse * inverse * inverse) * inner


def pick(core, value, axis, other=False):
    half = value.shape[axis] // CORES
    low, high = lax.slice_in_dim(value, 0, half, axis=axis), lax.slice_in_dim(value, half, 2 * half, axis=axis)
    return jnp.where(core == (1 if other else 0), low, high)


def in_place_order(core, own_ref, peer_ref):
    own, peer = own_ref[...].astype(F32), peer_ref[...].astype(F32)
    return jnp.concatenate([jnp.where(core == 0, own, peer), jnp.where(core == 0, peer, own)], axis=0)


def place_rows(half, at):
    zero = jnp.zeros_like(half)
    return jnp.concatenate([half, zero] if at == 0 else [zero, half], axis=0)


def place_lanes(pair, source, at):
    lane = lax.broadcasted_iota(jnp.int32, pair.shape, 1)
    if source != at:
        pair = jnp.concatenate([pair[:, HEAD:], pair[:, :HEAD]], axis=1)
    return jnp.where((lane < HEAD) == (at == 0), pair, jnp.zeros_like(pair))


def near_tiles(table_row):
    skewed = pltpu.roll(jnp.broadcast_to(table_row, (NEAR, 2 * NEAR)), 0, 1, stride=1, stride_axis=0)
    key_at = lax.broadcasted_iota(jnp.int32, (NEAR, NEAR), 0)
    row_at = lax.broadcasted_iota(jnp.int32, (NEAR, NEAR), 1)
    return (jnp.where(key_at <= row_at, skewed[:, :NEAR], NEGATIVE), skewed[:, NEAR:])


def heads_of(pair_turned, cols):
    return jnp.concatenate(
        [place_rows(pair_turned[h * HEAD : (h + 1) * HEAD, cols], h // 2) for h in range(4)], axis=1
    )


def add_corner(scores, tiles):
    rows = scores.shape[0]
    last = scores[rows - NEAR :]
    pieces = []
    for h in range(4):
        pieces += [last[:, h * TILE : h * TILE + NEAR] + tiles[h][1], last[:, h * TILE + NEAR : (h + 1) * TILE]]
    return jnp.concatenate([scores[: rows - NEAR], jnp.concatenate(pieces, axis=1)], axis=0)


def add_diagonal(scores, tiles):
    rows = scores.shape[0]
    first = scores[rows - TILE : rows - NEAR]
    second = scores[rows - NEAR :]
    upper, lower = [], []
    for h in range(4):
        left, right = slice(h * TILE, h * TILE + NEAR), slice(h * TILE + NEAR, (h + 1) * TILE)
        upper += [first[:, left] + tiles[h][0], first[:, right] + tiles[h][1]]
        lower += [jnp.full((NEAR, NEAR), NEGATIVE, F32), second[:, right] + tiles[h][0]]
    last = [jnp.concatenate(upper, axis=1), jnp.concatenate(lower, axis=1)]
    if rows > TILE:
        last = [add_corner(scores[: rows - TILE], tiles)] + last
    return jnp.concatenate(last, axis=0)


def by_distance(near):
    level = near[:8]
    for first in range(8, NEAR, 8):
        level = level + pltpu.roll(near[first : first + 8], 2 * NEAR - first, 1)
    row = lax.broadcasted_iota(jnp.int32, level.shape, 0)
    for bit in (1, 2, 4):
        level = jnp.where(row & bit > 0, pltpu.roll(level, 2 * NEAR - bit, 1), level)
    return jnp.sum(level, axis=0, keepdims=True)


def soft(scores):
    peak = jnp.max(scores, axis=0, keepdims=True)
    weights = jnp.exp(scores - peak)
    return peak, weights.astype(BF16), jnp.sum(weights, axis=0, keepdims=True)


def finish(o_ref, lse_ref, cols, peak, summed, acc):
    out = acc / summed
    lse = peak + jnp.log(summed)
    pieces = []
    for h in range(4):
        e = h // 2
        lanes = slice(h * TILE, (h + 1) * TILE)
        pieces.append(out[e * HEAD : (e + 1) * HEAD, lanes])
        lse_ref[0, h : h + 1, cols] = lse[:, lanes]
    o_ref[cols, :] = jnp.concatenate(pieces, axis=0).T.astype(BF16)


def self_diagonal_block(table_ref, q_ref, k_ref, v_ref, peak_ref, sum_ref, acc_ref):
    rows = q_ref.shape[0]
    v_turned = v_ref[...].T
    q_turned = q_ref[...].T
    tiles = [near_tiles(table_ref[0, h : h + 1, :]) for h in range(4)]
    spans = [slice(t * TILE, (t + 1) * TILE) for t in range(rows // TILE)]
    scores = [add_diagonal(dot(k_ref[: cols.stop], heads_of(q_turned, cols)), tiles) for cols in spans]
    parts = [soft(score) for score in scores]
    for t, cols in enumerate(spans):
        peak_ref[t], sum_ref[t] = parts[t][0], parts[t][2]
        acc_ref[t] = dot(v_turned[:, : cols.stop], parts[t][1])


def self_past_blocks(valid_ref, blocks, *, earlier):
    steps = blocks[0][1].shape[0] // TILE
    spans = [slice(t * TILE, (t + 1) * TILE) for t in range(steps)]
    units = [(p, t) for p in range(len(blocks)) for t in range(steps)]
    for s in range(earlier):

        @pl.when(valid_ref[3 + s] > 0)
        def _(s=s):
            turned = [block[1][...].T for block in blocks]
            values = [block[3][s].T for block in blocks]

            def scores_of(p, t):
                scores = dot(blocks[p][2][s], heads_of(turned[p], spans[t]))
                if s == 0 and t == 0:
                    table_ref = blocks[p][0]
                    scores = add_corner(scores, [near_tiles(table_ref[0, h : h + 1, :]) for h in range(4)])
                return scores

            ready = scores_of(*units[0])
            for at, (p, t) in enumerate(units):
                scores = ready
                if at + 1 < len(units):
                    ready = scores_of(*units[at + 1])
                _, _, _, _, peak_in, sum_in, acc_in, o_ref, lse_ref, peak_ref, sum_ref, acc_ref = blocks[p]
                old = (peak_in, sum_in, acc_in) if s == 0 else (peak_ref, sum_ref, acc_ref)
                peak = old[0][t]
                new_peak = jnp.maximum(peak, jnp.max(scores, axis=0, keepdims=True))
                rescale = jnp.exp(peak - new_peak)
                weights = jnp.exp(scores - new_peak)
                summed = old[1][t] * rescale + jnp.sum(weights, axis=0, keepdims=True)
                acc = old[2][t] * rescale + dot(values[p], weights.astype(BF16))
                if s + 1 < earlier:
                    peak_ref[t], sum_ref[t], acc_ref[t] = new_peak, summed, acc
                else:
                    finish(o_ref, lse_ref, spans[t], new_peak, summed, acc)

        @pl.when(valid_ref[3 + s] == 0)
        def _(s=s):
            for p, t in units:
                _, _, _, _, peak_in, sum_in, acc_in, o_ref, lse_ref, peak_ref, sum_ref, acc_ref = blocks[p]
                old = (peak_in, sum_in, acc_in) if s == 0 else (peak_ref, sum_ref, acc_ref)
                if s + 1 < earlier:
                    peak_ref[t], sum_ref[t], acc_ref[t] = old[0][t], old[1][t], old[2][t]
                else:
                    finish(o_ref, lse_ref, spans[t], old[0][t], old[1][t], old[2][t])


def placed_heads(block, cols):
    rows = []
    for h in range(4):
        pair = block[cols, (h // 2) * 2 * HEAD : (h // 2 + 1) * 2 * HEAD]
        rows.append(place_lanes(pair, h % 2, h // 2))
    return jnp.concatenate(rows, axis=0)


def row_of_heads(ref, cols):
    return jnp.concatenate([ref[0, h : h + 1, cols] for h in range(4)], axis=1)


def deltas(product, cols):
    return jnp.concatenate(
        [jnp.sum(product[h * HEAD : (h + 1) * HEAD, cols], axis=0, keepdims=True) for h in range(4)], axis=1
    )


def back_scores(scores, lse, d_prob, delta):
    prob = jnp.exp(scores - lse)
    d_score = prob * (d_prob - delta)
    return prob.astype(BF16), d_score.astype(BF16)


def query_rows(d_query):
    pieces = [
        d_query[(h // 2) * HEAD : (h // 2 + 1) * HEAD, h * TILE : (h + 1) * TILE] for h in range(4)
    ]
    return jnp.concatenate(pieces, axis=0).T.astype(BF16)


def self_backward_block(
    valid_ref, table_ref, q_ref, k_ref, v_ref, kp_ref, vp_ref, do_ref, o_ref, lse_ref,
    dq_ref, dk_ref, dv_ref, past_ref, db_ref, total_ref,
    near_sum, dq_sum, *, earlier,
):
    rows = q_ref.shape[0]
    steps = rows // TILE
    spans = [slice(t * TILE, (t + 1) * TILE) for t in range(steps)]
    k_turned = k_ref[...].T
    q_turned = q_ref[...].T
    do_turned = do_ref[...].T
    product = (do_ref[...].astype(F32) * o_ref[...].astype(F32)).T
    tiles = [near_tiles(table_ref[0, h : h + 1, :]) for h in range(4)]
    queries = [heads_of(q_turned, cols) for cols in spans]
    outs = [heads_of(do_turned, cols) for cols in spans]
    q_placed = [placed_heads(q_ref, cols) for cols in spans]
    do_placed = [placed_heads(do_ref, cols) for cols in spans]
    lses = [row_of_heads(lse_ref, cols) for cols in spans]
    delta = [deltas(product, cols) for cols in spans]

    for t, cols in enumerate(spans):
        seen = cols.stop
        scores = add_diagonal(dot(k_ref[:seen], queries[t]), tiles)
        prob, d_score = back_scores(scores, lses[t], dot(v_ref[:seen], outs[t]), delta[t])
        d_value = dot(prob, do_placed[t])
        d_key = dot(d_score, q_placed[t])
        if t == 0:
            dv_whole, dk_whole = d_value, d_key
        else:
            more = seen - dv_whole.shape[0]
            dv_whole = jnp.concatenate([dv_whole + d_value[: seen - more], d_value[seen - more :]], axis=0)
            dk_whole = jnp.concatenate([dk_whole + d_key[: seen - more], d_key[seen - more :]], axis=0)
        dq_sum[t] = dot(k_turned[:, :seen], d_score)
        d_wide = d_score.astype(F32)
        total = jnp.sum(d_wide, axis=0, keepdims=True)
        base = seen - TILE
        for h in range(4):
            left, right = slice(h * TILE, h * TILE + NEAR), slice(h * TILE + NEAR, (h + 1) * TILE)
            zero_part = d_wide[base : base + NEAR, left] + d_wide[base + NEAR :, right]
            one_part = d_wide[base : base + NEAR, right]
            if t > 0:
                one_part = one_part + d_wide[base - NEAR : base, left]
            both = jnp.concatenate([zero_part, one_part], axis=1)
            part = total[:, h * TILE : (h + 1) * TILE]
            if t == 0:
                near_sum[h] = both
                total_ref[0, h : h + 1, :] = part
            else:
                near_sum[h] += both
                total_ref[0, h : h + 1, :] += part
    dk_ref[...] = dk_whole.astype(BF16)
    dv_ref[...] = dv_whole.astype(BF16)

    for s in range(earlier):

        @pl.when(valid_ref[3 + s] > 0)
        def _(s=s):
            kp_turned = kp_ref[s].T
            for t in range(steps):
                scores = dot(kp_ref[s], queries[t])
                if s == 0 and t == 0:
                    scores = add_corner(scores, tiles)
                prob, d_score = back_scores(scores, lses[t], dot(vp_ref[s], outs[t]), delta[t])
                d_value = dot(prob, do_placed[t])
                d_key = dot(d_score, q_placed[t])
                dv_whole = d_value if t == 0 else dv_whole + d_value
                dk_whole = d_key if t == 0 else dk_whole + d_key
                dq_sum[t] += dot(kp_turned, d_score)
                d_wide = d_score.astype(F32)
                total = jnp.sum(d_wide, axis=0, keepdims=True)
                for h in range(4):
                    total_ref[0, h : h + 1, :] += total[:, h * TILE : (h + 1) * TILE]
                    if s == 0 and t == 0:
                        near_sum[h, :, NEAR:] += d_wide[rows - NEAR :, h * TILE : h * TILE + NEAR]
            past_ref[s, 0] = dk_whole.astype(BF16)
            past_ref[s, 1] = dv_whole.astype(BF16)

        @pl.when(valid_ref[3 + s] == 0)
        def _(s=s):
            past_ref[s] = jnp.zeros_like(past_ref[s])

    for t, cols in enumerate(spans):
        dq_ref[cols, :] = query_rows(dq_sum[t])
    for h in range(4):
        db_ref[0, h : h + 1, :] = by_distance(near_sum[h])
    db_ref[0, 4:, :] = jnp.zeros((4, 2 * NEAR), F32)
    total_ref[0, 4:, :] = jnp.zeros((4, 2 * NEAR), F32)


def cross_forward_block(q_ref, k_ref, v_ref, own_ref, o_ref, lse_ref, *, masked):
    rows = q_ref.shape[0]
    v_turned = v_ref[...].T
    q_turned = q_ref[...].T
    spans = [slice(t * TILE, (t + 1) * TILE) for t in range(rows // TILE)]
    scores = [dot(k_ref[...], heads_of(q_turned, cols)) for cols in spans]
    if masked:
        blocked = jnp.where(own_ref[...] > 0, 0.0, NEGATIVE)
        blocked = jnp.concatenate([blocked] * 4, axis=1)
        scores = [score + blocked for score in scores]
    for t, cols in enumerate(spans):
        peak, weights, summed = soft(scores[t])
        finish(o_ref, lse_ref, cols, peak, summed, dot(v_turned, weights))


def cross_backward_block(
    q_ref, k_ref, v_ref, own_ref, do_ref, o_ref, lse_ref, dq_ref, dk_ref, dv_ref, *, masked
):
    rows = q_ref.shape[0]
    k_turned = k_ref[...].T
    q_turned = q_ref[...].T
    do_turned = do_ref[...].T
    product = (do_ref[...].astype(F32) * o_ref[...].astype(F32)).T
    spans = [slice(t * TILE, (t + 1) * TILE) for t in range(rows // TILE)]
    dk_whole, dv_whole = 0.0, 0.0
    for t, cols in enumerate(spans):
        scores = dot(k_ref[...], heads_of(q_turned, cols))
        if masked:
            blocked = jnp.where(own_ref[...] > 0, 0.0, NEGATIVE)
            scores = scores + jnp.concatenate([blocked] * 4, axis=1)
        d_prob = dot(v_ref[...], heads_of(do_turned, cols))
        prob, d_score = back_scores(scores, row_of_heads(lse_ref, cols), d_prob, deltas(product, cols))
        dv_whole = dv_whole + dot(prob, placed_heads(do_ref, cols))
        dk_whole = dk_whole + dot(d_score, placed_heads(q_ref, cols))
        dq_ref[cols, :] = query_rows(dot(k_turned, d_score))
    dk_ref[...] = dk_whole.astype(BF16)
    dv_ref[...] = dv_whole.astype(BF16)


def wide_view(ref, p):
    return ref.at[:, pl.ds(p * 4 * HEAD, 4 * HEAD)]


def slim_view(ref, p):
    return ref.at[:, pl.ds(p * 2 * HEAD, 2 * HEAD)]


def past_view(ref, p):
    return ref.at[:, :, pl.ds(p * 2 * HEAD, 2 * HEAD)]


def page_view(ref, p):
    return ref.at[pl.ds(p, 1)]


def self_diagonal(place, table, q, k, v, fetch):
    rows, blocks = q.shape[0], k.shape[1] // (2 * HEAD)
    steps = rows // TILE

    def body(place_ref, arrays, weight, outs, scratch):
        table_ref, q_ref, k_ref, v_ref = arrays
        for p in range(blocks):
            self_diagonal_block(
                page_view(table_ref, p), wide_view(q_ref, p), slim_view(k_ref, p), slim_view(v_ref, p),
                *[ref.at[p] for ref in outs],
            )

    state = [(blocks, steps, 1, 4 * TILE), (blocks, steps, 1, 4 * TILE), (blocks, steps, 2 * HEAD, 4 * TILE)]
    return whole_kernel(body, place, [table, q, k, v], [], [shaped(shape, F32) for shape in state], "self_diagonal", fetch=fetch)


def self_past(place, table, q, kp, vp, peak, summed, acc, fetch):
    rows, blocks, earlier = q.shape[0], kp.shape[2] // (2 * HEAD), kp.shape[0]

    def body(place_ref, arrays, weight, outs, scratch):
        table_ref, q_ref, kp_ref, vp_ref, peak_ref, sum_ref, acc_ref = arrays
        views = [
            (
                page_view(table_ref, p), wide_view(q_ref, p), past_view(kp_ref, p), past_view(vp_ref, p),
                peak_ref.at[p], sum_ref.at[p], acc_ref.at[p], wide_view(outs[0], p), page_view(outs[1], p),
                *([ref.at[p] for ref in scratch] if earlier > 1 else [None] * 3),
            )
            for p in range(blocks)
        ]
        self_past_blocks(place_ref, views, earlier=earlier)

    return whole_kernel(
        body,
        place,
        [table, q, kp, vp, peak, summed, acc],
        [],
        [shaped(q.shape), shaped((blocks, 8, rows), F32)],
        "self_past",
        [pltpu.VMEM(a.shape, F32) for a in (peak, summed, acc)] if earlier > 1 else [],
        fetch=fetch,
    )


def self_backward(place, table, q, k, v, kp, vp, do, o, lse, fetch):
    rows, blocks, earlier = q.shape[0], k.shape[1] // (2 * HEAD), kp.shape[0]
    steps = rows // TILE

    def body(place_ref, arrays, weight, outs, scratch):
        table_ref, q_ref, k_ref, v_ref, kp_ref, vp_ref, do_ref, o_ref, lse_ref = arrays
        dq_ref, dk_ref, dv_ref, past_ref, db_ref, total_ref = outs
        for p in range(blocks):
            self_backward_block(
                place_ref, page_view(table_ref, p), wide_view(q_ref, p), slim_view(k_ref, p), slim_view(v_ref, p),
                past_view(kp_ref, p), past_view(vp_ref, p), wide_view(do_ref, p), wide_view(o_ref, p),
                page_view(lse_ref, p), wide_view(dq_ref, p), slim_view(dk_ref, p), slim_view(dv_ref, p),
                past_ref.at[:, :, :, pl.ds(p * 2 * HEAD, 2 * HEAD)], page_view(db_ref, p), page_view(total_ref, p),
                *[ref.at[p] for ref in scratch], earlier=earlier,
            )

    return whole_kernel(
        body,
        place,
        [table, q, k, v, kp, vp, do, o, lse],
        [],
        [
            shaped(q.shape),
            shaped(k.shape),
            shaped(k.shape),
            shaped((earlier, 2) + k.shape),
            shaped(table.shape, F32),
            shaped(table.shape, F32),
        ],
        "self_backward",
        [pltpu.VMEM((blocks, 4, NEAR, 2 * NEAR), F32), pltpu.VMEM((blocks, steps, 2 * HEAD, 4 * TILE), F32)],
        fetch=fetch,
    )


def cross_forward(place, q, k, v, own):
    rows, blocks = q.shape[0], k.shape[1] // (2 * HEAD)

    def body(place_ref, arrays, weight, outs, scratch):
        q_ref, k_ref, v_ref = arrays[:3]
        for p in range(blocks):
            cross_forward_block(
                wide_view(q_ref, p), slim_view(k_ref, p), slim_view(v_ref, p), arrays[-1], wide_view(outs[0], p),
                page_view(outs[1], p), masked=len(own) > 0,
            )

    outs = [shaped(q.shape), shaped((blocks, 8, rows), F32)]
    return whole_kernel(body, place, [q, k, v] + own, [], outs, "cross_forward")


def cross_backward(place, q, k, v, own, do, o, lse, fetch):
    blocks = k.shape[1] // (2 * HEAD)

    def body(place_ref, arrays, weight, outs, scratch):
        q_ref, k_ref, v_ref, do_ref, o_ref, lse_ref = arrays[:6]
        for p in range(blocks):
            cross_backward_block(
                wide_view(q_ref, p), slim_view(k_ref, p), slim_view(v_ref, p), arrays[-1], wide_view(do_ref, p),
                wide_view(o_ref, p), page_view(lse_ref, p), wide_view(outs[0], p), slim_view(outs[1], p),
                slim_view(outs[2], p), masked=len(own) > 0,
            )

    outs = [shaped(q.shape), shaped(k.shape), shaped(k.shape)]
    return whole_kernel(body, place, [q, k, v, do, o, lse] + own, [], outs, "cross_backward", fetch=fetch)


def project(place, own, peer, gain, wq, wk, wv):
    rows, model = own.shape
    wide, slim = wq.shape[1] // CORES, wk.shape[1] // CORES

    def body(place_ref, arrays, weight, outs, scratch):
        hidden = in_place_order(place_ref[1], arrays[0], arrays[1])
        low = norm_low(hidden, inverse_norm(hidden), arrays[2][...].astype(F32))
        outs[0][...] = low
        for at in range(3):
            outs[1 + at][...] = dot(low, weight(at)[...]).astype(BF16)

    return whole_kernel(
        body,
        place,
        [own, peer, gain],
        [(wq, 1, False), (wk, 1, False), (wv, 1, False)],
        [shaped((CORES * rows, n)) for n in (model, wide, slim, slim)],
        "project",
    )


def project_past(place, owns, peers, gain, wk, wv, fetch):
    rows, model = owns[0].shape
    earlier = len(owns)
    slim = wk.shape[1] // CORES

    def body(place_ref, arrays, weight, outs, scratch):
        own_refs, peer_refs = arrays[:earlier], arrays[earlier : 2 * earlier]
        gain_value = arrays[-1][...].astype(F32)
        for s in range(earlier):
            hidden = in_place_order(place_ref[1], own_refs[s], peer_refs[s])
            low = norm_low(hidden, inverse_norm(hidden), gain_value)
            outs[s][...] = low
            outs[earlier][s] = dot(low, weight(0)[...]).astype(BF16)
            outs[earlier + 1][s] = dot(low, weight(1)[...]).astype(BF16)

    made = whole_kernel(
        body,
        place,
        owns + peers + [gain],
        [(wk, 1, False), (wv, 1, False)],
        [shaped((CORES * rows, model))] * earlier + [shaped((earlier, CORES * rows, slim))] * 2,
        "project_past",
        fetch=fetch,
    )
    return made[:earlier], *made[earlier:]


def project_memory(place, mems, wk, wv):
    groups = len(mems)
    rows, model = mems[0].shape
    slim = wk.shape[1] // CORES

    def body(place_ref, arrays, weight, outs, scratch):
        for at, piece_ref in enumerate(arrays):
            block = jnp.bitwise_xor(place_ref[2], jnp.int32(at))
            outs[0][pl.ds(pl.multiple_of(block * rows, rows), rows)] = piece_ref[...]
        mem = outs[0][...]
        outs[1][...] = dot(mem, weight(0)[...]).astype(BF16)
        outs[2][...] = dot(mem, weight(1)[...]).astype(BF16)

    return whole_kernel(
        body,
        place,
        mems,
        [(wk, 1, False), (wv, 1, False)],
        [shaped((groups * rows, n)) for n in (model, slim, slim)],
        "project_memory",
        cost=8,
    )


def mid_forward(place, own, peer, att, att_peer, gain, wo, wo_peer, wq):
    rows, model = own.shape

    def body(place_ref, arrays, weight, outs, scratch):
        own_ref, peer_ref, att_ref, att_peer_ref, gain_ref = arrays
        hidden = in_place_order(place_ref[1], own_ref, peer_ref)
        hidden = hidden + dot(att_ref[...], weight(0)[...]) + dot(att_peer_ref[...], weight(1)[...])
        outs[0][...] = hidden.astype(BF16)
        low = norm_low(hidden, inverse_norm(hidden), gain_ref[...].astype(F32))
        outs[1][...] = low
        outs[2][...] = dot(low, weight(2)[...]).astype(BF16)

    return whole_kernel(
        body,
        place,
        [own, peer, att, att_peer, gain],
        [wo, wo_peer, wq],
        [shaped((CORES * rows, model))] * 2 + [shaped((CORES * rows, wq.shape[1]))],
        "mid_forward",
    )


def cotangent_inner(place, cot, cot_peer, wd):
    rows, model = cot.shape

    def body(place_ref, arrays, weight, outs, scratch):
        value = in_place_order(place_ref[1], arrays[0], arrays[1]).astype(BF16)
        outs[0][...] = pick(place_ref[1], value, 1)
        outs[1][...] = dot_right(value, weight(0)[...]).astype(BF16)

    outs = [shaped((CORES * rows, model // CORES)), shaped((CORES * rows, wd.shape[0]))]
    return whole_kernel(body, place, [cot, cot_peer], [wd], outs, "cotangent_inner", cost=8)


def ffn(place, mid, crs, crs_peer, gain, d_inner, wc, wc_peer, wg, wu):
    rows, model = mid.shape
    hidden_half = wg.shape[1]
    steps = [256] * (hidden_half // 256) + [hidden_half % 256] * (hidden_half % 256 > 0)
    scale = 0.7978845608028654

    def body(place_ref, arrays, weight, outs, scratch):
        mid_ref, crs_ref, crs_peer_ref, gain_ref, d_inner_ref = arrays
        late_ref, low_ref, inner_ref, dg_ref, du_ref, dz_ref = outs
        hidden = mid_ref[...].astype(F32) + dot(crs_ref[...], weight(0)[...]) + dot(crs_peer_ref[...], weight(1)[...])
        late_ref[...] = hidden.astype(BF16)
        low = norm_low(hidden, inverse_norm(hidden), gain_ref[...].astype(F32))
        low_ref[...] = low
        start = 0
        for width in steps:
            cols = slice(start, start + width)
            start += width
            gate = dot(low, weight(2)[:, cols])
            up = dot(low, weight(3)[:, cols])
            d_inner = d_inner_ref[:, cols].astype(F32)
            square = gate * gate
            bent = jnp.tanh(gate * (scale + (scale * 0.044715) * square))
            whole = 0.5 + 0.5 * bent
            slope = whole + (0.5 * gate) * (1.0 - bent * bent) * (scale + (3 * scale * 0.044715) * square)
            curve = gate * whole
            inner_ref[:, cols] = (curve * up).astype(BF16)
            dg_ref[:, cols] = (d_inner * up * slope).astype(BF16)
            du_ref[:, cols] = (d_inner * curve).astype(BF16)
        dz_ref[...] = (dot_right(dg_ref[...], weight(2)[...]) + dot_right(du_ref[...], weight(3)[...])).astype(BF16)

    return whole_kernel(
        body,
        place,
        [mid, crs, crs_peer, gain, d_inner],
        [wc, wc_peer, wg, wu],
        [shaped((rows, model))] * 2
        + [shaped((rows, hidden_half))] * 3
        + [shaped((rows, model))],
        "ffn",
        room=16 * 1024 * 1024,
    )


def late_backward(place, dz, dz_peer, late, cot, cot_peer, gain, wc):
    rows, model = late.shape

    def body(place_ref, arrays, weight, outs, scratch):
        dz_ref, dz_peer_ref, late_ref, cot_ref, cot_peer_ref, gain_ref = arrays
        dz_value = dz_ref[...].astype(F32) + dz_peer_ref[...].astype(F32)
        hidden = late_ref[...].astype(F32)
        inverse = inverse_norm(hidden)
        outs[3][...] = jnp.sum(dz_value * hidden * inverse, axis=0, keepdims=True)
        grad = in_place_order(place_ref[1], cot_ref, cot_peer_ref)
        grad = grad + norm_back(hidden, inverse, gain_ref[...].astype(F32), dz_value)
        low = grad.astype(BF16)
        outs[0][...] = low
        outs[1][...] = pick(place_ref[1], low, 1)
        outs[2][...] = dot_right(low, weight(0)[...]).astype(BF16)

    return whole_kernel(
        body,
        place,
        [dz, dz_peer, late, cot, cot_peer, gain],
        [wc],
        [
            shaped((rows, model)),
            shaped((rows, model // CORES)),
            shaped((rows, wc.shape[0])),
            shaped((1, model), F32),
        ],
        "late_backward",
    )


def mid_backward(place, dq, dq_peer, mid, g_late, gain, wq, wq_peer, wo):
    rows, model = mid.shape

    def body(place_ref, arrays, weight, outs, scratch):
        dq_ref, dq_peer_ref, mid_ref, g_ref, gain_ref = arrays
        dz = dot_right(dq_ref[...], weight(0)[...]) + dot_right(dq_peer_ref[...], weight(1)[...])
        hidden = mid_ref[...].astype(F32)
        inverse = inverse_norm(hidden)
        outs[3][...] = jnp.sum(dz * hidden * inverse, axis=0, keepdims=True)
        grad = g_ref[...].astype(F32) + norm_back(hidden, inverse, gain_ref[...].astype(F32), dz)
        low = grad.astype(BF16)
        outs[0][...] = pick(place_ref[1], low, 0)
        outs[1][...] = pick(place_ref[1], low, 1)
        outs[2][...] = dot_right(low, weight(2)[...]).astype(BF16)

    return whole_kernel(
        body,
        place,
        [dq, dq_peer, mid, g_late, gain],
        [wq, wq_peer, wo],
        [
            shaped((rows // CORES, model)),
            shaped((rows, model // CORES)),
            shaped((rows, wo.shape[0])),
            shaped((1, model), F32),
        ],
        "mid_backward",
    )


def first_backward(place, dz, past, riders, mem_parts, wk, wv):
    rows, model = dz.shape
    slim = wk.shape[1]
    own_rows = rows // CORES
    joint = riders is not None
    mem_rows = mem_parts.shape[0] // (CORES * CORES) if joint else 0

    def body(place_ref, arrays, weight, outs, scratch):
        core = place_ref[1]
        pairs = []
        if joint:
            past_at, mem_at = past[0][1], riders[0][1]
            blocks = [arrays[1][past_at + at * rows : past_at + (at + 1) * rows] for at in range(2 * slim // LANES)]
            pairs.append((jnp.concatenate(blocks[: slim // LANES], 1), jnp.concatenate(blocks[slim // LANES :], 1)))
        else:
            pairs += [(ref[0], ref[1]) for ref in arrays[1:]]
        total = arrays[0][...].astype(F32)
        for dk, dv in pairs:
            total = total + dot_right(dk, weight(0)[...]) + dot_right(dv, weight(1)[...])
        outs[0][...] = pick(core, total, 0)
        outs[1][:own_rows] = pick(core, total, 0, True).astype(BF16)
        if joint:
            half = CORES * mem_rows
            mine = pick(place_ref[2] // CORES, arrays[3][...].astype(F32), 0)
            got = [arrays[2][mem_at + at * half : mem_at + (at + 1) * half].astype(F32) for at in range(model // LANES)]
            mine = mine + jnp.concatenate(got, axis=1)
            outs[2][...] = pick(core, mine, 0)
            outs[1][own_rows:] = pick(core, mine, 0, True).astype(BF16)

    outs = [shaped((own_rows, model), F32), shaped((own_rows + mem_rows, model))]
    if joint:
        outs.append(shaped((mem_rows, model), F32))
    return whole_kernel(
        body, place, [dz] + ([past[0][0], riders[0][0], mem_parts] if joint else past), [wk, wv], outs, "first_backward"
    )


def tokens_backward(place, dz, dz_got, mem, tokens, g_mid, gain):
    rows = tokens.shape[0]

    def body(place_ref, arrays, weight, outs, scratch):
        dz_ref, dz_got_ref, tokens_ref, g_ref, gain_ref = arrays[:5]
        dz_value = dz_ref[...] + dz_got_ref[:rows].astype(F32)
        hidden = tokens_ref[...].astype(F32)
        grad = norm_back(hidden, inverse_norm(hidden), gain_ref[...].astype(F32), dz_value)
        outs[0][...] = (g_ref[...].astype(F32) + grad).astype(BF16)
        if mem:
            outs[1][...] = (arrays[5][...] + dz_got_ref[rows:].astype(F32)).astype(BF16)

    outs = [shaped(tokens.shape)] + [shaped(m.shape) for m in mem]
    return whole_kernel(body, place, [dz, dz_got, tokens, g_mid, gain] + mem, [], outs, "tokens_backward")


def layer_output(place, late, inner, inner_peer, wd, wd_peer):
    rows, model = late.shape

    def body(place_ref, arrays, weight, outs, scratch):
        own, inner_own, inner_other = (pick(place_ref[1], ref[...], 0) for ref in arrays)
        total = own.astype(F32) + dot(inner_own, weight(0)[...]) + dot(inner_other, weight(1)[...])
        outs[0][...] = total.astype(BF16)

    return whole_kernel(
        body,
        place,
        [late, inner, inner_peer],
        [wd, wd_peer],
        [shaped((rows // CORES, model))],
        "layer_output",
        cost=10,
    )[0]


def memory_backward(place, dk, dv, wk, wv):
    def body(place_ref, arrays, weight, outs, scratch):
        grad = dot_right(arrays[0][...], weight(0)[...]) + dot_right(arrays[1][...], weight(1)[...])
        outs[0][...] = grad.astype(BF16)

    weights = [(wk, 1, False), (wv, 1, False)]
    return whole_kernel(body, place, [dk, dv], weights, [shaped((dk.shape[0], wk.shape[0]))], "memory_backward")[0]


def small_sums(place, dq, dk, dv, d_past, own, peer, past_own, past_peer, two, three, near, total, buckets, weights, chips, fetch):
    rows, model = dq.shape[0], own.shape[1]
    earlier = len(past_own)
    heads = HEADS // CORES

    def body(place_ref, arrays, weight, outs, scratch):
        dq_ref, dk_ref, dv_ref, past_ref, own_ref, peer_ref = arrays[:6]
        past_own_refs, past_peer_refs = arrays[6 : 6 + earlier], arrays[6 + earlier : 6 + 2 * earlier]
        two_ref, three_ref, near_ref, total_ref, bucket_ref = arrays[6 + 2 * earlier :]
        core = place_ref[1]
        first = core == 0

        def gain_part(dz, own_ref, peer_ref):
            hidden = in_place_order(core, own_ref, peer_ref)
            return jnp.sum(dz * (hidden * inverse_norm(hidden)), axis=0, keepdims=True)

        dz = dot_right(dq_ref[...], weight(0)[...])
        dz = dz + dot_right(dk_ref[...], weight(1)[...]) + dot_right(dv_ref[...], weight(2)[...])
        outs[0][...] = dz.astype(BF16)
        one = gain_part(dz, own_ref, peer_ref)
        for s in range(earlier):
            dz = dot_right(past_ref[s, 0], weight(1)[...]) + dot_right(past_ref[s, 1], weight(2)[...])
            one = one + gain_part(dz, past_own_refs[s], past_peer_refs[s])
        gains = [one, jnp.where(first, two_ref[...], 0.0), jnp.where(first, three_ref[...], 0.0)]
        near = jnp.concatenate([near_ref[p, :4] for p in range(heads // 4)], axis=0)
        total = jnp.concatenate([total_ref[p, :4] for p in range(heads // 4)], axis=0)
        far = jnp.sum(total, axis=1, keepdims=True) - jnp.sum(near, axis=1, keepdims=True)
        last = lax.broadcasted_iota(jnp.int32, near.shape, 1) == near.shape[1] - 1
        near = near + jnp.where(last, far, 0.0)
        entries = BUCKETS * HEADS
        entry = lax.broadcasted_iota(jnp.int32, (near.shape[1], entries), 1)
        same = (lax.shift_right_logical(entry, jnp.int32(HEADS.bit_length() - 1)) == bucket_ref[...]).astype(F32)
        sums = jnp.dot(near, same, precision=lax.Precision.HIGHEST, preferred_element_type=F32)
        head = lax.broadcasted_iota(jnp.int32, sums.shape, 0) + core * heads
        of_entry = jnp.bitwise_and(lax.broadcasted_iota(jnp.int32, sums.shape, 1), jnp.int32(HEADS - 1))
        vectors = gains + [jnp.sum(jnp.where(head == of_entry, sums, 0.0), axis=0, keepdims=True)]
        for block in range(chips):
            lines = []
            for vector in vectors:
                size = vector.shape[1] // chips
                line = vector[:, block * size : (block + 1) * size]
                lines.append(jnp.concatenate([line, jnp.zeros((1, LANES - size), F32)], axis=1))
            lines.append(jnp.zeros((12, LANES), F32))
            outs[1][block * 16 : (block + 1) * 16] = jnp.concatenate(lines, axis=0).astype(BF16)

    arrays = [dq, dk, dv, d_past, own, peer] + past_own + past_peer + [two, three, near, total, buckets]
    return whole_kernel(
        body, place, arrays, weights, [shaped((rows, model)), shaped((chips * 16, LANES))], "small_sums", fetch=fetch
    )


def gather_sums(place, parts, name):
    def body(place_ref, arrays, weight, outs, scratch):
        for array, out in zip(arrays, outs):
            total = array[0].astype(F32)
            for at in range(1, array.shape[0]):
                total = total + array[at].astype(F32)
            out[...] = total.astype(out.dtype)

    return whole_kernel(body, place, parts, [], [shaped(a.shape[1:], a.dtype) for a in parts], name)


def up_to(value, multiple):
    return (value + multiple - 1) // multiple * multiple


def array_of(y):
    return y[0] if isinstance(y, tuple) else y


class Flow:
    def __init__(self, name, pieces, order, extra=None):
        self.name, self.pieces, self.order, self.extra = name, pieces, order, extra
        self.hops = [bit + 1 for bit in order]
        self.chips = 1 << len(order)
        self.layout = []
        start = 0
        for terms, rows in pieces:
            half = rows // self.chips // CORES
            padded = up_to(half, 8)
            width = array_of(terms[0][1]).shape[-1]
            self.layout.append((start, half, padded, width))
            start += CORES * padded * (width // LANES)
        self.extra_at = start
        self.rows = start + (16 if extra is not None else 0)
        self.keep = self.got = None

    def spread(self, x):
        half, padded = self.layout[0][1:3]
        if half == padded:
            return x
        chunks = x.reshape(x.shape[0], -1, half)
        return jnp.pad(chunks, ((0, 0), (0, 0), (0, padded - half))).reshape(x.shape[0], -1)


def chip_of(spot, order):
    number = 0
    for at, bit in enumerate(order):
        number |= (spot >> (len(order) - 1 - at) & 1) << bit
    return number


def sum_flow(flow, refs_of, place_ref, turned, free, send_ref, base, keep_ref):
    chip, core = place_ref[0], place_ref[1]
    half = flow.chips // 2
    for (terms, _), (start, _, padded, width) in zip(flow.pieces, flow.layout):
        chunk = CORES * padded
        lefts = []
        for xs, y in terms:
            key = (tuple(id(x) for x in xs), flow.order)
            if key not in turned:
                straight_ref, turned[key] = free.pop(0), free.pop(0)
                if len(xs) == 1:
                    straight_ref[...] = refs_of[id(xs[0])][...].T
                else:
                    size = straight_ref.shape[0] // CORES
                    for part, x in enumerate(xs):
                        at = (core if part == 0 else 1 - core) * size
                        straight_ref[pl.ds(pl.multiple_of(at, 16), size)] = refs_of[id(x)][...].T
                for spot in range(flow.chips):
                    at = jnp.bitwise_xor(jnp.int32(chip_of(spot, flow.order)), chip) * chunk
                    turned[key][spot * chunk : (spot + 1) * chunk] = straight_ref[pl.ds(pl.multiple_of(at, 16), chunk)]
            lefts.append(turned[key])
        count = max(1, min(flow.chips, 512 // chunk))
        while flow.chips % count:
            count -= 1
        for first in range(0, flow.chips, count):
            tile = None
            for left, (_, y) in zip(lefts, terms):
                y_ref = refs_of[id(array_of(y))]
                y_value = y_ref[y[1]] if isinstance(y, tuple) else y_ref[...]
                term = dot(left[first * chunk : (first + count) * chunk], y_value)
                tile = term if tile is None else tile + term
            tile = tile.astype(BF16)
            for inner in range(count):
                spot = first + inner
                for block in range(width // LANES):
                    value = tile[inner * chunk : (inner + 1) * chunk, block * LANES : (block + 1) * LANES]
                    at = start + block * chunk
                    if spot < half:
                        keep_ref[spot, at : at + chunk] = value
                    else:
                        at += base + (spot - half) * flow.rows
                        send_ref[at : at + chunk] = value


def copy_extra(flow, extra_ref, place_ref, send_ref, base, keep_ref):
    half = flow.chips // 2
    for spot in range(flow.chips):
        at = jnp.bitwise_xor(jnp.int32(chip_of(spot, flow.order)), place_ref[0]) * 16
        value = extra_ref[pl.ds(pl.multiple_of(at, 16), 16)]
        if spot < half:
            keep_ref[spot, flow.extra_at : flow.extra_at + 16] = value
        else:
            to = base + (spot - half) * flow.rows + flow.extra_at
            send_ref[to : to + 16] = value


def add_flow(flow, old_ref, got_ref, got_at, send_ref, base, keep_ref):
    half = old_ref.shape[0] // 2
    for spot in range(2 * half):
        at = got_at + spot * flow.rows
        total = (old_ref[spot].astype(F32) + got_ref[at : at + flow.rows].astype(F32)).astype(BF16)
        if spot < half:
            keep_ref[spot] = total
        else:
            send_ref[base + (spot - half) * flow.rows : base + (spot - half + 1) * flow.rows] = total


def hop(place, swap, sums, adds, after, name, cost=0, riders=(), fetch=()):
    arrays, seen = [], {}

    def take(array):
        if id(array) not in seen:
            seen[id(array)] = len(arrays)
            arrays.append(array)

    for flow in sums:
        for terms, _ in flow.pieces:
            for xs, y in terms:
                for array in (*xs, array_of(y)):
                    take(array)
        if flow.extra is not None:
            take(flow.extra)
    for flow in adds:
        take(flow.keep)
        take(flow.got[0])
    bits, sends, keeps = {}, {}, {}
    for flow in sums + adds:
        half = (flow.chips if flow in sums else flow.keep.shape[0]) // 2
        bit = flow.hops[0]
        base = bits.setdefault(bit, 0)
        sends[flow.name] = (bit, base)
        bits[bit] = base + half * flow.rows
        keeps[flow.name] = shaped((half, flow.rows, LANES))
    rider_at = []
    for rider, bit, size, _ in riders:
        take(rider)
        rider_at.append(bits.setdefault(bit, 0))
        bits[bit] = rider_at[-1] + size
    order = list(bits)
    outs = [shaped((bits[bit], LANES)) for bit in order] + list(keeps.values())

    def body(place_ref, refs, weight, out_refs, scratch):
        refs_of = {key: refs[at] for key, at in seen.items()}
        turned, free = {}, list(scratch)
        for at, flow in enumerate(sums + adds):
            bit, base = sends[flow.name]
            send_ref, keep_ref = out_refs[order.index(bit)], out_refs[len(order) + at]
            if flow in sums:
                sum_flow(flow, refs_of, place_ref, turned, free, send_ref, base, keep_ref)
                if flow.extra is not None:
                    copy_extra(flow, refs_of[id(flow.extra)], place_ref, send_ref, base, keep_ref)
            else:
                add_flow(
                    flow, refs_of[id(flow.keep)], refs_of[id(flow.got[0])], flow.got[1], send_ref, base, keep_ref
                )
        for (rider, bit, _, write), at in zip(riders, rider_at):
            write(refs_of[id(rider)], out_refs[order.index(bit)], at, place_ref)

    needed = {}
    for flow in sums:
        for terms, _ in flow.pieces:
            for xs, _ in terms:
                shape = (sum(x.shape[1] for x in xs), xs[0].shape[0])
                needed[(tuple(id(x) for x in xs), flow.order)] = [pltpu.VMEM(shape, BF16)] * 2
    scratch = sum(needed.values(), [])
    made = whole_kernel(body, place, follow(arrays, after), [], outs, name, scratch, cost=cost, fetch=fetch)
    moved = [swap(array, bit) for array, bit in zip(made, order)]
    for at, flow in enumerate(sums + adds):
        bit, base = sends[flow.name]
        flow.keep, flow.got, flow.hops = made[len(order) + at], (moved[order.index(bit)], base), flow.hops[1:]
    if riders:
        return list(made), (moved[order.index(riders[0][1])], *rider_at)
    return list(made)


def write_past(past_ref, send_ref, at, place_ref):
    _, pages, rows, width = past_ref.shape
    for page in range(pages):
        for block in range(width // LANES):
            send_ref[at : at + rows] = past_ref[0, page, :, block * LANES : (block + 1) * LANES]
            at += rows


def write_memory(mem_ref, send_ref, at, place_ref):
    rows = mem_ref.shape[0] // CORES
    there = pl.ds(pl.multiple_of((1 - place_ref[2] // CORES) * rows, rows), rows)
    for block in range(mem_ref.shape[1] // LANES):
        send_ref[at : at + rows] = mem_ref[there, block * LANES : (block + 1) * LANES]
        at += rows


def last_hop(place, swap, flows, after, name, shares=()):
    arrays, seen = [], {}
    for flow in flows:
        for array in (flow.keep, flow.got[0]):
            if id(array) not in seen:
                seen[id(array)] = len(arrays)
                arrays.append(array)
    blocks = []
    size = 0
    for f, flow in enumerate(flows):
        for piece, (start, half, padded, width) in enumerate(flow.layout):
            for block in range(width // LANES):
                blocks.append((f, piece, start + block * CORES * padded, padded, block, size))
                size += up_to(padded, 16)
    extras = [(f, flow.extra_at, size + 16 * sum(x.extra is not None for x in flows[:f])) for f, flow in enumerate(flows) if flow.extra is not None]
    size += 16 * len(extras)
    own_outs = [
        shaped((padded, width), F32) for flow in flows for _, _, padded, width in flow.layout
    ]
    own_outs += [shaped((16, LANES), F32) for _ in extras]
    n_pieces = len(own_outs) - len(extras)
    first = [sum(len(flow.layout) for flow in flows[:f]) for f in range(len(flows))]

    def add_body(place_ref, refs, weight, outs, scratch):
        core = place_ref[1]
        for f, piece, at, padded, block, leave_at in blocks:
            flow = flows[f]
            got_at = flow.got[1] + at
            total = refs[seen[id(flow.keep)]][0, at : at + CORES * padded].astype(F32)
            total = total + refs[seen[id(flow.got[0])]][got_at : got_at + CORES * padded].astype(F32)
            own, leave = pick(core, total, 0), pick(core, total, 0, True)
            outs[1 + first[f] + piece][:, block * LANES : (block + 1) * LANES] = own
            full = up_to(padded, 16)
            if full > padded:
                leave = jnp.concatenate([leave, jnp.zeros((full - padded, LANES), F32)], axis=0)
            outs[0][leave_at : leave_at + full] = leave.astype(BF16)
        for at, (f, start, leave_at) in enumerate(extras):
            flow = flows[f]
            got_at = flow.got[1] + start
            total = refs[seen[id(flow.keep)]][0, start : start + 16].astype(F32)
            total = total + refs[seen[id(flow.got[0])]][got_at : got_at + 16].astype(F32)
            outs[1 + n_pieces + at][...] = total
            outs[0][leave_at : leave_at + 16] = total.astype(BF16)

    made = whole_kernel(add_body, place, follow(arrays, after), [], [shaped((size, LANES))] + own_outs, "last_" + name)
    got = swap(made[0], 0)

    def join_body(place_ref, refs, weight, outs, scratch):
        core = place_ref[1]
        for f, piece, _, padded, block, leave_at in blocks:
            at = first[f] + piece
            width = refs[1 + at].shape[1]
            own = refs[1 + at][:, block * LANES : (block + 1) * LANES]
            other = refs[0][leave_at : leave_at + up_to(padded, 16)].astype(F32)[:padded]
            low, high = slice(block * LANES, (block + 1) * LANES), slice(width + block * LANES, width + (block + 1) * LANES)
            outs[at][:, low] = jnp.where(core == 0, own, other)
            outs[at][:, high] = jnp.where(core == 0, other, own)
        for at, (_, _, leave_at) in enumerate(extras):
            total = refs[1 + n_pieces + at][...] + refs[0][leave_at : leave_at + 16].astype(F32)
            for line, (out, share) in enumerate(zip(outs[n_pieces:], shares)):
                out[...] = jnp.where(core == 0, total[line, :share], total[line, share : 2 * share])

    joined = whole_kernel(
        join_body,
        place,
        [got] + list(made[1:]),
        [],
        [shaped((a.shape[0], CORES * a.shape[1]), F32) for a in own_outs[:n_pieces]]
        + [shaped((share,), F32) for _ in extras for share in shares],
        "join_" + name,
    )
    results = {}
    for f, flow in enumerate(flows):
        results[flow.name] = [
            joined[first[f] + piece][:half] for piece, (_, half, _, _) in enumerate(flow.layout)
        ]
    if extras:
        results["small"] = joined[n_pieces:]
    return results, list(made)


def follow(value, after):
    return lax.optimization_barrier((value, after))[0]


def rel_bucket(distance):
    beyond = 16 + sum((distance >= border).astype(jnp.int32) for border in THRESHOLDS)
    return jnp.where(distance < 16, distance, beyond)


def shards(
    tokens, memory, cotangent, bucket, gain_self, self_query, self_key, self_value, self_out, rel_bias,
    gain_cross, cross_query, cross_key, cross_value, cross_out, gain_ffn, ffn_gate, ffn_up, ffn_down,
):
    groups = lax.axis_size("grp")
    dp_size = lax.axis_size("dp")
    n_chips = groups // CORES
    more = n_chips - 1
    chips = dp_size * n_chips
    devices = chips * CORES
    grp_at = lax.axis_index("grp")
    core = grp_at % CORES
    y_at = grp_at // CORES
    chip = lax.axis_index("dp") * n_chips + y_at
    rows, model = tokens.shape
    chip_rows = rows * CORES
    group_rows = chip_rows * n_chips
    hidden_units = ffn_down.shape[0]
    length = jnp.minimum(group_rows, jnp.maximum(SHORT, jnp.right_shift(jnp.int32(group_rows), bucket[0])))
    y_bits = n_chips.bit_length() - 1
    bits = chips.bit_length() - 1
    first_chip = y_at * chip_rows // length * length // chip_rows
    valid = [(y_at - s >= first_chip).astype(jnp.int32) for s in range(1, n_chips)]
    place = jnp.stack([chip, core, grp_at] + valid).astype(jnp.int32)

    def swap(v, bit):
        return lax.ppermute(v, ("dp", "grp"), [(i, i ^ (1 << bit)) for i in range(devices)])

    gain_one, gain_two, gain_three = (g.reshape(1, model) for g in (gain_self, gain_cross, gain_ffn))

    past_own = [
        lax.ppermute(tokens, "grp", [(g, g + CORES * s) for g in range(groups - CORES * s)]) for s in range(1, n_chips)
    ]
    tokens_peer = swap(tokens, 0)
    mems = [memory] + [
        lax.ppermute(memory, "grp", [(g, g ^ other) for g in range(groups)]) for other in range(1, groups)
    ]

    distances = jnp.arange(2 * NEAR, dtype=jnp.int32)
    buckets = rel_bucket(distances)[:, None]
    onehot = (buckets == jnp.arange(BUCKETS, dtype=jnp.int32)).astype(F32)
    heads = HEADS // CORES
    rel_local = lax.dynamic_slice_in_dim(rel_bias.astype(F32), core * heads, heads, 1)
    by_dist = jnp.dot(onehot, rel_local - rel_local[BUCKETS - 1 :], precision=lax.Precision.HIGHEST)
    table = jnp.pad(by_dist.T.reshape(heads // 4, 4, 2 * NEAR), ((0, 0), (0, 4), (0, 0)))

    low_one, q, k, v = project(place, tokens, tokens_peer, gain_one, self_query, self_key, self_value)
    *diagonal, w_gate, w_up = self_diagonal(place, table, q, k, v, [(ffn_gate, 1, False), (ffn_up, 1, False)])
    past_own = follow(past_own, diagonal)
    past_peer = [swap(own, 0) for own in past_own]
    cot_peer = swap(follow(cotangent, diagonal[0]), 0)
    low_past, k_past, v_past, w_down = project_past(
        place, past_own, past_peer, gain_one, self_key, self_value, [(ffn_down, 0, False)]
    )
    att, lse_self, w_out, w_out_peer, w_query, w_cross, w_cross_peer = self_past(
        place, table, q, k_past, v_past, *diagonal,
        [(self_out, 0, False), (self_out, 0, True), (cross_query, 1, False), (cross_out, 0, False), (cross_out, 0, True)],
    )
    att_peer = swap(att, 0)
    mem_all, km, vm = project_memory(place, follow(mems, att), cross_key, cross_value)
    att_peer = follow(att_peer, km)
    mid, low_two, cq = mid_forward(
        place, tokens, tokens_peer, att, att_peer, gain_two, w_out, w_out_peer, w_query
    )
    own_doc = []
    if group_rows > SHORT:
        mem_doc = jnp.arange(mem_all.shape[0], dtype=jnp.int32) // (length // RATIO)
        own = (mem_doc == y_at * chip_rows // length).astype(F32)
        own_doc = [jnp.broadcast_to(own[:, None], (mem_all.shape[0], TILE))]
    crs, lse_cross = cross_forward(place, cq, km, vm, own_doc)
    crs_peer = swap(crs, 0)
    cot_half, d_inner = cotangent_inner(place, follow(cotangent, crs), cot_peer, w_down)
    crs_peer = follow(crs_peer, d_inner)
    late, low_three, inner, d_gate, d_up, dz = ffn(
        place, mid, crs, crs_peer, gain_three, d_inner, w_cross, w_cross_peer, w_gate, w_up
    )

    axes = {
        "y": tuple(range(y_bits)),
        "x": (y_bits,),
        "z": (y_bits + 1,),
        "f": tuple(range(y_bits + 2, bits)),
    }

    def order_of(letters):
        return sum((axes[letter] for letter in letters), ())

    dz_peer = swap(dz, 0)
    inner_peer = swap(inner, 0)
    gate = Flow("gate", [([((low_three,), d_gate)], model)], order_of("xyzf"))
    up = Flow("up", [([((low_three,), d_up)], model)], order_of("yzfx"))
    last = hop(place, swap, [gate], [], place, "gate")
    last = hop(place, swap, [up], [], last, "up")
    down = Flow("down", [([((inner, inner_peer), cot_half)], hidden_units)], order_of("zxyf"))
    spread = (down.spread(inner), down.spread(inner_peer))
    down = Flow("down", [([(spread, cot_half)], hidden_units)], order_of("zxyf"))
    last = hop(place, swap, [down], [], last, "down")
    ffn_flows = [gate, up, down]

    g_late, late_half, d_crs, d_gain_three = late_backward(
        place, follow(dz, last), dz_peer, late, cotangent, cot_peer, gain_three, w_cross
    )
    dcq, dkm, dvm, w_query_peer = cross_backward(
        place, cq, km, vm, own_doc, d_crs, crs, lse_cross, [(cross_query, 1, True)]
    )
    dcq_peer = swap(dcq, 0)
    crs_mem = Flow(
        "crs_mem",
        [([((crs, crs_peer), late_half)], model), ([((mem_all,), dkm)], model), ([((mem_all,), dvm)], model)],
        order_of("zxyf"),
    )
    last = hop(place, swap, [crs_mem], [], dcq, "crs_mem", cost=5)
    g_mid, mid_half, d_att, d_gain_two = mid_backward(
        place, dcq, follow(dcq_peer, last), mid, g_late, gain_two, w_query, w_query_peer, w_out
    )
    att_cq = Flow("att_cq", [([((att, att_peer), mid_half)], model), ([((low_two,), dcq)], model)], order_of("xyzf"))
    last = hop(place, swap, [att_cq], [], d_att, "att_cq")
    dq, dk, dv, d_past, d_near, d_total, *w_first = self_backward(
        place, table, q, k, v, k_past, v_past, follow(d_att, last), att, lse_self,
        [(self_query, 1, False), (self_key, 1, False), (self_value, 1, False)],
    )
    mem_parts = memory_backward(place, follow(dkm, dq), dvm, cross_key, cross_value)
    past_moved, riders = [], None
    if n_chips == 2:
        y_bit = 1
        last, riders = hop(
            place, swap, [], ffn_flows, mem_parts, "ffn_1",
            riders=[(mem_parts, y_bit, mem_parts.size // CORES // LANES, write_memory)],
        )
    else:
        past_moved = [
            lax.ppermute(d_past[s - 1], "grp", [(g, g - CORES * s) for g in range(CORES * s, groups)])
            for s in range(1, n_chips)
        ]
        last = hop(place, swap, [], ffn_flows, mem_parts, "ffn_1")
    dz, small, w_down, w_down_peer = small_sums(
        place, follow(dq, last), dk, dv, d_past, tokens, tokens_peer, past_own, past_peer, d_gain_two, d_gain_three,
        d_near, d_total, buckets, w_first, chips, [(ffn_down, 0, False), (ffn_down, 0, True)],
    )
    query = Flow("query", [([((low_one,), dq)], model)], order_of("xyzf"), small)
    kv = Flow(
        "kv",
        [
            ([((low_one,), d)] + [((low_past[s],), (d_past, (s, which))) for s in range(more)], model)
            for which, d in ((0, dk), (1, dv))
        ],
        order_of("yxzf"),
    )
    attention = [att_cq, crs_mem, query, kv]
    last = hop(place, swap, [query, kv], [att_cq, crs_mem], dz, "attention_1", cost=5)

    results = {}
    names = {"ffn": ffn_flows, "attention": attention}

    def step(label, after, riders=(), fetch=()):
        flows = names[label]
        if label in results:
            return after
        moving = [flow for flow in flows if flow.hops]
        if moving:
            return hop(place, swap, [], moving, after, f"{label}_{len(moving[0].hops)}", cost=30, riders=riders, fetch=fetch)
        results[label], made = last_hop(place, swap, flows, after, label, [model // devices] * 3 + [BUCKETS * HEADS // devices])
        return made

    for label in ("ffn", "attention", "ffn"):
        last = step(label, last)
    if n_chips == 2:
        last, past_rider = step("attention", last, [(d_past, y_bit, d_past.size // LANES, write_past)])
        past_moved, riders = [past_rider], [riders]
    else:
        last = step("attention", last)
    waiting = True
    while len(results) < 2:
        if "attention" not in results and not any(flow.hops for flow in attention):
            last = last + sum(results.get("ffn", {}).values(), [])
        last = step("ffn", last)
        if waiting and not any(flow.hops for flow in attention):
            waiting = False
            dz_own, dz_leave, *mem_own = first_backward(
                place, follow(dz, last), past_moved, riders, mem_parts, *w_first[1:]
            )
            dz_got = swap(dz_leave, 0)
            layer_out = layer_output(place, follow(late, dz_leave), inner, inner_peer, w_down, w_down_peer)
            dz_got = follow(dz_got, layer_out)
            grad_tokens, *grad_memory = tokens_backward(place, dz_own, dz_got, mem_own, tokens, g_mid, gain_one)
            if not grad_memory:
                parts = lax.all_to_all(mem_parts, "grp", split_axis=0, concat_axis=0, tiled=True)
                grad_memory = gather_sums(place, [parts.reshape(groups, -1, model)], "memory_sums")
            last = last + [grad_tokens]
        last = step("attention", last)
    got = {**results["ffn"], **results["attention"]}
    *gains, relative = got["small"]
    return (
        layer_out,
        grad_tokens,
        grad_memory[0],
        gains[0],
        got["query"][0],
        got["kv"][0],
        got["kv"][1],
        got["att_cq"][0],
        relative,
        gains[1],
        got["att_cq"][1],
        got["crs_mem"][1],
        got["crs_mem"][2],
        got["crs_mem"][0],
        gains[2],
        got["gate"][0],
        got["up"][0],
        got["down"][0],
    )


def solution(mesh):
    rows = P(("dp", "grp"), None)
    flat = P(("dp", "grp"))
    in_specs = (rows, rows, rows, P("dp")) + (P(),) * 15
    out_specs = (rows,) * 3 + (flat,) + (rows,) * 4 + (flat,) * 2 + (rows,) * 4 + (flat,) + (rows,) * 3
    return jax.shard_map(shards, mesh=mesh, in_specs=in_specs, out_specs=out_specs, check_vma=False)
```

```python
import functools

import jax
import jax.numpy as jnp
from jax import lax
from jax.experimental import pallas as pl
from jax.experimental.pallas import tpu as pltpu
from jax.sharding import PartitionSpec as P

SHORT = 1024
RATIO = 4
BUCKETS = 32
HEADS = 16
EPSILON = 1e-06
THRESHOLDS = (19, 21, 24, 27, 31, 35, 40, 46, 52, 59, 67, 77, 87, 99, 113)
CORES = 2
BF16 = jnp.bfloat16
F32 = jnp.float32
NEGATIVE = -1e30
HEAD = 64
TILE = 256
NEAR = 128
LANES = 128
ROOM = 16 * 1024 * 1024


def dot(a, b):
    return jnp.dot(a, b, preferred_element_type=F32)


def dot_right(a, b):
    return lax.dot_general(a, b, (((1,), (1,)), ((), ())), preferred_element_type=F32)


def shaped(shape, dtype=BF16):
    return jax.ShapeDtypeStruct(tuple(shape), dtype)


def half_shape(array, axis):
    shape = list(array.shape)
    shape[axis] //= CORES
    return tuple(shape)


def whole_kernel(body, place, arrays, weights, outs, name, scratch=(), room=ROOM, cost=0, fetch=()):
    ready = [w for w in weights if not isinstance(w, tuple)]
    far = [w for w in weights if isinstance(w, tuple)]
    n_a, n_r, n_w, n_o, n_f = len(arrays), len(ready), len(far), len(outs), len(fetch)
    buffers = [pltpu.VMEM(half_shape(array, axis), array.dtype) for array, axis, _ in far]
    fetched = [shaped(half_shape(array, axis), array.dtype) for array, axis, _ in fetch]

    def kernel(place_ref, *refs):
        array_refs, refs = refs[:n_a], refs[n_a:]
        ready_refs, refs = refs[:n_r], refs[n_r:]
        far_refs, refs = refs[: n_w + n_f], refs[n_w + n_f :]
        out_refs, refs = refs[:n_o], refs[n_o:]
        fetch_refs, refs = refs[:n_f], refs[n_f:]
        buffer_refs, refs = refs[:n_w], refs[n_w:]
        copies = []
        for at, (ref, buffer, (_, axis, other)) in enumerate(
            zip(far_refs, (*buffer_refs, *fetch_refs), (*far, *fetch))
        ):
            size = buffer.shape[axis]
            start = pl.multiple_of((1 - place_ref[1] if other else place_ref[1]) * size, size)
            source = ref.at[pl.ds(start, size)] if axis == 0 else ref.at[:, pl.ds(start, size)]
            copies.append(pltpu.make_async_copy(source, buffer, refs[0].at[at]))
        for copy in copies:
            copy.start()
        arrived = set()
        places = []
        for w in weights:
            places.append((isinstance(w, tuple), sum(isinstance(x, tuple) == isinstance(w, tuple) for x in weights[: len(places)])))

        def weight(at):
            distant, spot = places[at]
            if not distant:
                return ready_refs[spot]
            if spot not in arrived:
                copies[spot].wait()
                arrived.add(spot)
            return buffer_refs[spot]

        body(place_ref, array_refs, weight, out_refs, refs[1:] if n_w + n_f else refs)
        for copy in copies[n_w:]:
            copy.wait()

    inside = pl.BlockSpec(memory_space=pltpu.VMEM)
    scratch = buffers + ([pltpu.SemaphoreType.DMA((n_w + n_f,))] if n_w + n_f else []) + list(scratch)
    return pl.pallas_call(
        kernel,
        in_specs=[pl.BlockSpec(memory_space=pltpu.SMEM)]
        + [inside] * (n_a + n_r)
        + [pl.BlockSpec(memory_space=pltpu.HBM)] * (n_w + n_f),
        out_specs=[inside] * (n_o + n_f),
        out_shape=list(outs) + fetched,
        scratch_shapes=scratch,
        compiler_params=pltpu.CompilerParams(vmem_limit_bytes=room),
        cost_estimate=pl.CostEstimate(
            flops=int(1.15e9 * cost), bytes_accessed=int(3.69e6 * cost), transcendentals=0
        ),
        name=name,
    )(
        place,
        *arrays,
        *ready,
        *[pltpu.with_memory_space_constraint(array, pltpu.HBM) for array, _, _ in (*far, *fetch)],
    )


def inverse_norm(hidden):
    return lax.rsqrt(jnp.mean(hidden * hidden, axis=-1, keepdims=True) + EPSILON)


def norm_low(hidden, inverse, gain):
    return (hidden * inverse * gain).astype(BF16)


def norm_back(hidden, inverse, gain, dz):
    scaled = gain * dz
    inner = jnp.mean(scaled * hidden, axis=-1, keepdims=True)
    return inverse * scaled - hidden * (inverse * inverse * inverse) * inner


def pick(core, value, axis, other=False):
    half = value.shape[axis] // CORES
    low, high = lax.slice_in_dim(value, 0, half, axis=axis), lax.slice_in_dim(value, half, 2 * half, axis=axis)
    return jnp.where(core == (1 if other else 0), low, high)


def in_place_order(core, own_ref, peer_ref):
    own, peer = own_ref[...].astype(F32), peer_ref[...].astype(F32)
    return jnp.concatenate([jnp.where(core == 0, own, peer), jnp.where(core == 0, peer, own)], axis=0)


def place_rows(half, at):
    zero = jnp.zeros_like(half)
    return jnp.concatenate([half, zero] if at == 0 else [zero, half], axis=0)


def place_lanes(pair, source, at):
    lane = lax.broadcasted_iota(jnp.int32, pair.shape, 1)
    if source != at:
        pair = jnp.concatenate([pair[:, HEAD:], pair[:, :HEAD]], axis=1)
    return jnp.where((lane < HEAD) == (at == 0), pair, jnp.zeros_like(pair))


def near_tiles(table_row):
    skewed = pltpu.roll(jnp.broadcast_to(table_row, (NEAR, 2 * NEAR)), 0, 1, stride=1, stride_axis=0)
    key_at = lax.broadcasted_iota(jnp.int32, (NEAR, NEAR), 0)
    row_at = lax.broadcasted_iota(jnp.int32, (NEAR, NEAR), 1)
    return (jnp.where(key_at <= row_at, skewed[:, :NEAR], NEGATIVE), skewed[:, NEAR:])


def heads_of(pair_turned, cols):
    return jnp.concatenate(
        [place_rows(pair_turned[h * HEAD : (h + 1) * HEAD, cols], h // 2) for h in range(4)], axis=1
    )


def add_corner(scores, tiles):
    rows = scores.shape[0]
    last = scores[rows - NEAR :]
    pieces = []
    for h in range(4):
        pieces += [last[:, h * TILE : h * TILE + NEAR] + tiles[h][1], last[:, h * TILE + NEAR : (h + 1) * TILE]]
    return jnp.concatenate([scores[: rows - NEAR], jnp.concatenate(pieces, axis=1)], axis=0)


def add_diagonal(scores, tiles):
    rows = scores.shape[0]
    first = scores[rows - TILE : rows - NEAR]
    second = scores[rows - NEAR :]
    upper, lower = [], []
    for h in range(4):
        left, right = slice(h * TILE, h * TILE + NEAR), slice(h * TILE + NEAR, (h + 1) * TILE)
        upper += [first[:, left] + tiles[h][0], first[:, right] + tiles[h][1]]
        lower += [jnp.full((NEAR, NEAR), NEGATIVE, F32), second[:, right] + tiles[h][0]]
    last = [jnp.concatenate(upper, axis=1), jnp.concatenate(lower, axis=1)]
    if rows > TILE:
        last = [add_corner(scores[: rows - TILE], tiles)] + last
    return jnp.concatenate(last, axis=0)


def by_distance(near):
    level = near[:8]
    for first in range(8, NEAR, 8):
        level = level + pltpu.roll(near[first : first + 8], 2 * NEAR - first, 1)
    row = lax.broadcasted_iota(jnp.int32, level.shape, 0)
    for bit in (1, 2, 4):
        level = jnp.where(row & bit > 0, pltpu.roll(level, 2 * NEAR - bit, 1), level)
    return jnp.sum(level, axis=0, keepdims=True)


def soft(scores):
    peak = jnp.max(scores, axis=0, keepdims=True)
    weights = jnp.exp(scores - peak)
    return peak, weights.astype(BF16), jnp.sum(weights, axis=0, keepdims=True)


def finish(o_ref, lse_ref, cols, peak, summed, acc):
    out = acc / summed
    lse = peak + jnp.log(summed)
    pieces = []
    for h in range(4):
        e = h // 2
        lanes = slice(h * TILE, (h + 1) * TILE)
        pieces.append(out[e * HEAD : (e + 1) * HEAD, lanes])
        lse_ref[0, h : h + 1, cols] = lse[:, lanes]
    o_ref[cols, :] = jnp.concatenate(pieces, axis=0).T.astype(BF16)


def self_diagonal_block(table_ref, q_ref, k_ref, v_ref, peak_ref, sum_ref, acc_ref):
    rows = q_ref.shape[0]
    v_turned = v_ref[...].T
    q_turned = q_ref[...].T
    tiles = [near_tiles(table_ref[0, h : h + 1, :]) for h in range(4)]
    spans = [slice(t * TILE, (t + 1) * TILE) for t in range(rows // TILE)]
    scores = [add_diagonal(dot(k_ref[: cols.stop], heads_of(q_turned, cols)), tiles) for cols in spans]
    parts = [soft(score) for score in scores]
    for t, cols in enumerate(spans):
        peak_ref[t], sum_ref[t] = parts[t][0], parts[t][2]
        acc_ref[t] = dot(v_turned[:, : cols.stop], parts[t][1])


def self_past_blocks(valid_ref, blocks, *, earlier):
    steps = blocks[0][1].shape[0] // TILE
    spans = [slice(t * TILE, (t + 1) * TILE) for t in range(steps)]
    units = [(p, t) for p in range(len(blocks)) for t in range(steps)]
    for s in range(earlier):

        @pl.when(valid_ref[3 + s] > 0)
        def _(s=s):
            turned = [block[1][...].T for block in blocks]
            values = [block[3][s].T for block in blocks]

            def scores_of(p, t):
                scores = dot(blocks[p][2][s], heads_of(turned[p], spans[t]))
                if s == 0 and t == 0:
                    table_ref = blocks[p][0]
                    scores = add_corner(scores, [near_tiles(table_ref[0, h : h + 1, :]) for h in range(4)])
                return scores

            ready = scores_of(*units[0])
            for at, (p, t) in enumerate(units):
                scores = ready
                if at + 1 < len(units):
                    ready = scores_of(*units[at + 1])
                _, _, _, _, peak_in, sum_in, acc_in, o_ref, lse_ref, peak_ref, sum_ref, acc_ref = blocks[p]
                old = (peak_in, sum_in, acc_in) if s == 0 else (peak_ref, sum_ref, acc_ref)
                peak = old[0][t]
                new_peak = jnp.maximum(peak, jnp.max(scores, axis=0, keepdims=True))
                rescale = jnp.exp(peak - new_peak)
                weights = jnp.exp(scores - new_peak)
                summed = old[1][t] * rescale + jnp.sum(weights, axis=0, keepdims=True)
                acc = old[2][t] * rescale + dot(values[p], weights.astype(BF16))
                if s + 1 < earlier:
                    peak_ref[t], sum_ref[t], acc_ref[t] = new_peak, summed, acc
                else:
                    finish(o_ref, lse_ref, spans[t], new_peak, summed, acc)

        @pl.when(valid_ref[3 + s] == 0)
        def _(s=s):
            for p, t in units:
                _, _, _, _, peak_in, sum_in, acc_in, o_ref, lse_ref, peak_ref, sum_ref, acc_ref = blocks[p]
                old = (peak_in, sum_in, acc_in) if s == 0 else (peak_ref, sum_ref, acc_ref)
                if s + 1 < earlier:
                    peak_ref[t], sum_ref[t], acc_ref[t] = old[0][t], old[1][t], old[2][t]
                else:
                    finish(o_ref, lse_ref, spans[t], old[0][t], old[1][t], old[2][t])


def placed_heads(block, cols):
    rows = []
    for h in range(4):
        pair = block[cols, (h // 2) * 2 * HEAD : (h // 2 + 1) * 2 * HEAD]
        rows.append(place_lanes(pair, h % 2, h // 2))
    return jnp.concatenate(rows, axis=0)


def row_of_heads(ref, cols):
    return jnp.concatenate([ref[0, h : h + 1, cols] for h in range(4)], axis=1)


def deltas(product, cols):
    return jnp.concatenate(
        [jnp.sum(product[h * HEAD : (h + 1) * HEAD, cols], axis=0, keepdims=True) for h in range(4)], axis=1
    )


def back_scores(scores, lse, d_prob, delta):
    prob = jnp.exp(scores - lse)
    d_score = prob * (d_prob - delta)
    return prob.astype(BF16), d_score.astype(BF16)


def query_rows(d_query):
    pieces = [
        d_query[(h // 2) * HEAD : (h // 2 + 1) * HEAD, h * TILE : (h + 1) * TILE] for h in range(4)
    ]
    return jnp.concatenate(pieces, axis=0).T.astype(BF16)


def self_backward_block(
    valid_ref, table_ref, q_ref, k_ref, v_ref, kp_ref, vp_ref, do_ref, o_ref, lse_ref,
    dq_ref, dk_ref, dv_ref, past_ref, db_ref, total_ref,
    near_sum, dq_sum, *, earlier,
):
    rows = q_ref.shape[0]
    steps = rows // TILE
    spans = [slice(t * TILE, (t + 1) * TILE) for t in range(steps)]
    k_turned = k_ref[...].T
    q_turned = q_ref[...].T
    do_turned = do_ref[...].T
    product = (do_ref[...].astype(F32) * o_ref[...].astype(F32)).T
    tiles = [near_tiles(table_ref[0, h : h + 1, :]) for h in range(4)]
    queries = [heads_of(q_turned, cols) for cols in spans]
    outs = [heads_of(do_turned, cols) for cols in spans]
    q_placed = [placed_heads(q_ref, cols) for cols in spans]
    do_placed = [placed_heads(do_ref, cols) for cols in spans]
    lses = [row_of_heads(lse_ref, cols) for cols in spans]
    delta = [deltas(product, cols) for cols in spans]

    for t, cols in enumerate(spans):
        seen = cols.stop
        scores = add_diagonal(dot(k_ref[:seen], queries[t]), tiles)
        prob, d_score = back_scores(scores, lses[t], dot(v_ref[:seen], outs[t]), delta[t])
        d_value = dot(prob, do_placed[t])
        d_key = dot(d_score, q_placed[t])
        if t == 0:
            dv_whole, dk_whole = d_value, d_key
        else:
            more = seen - dv_whole.shape[0]
            dv_whole = jnp.concatenate([dv_whole + d_value[: seen - more], d_value[seen - more :]], axis=0)
            dk_whole = jnp.concatenate([dk_whole + d_key[: seen - more], d_key[seen - more :]], axis=0)
        dq_sum[t] = dot(k_turned[:, :seen], d_score)
        d_wide = d_score.astype(F32)
        total = jnp.sum(d_wide, axis=0, keepdims=True)
        base = seen - TILE
        for h in range(4):
            left, right = slice(h * TILE, h * TILE + NEAR), slice(h * TILE + NEAR, (h + 1) * TILE)
            zero_part = d_wide[base : base + NEAR, left] + d_wide[base + NEAR :, right]
            one_part = d_wide[base : base + NEAR, right]
            if t > 0:
                one_part = one_part + d_wide[base - NEAR : base, left]
            both = jnp.concatenate([zero_part, one_part], axis=1)
            part = total[:, h * TILE : (h + 1) * TILE]
            if t == 0:
                near_sum[h] = both
                total_ref[0, h : h + 1, :] = part
            else:
                near_sum[h] += both
                total_ref[0, h : h + 1, :] += part
    dk_ref[...] = dk_whole.astype(BF16)
    dv_ref[...] = dv_whole.astype(BF16)

    for s in range(earlier):

        @pl.when(valid_ref[3 + s] > 0)
        def _(s=s):
            kp_turned = kp_ref[s].T
            for t in range(steps):
                scores = dot(kp_ref[s], queries[t])
                if s == 0 and t == 0:
                    scores = add_corner(scores, tiles)
                prob, d_score = back_scores(scores, lses[t], dot(vp_ref[s], outs[t]), delta[t])
                d_value = dot(prob, do_placed[t])
                d_key = dot(d_score, q_placed[t])
                dv_whole = d_value if t == 0 else dv_whole + d_value
                dk_whole = d_key if t == 0 else dk_whole + d_key
                dq_sum[t] += dot(kp_turned, d_score)
                d_wide = d_score.astype(F32)
                total = jnp.sum(d_wide, axis=0, keepdims=True)
                for h in range(4):
                    total_ref[0, h : h + 1, :] += total[:, h * TILE : (h + 1) * TILE]
                    if s == 0 and t == 0:
                        near_sum[h, :, NEAR:] += d_wide[rows - NEAR :, h * TILE : h * TILE + NEAR]
            past_ref[s, 0] = dk_whole.astype(BF16)
            past_ref[s, 1] = dv_whole.astype(BF16)

        @pl.when(valid_ref[3 + s] == 0)
        def _(s=s):
            past_ref[s] = jnp.zeros_like(past_ref[s])

    for t, cols in enumerate(spans):
        dq_ref[cols, :] = query_rows(dq_sum[t])
    for h in range(4):
        db_ref[0, h : h + 1, :] = by_distance(near_sum[h])
    db_ref[0, 4:, :] = jnp.zeros((4, 2 * NEAR), F32)
    total_ref[0, 4:, :] = jnp.zeros((4, 2 * NEAR), F32)


def cross_forward_block(q_ref, k_ref, v_ref, own_ref, o_ref, lse_ref, *, masked):
    rows = q_ref.shape[0]
    v_turned = v_ref[...].T
    q_turned = q_ref[...].T
    spans = [slice(t * TILE, (t + 1) * TILE) for t in range(rows // TILE)]
    scores = [dot(k_ref[...], heads_of(q_turned, cols)) for cols in spans]
    if masked:
        blocked = jnp.where(own_ref[...] > 0, 0.0, NEGATIVE)
        blocked = jnp.concatenate([blocked] * 4, axis=1)
        scores = [score + blocked for score in scores]
    for t, cols in enumerate(spans):
        peak, weights, summed = soft(scores[t])
        finish(o_ref, lse_ref, cols, peak, summed, dot(v_turned, weights))


def cross_backward_block(
    q_ref, k_ref, v_ref, own_ref, do_ref, o_ref, lse_ref, dq_ref, dk_ref, dv_ref, *, masked
):
    rows = q_ref.shape[0]
    k_turned = k_ref[...].T
    q_turned = q_ref[...].T
    do_turned = do_ref[...].T
    product = (do_ref[...].astype(F32) * o_ref[...].astype(F32)).T
    spans = [slice(t * TILE, (t + 1) * TILE) for t in range(rows // TILE)]
    dk_whole, dv_whole = 0.0, 0.0
    for t, cols in enumerate(spans):
        scores = dot(k_ref[...], heads_of(q_turned, cols))
        if masked:
            blocked = jnp.where(own_ref[...] > 0, 0.0, NEGATIVE)
            scores = scores + jnp.concatenate([blocked] * 4, axis=1)
        d_prob = dot(v_ref[...], heads_of(do_turned, cols))
        prob, d_score = back_scores(scores, row_of_heads(lse_ref, cols), d_prob, deltas(product, cols))
        dv_whole = dv_whole + dot(prob, placed_heads(do_ref, cols))
        dk_whole = dk_whole + dot(d_score, placed_heads(q_ref, cols))
        dq_ref[cols, :] = query_rows(dot(k_turned, d_score))
    dk_ref[...] = dk_whole.astype(BF16)
    dv_ref[...] = dv_whole.astype(BF16)


def wide_view(ref, p):
    return ref.at[:, pl.ds(p * 4 * HEAD, 4 * HEAD)]


def slim_view(ref, p):
    return ref.at[:, pl.ds(p * 2 * HEAD, 2 * HEAD)]


def past_view(ref, p):
    return ref.at[:, :, pl.ds(p * 2 * HEAD, 2 * HEAD)]


def page_view(ref, p):
    return ref.at[pl.ds(p, 1)]


def self_diagonal(place, table, q, k, v, fetch):
    rows, blocks = q.shape[0], k.shape[1] // (2 * HEAD)
    steps = rows // TILE

    def body(place_ref, arrays, weight, outs, scratch):
        table_ref, q_ref, k_ref, v_ref = arrays
        for p in range(blocks):
            self_diagonal_block(
                page_view(table_ref, p), wide_view(q_ref, p), slim_view(k_ref, p), slim_view(v_ref, p),
                *[ref.at[p] for ref in outs],
            )

    state = [(blocks, steps, 1, 4 * TILE), (blocks, steps, 1, 4 * TILE), (blocks, steps, 2 * HEAD, 4 * TILE)]
    return whole_kernel(body, place, [table, q, k, v], [], [shaped(shape, F32) for shape in state], "self_diagonal", fetch=fetch)


def self_past(place, table, q, kp, vp, peak, summed, acc, fetch):
    rows, blocks, earlier = q.shape[0], kp.shape[2] // (2 * HEAD), kp.shape[0]

    def body(place_ref, arrays, weight, outs, scratch):
        table_ref, q_ref, kp_ref, vp_ref, peak_ref, sum_ref, acc_ref = arrays
        views = [
            (
                page_view(table_ref, p), wide_view(q_ref, p), past_view(kp_ref, p), past_view(vp_ref, p),
                peak_ref.at[p], sum_ref.at[p], acc_ref.at[p], wide_view(outs[0], p), page_view(outs[1], p),
                *([ref.at[p] for ref in scratch] if earlier > 1 else [None] * 3),
            )
            for p in range(blocks)
        ]
        self_past_blocks(place_ref, views, earlier=earlier)

    return whole_kernel(
        body,
        place,
        [table, q, kp, vp, peak, summed, acc],
        [],
        [shaped(q.shape), shaped((blocks, 8, rows), F32)],
        "self_past",
        [pltpu.VMEM(a.shape, F32) for a in (peak, summed, acc)] if earlier > 1 else [],
        fetch=fetch,
    )


def self_backward(place, table, q, k, v, kp, vp, do, o, lse, fetch):
    rows, blocks, earlier = q.shape[0], k.shape[1] // (2 * HEAD), kp.shape[0]
    steps = rows // TILE

    def body(place_ref, arrays, weight, outs, scratch):
        table_ref, q_ref, k_ref, v_ref, kp_ref, vp_ref, do_ref, o_ref, lse_ref = arrays
        dq_ref, dk_ref, dv_ref, past_ref, db_ref, total_ref = outs
        for p in range(blocks):
            self_backward_block(
                place_ref, page_view(table_ref, p), wide_view(q_ref, p), slim_view(k_ref, p), slim_view(v_ref, p),
                past_view(kp_ref, p), past_view(vp_ref, p), wide_view(do_ref, p), wide_view(o_ref, p),
                page_view(lse_ref, p), wide_view(dq_ref, p), slim_view(dk_ref, p), slim_view(dv_ref, p),
                past_ref.at[:, :, :, pl.ds(p * 2 * HEAD, 2 * HEAD)], page_view(db_ref, p), page_view(total_ref, p),
                *[ref.at[p] for ref in scratch], earlier=earlier,
            )

    return whole_kernel(
        body,
        place,
        [table, q, k, v, kp, vp, do, o, lse],
        [],
        [
            shaped(q.shape),
            shaped(k.shape),
            shaped(k.shape),
            shaped((earlier, 2) + k.shape),
            shaped(table.shape, F32),
            shaped(table.shape, F32),
        ],
        "self_backward",
        [pltpu.VMEM((blocks, 4, NEAR, 2 * NEAR), F32), pltpu.VMEM((blocks, steps, 2 * HEAD, 4 * TILE), F32)],
        fetch=fetch,
    )


def cross_forward(place, q, k, v, own):
    rows, blocks = q.shape[0], k.shape[1] // (2 * HEAD)

    def body(place_ref, arrays, weight, outs, scratch):
        q_ref, k_ref, v_ref = arrays[:3]
        for p in range(blocks):
            cross_forward_block(
                wide_view(q_ref, p), slim_view(k_ref, p), slim_view(v_ref, p), arrays[-1], wide_view(outs[0], p),
                page_view(outs[1], p), masked=len(own) > 0,
            )

    outs = [shaped(q.shape), shaped((blocks, 8, rows), F32)]
    return whole_kernel(body, place, [q, k, v] + own, [], outs, "cross_forward")


def cross_backward(place, q, k, v, own, do, o, lse, fetch):
    blocks = k.shape[1] // (2 * HEAD)

    def body(place_ref, arrays, weight, outs, scratch):
        q_ref, k_ref, v_ref, do_ref, o_ref, lse_ref = arrays[:6]
        for p in range(blocks):
            cross_backward_block(
                wide_view(q_ref, p), slim_view(k_ref, p), slim_view(v_ref, p), arrays[-1], wide_view(do_ref, p),
                wide_view(o_ref, p), page_view(lse_ref, p), wide_view(outs[0], p), slim_view(outs[1], p),
                slim_view(outs[2], p), masked=len(own) > 0,
            )

    outs = [shaped(q.shape), shaped(k.shape), shaped(k.shape)]
    return whole_kernel(body, place, [q, k, v, do, o, lse] + own, [], outs, "cross_backward", fetch=fetch)


def project(place, own, peer, gain, wq, wk, wv):
    rows, model = own.shape
    wide, slim = wq.shape[1] // CORES, wk.shape[1] // CORES

    def body(place_ref, arrays, weight, outs, scratch):
        hidden = in_place_order(place_ref[1], arrays[0], arrays[1])
        low = norm_low(hidden, inverse_norm(hidden), arrays[2][...].astype(F32))
        outs[0][...] = low
        for at in range(3):
            outs[1 + at][...] = dot(low, weight(at)[...]).astype(BF16)

    return whole_kernel(
        body,
        place,
        [own, peer, gain],
        [(wq, 1, False), (wk, 1, False), (wv, 1, False)],
        [shaped((CORES * rows, n)) for n in (model, wide, slim, slim)],
        "project",
    )


def project_past(place, owns, peers, gain, wk, wv, fetch):
    rows, model = owns[0].shape
    earlier = len(owns)
    slim = wk.shape[1] // CORES

    def body(place_ref, arrays, weight, outs, scratch):
        own_refs, peer_refs = arrays[:earlier], arrays[earlier : 2 * earlier]
        gain_value = arrays[-1][...].astype(F32)
        for s in range(earlier):
            hidden = in_place_order(place_ref[1], own_refs[s], peer_refs[s])
            low = norm_low(hidden, inverse_norm(hidden), gain_value)
            outs[s][...] = low
            outs[earlier][s] = dot(low, weight(0)[...]).astype(BF16)
            outs[earlier + 1][s] = dot(low, weight(1)[...]).astype(BF16)

    made = whole_kernel(
        body,
        place,
        owns + peers + [gain],
        [(wk, 1, False), (wv, 1, False)],
        [shaped((CORES * rows, model))] * earlier + [shaped((earlier, CORES * rows, slim))] * 2,
        "project_past",
        fetch=fetch,
    )
    return made[:earlier], *made[earlier:]


def project_memory(place, mems, wk, wv):
    groups = len(mems)
    rows, model = mems[0].shape
    slim = wk.shape[1] // CORES

    def body(place_ref, arrays, weight, outs, scratch):
        for at, piece_ref in enumerate(arrays):
            block = jnp.bitwise_xor(place_ref[2], jnp.int32(at))
            outs[0][pl.ds(pl.multiple_of(block * rows, rows), rows)] = piece_ref[...]
        mem = outs[0][...]
        outs[1][...] = dot(mem, weight(0)[...]).astype(BF16)
        outs[2][...] = dot(mem, weight(1)[...]).astype(BF16)

    return whole_kernel(
        body,
        place,
        mems,
        [(wk, 1, False), (wv, 1, False)],
        [shaped((groups * rows, n)) for n in (model, slim, slim)],
        "project_memory",
        cost=8,
    )


def mid_forward(place, own, peer, att, att_peer, gain, wo, wo_peer, wq):
    rows, model = own.shape

    def body(place_ref, arrays, weight, outs, scratch):
        own_ref, peer_ref, att_ref, att_peer_ref, gain_ref = arrays
        hidden = in_place_order(place_ref[1], own_ref, peer_ref)
        hidden = hidden + dot(att_ref[...], weight(0)[...]) + dot(att_peer_ref[...], weight(1)[...])
        outs[0][...] = hidden.astype(BF16)
        low = norm_low(hidden, inverse_norm(hidden), gain_ref[...].astype(F32))
        outs[1][...] = low
        outs[2][...] = dot(low, weight(2)[...]).astype(BF16)

    return whole_kernel(
        body,
        place,
        [own, peer, att, att_peer, gain],
        [wo, wo_peer, wq],
        [shaped((CORES * rows, model))] * 2 + [shaped((CORES * rows, wq.shape[1]))],
        "mid_forward",
    )


def cotangent_inner(place, cot, cot_peer, wd):
    rows, model = cot.shape

    def body(place_ref, arrays, weight, outs, scratch):
        value = in_place_order(place_ref[1], arrays[0], arrays[1]).astype(BF16)
        outs[0][...] = pick(place_ref[1], value, 1)
        outs[1][...] = dot_right(value, weight(0)[...]).astype(BF16)

    outs = [shaped((CORES * rows, model // CORES)), shaped((CORES * rows, wd.shape[0]))]
    return whole_kernel(body, place, [cot, cot_peer], [wd], outs, "cotangent_inner", cost=8)


def ffn(place, mid, crs, crs_peer, gain, d_inner, wc, wc_peer, wg, wu):
    rows, model = mid.shape
    hidden_half = wg.shape[1]
    steps = [256] * (hidden_half // 256) + [hidden_half % 256] * (hidden_half % 256 > 0)
    scale = 0.7978845608028654

    def body(place_ref, arrays, weight, outs, scratch):
        mid_ref, crs_ref, crs_peer_ref, gain_ref, d_inner_ref = arrays
        late_ref, low_ref, inner_ref, dg_ref, du_ref, dz_ref = outs
        hidden = mid_ref[...].astype(F32) + dot(crs_ref[...], weight(0)[...]) + dot(crs_peer_ref[...], weight(1)[...])
        late_ref[...] = hidden.astype(BF16)
        low = norm_low(hidden, inverse_norm(hidden), gain_ref[...].astype(F32))
        low_ref[...] = low
        start = 0
        for width in steps:
            cols = slice(start, start + width)
            start += width
            gate = dot(low, weight(2)[:, cols])
            up = dot(low, weight(3)[:, cols])
            d_inner = d_inner_ref[:, cols].astype(F32)
            square = gate * gate
            bent = jnp.tanh(gate * (scale + (scale * 0.044715) * square))
            whole = 0.5 + 0.5 * bent
            slope = whole + (0.5 * gate) * (1.0 - bent * bent) * (scale + (3 * scale * 0.044715) * square)
            curve = gate * whole
            inner_ref[:, cols] = (curve * up).astype(BF16)
            dg_ref[:, cols] = (d_inner * up * slope).astype(BF16)
            du_ref[:, cols] = (d_inner * curve).astype(BF16)
        dz_ref[...] = (dot_right(dg_ref[...], weight(2)[...]) + dot_right(du_ref[...], weight(3)[...])).astype(BF16)

    return whole_kernel(
        body,
        place,
        [mid, crs, crs_peer, gain, d_inner],
        [wc, wc_peer, wg, wu],
        [shaped((rows, model))] * 2
        + [shaped((rows, hidden_half))] * 3
        + [shaped((rows, model))],
        "ffn",
        room=16 * 1024 * 1024,
    )


def late_backward(place, dz, dz_peer, late, cot, cot_peer, gain, wc):
    rows, model = late.shape

    def body(place_ref, arrays, weight, outs, scratch):
        dz_ref, dz_peer_ref, late_ref, cot_ref, cot_peer_ref, gain_ref = arrays
        dz_value = dz_ref[...].astype(F32) + dz_peer_ref[...].astype(F32)
        hidden = late_ref[...].astype(F32)
        inverse = inverse_norm(hidden)
        outs[3][...] = jnp.sum(dz_value * hidden * inverse, axis=0, keepdims=True)
        grad = in_place_order(place_ref[1], cot_ref, cot_peer_ref)
        grad = grad + norm_back(hidden, inverse, gain_ref[...].astype(F32), dz_value)
        low = grad.astype(BF16)
        outs[0][...] = low
        outs[1][...] = pick(place_ref[1], low, 1)
        outs[2][...] = dot_right(low, weight(0)[...]).astype(BF16)

    return whole_kernel(
        body,
        place,
        [dz, dz_peer, late, cot, cot_peer, gain],
        [wc],
        [
            shaped((rows, model)),
            shaped((rows, model // CORES)),
            shaped((rows, wc.shape[0])),
            shaped((1, model), F32),
        ],
        "late_backward",
    )


def mid_backward(place, dq, dq_peer, mid, g_late, gain, wq, wq_peer, wo):
    rows, model = mid.shape

    def body(place_ref, arrays, weight, outs, scratch):
        dq_ref, dq_peer_ref, mid_ref, g_ref, gain_ref = arrays
        dz = dot_right(dq_ref[...], weight(0)[...]) + dot_right(dq_peer_ref[...], weight(1)[...])
        hidden = mid_ref[...].astype(F32)
        inverse = inverse_norm(hidden)
        outs[3][...] = jnp.sum(dz * hidden * inverse, axis=0, keepdims=True)
        grad = g_ref[...].astype(F32) + norm_back(hidden, inverse, gain_ref[...].astype(F32), dz)
        low = grad.astype(BF16)
        outs[0][...] = pick(place_ref[1], low, 0)
        outs[1][...] = pick(place_ref[1], low, 1)
        outs[2][...] = dot_right(low, weight(2)[...]).astype(BF16)

    return whole_kernel(
        body,
        place,
        [dq, dq_peer, mid, g_late, gain],
        [wq, wq_peer, wo],
        [
            shaped((rows // CORES, model)),
            shaped((rows, model // CORES)),
            shaped((rows, wo.shape[0])),
            shaped((1, model), F32),
        ],
        "mid_backward",
    )


def first_backward(place, dz, past, riders, mem_parts, wk, wv):
    rows, model = dz.shape
    slim = wk.shape[1]
    own_rows = rows // CORES
    joint = riders is not None
    mem_rows = mem_parts.shape[0] // (CORES * CORES) if joint else 0

    def body(place_ref, arrays, weight, outs, scratch):
        core = place_ref[1]
        pairs = []
        if joint:
            past_at, mem_at = past[0][1], riders[0][1]
            blocks = [arrays[1][past_at + at * rows : past_at + (at + 1) * rows] for at in range(2 * slim // LANES)]
            pairs.append((jnp.concatenate(blocks[: slim // LANES], 1), jnp.concatenate(blocks[slim // LANES :], 1)))
        else:
            pairs += [(ref[0], ref[1]) for ref in arrays[1:]]
        total = arrays[0][...].astype(F32)
        for dk, dv in pairs:
            total = total + dot_right(dk, weight(0)[...]) + dot_right(dv, weight(1)[...])
        outs[0][...] = pick(core, total, 0)
        outs[1][:own_rows] = pick(core, total, 0, True).astype(BF16)
        if joint:
            half = CORES * mem_rows
            mine = pick(place_ref[2] // CORES, arrays[3][...].astype(F32), 0)
            got = [arrays[2][mem_at + at * half : mem_at + (at + 1) * half].astype(F32) for at in range(model // LANES)]
            mine = mine + jnp.concatenate(got, axis=1)
            outs[2][...] = pick(core, mine, 0)
            outs[1][own_rows:] = pick(core, mine, 0, True).astype(BF16)

    outs = [shaped((own_rows, model), F32), shaped((own_rows + mem_rows, model))]
    if joint:
        outs.append(shaped((mem_rows, model), F32))
    return whole_kernel(
        body, place, [dz] + ([past[0][0], riders[0][0], mem_parts] if joint else past), [wk, wv], outs, "first_backward"
    )


def tokens_backward(place, dz, dz_got, mem, tokens, g_mid, gain):
    rows = tokens.shape[0]

    def body(place_ref, arrays, weight, outs, scratch):
        dz_ref, dz_got_ref, tokens_ref, g_ref, gain_ref = arrays[:5]
        dz_value = dz_ref[...] + dz_got_ref[:rows].astype(F32)
        hidden = tokens_ref[...].astype(F32)
        grad = norm_back(hidden, inverse_norm(hidden), gain_ref[...].astype(F32), dz_value)
        outs[0][...] = (g_ref[...].astype(F32) + grad).astype(BF16)
        if mem:
            outs[1][...] = (arrays[5][...] + dz_got_ref[rows:].astype(F32)).astype(BF16)

    outs = [shaped(tokens.shape)] + [shaped(m.shape) for m in mem]
    return whole_kernel(body, place, [dz, dz_got, tokens, g_mid, gain] + mem, [], outs, "tokens_backward")


def layer_output(place, late, inner, inner_peer, wd, wd_peer):
    rows, model = late.shape

    def body(place_ref, arrays, weight, outs, scratch):
        own, inner_own, inner_other = (pick(place_ref[1], ref[...], 0) for ref in arrays)
        total = own.astype(F32) + dot(inner_own, weight(0)[...]) + dot(inner_other, weight(1)[...])
        outs[0][...] = total.astype(BF16)

    return whole_kernel(
        body,
        place,
        [late, inner, inner_peer],
        [wd, wd_peer],
        [shaped((rows // CORES, model))],
        "layer_output",
        cost=10,
    )[0]


def memory_backward(place, dk, dv, wk, wv):
    def body(place_ref, arrays, weight, outs, scratch):
        grad = dot_right(arrays[0][...], weight(0)[...]) + dot_right(arrays[1][...], weight(1)[...])
        outs[0][...] = grad.astype(BF16)

    weights = [(wk, 1, False), (wv, 1, False)]
    return whole_kernel(body, place, [dk, dv], weights, [shaped((dk.shape[0], wk.shape[0]))], "memory_backward")[0]


def small_sums(place, dq, dk, dv, d_past, own, peer, past_own, past_peer, two, three, near, total, buckets, weights, chips, fetch):
    rows, model = dq.shape[0], own.shape[1]
    earlier = len(past_own)
    heads = HEADS // CORES

    def body(place_ref, arrays, weight, outs, scratch):
        dq_ref, dk_ref, dv_ref, past_ref, own_ref, peer_ref = arrays[:6]
        past_own_refs, past_peer_refs = arrays[6 : 6 + earlier], arrays[6 + earlier : 6 + 2 * earlier]
        two_ref, three_ref, near_ref, total_ref, bucket_ref = arrays[6 + 2 * earlier :]
        core = place_ref[1]
        first = core == 0

        def gain_part(dz, own_ref, peer_ref):
            hidden = in_place_order(core, own_ref, peer_ref)
            return jnp.sum(dz * (hidden * inverse_norm(hidden)), axis=0, keepdims=True)

        dz = dot_right(dq_ref[...], weight(0)[...])
        dz = dz + dot_right(dk_ref[...], weight(1)[...]) + dot_right(dv_ref[...], weight(2)[...])
        outs[0][...] = dz.astype(BF16)
        one = gain_part(dz, own_ref, peer_ref)
        for s in range(earlier):
            dz = dot_right(past_ref[s, 0], weight(1)[...]) + dot_right(past_ref[s, 1], weight(2)[...])
            one = one + gain_part(dz, past_own_refs[s], past_peer_refs[s])
        gains = [one, jnp.where(first, two_ref[...], 0.0), jnp.where(first, three_ref[...], 0.0)]
        near = jnp.concatenate([near_ref[p, :4] for p in range(heads // 4)], axis=0)
        total = jnp.concatenate([total_ref[p, :4] for p in range(heads // 4)], axis=0)
        far = jnp.sum(total, axis=1, keepdims=True) - jnp.sum(near, axis=1, keepdims=True)
        last = lax.broadcasted_iota(jnp.int32, near.shape, 1) == near.shape[1] - 1
        near = near + jnp.where(last, far, 0.0)
        entries = BUCKETS * HEADS
        entry = lax.broadcasted_iota(jnp.int32, (near.shape[1], entries), 1)
        same = (lax.shift_right_logical(entry, jnp.int32(HEADS.bit_length() - 1)) == bucket_ref[...]).astype(F32)
        sums = jnp.dot(near, same, precision=lax.Precision.HIGHEST, preferred_element_type=F32)
        head = lax.broadcasted_iota(jnp.int32, sums.shape, 0) + core * heads
        of_entry = jnp.bitwise_and(lax.broadcasted_iota(jnp.int32, sums.shape, 1), jnp.int32(HEADS - 1))
        vectors = gains + [jnp.sum(jnp.where(head == of_entry, sums, 0.0), axis=0, keepdims=True)]
        for block in range(chips):
            lines = []
            for vector in vectors:
                size = vector.shape[1] // chips
                line = vector[:, block * size : (block + 1) * size]
                lines.append(jnp.concatenate([line, jnp.zeros((1, LANES - size), F32)], axis=1))
            lines.append(jnp.zeros((12, LANES), F32))
            outs[1][block * 16 : (block + 1) * 16] = jnp.concatenate(lines, axis=0).astype(BF16)

    arrays = [dq, dk, dv, d_past, own, peer] + past_own + past_peer + [two, three, near, total, buckets]
    return whole_kernel(
        body, place, arrays, weights, [shaped((rows, model)), shaped((chips * 16, LANES))], "small_sums", fetch=fetch
    )


def gather_sums(place, parts, name):
    def body(place_ref, arrays, weight, outs, scratch):
        for array, out in zip(arrays, outs):
            total = array[0].astype(F32)
            for at in range(1, array.shape[0]):
                total = total + array[at].astype(F32)
            out[...] = total.astype(out.dtype)

    return whole_kernel(body, place, parts, [], [shaped(a.shape[1:], a.dtype) for a in parts], name)


def up_to(value, multiple):
    return (value + multiple - 1) // multiple * multiple


def array_of(y):
    return y[0] if isinstance(y, tuple) else y


class Flow:
    def __init__(self, name, pieces, order, extra=None):
        self.name, self.pieces, self.order, self.extra = name, pieces, order, extra
        self.hops = [bit + 1 for bit in order]
        self.chips = 1 << len(order)
        self.layout = []
        start = 0
        for terms, rows in pieces:
            half = rows // self.chips // CORES
            padded = up_to(half, 8)
            width = array_of(terms[0][1]).shape[-1]
            self.layout.append((start, half, padded, width))
            start += CORES * padded * (width // LANES)
        self.extra_at = start
        self.rows = start + (16 if extra is not None else 0)
        self.keep = self.got = None

    def spread(self, x):
        half, padded = self.layout[0][1:3]
        if half == padded:
            return x
        chunks = x.reshape(x.shape[0], -1, half)
        return jnp.pad(chunks, ((0, 0), (0, 0), (0, padded - half))).reshape(x.shape[0], -1)


def chip_of(spot, order):
    number = 0
    for at, bit in enumerate(order):
        number |= (spot >> (len(order) - 1 - at) & 1) << bit
    return number


def sum_flow(flow, refs_of, place_ref, turned, free, send_ref, base, keep_ref):
    chip, core = place_ref[0], place_ref[1]
    half = flow.chips // 2
    for (terms, _), (start, _, padded, width) in zip(flow.pieces, flow.layout):
        chunk = CORES * padded
        lefts = []
        for xs, y in terms:
            key = (tuple(id(x) for x in xs), flow.order)
            if key not in turned:
                straight_ref, turned[key] = free.pop(0), free.pop(0)
                if len(xs) == 1:
                    straight_ref[...] = refs_of[id(xs[0])][...].T
                else:
                    size = straight_ref.shape[0] // CORES
                    for part, x in enumerate(xs):
                        at = (core if part == 0 else 1 - core) * size
                        straight_ref[pl.ds(pl.multiple_of(at, 16), size)] = refs_of[id(x)][...].T
                for spot in range(flow.chips):
                    at = jnp.bitwise_xor(jnp.int32(chip_of(spot, flow.order)), chip) * chunk
                    turned[key][spot * chunk : (spot + 1) * chunk] = straight_ref[pl.ds(pl.multiple_of(at, 16), chunk)]
            lefts.append(turned[key])
        count = max(1, min(flow.chips, 512 // chunk))
        while flow.chips % count:
            count -= 1
        for first in range(0, flow.chips, count):
            tile = None
            for left, (_, y) in zip(lefts, terms):
                y_ref = refs_of[id(array_of(y))]
                y_value = y_ref[y[1]] if isinstance(y, tuple) else y_ref[...]
                term = dot(left[first * chunk : (first + count) * chunk], y_value)
                tile = term if tile is None else tile + term
            tile = tile.astype(BF16)
            for inner in range(count):
                spot = first + inner
                for block in range(width // LANES):
                    value = tile[inner * chunk : (inner + 1) * chunk, block * LANES : (block + 1) * LANES]
                    at = start + block * chunk
                    if spot < half:
                        keep_ref[spot, at : at + chunk] = value
                    else:
                        at += base + (spot - half) * flow.rows
                        send_ref[at : at + chunk] = value


def copy_extra(flow, extra_ref, place_ref, send_ref, base, keep_ref):
    half = flow.chips // 2
    for spot in range(flow.chips):
        at = jnp.bitwise_xor(jnp.int32(chip_of(spot, flow.order)), place_ref[0]) * 16
        value = extra_ref[pl.ds(pl.multiple_of(at, 16), 16)]
        if spot < half:
            keep_ref[spot, flow.extra_at : flow.extra_at + 16] = value
        else:
            to = base + (spot - half) * flow.rows + flow.extra_at
            send_ref[to : to + 16] = value


def add_flow(flow, old_ref, got_ref, got_at, send_ref, base, keep_ref):
    half = old_ref.shape[0] // 2
    for spot in range(2 * half):
        at = got_at + spot * flow.rows
        total = (old_ref[spot].astype(F32) + got_ref[at : at + flow.rows].astype(F32)).astype(BF16)
        if spot < half:
            keep_ref[spot] = total
        else:
            send_ref[base + (spot - half) * flow.rows : base + (spot - half + 1) * flow.rows] = total


def hop(place, swap, sums, adds, after, name, cost=0, riders=(), fetch=()):
    arrays, seen = [], {}

    def take(array):
        if id(array) not in seen:
            seen[id(array)] = len(arrays)
            arrays.append(array)

    for flow in sums:
        for terms, _ in flow.pieces:
            for xs, y in terms:
                for array in (*xs, array_of(y)):
                    take(array)
        if flow.extra is not None:
            take(flow.extra)
    for flow in adds:
        take(flow.keep)
        take(flow.got[0])
    bits, sends, keeps = {}, {}, {}
    for flow in sums + adds:
        half = (flow.chips if flow in sums else flow.keep.shape[0]) // 2
        bit = flow.hops[0]
        base = bits.setdefault(bit, 0)
        sends[flow.name] = (bit, base)
        bits[bit] = base + half * flow.rows
        keeps[flow.name] = shaped((half, flow.rows, LANES))
    rider_at = []
    for rider, bit, size, _ in riders:
        take(rider)
        rider_at.append(bits.setdefault(bit, 0))
        bits[bit] = rider_at[-1] + size
    order = list(bits)
    outs = [shaped((bits[bit], LANES)) for bit in order] + list(keeps.values())

    def body(place_ref, refs, weight, out_refs, scratch):
        refs_of = {key: refs[at] for key, at in seen.items()}
        turned, free = {}, list(scratch)
        for at, flow in enumerate(sums + adds):
            bit, base = sends[flow.name]
            send_ref, keep_ref = out_refs[order.index(bit)], out_refs[len(order) + at]
            if flow in sums:
                sum_flow(flow, refs_of, place_ref, turned, free, send_ref, base, keep_ref)
                if flow.extra is not None:
                    copy_extra(flow, refs_of[id(flow.extra)], place_ref, send_ref, base, keep_ref)
            else:
                add_flow(
                    flow, refs_of[id(flow.keep)], refs_of[id(flow.got[0])], flow.got[1], send_ref, base, keep_ref
                )
        for (rider, bit, _, write), at in zip(riders, rider_at):
            write(refs_of[id(rider)], out_refs[order.index(bit)], at, place_ref)

    needed = {}
    for flow in sums:
        for terms, _ in flow.pieces:
            for xs, _ in terms:
                shape = (sum(x.shape[1] for x in xs), xs[0].shape[0])
                needed[(tuple(id(x) for x in xs), flow.order)] = [pltpu.VMEM(shape, BF16)] * 2
    scratch = sum(needed.values(), [])
    made = whole_kernel(body, place, follow(arrays, after), [], outs, name, scratch, cost=cost, fetch=fetch)
    moved = [swap(array, bit) for array, bit in zip(made, order)]
    for at, flow in enumerate(sums + adds):
        bit, base = sends[flow.name]
        flow.keep, flow.got, flow.hops = made[len(order) + at], (moved[order.index(bit)], base), flow.hops[1:]
    if riders:
        return list(made), [(moved[order.index(bit)], at) for (_, bit, _, _), at in zip(riders, rider_at)]
    return list(made)


def write_flat(ref, send_ref, at, place_ref):
    send_ref[at : at + ref.shape[0]] = ref[...]


def write_past(past_ref, send_ref, at, place_ref):
    _, pages, rows, width = past_ref.shape
    for page in range(pages):
        for block in range(width // LANES):
            send_ref[at : at + rows] = past_ref[0, page, :, block * LANES : (block + 1) * LANES]
            at += rows


def write_memory(mem_ref, send_ref, at, place_ref):
    rows = mem_ref.shape[0] // CORES
    there = pl.ds(pl.multiple_of((1 - place_ref[2] // CORES) * rows, rows), rows)
    for block in range(mem_ref.shape[1] // LANES):
        send_ref[at : at + rows] = mem_ref[there, block * LANES : (block + 1) * LANES]
        at += rows


def last_hop(place, swap, flows, after, name, shares=()):
    arrays, seen = [], {}
    for flow in flows:
        for array in (flow.keep, flow.got[0]):
            if id(array) not in seen:
                seen[id(array)] = len(arrays)
                arrays.append(array)
    blocks = []
    size = 0
    for f, flow in enumerate(flows):
        for piece, (start, half, padded, width) in enumerate(flow.layout):
            for block in range(width // LANES):
                blocks.append((f, piece, start + block * CORES * padded, padded, block, size))
                size += up_to(padded, 16)
    extras = [(f, flow.extra_at, size + 16 * sum(x.extra is not None for x in flows[:f])) for f, flow in enumerate(flows) if flow.extra is not None]
    size += 16 * len(extras)
    own_outs = [
        shaped((padded, width), F32) for flow in flows for _, _, padded, width in flow.layout
    ]
    own_outs += [shaped((16, LANES), F32) for _ in extras]
    n_pieces = len(own_outs) - len(extras)
    first = [sum(len(flow.layout) for flow in flows[:f]) for f in range(len(flows))]

    def add_body(place_ref, refs, weight, outs, scratch):
        core = place_ref[1]
        for f, piece, at, padded, block, leave_at in blocks:
            flow = flows[f]
            got_at = flow.got[1] + at
            total = refs[seen[id(flow.keep)]][0, at : at + CORES * padded].astype(F32)
            total = total + refs[seen[id(flow.got[0])]][got_at : got_at + CORES * padded].astype(F32)
            own, leave = pick(core, total, 0), pick(core, total, 0, True)
            outs[1 + first[f] + piece][:, block * LANES : (block + 1) * LANES] = own
            full = up_to(padded, 16)
            if full > padded:
                leave = jnp.concatenate([leave, jnp.zeros((full - padded, LANES), F32)], axis=0)
            outs[0][leave_at : leave_at + full] = leave.astype(BF16)
        for at, (f, start, leave_at) in enumerate(extras):
            flow = flows[f]
            got_at = flow.got[1] + start
            total = refs[seen[id(flow.keep)]][0, start : start + 16].astype(F32)
            total = total + refs[seen[id(flow.got[0])]][got_at : got_at + 16].astype(F32)
            outs[1 + n_pieces + at][...] = total
            outs[0][leave_at : leave_at + 16] = total.astype(BF16)

    made = whole_kernel(add_body, place, follow(arrays, after), [], [shaped((size, LANES))] + own_outs, "last_" + name)
    got = swap(made[0], 0)

    def join_body(place_ref, refs, weight, outs, scratch):
        core = place_ref[1]
        for f, piece, _, padded, block, leave_at in blocks:
            at = first[f] + piece
            width = refs[1 + at].shape[1]
            own = refs[1 + at][:, block * LANES : (block + 1) * LANES]
            other = refs[0][leave_at : leave_at + up_to(padded, 16)].astype(F32)[:padded]
            low, high = slice(block * LANES, (block + 1) * LANES), slice(width + block * LANES, width + (block + 1) * LANES)
            outs[at][:, low] = jnp.where(core == 0, own, other)
            outs[at][:, high] = jnp.where(core == 0, other, own)
        for at, (_, _, leave_at) in enumerate(extras):
            total = refs[1 + n_pieces + at][...] + refs[0][leave_at : leave_at + 16].astype(F32)
            for line, (out, share) in enumerate(zip(outs[n_pieces:], shares)):
                out[...] = jnp.where(core == 0, total[line, :share], total[line, share : 2 * share])

    joined = whole_kernel(
        join_body,
        place,
        [got] + list(made[1:]),
        [],
        [shaped((a.shape[0], CORES * a.shape[1]), F32) for a in own_outs[:n_pieces]]
        + [shaped((share,), F32) for _ in extras for share in shares],
        "join_" + name,
    )
    results = {}
    for f, flow in enumerate(flows):
        results[flow.name] = [
            joined[first[f] + piece][:half] for piece, (_, half, _, _) in enumerate(flow.layout)
        ]
    if extras:
        results["small"] = joined[n_pieces:]
    return results, list(made)


def follow(value, after):
    return lax.optimization_barrier((value, after))[0]


def rel_bucket(distance):
    beyond = 16 + sum((distance >= border).astype(jnp.int32) for border in THRESHOLDS)
    return jnp.where(distance < 16, distance, beyond)


def shards(
    tokens, memory, cotangent, bucket, gain_self, self_query, self_key, self_value, self_out, rel_bias,
    gain_cross, cross_query, cross_key, cross_value, cross_out, gain_ffn, ffn_gate, ffn_up, ffn_down,
):
    groups = lax.axis_size("grp")
    dp_size = lax.axis_size("dp")
    n_chips = groups // CORES
    more = n_chips - 1
    chips = dp_size * n_chips
    devices = chips * CORES
    grp_at = lax.axis_index("grp")
    core = grp_at % CORES
    y_at = grp_at // CORES
    chip = lax.axis_index("dp") * n_chips + y_at
    rows, model = tokens.shape
    chip_rows = rows * CORES
    group_rows = chip_rows * n_chips
    hidden_units = ffn_down.shape[0]
    length = jnp.minimum(group_rows, jnp.maximum(SHORT, jnp.right_shift(jnp.int32(group_rows), bucket[0])))
    y_bits = n_chips.bit_length() - 1
    bits = chips.bit_length() - 1
    first_chip = y_at * chip_rows // length * length // chip_rows
    valid = [(y_at - s >= first_chip).astype(jnp.int32) for s in range(1, n_chips)]
    place = jnp.stack([chip, core, grp_at] + valid).astype(jnp.int32)

    def swap(v, bit):
        return lax.ppermute(v, ("dp", "grp"), [(i, i ^ (1 << bit)) for i in range(devices)])

    gain_one, gain_two, gain_three = (g.reshape(1, model) for g in (gain_self, gain_cross, gain_ffn))

    past_own = [
        lax.ppermute(tokens, "grp", [(g, g + CORES * s) for g in range(groups - CORES * s)]) for s in range(1, n_chips)
    ]
    tokens_peer = swap(tokens, 0)
    mems = [memory] + [
        lax.ppermute(memory, "grp", [(g, g ^ other) for g in range(groups)]) for other in range(1, groups)
    ]

    distances = jnp.arange(2 * NEAR, dtype=jnp.int32)
    buckets = rel_bucket(distances)[:, None]
    onehot = (buckets == jnp.arange(BUCKETS, dtype=jnp.int32)).astype(F32)
    heads = HEADS // CORES
    rel_local = lax.dynamic_slice_in_dim(rel_bias.astype(F32), core * heads, heads, 1)
    by_dist = jnp.dot(onehot, rel_local - rel_local[BUCKETS - 1 :], precision=lax.Precision.HIGHEST)
    table = jnp.pad(by_dist.T.reshape(heads // 4, 4, 2 * NEAR), ((0, 0), (0, 4), (0, 0)))

    low_one, q, k, v = project(place, tokens, tokens_peer, gain_one, self_query, self_key, self_value)
    *diagonal, w_gate, w_up = self_diagonal(place, table, q, k, v, [(ffn_gate, 1, False), (ffn_up, 1, False)])
    past_own = follow(past_own, diagonal)
    past_peer = [swap(own, 0) for own in past_own]
    cot_peer = swap(follow(cotangent, diagonal[0]), 0)
    low_past, k_past, v_past, w_down = project_past(
        place, past_own, past_peer, gain_one, self_key, self_value, [(ffn_down, 0, False)]
    )
    att, lse_self, w_out, w_out_peer, w_query, w_cross, w_cross_peer = self_past(
        place, table, q, k_past, v_past, *diagonal,
        [(self_out, 0, False), (self_out, 0, True), (cross_query, 1, False), (cross_out, 0, False), (cross_out, 0, True)],
    )
    att_peer = swap(att, 0)
    mem_all, km, vm = project_memory(place, follow(mems, att), cross_key, cross_value)
    att_peer = follow(att_peer, km)
    mid, low_two, cq = mid_forward(
        place, tokens, tokens_peer, att, att_peer, gain_two, w_out, w_out_peer, w_query
    )
    own_doc = []
    if group_rows > SHORT:
        mem_doc = jnp.arange(mem_all.shape[0], dtype=jnp.int32) // (length // RATIO)
        own = (mem_doc == y_at * chip_rows // length).astype(F32)
        own_doc = [jnp.broadcast_to(own[:, None], (mem_all.shape[0], TILE))]
    crs, lse_cross = cross_forward(place, cq, km, vm, own_doc)
    crs_peer = swap(crs, 0)
    cot_half, d_inner = cotangent_inner(place, follow(cotangent, crs), cot_peer, w_down)
    crs_peer = follow(crs_peer, d_inner)
    late, low_three, inner, d_gate, d_up, dz = ffn(
        place, mid, crs, crs_peer, gain_three, d_inner, w_cross, w_cross_peer, w_gate, w_up
    )

    axes = {
        "y": tuple(range(y_bits)),
        "x": (y_bits,),
        "z": (y_bits + 1,),
        "f": tuple(range(y_bits + 2, bits)),
    }

    def order_of(letters):
        return sum((axes[letter] for letter in letters), ())

    dz_peer = swap(dz, 0)
    inner_peer = swap(inner, 0)
    gate = Flow("gate", [([((low_three,), d_gate)], model)], order_of("xyzf"))
    up = Flow("up", [([((low_three,), d_up)], model)], order_of("yzfx"))
    last = hop(place, swap, [gate], [], place, "gate")
    last = hop(place, swap, [up], [], last, "up")
    down = Flow("down", [([((inner, inner_peer), cot_half)], hidden_units)], order_of("zxyf"))
    spread = (down.spread(inner), down.spread(inner_peer))
    down = Flow("down", [([(spread, cot_half)], hidden_units)], order_of("zxyf"))
    last = hop(place, swap, [down], [], last, "down")
    ffn_flows = [gate, up, down]

    g_late, late_half, d_crs, d_gain_three = late_backward(
        place, follow(dz, last), dz_peer, late, cotangent, cot_peer, gain_three, w_cross
    )
    dcq, dkm, dvm, w_query_peer = cross_backward(
        place, cq, km, vm, own_doc, d_crs, crs, lse_cross, [(cross_query, 1, True)]
    )
    dcq_peer = swap(dcq, 0)
    crs_mem = Flow(
        "crs_mem",
        [([((crs, crs_peer), late_half)], model), ([((mem_all,), dkm)], model), ([((mem_all,), dvm)], model)],
        order_of("zxyf"),
    )
    last = hop(place, swap, [crs_mem], [], dcq, "crs_mem", cost=5)
    g_mid, mid_half, d_att, d_gain_two = mid_backward(
        place, dcq, follow(dcq_peer, last), mid, g_late, gain_two, w_query, w_query_peer, w_out
    )
    att_cq = Flow("att_cq", [([((att, att_peer), mid_half)], model), ([((low_two,), dcq)], model)], order_of("xyzf"))
    last = hop(place, swap, [att_cq], [], d_att, "att_cq")
    dq, dk, dv, d_past, d_near, d_total, *w_first = self_backward(
        place, table, q, k, v, k_past, v_past, follow(d_att, last), att, lse_self,
        [(self_query, 1, False), (self_key, 1, False), (self_value, 1, False)],
    )
    mem_parts = memory_backward(place, follow(dkm, dq), dvm, cross_key, cross_value)
    past_moved, riders = [], None
    if n_chips == 2:
        y_bit = 1
        last, (riders,) = hop(
            place, swap, [], ffn_flows, mem_parts, "ffn_1",
            riders=[(mem_parts, y_bit, mem_parts.size // CORES // LANES, write_memory)],
        )
    else:
        past_moved = [
            lax.ppermute(d_past[s - 1], "grp", [(g, g - CORES * s) for g in range(CORES * s, groups)])
            for s in range(1, n_chips)
        ]
        last = hop(place, swap, [], ffn_flows, mem_parts, "ffn_1")
    dz, small, w_down, w_down_peer = small_sums(
        place, follow(dq, last), dk, dv, d_past, tokens, tokens_peer, past_own, past_peer, d_gain_two, d_gain_three,
        d_near, d_total, buckets, w_first, chips, [(ffn_down, 0, False), (ffn_down, 0, True)],
    )
    query = Flow("query", [([((low_one,), dq)], model)], order_of("xyzf"), small)
    kv = Flow(
        "kv",
        [
            ([((low_one,), d)] + [((low_past[s],), (d_past, (s, which))) for s in range(more)], model)
            for which, d in ((0, dk), (1, dv))
        ],
        order_of("yxzf"),
    )
    attention = [att_cq, crs_mem, query, kv]
    last = hop(place, lambda v, bit: v, [query, kv], [], dz, "query_kv")
    sent = [(flow.got[0], flow.order[0] + 1, flow.got[0].shape[0], write_flat) for flow in (query, kv)]
    last, (query.got, kv.got) = hop(
        place, swap, [], [att_cq, crs_mem], last, "attention_1", cost=5, riders=sent
    )

    results = {}
    names = {"ffn": ffn_flows, "attention": attention}

    def step(label, after, riders=(), fetch=()):
        flows = names[label]
        if label in results:
            return after
        moving = [flow for flow in flows if flow.hops]
        if moving:
            return hop(place, swap, [], moving, after, f"{label}_{len(moving[0].hops)}", cost=30, riders=riders, fetch=fetch)
        results[label], made = last_hop(place, swap, flows, after, label, [model // devices] * 3 + [BUCKETS * HEADS // devices])
        return made

    for label in ("ffn", "attention", "ffn"):
        last = step(label, last)
    if n_chips == 2:
        last, (past_rider,) = step("attention", last, [(d_past, y_bit, d_past.size // LANES, write_past)])
        past_moved, riders = [past_rider], [riders]
    else:
        last = step("attention", last)
    waiting = True
    while len(results) < 2:
        if "attention" not in results and not any(flow.hops for flow in attention):
            last = last + sum(results.get("ffn", {}).values(), [])
        last = step("ffn", last)
        if waiting and not any(flow.hops for flow in attention):
            waiting = False
            dz_own, dz_leave, *mem_own = first_backward(
                place, follow(dz, last), past_moved, riders, mem_parts, *w_first[1:]
            )
            dz_got = swap(dz_leave, 0)
            layer_out = layer_output(place, follow(late, dz_leave), inner, inner_peer, w_down, w_down_peer)
            dz_got = follow(dz_got, layer_out)
            grad_tokens, *grad_memory = tokens_backward(place, dz_own, dz_got, mem_own, tokens, g_mid, gain_one)
            if not grad_memory:
                parts = lax.all_to_all(mem_parts, "grp", split_axis=0, concat_axis=0, tiled=True)
                grad_memory = gather_sums(place, [parts.reshape(groups, -1, model)], "memory_sums")
            last = last + [grad_tokens]
        last = step("attention", last)
    got = {**results["ffn"], **results["attention"]}
    *gains, relative = got["small"]
    return (
        layer_out,
        grad_tokens,
        grad_memory[0],
        gains[0],
        got["query"][0],
        got["kv"][0],
        got["kv"][1],
        got["att_cq"][0],
        relative,
        gains[1],
        got["att_cq"][1],
        got["crs_mem"][1],
        got["crs_mem"][2],
        got["crs_mem"][0],
        gains[2],
        got["gate"][0],
        got["up"][0],
        got["down"][0],
    )


def solution(mesh):
    rows = P(("dp", "grp"), None)
    flat = P(("dp", "grp"))
    in_specs = (rows, rows, rows, P("dp")) + (P(),) * 15
    out_specs = (rows,) * 3 + (flat,) + (rows,) * 4 + (flat,) * 2 + (rows,) * 4 + (flat,) + (rows,) * 3
    return jax.shard_map(shards, mesh=mesh, in_specs=in_specs, out_specs=out_specs, check_vma=False)
```

```python
import functools

import jax
import jax.numpy as jnp
from jax import lax
from jax.experimental import pallas as pl
from jax.experimental.pallas import tpu as pltpu
from jax.sharding import PartitionSpec as P

SHORT = 1024
RATIO = 4
BUCKETS = 32
HEADS = 16
EPSILON = 1e-06
THRESHOLDS = (19, 21, 24, 27, 31, 35, 40, 46, 52, 59, 67, 77, 87, 99, 113)
CORES = 2
BF16 = jnp.bfloat16
F32 = jnp.float32
NEGATIVE = -1e30
HEAD = 64
TILE = 256
NEAR = 128
LANES = 128
ROOM = 16 * 1024 * 1024


def dot(a, b):
    return jnp.dot(a, b, preferred_element_type=F32)


def dot_right(a, b):
    return lax.dot_general(a, b, (((1,), (1,)), ((), ())), preferred_element_type=F32)


def shaped(shape, dtype=BF16):
    return jax.ShapeDtypeStruct(tuple(shape), dtype)


def half_shape(array, axis):
    shape = list(array.shape)
    shape[axis] //= CORES
    return tuple(shape)


def whole_kernel(body, place, arrays, weights, outs, name, scratch=(), room=ROOM, cost=0, fetch=()):
    ready = [w for w in weights if not isinstance(w, tuple)]
    far = [w for w in weights if isinstance(w, tuple)]
    n_a, n_r, n_w, n_o, n_f = len(arrays), len(ready), len(far), len(outs), len(fetch)
    buffers = [pltpu.VMEM(half_shape(array, axis), array.dtype) for array, axis, _ in far]
    fetched = [shaped(half_shape(array, axis), array.dtype) for array, axis, _ in fetch]

    def kernel(place_ref, *refs):
        array_refs, refs = refs[:n_a], refs[n_a:]
        ready_refs, refs = refs[:n_r], refs[n_r:]
        far_refs, refs = refs[: n_w + n_f], refs[n_w + n_f :]
        out_refs, refs = refs[:n_o], refs[n_o:]
        fetch_refs, refs = refs[:n_f], refs[n_f:]
        buffer_refs, refs = refs[:n_w], refs[n_w:]
        copies = []
        for at, (ref, buffer, (_, axis, other)) in enumerate(
            zip(far_refs, (*buffer_refs, *fetch_refs), (*far, *fetch))
        ):
            size = buffer.shape[axis]
            start = pl.multiple_of((1 - place_ref[1] if other else place_ref[1]) * size, size)
            source = ref.at[pl.ds(start, size)] if axis == 0 else ref.at[:, pl.ds(start, size)]
            copies.append(pltpu.make_async_copy(source, buffer, refs[0].at[at]))
        for copy in copies:
            copy.start()
        arrived = set()
        places = []
        for w in weights:
            places.append((isinstance(w, tuple), sum(isinstance(x, tuple) == isinstance(w, tuple) for x in weights[: len(places)])))

        def weight(at):
            distant, spot = places[at]
            if not distant:
                return ready_refs[spot]
            if spot not in arrived:
                copies[spot].wait()
                arrived.add(spot)
            return buffer_refs[spot]

        body(place_ref, array_refs, weight, out_refs, refs[1:] if n_w + n_f else refs)
        for copy in copies[n_w:]:
            copy.wait()

    inside = pl.BlockSpec(memory_space=pltpu.VMEM)
    scratch = buffers + ([pltpu.SemaphoreType.DMA((n_w + n_f,))] if n_w + n_f else []) + list(scratch)
    return pl.pallas_call(
        kernel,
        in_specs=[pl.BlockSpec(memory_space=pltpu.SMEM)]
        + [inside] * (n_a + n_r)
        + [pl.BlockSpec(memory_space=pltpu.HBM)] * (n_w + n_f),
        out_specs=[inside] * (n_o + n_f),
        out_shape=list(outs) + fetched,
        scratch_shapes=scratch,
        compiler_params=pltpu.CompilerParams(vmem_limit_bytes=room),
        cost_estimate=pl.CostEstimate(
            flops=int(1.15e9 * cost), bytes_accessed=int(3.69e6 * cost), transcendentals=0
        ),
        name=name,
    )(
        place,
        *arrays,
        *ready,
        *[pltpu.with_memory_space_constraint(array, pltpu.HBM) for array, _, _ in (*far, *fetch)],
    )


def inverse_norm(hidden):
    return lax.rsqrt(jnp.mean(hidden * hidden, axis=-1, keepdims=True) + EPSILON)


def norm_low(hidden, inverse, gain):
    return (hidden * inverse * gain).astype(BF16)


def norm_back(hidden, inverse, gain, dz):
    scaled = gain * dz
    inner = jnp.mean(scaled * hidden, axis=-1, keepdims=True)
    return inverse * scaled - hidden * (inverse * inverse * inverse) * inner


def pick(core, value, axis, other=False):
    half = value.shape[axis] // CORES
    low, high = lax.slice_in_dim(value, 0, half, axis=axis), lax.slice_in_dim(value, half, 2 * half, axis=axis)
    return jnp.where(core == (1 if other else 0), low, high)


def in_place_order(core, own_ref, peer_ref):
    own, peer = own_ref[...].astype(F32), peer_ref[...].astype(F32)
    return jnp.concatenate([jnp.where(core == 0, own, peer), jnp.where(core == 0, peer, own)], axis=0)


def place_rows(half, at):
    zero = jnp.zeros_like(half)
    return jnp.concatenate([half, zero] if at == 0 else [zero, half], axis=0)


def place_lanes(pair, source, at):
    lane = lax.broadcasted_iota(jnp.int32, pair.shape, 1)
    if source != at:
        pair = jnp.concatenate([pair[:, HEAD:], pair[:, :HEAD]], axis=1)
    return jnp.where((lane < HEAD) == (at == 0), pair, jnp.zeros_like(pair))


def near_tiles(table_row):
    skewed = pltpu.roll(jnp.broadcast_to(table_row, (NEAR, 2 * NEAR)), 0, 1, stride=1, stride_axis=0)
    key_at = lax.broadcasted_iota(jnp.int32, (NEAR, NEAR), 0)
    row_at = lax.broadcasted_iota(jnp.int32, (NEAR, NEAR), 1)
    return (jnp.where(key_at <= row_at, skewed[:, :NEAR], NEGATIVE), skewed[:, NEAR:])


def heads_of(pair_turned, cols):
    return jnp.concatenate(
        [place_rows(pair_turned[h * HEAD : (h + 1) * HEAD, cols], h // 2) for h in range(4)], axis=1
    )


def add_corner(scores, tiles):
    rows = scores.shape[0]
    last = scores[rows - NEAR :]
    pieces = []
    for h in range(4):
        pieces += [last[:, h * TILE : h * TILE + NEAR] + tiles[h][1], last[:, h * TILE + NEAR : (h + 1) * TILE]]
    return jnp.concatenate([scores[: rows - NEAR], jnp.concatenate(pieces, axis=1)], axis=0)


def add_diagonal(scores, tiles):
    rows = scores.shape[0]
    first = scores[rows - TILE : rows - NEAR]
    second = scores[rows - NEAR :]
    upper, lower = [], []
    for h in range(4):
        left, right = slice(h * TILE, h * TILE + NEAR), slice(h * TILE + NEAR, (h + 1) * TILE)
        upper += [first[:, left] + tiles[h][0], first[:, right] + tiles[h][1]]
        lower += [jnp.full((NEAR, NEAR), NEGATIVE, F32), second[:, right] + tiles[h][0]]
    last = [jnp.concatenate(upper, axis=1), jnp.concatenate(lower, axis=1)]
    if rows > TILE:
        last = [add_corner(scores[: rows - TILE], tiles)] + last
    return jnp.concatenate(last, axis=0)


def by_distance(near):
    level = near[:8]
    for first in range(8, NEAR, 8):
        level = level + pltpu.roll(near[first : first + 8], 2 * NEAR - first, 1)
    row = lax.broadcasted_iota(jnp.int32, level.shape, 0)
    for bit in (1, 2, 4):
        level = jnp.where(row & bit > 0, pltpu.roll(level, 2 * NEAR - bit, 1), level)
    return jnp.sum(level, axis=0, keepdims=True)


def soft(scores):
    peak = jnp.max(scores, axis=0, keepdims=True)
    weights = jnp.exp(scores - peak)
    return peak, weights.astype(BF16), jnp.sum(weights, axis=0, keepdims=True)


def finish(o_ref, lse_ref, cols, peak, summed, acc):
    out = acc / summed
    lse = peak + jnp.log(summed)
    pieces = []
    for h in range(4):
        e = h // 2
        lanes = slice(h * TILE, (h + 1) * TILE)
        pieces.append(out[e * HEAD : (e + 1) * HEAD, lanes])
        lse_ref[0, h : h + 1, cols] = lse[:, lanes]
    o_ref[cols, :] = jnp.concatenate(pieces, axis=0).T.astype(BF16)


def self_diagonal_block(table_ref, q_ref, k_ref, v_ref, peak_ref, sum_ref, acc_ref):
    rows = q_ref.shape[0]
    v_turned = v_ref[...].T
    q_turned = q_ref[...].T
    tiles = [near_tiles(table_ref[0, h : h + 1, :]) for h in range(4)]
    spans = [slice(t * TILE, (t + 1) * TILE) for t in range(rows // TILE)]
    scores = [add_diagonal(dot(k_ref[: cols.stop], heads_of(q_turned, cols)), tiles) for cols in spans]
    parts = [soft(score) for score in scores]
    for t, cols in enumerate(spans):
        peak_ref[t], sum_ref[t] = parts[t][0], parts[t][2]
        acc_ref[t] = dot(v_turned[:, : cols.stop], parts[t][1])


def self_past_blocks(valid_ref, blocks, *, earlier):
    steps = blocks[0][1].shape[0] // TILE
    spans = [slice(t * TILE, (t + 1) * TILE) for t in range(steps)]
    units = [(p, t) for p in range(len(blocks)) for t in range(steps)]
    for s in range(earlier):

        @pl.when(valid_ref[3 + s] > 0)
        def _(s=s):
            turned = [block[1][...].T for block in blocks]
            values = [block[3][s].T for block in blocks]

            def scores_of(p, t):
                scores = dot(blocks[p][2][s], heads_of(turned[p], spans[t]))
                if s == 0 and t == 0:
                    table_ref = blocks[p][0]
                    scores = add_corner(scores, [near_tiles(table_ref[0, h : h + 1, :]) for h in range(4)])
                return scores

            ready = scores_of(*units[0])
            for at, (p, t) in enumerate(units):
                scores = ready
                if at + 1 < len(units):
                    ready = scores_of(*units[at + 1])
                _, _, _, _, peak_in, sum_in, acc_in, o_ref, lse_ref, peak_ref, sum_ref, acc_ref = blocks[p]
                old = (peak_in, sum_in, acc_in) if s == 0 else (peak_ref, sum_ref, acc_ref)
                peak = old[0][t]
                new_peak = jnp.maximum(peak, jnp.max(scores, axis=0, keepdims=True))
                rescale = jnp.exp(peak - new_peak)
                weights = jnp.exp(scores - new_peak)
                summed = old[1][t] * rescale + jnp.sum(weights, axis=0, keepdims=True)
                acc = old[2][t] * rescale + dot(values[p], weights.astype(BF16))
                if s + 1 < earlier:
                    peak_ref[t], sum_ref[t], acc_ref[t] = new_peak, summed, acc
                else:
                    finish(o_ref, lse_ref, spans[t], new_peak, summed, acc)

        @pl.when(valid_ref[3 + s] == 0)
        def _(s=s):
            for p, t in units:
                _, _, _, _, peak_in, sum_in, acc_in, o_ref, lse_ref, peak_ref, sum_ref, acc_ref = blocks[p]
                old = (peak_in, sum_in, acc_in) if s == 0 else (peak_ref, sum_ref, acc_ref)
                if s + 1 < earlier:
                    peak_ref[t], sum_ref[t], acc_ref[t] = old[0][t], old[1][t], old[2][t]
                else:
                    finish(o_ref, lse_ref, spans[t], old[0][t], old[1][t], old[2][t])


def placed_heads(block, cols):
    rows = []
    for h in range(4):
        pair = block[cols, (h // 2) * 2 * HEAD : (h // 2 + 1) * 2 * HEAD]
        rows.append(place_lanes(pair, h % 2, h // 2))
    return jnp.concatenate(rows, axis=0)


def row_of_heads(ref, cols):
    return jnp.concatenate([ref[0, h : h + 1, cols] for h in range(4)], axis=1)


def deltas(product, cols):
    return jnp.concatenate(
        [jnp.sum(product[h * HEAD : (h + 1) * HEAD, cols], axis=0, keepdims=True) for h in range(4)], axis=1
    )


def back_scores(scores, lse, d_prob, delta):
    prob = jnp.exp(scores - lse)
    d_score = prob * (d_prob - delta)
    return prob.astype(BF16), d_score.astype(BF16)


def query_rows(d_query):
    pieces = [
        d_query[(h // 2) * HEAD : (h // 2 + 1) * HEAD, h * TILE : (h + 1) * TILE] for h in range(4)
    ]
    return jnp.concatenate(pieces, axis=0).T.astype(BF16)


def self_backward_block(
    valid_ref, table_ref, q_ref, k_ref, v_ref, kp_ref, vp_ref, do_ref, o_ref, lse_ref,
    dq_ref, dk_ref, dv_ref, past_ref, db_ref, total_ref,
    near_sum, dq_sum, *, earlier,
):
    rows = q_ref.shape[0]
    steps = rows // TILE
    spans = [slice(t * TILE, (t + 1) * TILE) for t in range(steps)]
    k_turned = k_ref[...].T
    q_turned = q_ref[...].T
    do_turned = do_ref[...].T
    product = (do_ref[...].astype(F32) * o_ref[...].astype(F32)).T
    tiles = [near_tiles(table_ref[0, h : h + 1, :]) for h in range(4)]
    queries = [heads_of(q_turned, cols) for cols in spans]
    outs = [heads_of(do_turned, cols) for cols in spans]
    q_placed = [placed_heads(q_ref, cols) for cols in spans]
    do_placed = [placed_heads(do_ref, cols) for cols in spans]
    lses = [row_of_heads(lse_ref, cols) for cols in spans]
    delta = [deltas(product, cols) for cols in spans]

    for t, cols in enumerate(spans):
        seen = cols.stop
        scores = add_diagonal(dot(k_ref[:seen], queries[t]), tiles)
        prob, d_score = back_scores(scores, lses[t], dot(v_ref[:seen], outs[t]), delta[t])
        d_value = dot(prob, do_placed[t])
        d_key = dot(d_score, q_placed[t])
        if t == 0:
            dv_whole, dk_whole = d_value, d_key
        else:
            more = seen - dv_whole.shape[0]
            dv_whole = jnp.concatenate([dv_whole + d_value[: seen - more], d_value[seen - more :]], axis=0)
            dk_whole = jnp.concatenate([dk_whole + d_key[: seen - more], d_key[seen - more :]], axis=0)
        dq_sum[t] = dot(k_turned[:, :seen], d_score)
        d_wide = d_score.astype(F32)
        total = jnp.sum(d_wide, axis=0, keepdims=True)
        base = seen - TILE
        for h in range(4):
            left, right = slice(h * TILE, h * TILE + NEAR), slice(h * TILE + NEAR, (h + 1) * TILE)
            zero_part = d_wide[base : base + NEAR, left] + d_wide[base + NEAR :, right]
            one_part = d_wide[base : base + NEAR, right]
            if t > 0:
                one_part = one_part + d_wide[base - NEAR : base, left]
            both = jnp.concatenate([zero_part, one_part], axis=1)
            part = total[:, h * TILE : (h + 1) * TILE]
            if t == 0:
                near_sum[h] = both
                total_ref[0, h : h + 1, :] = part
            else:
                near_sum[h] += both
                total_ref[0, h : h + 1, :] += part
    dk_ref[...] = dk_whole.astype(BF16)
    dv_ref[...] = dv_whole.astype(BF16)

    for s in range(earlier):

        @pl.when(valid_ref[3 + s] > 0)
        def _(s=s):
            kp_turned = kp_ref[s].T
            for t in range(steps):
                scores = dot(kp_ref[s], queries[t])
                if s == 0 and t == 0:
                    scores = add_corner(scores, tiles)
                prob, d_score = back_scores(scores, lses[t], dot(vp_ref[s], outs[t]), delta[t])
                d_value = dot(prob, do_placed[t])
                d_key = dot(d_score, q_placed[t])
                dv_whole = d_value if t == 0 else dv_whole + d_value
                dk_whole = d_key if t == 0 else dk_whole + d_key
                dq_sum[t] += dot(kp_turned, d_score)
                d_wide = d_score.astype(F32)
                total = jnp.sum(d_wide, axis=0, keepdims=True)
                for h in range(4):
                    total_ref[0, h : h + 1, :] += total[:, h * TILE : (h + 1) * TILE]
                    if s == 0 and t == 0:
                        near_sum[h, :, NEAR:] += d_wide[rows - NEAR :, h * TILE : h * TILE + NEAR]
            past_ref[s, 0] = dk_whole.astype(BF16)
            past_ref[s, 1] = dv_whole.astype(BF16)

        @pl.when(valid_ref[3 + s] == 0)
        def _(s=s):
            past_ref[s] = jnp.zeros_like(past_ref[s])

    for t, cols in enumerate(spans):
        dq_ref[cols, :] = query_rows(dq_sum[t])
    for h in range(4):
        db_ref[0, h : h + 1, :] = by_distance(near_sum[h])
    db_ref[0, 4:, :] = jnp.zeros((4, 2 * NEAR), F32)
    total_ref[0, 4:, :] = jnp.zeros((4, 2 * NEAR), F32)


def cross_forward_block(q_ref, k_ref, v_ref, own_ref, o_ref, lse_ref, *, masked):
    rows = q_ref.shape[0]
    v_turned = v_ref[...].T
    q_turned = q_ref[...].T
    spans = [slice(t * TILE, (t + 1) * TILE) for t in range(rows // TILE)]
    scores = [dot(k_ref[...], heads_of(q_turned, cols)) for cols in spans]
    if masked:
        blocked = jnp.where(own_ref[...] > 0, 0.0, NEGATIVE)
        blocked = jnp.concatenate([blocked] * 4, axis=1)
        scores = [score + blocked for score in scores]
    for t, cols in enumerate(spans):
        peak, weights, summed = soft(scores[t])
        finish(o_ref, lse_ref, cols, peak, summed, dot(v_turned, weights))


def cross_backward_block(
    q_ref, k_ref, v_ref, own_ref, do_ref, o_ref, lse_ref, dq_ref, dk_ref, dv_ref, *, masked
):
    rows = q_ref.shape[0]
    k_turned = k_ref[...].T
    q_turned = q_ref[...].T
    do_turned = do_ref[...].T
    product = (do_ref[...].astype(F32) * o_ref[...].astype(F32)).T
    spans = [slice(t * TILE, (t + 1) * TILE) for t in range(rows // TILE)]
    dk_whole, dv_whole = 0.0, 0.0
    for t, cols in enumerate(spans):
        scores = dot(k_ref[...], heads_of(q_turned, cols))
        if masked:
            blocked = jnp.where(own_ref[...] > 0, 0.0, NEGATIVE)
            scores = scores + jnp.concatenate([blocked] * 4, axis=1)
        d_prob = dot(v_ref[...], heads_of(do_turned, cols))
        prob, d_score = back_scores(scores, row_of_heads(lse_ref, cols), d_prob, deltas(product, cols))
        dv_whole = dv_whole + dot(prob, placed_heads(do_ref, cols))
        dk_whole = dk_whole + dot(d_score, placed_heads(q_ref, cols))
        dq_ref[cols, :] = query_rows(dot(k_turned, d_score))
    dk_ref[...] = dk_whole.astype(BF16)
    dv_ref[...] = dv_whole.astype(BF16)


def wide_view(ref, p):
    return ref.at[:, pl.ds(p * 4 * HEAD, 4 * HEAD)]


def slim_view(ref, p):
    return ref.at[:, pl.ds(p * 2 * HEAD, 2 * HEAD)]


def past_view(ref, p):
    return ref.at[:, :, pl.ds(p * 2 * HEAD, 2 * HEAD)]


def page_view(ref, p):
    return ref.at[pl.ds(p, 1)]


def self_diagonal(place, table, q, k, v, fetch):
    rows, blocks = q.shape[0], k.shape[1] // (2 * HEAD)
    steps = rows // TILE

    def body(place_ref, arrays, weight, outs, scratch):
        table_ref, q_ref, k_ref, v_ref = arrays
        for p in range(blocks):
            self_diagonal_block(
                page_view(table_ref, p), wide_view(q_ref, p), slim_view(k_ref, p), slim_view(v_ref, p),
                *[ref.at[p] for ref in outs],
            )

    state = [(blocks, steps, 1, 4 * TILE), (blocks, steps, 1, 4 * TILE), (blocks, steps, 2 * HEAD, 4 * TILE)]
    return whole_kernel(body, place, [table, q, k, v], [], [shaped(shape, F32) for shape in state], "self_diagonal", fetch=fetch)


def self_past(place, table, q, kp, vp, peak, summed, acc, fetch):
    rows, blocks, earlier = q.shape[0], kp.shape[2] // (2 * HEAD), kp.shape[0]

    def body(place_ref, arrays, weight, outs, scratch):
        table_ref, q_ref, kp_ref, vp_ref, peak_ref, sum_ref, acc_ref = arrays
        views = [
            (
                page_view(table_ref, p), wide_view(q_ref, p), past_view(kp_ref, p), past_view(vp_ref, p),
                peak_ref.at[p], sum_ref.at[p], acc_ref.at[p], wide_view(outs[0], p), page_view(outs[1], p),
                *([ref.at[p] for ref in scratch] if earlier > 1 else [None] * 3),
            )
            for p in range(blocks)
        ]
        self_past_blocks(place_ref, views, earlier=earlier)

    return whole_kernel(
        body,
        place,
        [table, q, kp, vp, peak, summed, acc],
        [],
        [shaped(q.shape), shaped((blocks, 8, rows), F32)],
        "self_past",
        [pltpu.VMEM(a.shape, F32) for a in (peak, summed, acc)] if earlier > 1 else [],
        fetch=fetch,
    )


def self_backward(place, table, q, k, v, kp, vp, do, o, lse, fetch):
    rows, blocks, earlier = q.shape[0], k.shape[1] // (2 * HEAD), kp.shape[0]
    steps = rows // TILE

    def body(place_ref, arrays, weight, outs, scratch):
        table_ref, q_ref, k_ref, v_ref, kp_ref, vp_ref, do_ref, o_ref, lse_ref = arrays
        dq_ref, dk_ref, dv_ref, past_ref, db_ref, total_ref = outs
        for p in range(blocks):
            self_backward_block(
                place_ref, page_view(table_ref, p), wide_view(q_ref, p), slim_view(k_ref, p), slim_view(v_ref, p),
                past_view(kp_ref, p), past_view(vp_ref, p), wide_view(do_ref, p), wide_view(o_ref, p),
                page_view(lse_ref, p), wide_view(dq_ref, p), slim_view(dk_ref, p), slim_view(dv_ref, p),
                past_ref.at[:, :, :, pl.ds(p * 2 * HEAD, 2 * HEAD)], page_view(db_ref, p), page_view(total_ref, p),
                *[ref.at[p] for ref in scratch], earlier=earlier,
            )

    return whole_kernel(
        body,
        place,
        [table, q, k, v, kp, vp, do, o, lse],
        [],
        [
            shaped(q.shape),
            shaped(k.shape),
            shaped(k.shape),
            shaped((earlier, 2) + k.shape),
            shaped(table.shape, F32),
            shaped(table.shape, F32),
        ],
        "self_backward",
        [pltpu.VMEM((blocks, 4, NEAR, 2 * NEAR), F32), pltpu.VMEM((blocks, steps, 2 * HEAD, 4 * TILE), F32)],
        fetch=fetch,
    )


def cross_forward(place, q, k, v, own):
    rows, blocks = q.shape[0], k.shape[1] // (2 * HEAD)

    def body(place_ref, arrays, weight, outs, scratch):
        q_ref, k_ref, v_ref = arrays[:3]
        for p in range(blocks):
            cross_forward_block(
                wide_view(q_ref, p), slim_view(k_ref, p), slim_view(v_ref, p), arrays[-1], wide_view(outs[0], p),
                page_view(outs[1], p), masked=len(own) > 0,
            )

    outs = [shaped(q.shape), shaped((blocks, 8, rows), F32)]
    return whole_kernel(body, place, [q, k, v] + own, [], outs, "cross_forward")


def cross_backward(place, q, k, v, own, do, o, lse, fetch):
    blocks = k.shape[1] // (2 * HEAD)

    def body(place_ref, arrays, weight, outs, scratch):
        q_ref, k_ref, v_ref, do_ref, o_ref, lse_ref = arrays[:6]
        for p in range(blocks):
            cross_backward_block(
                wide_view(q_ref, p), slim_view(k_ref, p), slim_view(v_ref, p), arrays[-1], wide_view(do_ref, p),
                wide_view(o_ref, p), page_view(lse_ref, p), wide_view(outs[0], p), slim_view(outs[1], p),
                slim_view(outs[2], p), masked=len(own) > 0,
            )

    outs = [shaped(q.shape), shaped(k.shape), shaped(k.shape)]
    return whole_kernel(body, place, [q, k, v, do, o, lse] + own, [], outs, "cross_backward", fetch=fetch)


def project(place, own, peer, gain, wq, wk, wv):
    rows, model = own.shape
    wide, slim = wq.shape[1] // CORES, wk.shape[1] // CORES

    def body(place_ref, arrays, weight, outs, scratch):
        hidden = in_place_order(place_ref[1], arrays[0], arrays[1])
        low = norm_low(hidden, inverse_norm(hidden), arrays[2][...].astype(F32))
        outs[0][...] = low
        for at in range(3):
            outs[1 + at][...] = dot(low, weight(at)[...]).astype(BF16)

    return whole_kernel(
        body,
        place,
        [own, peer, gain],
        [(wq, 1, False), (wk, 1, False), (wv, 1, False)],
        [shaped((CORES * rows, n)) for n in (model, wide, slim, slim)],
        "project",
    )


def project_past(place, owns, peers, gain, wk, wv, fetch):
    rows, model = owns[0].shape
    earlier = len(owns)
    slim = wk.shape[1] // CORES

    def body(place_ref, arrays, weight, outs, scratch):
        own_refs, peer_refs = arrays[:earlier], arrays[earlier : 2 * earlier]
        gain_value = arrays[-1][...].astype(F32)
        for s in range(earlier):
            hidden = in_place_order(place_ref[1], own_refs[s], peer_refs[s])
            low = norm_low(hidden, inverse_norm(hidden), gain_value)
            outs[s][...] = low
            outs[earlier][s] = dot(low, weight(0)[...]).astype(BF16)
            outs[earlier + 1][s] = dot(low, weight(1)[...]).astype(BF16)

    made = whole_kernel(
        body,
        place,
        owns + peers + [gain],
        [(wk, 1, False), (wv, 1, False)],
        [shaped((CORES * rows, model))] * earlier + [shaped((earlier, CORES * rows, slim))] * 2,
        "project_past",
        fetch=fetch,
    )
    return made[:earlier], *made[earlier:]


def project_memory(place, mems, wk, wv):
    groups = len(mems)
    rows, model = mems[0].shape
    slim = wk.shape[1] // CORES

    def body(place_ref, arrays, weight, outs, scratch):
        for at, piece_ref in enumerate(arrays):
            block = jnp.bitwise_xor(place_ref[2], jnp.int32(at))
            outs[0][pl.ds(pl.multiple_of(block * rows, rows), rows)] = piece_ref[...]
        mem = outs[0][...]
        outs[1][...] = dot(mem, weight(0)[...]).astype(BF16)
        outs[2][...] = dot(mem, weight(1)[...]).astype(BF16)

    return whole_kernel(
        body,
        place,
        mems,
        [(wk, 1, False), (wv, 1, False)],
        [shaped((groups * rows, n)) for n in (model, slim, slim)],
        "project_memory",
        cost=8,
    )


def mid_forward(place, own, peer, att, att_peer, gain, wo, wo_peer, wq):
    rows, model = own.shape

    def body(place_ref, arrays, weight, outs, scratch):
        own_ref, peer_ref, att_ref, att_peer_ref, gain_ref = arrays
        hidden = in_place_order(place_ref[1], own_ref, peer_ref)
        hidden = hidden + dot(att_ref[...], weight(0)[...]) + dot(att_peer_ref[...], weight(1)[...])
        outs[0][...] = hidden.astype(BF16)
        low = norm_low(hidden, inverse_norm(hidden), gain_ref[...].astype(F32))
        outs[1][...] = low
        outs[2][...] = dot(low, weight(2)[...]).astype(BF16)

    return whole_kernel(
        body,
        place,
        [own, peer, att, att_peer, gain],
        [wo, wo_peer, wq],
        [shaped((CORES * rows, model))] * 2 + [shaped((CORES * rows, wq.shape[1]))],
        "mid_forward",
    )


def cotangent_inner(place, cot, cot_peer, wd):
    rows, model = cot.shape

    def body(place_ref, arrays, weight, outs, scratch):
        value = in_place_order(place_ref[1], arrays[0], arrays[1]).astype(BF16)
        outs[0][...] = pick(place_ref[1], value, 1)
        outs[1][...] = dot_right(value, weight(0)[...]).astype(BF16)

    outs = [shaped((CORES * rows, model // CORES)), shaped((CORES * rows, wd.shape[0]))]
    return whole_kernel(body, place, [cot, cot_peer], [wd], outs, "cotangent_inner", cost=8)


def ffn(place, mid, crs, crs_peer, gain, d_inner, wc, wc_peer, wg, wu):
    rows, model = mid.shape
    hidden_half = wg.shape[1]
    steps = [256] * (hidden_half // 256) + [hidden_half % 256] * (hidden_half % 256 > 0)
    scale = 0.7978845608028654

    def body(place_ref, arrays, weight, outs, scratch):
        mid_ref, crs_ref, crs_peer_ref, gain_ref, d_inner_ref = arrays
        late_ref, low_ref, inner_ref, dg_ref, du_ref, dz_ref = outs
        hidden = mid_ref[...].astype(F32) + dot(crs_ref[...], weight(0)[...]) + dot(crs_peer_ref[...], weight(1)[...])
        late_ref[...] = hidden.astype(BF16)
        low = norm_low(hidden, inverse_norm(hidden), gain_ref[...].astype(F32))
        low_ref[...] = low
        start = 0
        for width in steps:
            cols = slice(start, start + width)
            start += width
            gate = dot(low, weight(2)[:, cols])
            up = dot(low, weight(3)[:, cols])
            d_inner = d_inner_ref[:, cols].astype(F32)
            square = gate * gate
            bent = jnp.tanh(gate * (scale + (scale * 0.044715) * square))
            whole = 0.5 + 0.5 * bent
            slope = whole + (0.5 * gate) * (1.0 - bent * bent) * (scale + (3 * scale * 0.044715) * square)
            curve = gate * whole
            inner_ref[:, cols] = (curve * up).astype(BF16)
            dg_ref[:, cols] = (d_inner * up * slope).astype(BF16)
            du_ref[:, cols] = (d_inner * curve).astype(BF16)
        dz_ref[...] = (dot_right(dg_ref[...], weight(2)[...]) + dot_right(du_ref[...], weight(3)[...])).astype(BF16)

    return whole_kernel(
        body,
        place,
        [mid, crs, crs_peer, gain, d_inner],
        [wc, wc_peer, wg, wu],
        [shaped((rows, model))] * 2
        + [shaped((rows, hidden_half))] * 3
        + [shaped((rows, model))],
        "ffn",
        room=16 * 1024 * 1024,
    )


def late_backward(place, dz, dz_peer, late, cot, cot_peer, gain, wc):
    rows, model = late.shape

    def body(place_ref, arrays, weight, outs, scratch):
        dz_ref, dz_peer_ref, late_ref, cot_ref, cot_peer_ref, gain_ref = arrays
        dz_value = dz_ref[...].astype(F32) + dz_peer_ref[...].astype(F32)
        hidden = late_ref[...].astype(F32)
        inverse = inverse_norm(hidden)
        outs[3][...] = jnp.sum(dz_value * hidden * inverse, axis=0, keepdims=True)
        grad = in_place_order(place_ref[1], cot_ref, cot_peer_ref)
        grad = grad + norm_back(hidden, inverse, gain_ref[...].astype(F32), dz_value)
        low = grad.astype(BF16)
        outs[0][...] = low
        outs[1][...] = pick(place_ref[1], low, 1)
        outs[2][...] = dot_right(low, weight(0)[...]).astype(BF16)

    return whole_kernel(
        body,
        place,
        [dz, dz_peer, late, cot, cot_peer, gain],
        [wc],
        [
            shaped((rows, model)),
            shaped((rows, model // CORES)),
            shaped((rows, wc.shape[0])),
            shaped((1, model), F32),
        ],
        "late_backward",
    )


def mid_backward(place, dq, dq_peer, mid, g_late, gain, wq, wq_peer, wo):
    rows, model = mid.shape

    def body(place_ref, arrays, weight, outs, scratch):
        dq_ref, dq_peer_ref, mid_ref, g_ref, gain_ref = arrays
        dz = dot_right(dq_ref[...], weight(0)[...]) + dot_right(dq_peer_ref[...], weight(1)[...])
        hidden = mid_ref[...].astype(F32)
        inverse = inverse_norm(hidden)
        outs[3][...] = jnp.sum(dz * hidden * inverse, axis=0, keepdims=True)
        grad = g_ref[...].astype(F32) + norm_back(hidden, inverse, gain_ref[...].astype(F32), dz)
        low = grad.astype(BF16)
        outs[0][...] = pick(place_ref[1], low, 0)
        outs[1][...] = pick(place_ref[1], low, 1)
        outs[2][...] = dot_right(low, weight(2)[...]).astype(BF16)

    return whole_kernel(
        body,
        place,
        [dq, dq_peer, mid, g_late, gain],
        [wq, wq_peer, wo],
        [
            shaped((rows // CORES, model)),
            shaped((rows, model // CORES)),
            shaped((rows, wo.shape[0])),
            shaped((1, model), F32),
        ],
        "mid_backward",
    )


def first_backward(place, dz, past, riders, mem_parts, wk, wv):
    rows, model = dz.shape
    slim = wk.shape[1]
    own_rows = rows // CORES
    joint = riders is not None
    mem_rows = mem_parts.shape[0] // (CORES * CORES) if joint else 0

    def body(place_ref, arrays, weight, outs, scratch):
        core = place_ref[1]
        pairs = []
        if joint:
            past_at, mem_at = past[0][1], riders[0][1]
            blocks = [arrays[1][past_at + at * rows : past_at + (at + 1) * rows] for at in range(2 * slim // LANES)]
            pairs.append((jnp.concatenate(blocks[: slim // LANES], 1), jnp.concatenate(blocks[slim // LANES :], 1)))
        else:
            pairs += [(ref[0], ref[1]) for ref in arrays[1:]]
        total = arrays[0][...].astype(F32)
        for dk, dv in pairs:
            total = total + dot_right(dk, weight(0)[...]) + dot_right(dv, weight(1)[...])
        outs[0][...] = pick(core, total, 0)
        outs[1][:own_rows] = pick(core, total, 0, True).astype(BF16)
        if joint:
            half = CORES * mem_rows
            mine = pick(place_ref[2] // CORES, arrays[3][...].astype(F32), 0)
            got = [arrays[2][mem_at + at * half : mem_at + (at + 1) * half].astype(F32) for at in range(model // LANES)]
            mine = mine + jnp.concatenate(got, axis=1)
            outs[2][...] = pick(core, mine, 0)
            outs[1][own_rows:] = pick(core, mine, 0, True).astype(BF16)

    outs = [shaped((own_rows, model), F32), shaped((own_rows + mem_rows, model))]
    if joint:
        outs.append(shaped((mem_rows, model), F32))
    return whole_kernel(
        body, place, [dz] + ([past[0][0], riders[0][0], mem_parts] if joint else past), [wk, wv], outs, "first_backward"
    )


def tokens_backward(place, dz, dz_got, mem, tokens, g_mid, gain):
    rows = tokens.shape[0]

    def body(place_ref, arrays, weight, outs, scratch):
        dz_ref, dz_got_ref, tokens_ref, g_ref, gain_ref = arrays[:5]
        dz_value = dz_ref[...] + dz_got_ref[:rows].astype(F32)
        hidden = tokens_ref[...].astype(F32)
        grad = norm_back(hidden, inverse_norm(hidden), gain_ref[...].astype(F32), dz_value)
        outs[0][...] = (g_ref[...].astype(F32) + grad).astype(BF16)
        if mem:
            outs[1][...] = (arrays[5][...] + dz_got_ref[rows:].astype(F32)).astype(BF16)

    outs = [shaped(tokens.shape)] + [shaped(m.shape) for m in mem]
    return whole_kernel(body, place, [dz, dz_got, tokens, g_mid, gain] + mem, [], outs, "tokens_backward")


def layer_output(place, late, inner, inner_peer, wd, wd_peer):
    rows, model = late.shape

    def body(place_ref, arrays, weight, outs, scratch):
        own, inner_own, inner_other = (pick(place_ref[1], ref[...], 0) for ref in arrays)
        total = own.astype(F32) + dot(inner_own, weight(0)[...]) + dot(inner_other, weight(1)[...])
        outs[0][...] = total.astype(BF16)

    return whole_kernel(
        body,
        place,
        [late, inner, inner_peer],
        [wd, wd_peer],
        [shaped((rows // CORES, model))],
        "layer_output",
        cost=10,
    )[0]


def memory_backward(place, dk, dv, wk, wv):
    def body(place_ref, arrays, weight, outs, scratch):
        grad = dot_right(arrays[0][...], weight(0)[...]) + dot_right(arrays[1][...], weight(1)[...])
        outs[0][...] = grad.astype(BF16)

    weights = [(wk, 1, False), (wv, 1, False)]
    return whole_kernel(body, place, [dk, dv], weights, [shaped((dk.shape[0], wk.shape[0]))], "memory_backward")[0]


def small_sums(place, dq, dk, dv, d_past, own, peer, past_own, past_peer, two, three, near, total, buckets, weights, chips, fetch):
    rows, model = dq.shape[0], own.shape[1]
    earlier = len(past_own)
    heads = HEADS // CORES

    def body(place_ref, arrays, weight, outs, scratch):
        dq_ref, dk_ref, dv_ref, past_ref, own_ref, peer_ref = arrays[:6]
        past_own_refs, past_peer_refs = arrays[6 : 6 + earlier], arrays[6 + earlier : 6 + 2 * earlier]
        two_ref, three_ref, near_ref, total_ref, bucket_ref = arrays[6 + 2 * earlier :]
        core = place_ref[1]
        first = core == 0

        def gain_part(dz, own_ref, peer_ref):
            hidden = in_place_order(core, own_ref, peer_ref)
            return jnp.sum(dz * (hidden * inverse_norm(hidden)), axis=0, keepdims=True)

        dz = dot_right(dq_ref[...], weight(0)[...])
        dz = dz + dot_right(dk_ref[...], weight(1)[...]) + dot_right(dv_ref[...], weight(2)[...])
        outs[0][...] = dz.astype(BF16)
        one = gain_part(dz, own_ref, peer_ref)
        for s in range(earlier):
            dz = dot_right(past_ref[s, 0], weight(1)[...]) + dot_right(past_ref[s, 1], weight(2)[...])
            one = one + gain_part(dz, past_own_refs[s], past_peer_refs[s])
        gains = [one, jnp.where(first, two_ref[...], 0.0), jnp.where(first, three_ref[...], 0.0)]
        near = jnp.concatenate([near_ref[p, :4] for p in range(heads // 4)], axis=0)
        total = jnp.concatenate([total_ref[p, :4] for p in range(heads // 4)], axis=0)
        far = jnp.sum(total, axis=1, keepdims=True) - jnp.sum(near, axis=1, keepdims=True)
        last = lax.broadcasted_iota(jnp.int32, near.shape, 1) == near.shape[1] - 1
        near = near + jnp.where(last, far, 0.0)
        entries = BUCKETS * HEADS
        entry = lax.broadcasted_iota(jnp.int32, (near.shape[1], entries), 1)
        same = (lax.shift_right_logical(entry, jnp.int32(HEADS.bit_length() - 1)) == bucket_ref[...]).astype(F32)
        sums = jnp.dot(near, same, precision=lax.Precision.HIGHEST, preferred_element_type=F32)
        head = lax.broadcasted_iota(jnp.int32, sums.shape, 0) + core * heads
        of_entry = jnp.bitwise_and(lax.broadcasted_iota(jnp.int32, sums.shape, 1), jnp.int32(HEADS - 1))
        vectors = gains + [jnp.sum(jnp.where(head == of_entry, sums, 0.0), axis=0, keepdims=True)]
        for block in range(chips):
            lines = []
            for vector in vectors:
                size = vector.shape[1] // chips
                line = vector[:, block * size : (block + 1) * size]
                lines.append(jnp.concatenate([line, jnp.zeros((1, LANES - size), F32)], axis=1))
            lines.append(jnp.zeros((12, LANES), F32))
            outs[1][block * 16 : (block + 1) * 16] = jnp.concatenate(lines, axis=0).astype(BF16)

    arrays = [dq, dk, dv, d_past, own, peer] + past_own + past_peer + [two, three, near, total, buckets]
    return whole_kernel(
        body, place, arrays, weights, [shaped((rows, model)), shaped((chips * 16, LANES))], "small_sums", fetch=fetch
    )


def gather_sums(place, parts, name):
    def body(place_ref, arrays, weight, outs, scratch):
        for array, out in zip(arrays, outs):
            total = array[0].astype(F32)
            for at in range(1, array.shape[0]):
                total = total + array[at].astype(F32)
            out[...] = total.astype(out.dtype)

    return whole_kernel(body, place, parts, [], [shaped(a.shape[1:], a.dtype) for a in parts], name)


def up_to(value, multiple):
    return (value + multiple - 1) // multiple * multiple


def array_of(y):
    return y[0] if isinstance(y, tuple) else y


class Flow:
    def __init__(self, name, pieces, order, extra=None):
        self.name, self.pieces, self.order, self.extra = name, pieces, order, extra
        self.hops = [bit + 1 for bit in order]
        self.chips = 1 << len(order)
        self.layout = []
        start = 0
        for terms, rows in pieces:
            half = rows // self.chips // CORES
            padded = up_to(half, 8)
            width = array_of(terms[0][1]).shape[-1]
            self.layout.append((start, half, padded, width))
            start += CORES * padded * (width // LANES)
        self.extra_at = start
        self.rows = start + (16 if extra is not None else 0)
        self.keep = self.got = None

    def spread(self, x):
        half, padded = self.layout[0][1:3]
        if half == padded:
            return x
        chunks = x.reshape(x.shape[0], -1, half)
        return jnp.pad(chunks, ((0, 0), (0, 0), (0, padded - half))).reshape(x.shape[0], -1)


def chip_of(spot, order):
    number = 0
    for at, bit in enumerate(order):
        number |= (spot >> (len(order) - 1 - at) & 1) << bit
    return number


def sum_flow(flow, refs_of, place_ref, turned, free, send_ref, base, keep_ref):
    chip, core = place_ref[0], place_ref[1]
    half = flow.chips // 2
    for (terms, _), (start, _, padded, width) in zip(flow.pieces, flow.layout):
        chunk = CORES * padded
        lefts = []
        for xs, y in terms:
            key = (tuple(id(x) for x in xs), flow.order)
            if key not in turned:
                straight_ref, turned[key] = free.pop(0), free.pop(0)
                if len(xs) == 1:
                    straight_ref[...] = refs_of[id(xs[0])][...].T
                else:
                    size = straight_ref.shape[0] // CORES
                    for part, x in enumerate(xs):
                        at = (core if part == 0 else 1 - core) * size
                        straight_ref[pl.ds(pl.multiple_of(at, 16), size)] = refs_of[id(x)][...].T
                for spot in range(flow.chips):
                    at = jnp.bitwise_xor(jnp.int32(chip_of(spot, flow.order)), chip) * chunk
                    turned[key][spot * chunk : (spot + 1) * chunk] = straight_ref[pl.ds(pl.multiple_of(at, 16), chunk)]
            lefts.append(turned[key])
        count = max(1, min(flow.chips, 512 // chunk))
        while flow.chips % count:
            count -= 1
        for first in range(0, flow.chips, count):
            tile = None
            for left, (_, y) in zip(lefts, terms):
                y_ref = refs_of[id(array_of(y))]
                y_value = y_ref[y[1]] if isinstance(y, tuple) else y_ref[...]
                term = dot(left[first * chunk : (first + count) * chunk], y_value)
                tile = term if tile is None else tile + term
            tile = tile.astype(BF16)
            for inner in range(count):
                spot = first + inner
                for block in range(width // LANES):
                    value = tile[inner * chunk : (inner + 1) * chunk, block * LANES : (block + 1) * LANES]
                    at = start + block * chunk
                    if spot < half:
                        keep_ref[spot, at : at + chunk] = value
                    else:
                        at += base + (spot - half) * flow.rows
                        send_ref[at : at + chunk] = value


def copy_extra(flow, extra_ref, place_ref, send_ref, base, keep_ref):
    half = flow.chips // 2
    for spot in range(flow.chips):
        at = jnp.bitwise_xor(jnp.int32(chip_of(spot, flow.order)), place_ref[0]) * 16
        value = extra_ref[pl.ds(pl.multiple_of(at, 16), 16)]
        if spot < half:
            keep_ref[spot, flow.extra_at : flow.extra_at + 16] = value
        else:
            to = base + (spot - half) * flow.rows + flow.extra_at
            send_ref[to : to + 16] = value


def add_flow(flow, old_ref, got_ref, got_at, send_ref, base, keep_ref):
    half = old_ref.shape[0] // 2
    for spot in range(2 * half):
        at = got_at + spot * flow.rows
        total = (old_ref[spot].astype(F32) + got_ref[at : at + flow.rows].astype(F32)).astype(BF16)
        if spot < half:
            keep_ref[spot] = total
        else:
            send_ref[base + (spot - half) * flow.rows : base + (spot - half + 1) * flow.rows] = total


def hop(place, swap, sums, adds, after, name, cost=0, riders=(), fetch=()):
    arrays, seen = [], {}

    def take(array):
        if id(array) not in seen:
            seen[id(array)] = len(arrays)
            arrays.append(array)

    for flow in sums:
        for terms, _ in flow.pieces:
            for xs, y in terms:
                for array in (*xs, array_of(y)):
                    take(array)
        if flow.extra is not None:
            take(flow.extra)
    for flow in adds:
        take(flow.keep)
        take(flow.got[0])
    bits, sends, keeps = {}, {}, {}
    for flow in sums + adds:
        half = (flow.chips if flow in sums else flow.keep.shape[0]) // 2
        bit = flow.hops[0]
        base = bits.setdefault(bit, 0)
        sends[flow.name] = (bit, base)
        bits[bit] = base + half * flow.rows
        keeps[flow.name] = shaped((half, flow.rows, LANES))
    rider_at = []
    for rider, bit, size, _ in riders:
        take(rider)
        rider_at.append(bits.setdefault(bit, 0))
        bits[bit] = rider_at[-1] + size
    order = list(bits)
    outs = [shaped((bits[bit], LANES)) for bit in order] + list(keeps.values())

    def body(place_ref, refs, weight, out_refs, scratch):
        refs_of = {key: refs[at] for key, at in seen.items()}
        turned, free = {}, list(scratch)
        for at, flow in enumerate(sums + adds):
            bit, base = sends[flow.name]
            send_ref, keep_ref = out_refs[order.index(bit)], out_refs[len(order) + at]
            if flow in sums:
                sum_flow(flow, refs_of, place_ref, turned, free, send_ref, base, keep_ref)
                if flow.extra is not None:
                    copy_extra(flow, refs_of[id(flow.extra)], place_ref, send_ref, base, keep_ref)
            else:
                add_flow(
                    flow, refs_of[id(flow.keep)], refs_of[id(flow.got[0])], flow.got[1], send_ref, base, keep_ref
                )
        for (rider, bit, _, write), at in zip(riders, rider_at):
            write(refs_of[id(rider)], out_refs[order.index(bit)], at, place_ref)

    needed = {}
    for flow in sums:
        for terms, _ in flow.pieces:
            for xs, _ in terms:
                shape = (sum(x.shape[1] for x in xs), xs[0].shape[0])
                needed[(tuple(id(x) for x in xs), flow.order)] = [pltpu.VMEM(shape, BF16)] * 2
    scratch = sum(needed.values(), [])
    made = whole_kernel(body, place, follow(arrays, after), [], outs, name, scratch, cost=cost, fetch=fetch)
    moved = [swap(array, bit) for array, bit in zip(made, order)]
    for at, flow in enumerate(sums + adds):
        bit, base = sends[flow.name]
        flow.keep, flow.got, flow.hops = made[len(order) + at], (moved[order.index(bit)], base), flow.hops[1:]
    if riders:
        return list(made), [(moved[order.index(bit)], at) for (_, bit, _, _), at in zip(riders, rider_at)]
    return list(made)


def write_flat(ref, send_ref, at, place_ref):
    send_ref[at : at + ref.shape[0]] = ref[...]


def write_past(past_ref, send_ref, at, place_ref):
    _, pages, rows, width = past_ref.shape
    for page in range(pages):
        for block in range(width // LANES):
            send_ref[at : at + rows] = past_ref[0, page, :, block * LANES : (block + 1) * LANES]
            at += rows


def write_memory(mem_ref, send_ref, at, place_ref):
    rows = mem_ref.shape[0] // CORES
    there = pl.ds(pl.multiple_of((1 - place_ref[2] // CORES) * rows, rows), rows)
    for block in range(mem_ref.shape[1] // LANES):
        send_ref[at : at + rows] = mem_ref[there, block * LANES : (block + 1) * LANES]
        at += rows


def last_hop(place, swap, flows, after, name, shares=()):
    arrays, seen = [], {}
    for flow in flows:
        for array in (flow.keep, flow.got[0]):
            if id(array) not in seen:
                seen[id(array)] = len(arrays)
                arrays.append(array)
    blocks = []
    size = 0
    for f, flow in enumerate(flows):
        for piece, (start, half, padded, width) in enumerate(flow.layout):
            for block in range(width // LANES):
                blocks.append((f, piece, start + block * CORES * padded, padded, block, size))
                size += up_to(padded, 16)
    extras = [(f, flow.extra_at, size + 16 * sum(x.extra is not None for x in flows[:f])) for f, flow in enumerate(flows) if flow.extra is not None]
    size += 16 * len(extras)
    own_outs = [
        shaped((padded, width), F32) for flow in flows for _, _, padded, width in flow.layout
    ]
    own_outs += [shaped((16, LANES), F32) for _ in extras]
    n_pieces = len(own_outs) - len(extras)
    first = [sum(len(flow.layout) for flow in flows[:f]) for f in range(len(flows))]

    def add_body(place_ref, refs, weight, outs, scratch):
        core = place_ref[1]
        for f, piece, at, padded, block, leave_at in blocks:
            flow = flows[f]
            got_at = flow.got[1] + at
            total = refs[seen[id(flow.keep)]][0, at : at + CORES * padded].astype(F32)
            total = total + refs[seen[id(flow.got[0])]][got_at : got_at + CORES * padded].astype(F32)
            own, leave = pick(core, total, 0), pick(core, total, 0, True)
            outs[1 + first[f] + piece][:, block * LANES : (block + 1) * LANES] = own
            full = up_to(padded, 16)
            if full > padded:
                leave = jnp.concatenate([leave, jnp.zeros((full - padded, LANES), F32)], axis=0)
            outs[0][leave_at : leave_at + full] = leave.astype(BF16)
        for at, (f, start, leave_at) in enumerate(extras):
            flow = flows[f]
            got_at = flow.got[1] + start
            total = refs[seen[id(flow.keep)]][0, start : start + 16].astype(F32)
            total = total + refs[seen[id(flow.got[0])]][got_at : got_at + 16].astype(F32)
            outs[1 + n_pieces + at][...] = total
            outs[0][leave_at : leave_at + 16] = total.astype(BF16)

    made = whole_kernel(add_body, place, follow(arrays, after), [], [shaped((size, LANES))] + own_outs, "last_" + name)
    got = swap(made[0], 0)

    def join_body(place_ref, refs, weight, outs, scratch):
        core = place_ref[1]
        for f, piece, _, padded, block, leave_at in blocks:
            at = first[f] + piece
            width = refs[1 + at].shape[1]
            own = refs[1 + at][:, block * LANES : (block + 1) * LANES]
            other = refs[0][leave_at : leave_at + up_to(padded, 16)].astype(F32)[:padded]
            low, high = slice(block * LANES, (block + 1) * LANES), slice(width + block * LANES, width + (block + 1) * LANES)
            outs[at][:, low] = jnp.where(core == 0, own, other)
            outs[at][:, high] = jnp.where(core == 0, other, own)
        for at, (_, _, leave_at) in enumerate(extras):
            total = refs[1 + n_pieces + at][...] + refs[0][leave_at : leave_at + 16].astype(F32)
            for line, (out, share) in enumerate(zip(outs[n_pieces:], shares)):
                out[...] = jnp.where(core == 0, total[line, :share], total[line, share : 2 * share])

    joined = whole_kernel(
        join_body,
        place,
        [got] + list(made[1:]),
        [],
        [shaped((a.shape[0], CORES * a.shape[1]), F32) for a in own_outs[:n_pieces]]
        + [shaped((share,), F32) for _ in extras for share in shares],
        "join_" + name,
    )
    results = {}
    for f, flow in enumerate(flows):
        results[flow.name] = [
            joined[first[f] + piece][:half] for piece, (_, half, _, _) in enumerate(flow.layout)
        ]
    if extras:
        results["small"] = joined[n_pieces:]
    return results, list(made)


def follow(value, after):
    return lax.optimization_barrier((value, after))[0]


def rel_bucket(distance):
    beyond = 16 + sum((distance >= border).astype(jnp.int32) for border in THRESHOLDS)
    return jnp.where(distance < 16, distance, beyond)


def shards(
    tokens, memory, cotangent, bucket, gain_self, self_query, self_key, self_value, self_out, rel_bias,
    gain_cross, cross_query, cross_key, cross_value, cross_out, gain_ffn, ffn_gate, ffn_up, ffn_down,
):
    groups = lax.axis_size("grp")
    dp_size = lax.axis_size("dp")
    n_chips = groups // CORES
    more = n_chips - 1
    chips = dp_size * n_chips
    devices = chips * CORES
    grp_at = lax.axis_index("grp")
    core = grp_at % CORES
    y_at = grp_at // CORES
    chip = lax.axis_index("dp") * n_chips + y_at
    rows, model = tokens.shape
    chip_rows = rows * CORES
    group_rows = chip_rows * n_chips
    hidden_units = ffn_down.shape[0]
    length = jnp.minimum(group_rows, jnp.maximum(SHORT, jnp.right_shift(jnp.int32(group_rows), bucket[0])))
    y_bits = n_chips.bit_length() - 1
    bits = chips.bit_length() - 1
    first_chip = y_at * chip_rows // length * length // chip_rows
    valid = [(y_at - s >= first_chip).astype(jnp.int32) for s in range(1, n_chips)]
    place = jnp.stack([chip, core, grp_at] + valid).astype(jnp.int32)

    def swap(v, bit):
        return lax.ppermute(v, ("dp", "grp"), [(i, i ^ (1 << bit)) for i in range(devices)])

    gain_one, gain_two, gain_three = (g.reshape(1, model) for g in (gain_self, gain_cross, gain_ffn))

    past_own = [
        lax.ppermute(tokens, "grp", [(g, g + CORES * s) for g in range(groups - CORES * s)]) for s in range(1, n_chips)
    ]
    tokens_peer = swap(tokens, 0)
    mems = [memory] + [
        lax.ppermute(memory, "grp", [(g, g ^ other) for g in range(groups)]) for other in range(1, groups)
    ]

    distances = jnp.arange(2 * NEAR, dtype=jnp.int32)
    buckets = rel_bucket(distances)[:, None]
    onehot = (buckets == jnp.arange(BUCKETS, dtype=jnp.int32)).astype(F32)
    heads = HEADS // CORES
    rel_local = lax.dynamic_slice_in_dim(rel_bias.astype(F32), core * heads, heads, 1)
    by_dist = jnp.dot(onehot, rel_local - rel_local[BUCKETS - 1 :], precision=lax.Precision.HIGHEST)
    table = jnp.pad(by_dist.T.reshape(heads // 4, 4, 2 * NEAR), ((0, 0), (0, 4), (0, 0)))

    low_one, q, k, v = project(place, tokens, tokens_peer, gain_one, self_query, self_key, self_value)
    *diagonal, w_gate, w_up = self_diagonal(place, table, q, k, v, [(ffn_gate, 1, False), (ffn_up, 1, False)])
    past_own = follow(past_own, diagonal)
    past_peer = [swap(own, 0) for own in past_own]
    cot_peer = swap(follow(cotangent, diagonal[0]), 0)
    low_past, k_past, v_past, w_down = project_past(
        place, past_own, past_peer, gain_one, self_key, self_value, [(ffn_down, 0, False)]
    )
    att, lse_self, w_out, w_out_peer, w_query, w_cross, w_cross_peer = self_past(
        place, table, q, k_past, v_past, *diagonal,
        [(self_out, 0, False), (self_out, 0, True), (cross_query, 1, False), (cross_out, 0, False), (cross_out, 0, True)],
    )
    att_peer = swap(att, 0)
    mem_all, km, vm = project_memory(place, follow(mems, att), cross_key, cross_value)
    att_peer = follow(att_peer, km)
    mid, low_two, cq = mid_forward(
        place, tokens, tokens_peer, att, att_peer, gain_two, w_out, w_out_peer, w_query
    )
    own_doc = []
    if group_rows > SHORT:
        mem_doc = jnp.arange(mem_all.shape[0], dtype=jnp.int32) // (length // RATIO)
        own = (mem_doc == y_at * chip_rows // length).astype(F32)
        own_doc = [jnp.broadcast_to(own[:, None], (mem_all.shape[0], TILE))]
    crs, lse_cross = cross_forward(place, cq, km, vm, own_doc)
    crs_peer = swap(crs, 0)
    cot_half, d_inner = cotangent_inner(place, follow(cotangent, crs), cot_peer, w_down)
    crs_peer = follow(crs_peer, d_inner)
    late, low_three, inner, d_gate, d_up, dz = ffn(
        place, mid, crs, crs_peer, gain_three, d_inner, w_cross, w_cross_peer, w_gate, w_up
    )

    axes = {
        "y": tuple(range(y_bits)),
        "x": (y_bits,),
        "z": (y_bits + 1,),
        "f": tuple(range(y_bits + 2, bits)),
    }

    def order_of(letters):
        return sum((axes[letter] for letter in letters), ())

    dz_peer = swap(dz, 0)
    inner_peer = swap(inner, 0)
    gate = Flow("gate", [([((low_three,), d_gate)], model)], order_of("xyzf"))
    last = hop(place, swap, [gate], [], place, "gate")
    down = Flow("down", [([((inner, inner_peer), cot_half)], hidden_units)], order_of("zxyf"))
    spread = (down.spread(inner), down.spread(inner_peer))
    down = Flow("down", [([(spread, cot_half)], hidden_units)], order_of("zxyf"))
    last = hop(place, swap, [down], [], last, "down")
    up = Flow("up", [([((low_three,), d_up)], model)], order_of("yzfx"))
    last = hop(place, swap, [up], [], last, "up")
    ffn_flows = [gate, up, down]

    g_late, late_half, d_crs, d_gain_three = late_backward(
        place, follow(dz, last), dz_peer, late, cotangent, cot_peer, gain_three, w_cross
    )
    dcq, dkm, dvm, w_query_peer = cross_backward(
        place, cq, km, vm, own_doc, d_crs, crs, lse_cross, [(cross_query, 1, True)]
    )
    dcq_peer = swap(dcq, 0)
    crs_mem = Flow(
        "crs_mem",
        [([((crs, crs_peer), late_half)], model), ([((mem_all,), dkm)], model), ([((mem_all,), dvm)], model)],
        order_of("zxyf"),
    )
    last = hop(place, swap, [crs_mem], [], dcq, "crs_mem", cost=5)
    g_mid, mid_half, d_att, d_gain_two = mid_backward(
        place, dcq, follow(dcq_peer, last), mid, g_late, gain_two, w_query, w_query_peer, w_out
    )
    att_cq = Flow("att_cq", [([((att, att_peer), mid_half)], model), ([((low_two,), dcq)], model)], order_of("xyzf"))
    last = hop(place, swap, [att_cq], [], d_att, "att_cq")
    dq, dk, dv, d_past, d_near, d_total, *w_first = self_backward(
        place, table, q, k, v, k_past, v_past, follow(d_att, last), att, lse_self,
        [(self_query, 1, False), (self_key, 1, False), (self_value, 1, False)],
    )
    mem_parts = memory_backward(place, follow(dkm, dq), dvm, cross_key, cross_value)
    past_moved, riders = [], None
    if n_chips == 2:
        y_bit = 1
        last, (riders,) = hop(
            place, swap, [], ffn_flows, mem_parts, "ffn_1",
            riders=[(mem_parts, y_bit, mem_parts.size // CORES // LANES, write_memory)],
        )
    else:
        past_moved = [
            lax.ppermute(d_past[s - 1], "grp", [(g, g - CORES * s) for g in range(CORES * s, groups)])
            for s in range(1, n_chips)
        ]
        last = hop(place, swap, [], ffn_flows, mem_parts, "ffn_1")
    dz, small, w_down, w_down_peer = small_sums(
        place, follow(dq, last), dk, dv, d_past, tokens, tokens_peer, past_own, past_peer, d_gain_two, d_gain_three,
        d_near, d_total, buckets, w_first, chips, [(ffn_down, 0, False), (ffn_down, 0, True)],
    )
    query = Flow("query", [([((low_one,), dq)], model)], order_of("xyzf"), small)
    kv = Flow(
        "kv",
        [
            ([((low_one,), d)] + [((low_past[s],), (d_past, (s, which))) for s in range(more)], model)
            for which, d in ((0, dk), (1, dv))
        ],
        order_of("yxzf"),
    )
    attention = [att_cq, crs_mem, query, kv]
    last = hop(place, lambda v, bit: v, [query, kv], [], dz, "query_kv")
    sent = [(flow.got[0], flow.order[0] + 1, flow.got[0].shape[0], write_flat) for flow in (query, kv)]
    last, (query.got, kv.got) = hop(
        place, swap, [], [att_cq, crs_mem], last, "attention_1", cost=5, riders=sent
    )

    results = {}
    names = {"ffn": ffn_flows, "attention": attention}

    def step(label, after, riders=(), fetch=()):
        flows = names[label]
        if label in results:
            return after
        moving = [flow for flow in flows if flow.hops]
        if moving:
            return hop(place, swap, [], moving, after, f"{label}_{len(moving[0].hops)}", cost=30, riders=riders, fetch=fetch)
        results[label], made = last_hop(place, swap, flows, after, label, [model // devices] * 3 + [BUCKETS * HEADS // devices])
        return made

    for label in ("ffn", "attention", "ffn"):
        last = step(label, last)
    if n_chips == 2:
        last, (past_rider,) = step("attention", last, [(d_past, y_bit, d_past.size // LANES, write_past)])
        past_moved, riders = [past_rider], [riders]
    else:
        last = step("attention", last)
    waiting = True
    while len(results) < 2:
        if "attention" not in results and not any(flow.hops for flow in attention):
            last = last + sum(results.get("ffn", {}).values(), [])
        last = step("ffn", last)
        if waiting and not any(flow.hops for flow in attention):
            waiting = False
            dz_own, dz_leave, *mem_own = first_backward(
                place, follow(dz, last), past_moved, riders, mem_parts, *w_first[1:]
            )
            dz_got = swap(dz_leave, 0)
            layer_out = layer_output(place, follow(late, dz_leave), inner, inner_peer, w_down, w_down_peer)
            dz_got = follow(dz_got, layer_out)
            grad_tokens, *grad_memory = tokens_backward(place, dz_own, dz_got, mem_own, tokens, g_mid, gain_one)
            if not grad_memory:
                parts = lax.all_to_all(mem_parts, "grp", split_axis=0, concat_axis=0, tiled=True)
                grad_memory = gather_sums(place, [parts.reshape(groups, -1, model)], "memory_sums")
            last = last + [grad_tokens]
        last = step("attention", last)
    got = {**results["ffn"], **results["attention"]}
    *gains, relative = got["small"]
    return (
        layer_out,
        grad_tokens,
        grad_memory[0],
        gains[0],
        got["query"][0],
        got["kv"][0],
        got["kv"][1],
        got["att_cq"][0],
        relative,
        gains[1],
        got["att_cq"][1],
        got["crs_mem"][1],
        got["crs_mem"][2],
        got["crs_mem"][0],
        gains[2],
        got["gate"][0],
        got["up"][0],
        got["down"][0],
    )


def solution(mesh):
    rows = P(("dp", "grp"), None)
    flat = P(("dp", "grp"))
    in_specs = (rows, rows, rows, P("dp")) + (P(),) * 15
    out_specs = (rows,) * 3 + (flat,) + (rows,) * 4 + (flat,) * 2 + (rows,) * 4 + (flat,) + (rows,) * 3
    return jax.shard_map(shards, mesh=mesh, in_specs=in_specs, out_specs=out_specs, check_vma=False)
```
